32 devices in a mesh: cell: 2 (over core), panel: 2 (over x), sc: 8 (over z, y).
Axes of the slice: x: 2, y: 2, z: 4, core: 2. Of those that a mesh axis runs over, the one named last changes fastest.
Arguments:
- channel: bfloat16 [4, 256, 2, 1024, 128], P('cell', 'sc', None, 'panel'), may hold values from -0.1875 to 0.1875
- received: bfloat16 [4, 256, 2, 14, 1024], P('cell', 'sc', None, None, 'panel'), may hold values from -6 to 6
- noise_power: float32 [4], P('cell'), may hold values from 0.05 to 0.5
- user_count: int32 [4, 16], P('cell', 'sc'), may hold values from 32 to 128
- serving_cell: int32 [4, 128, 1], P('cell'), may hold values from 0 to 3; in each aligned block of 256 rows (0 to 255, 256 to 511, ..., all dimensions but the last counted through in order) at most 128 rows name the same one
Outputs:
- routed_symbols: bfloat16 [4, 256, 2, 14, 256], P('cell', 'sc')
The draws below stay inside these ranges and needn't reach their ends.
Inputs may be any that keep to these rules, and one draw needn't show every extreme that they name: `serving_cell`: at most 128 user slots of one block of 2 consecutive cells name the same serving cell, and in every draw some serving cell is named exactly 128 times by one block.
All inputs are finite; a program needn't handle non-finite values.
Results may differ from the reference program's by a relative error of at most 0.0057.
Values may be sent and summed in bfloat16 or wider, within the bound.
No kernel may reach another device: no remote copies, remote signals or barrier semaphores. Data moves between devices by JAX's collectives and lax.ppermute only.
A program may use at most 128 MiB of HBM per device.

```python
import math
import jax
import jax.numpy as jnp
import numpy as np
from jax import lax

CELLS_PER_PART = 2
ANTENNA_COUNT = 1024
USER_SLOTS = 128
SYMBOL_COUNT = 14
GRP = 16
ITERS = 2
CELL_COUNT = 4
SUBCARRIER_COUNT = 256
GROUPS = 16
CAP = 128
SLOTS = 256
N_CELL = 2


def plant(result, key, smallest, top_value):
    longest = result.shape.index(max(result.shape))
    spots = []
    for shift in (0, 1):
        where = [jax.random.randint(jax.random.fold_in(key, axis), (), 0, length) for axis, length in enumerate(result.shape)]
        where[longest] = (where[longest] + shift) % result.shape[longest]
        spots.append(tuple(where))
    return result.at[spots[0]].set(smallest).at[spots[1]].set(top_value)


def levels(key, extent, cuts, least, largest):
    level, own = 1.0, jax.random.fold_in(key, 6)
    for axis_at, parts in cuts:
        heights = jnp.exp(jax.random.uniform(jax.random.fold_in(own, axis_at), (parts,), jnp.float32, least / len(cuts), largest / len(cuts)))
        level = level * jnp.repeat(heights, extent[axis_at] // parts).reshape([-1 if axis == axis_at else 1 for axis in range(len(extent))])
    return level


def shared_out(own_key, own, number, rows, count, top, bound, slope):
    order = jax.random.permutation(own_key, count)
    crowded, common = load_shares(count, rows * top, bound, slope, True), load_shares(count, rows * top, bound, slope, False)
    places = jnp.arange(count)

    def named(sizes, turn):
        used = int((sizes > 0).sum())
        fixed = max(1, used // 4)
        moved = fixed + (places - fixed + turn * (used - fixed)) % max(1, count - fixed)
        return jnp.zeros((count,), jnp.int32).at[order[jnp.where(places < fixed, places, moved)]].set(jnp.asarray(sizes, jnp.int32))

    sizes = jnp.where(number % 4 == 0, named(crowded, number // 4), named(common, number - number // 4 - 1))
    mixed = jax.random.permutation(jax.random.fold_in(own, 3), count)
    donor, sink = mixed[0:count // 2 * 2:2], mixed[1:count // 2 * 2:2]
    room = jnp.minimum(sizes[donor] - 1, bound - sizes[sink]) // 2
    room = jnp.where((donor == order[0]) | (sink == order[0]) | (sizes[sink] == 0), 0, jnp.maximum(room, 0))
    moved = jax.random.randint(jax.random.fold_in(own, 4), (count // 2,), 0, 1 << 20) % (room + 1)
    sizes = sizes.at[donor].add(-moved).at[sink].add(moved)
    labels = jnp.searchsorted(jnp.cumsum(sizes), jnp.arange(rows * top), side="right").astype(jnp.int32)
    grid = labels.reshape(top, rows).T
    grid = grid[jax.random.permutation(jax.random.fold_in(own, 1), rows)]
    turn = jax.random.randint(jax.random.fold_in(own, 2), (rows, 1), 0, top)
    return jnp.take_along_axis(grid, (jnp.arange(top)[None, :] + turn) % top, axis=1)


def load_shares(amount, total, bound, lean, full):
    portions = [(1 << 20) // math.isqrt(standing ** lean) + 1 for standing in range(1, amount + 1)]
    largest = bound if full else min(bound, max(-(-total // amount), total * portions[0] // sum(portions)))
    least = 1 if total - largest >= amount - 1 else 0
    given, rest = [largest] + [least] * (amount - 1), total - largest - least * (amount - 1)
    while rest > 0:
        movable = [i for i in range(1, amount) if given[i] < largest] or [i for i in range(1, amount) if given[i] < bound]
        pool, budget = sum([portions[i] for i in movable]), rest
        for i in movable:
            addition = min(bound - given[i], max(1, budget * portions[i] // pool), rest)
            given[i] = given[i] + addition
            rest = rest - addition
    return np.array(given)


def gaussian(own_key, shape, scale, reach, pieces=(), held_as=jnp.bfloat16):
    entries = scale * jax.random.normal(own_key, shape, jnp.float32)
    if pieces:
        entries = entries * levels(own_key, shape, pieces, -0.22, 0.18)
    return jnp.clip(entries, -reach, reach).astype(held_as)


def setup_inputs(seed: int = 0) -> dict:
    seeds = jax.random.split(jax.random.key(seed), 6)
    channel = gaussian(seeds[0], (CELL_COUNT, SUBCARRIER_COUNT, 2, ANTENNA_COUNT, USER_SLOTS), ANTENNA_COUNT ** -0.5, 0.1875, ((0, 2), (1, 8), (3, 2)))
    received = gaussian(seeds[1], (CELL_COUNT, SUBCARRIER_COUNT, 2, SYMBOL_COUNT, ANTENNA_COUNT), 1.0, 6.0, ((0, 2), (1, 8), (4, 2)))
    noise_power = jnp.clip(jnp.exp(math.log(0.5) - 2.3025851 * jax.random.uniform(seeds[2], (CELL_COUNT,), jnp.float32) ** levels(seeds[2], (CELL_COUNT,), ((0, 2),), -0.2, 0.2)), 0.05, 0.5)
    user_count = plant(jax.random.randint(seeds[3], (CELL_COUNT, GROUPS), USER_SLOTS // 4, USER_SLOTS + 1), jax.random.fold_in(seeds[3], 1), USER_SLOTS // 4, USER_SLOTS).astype(jnp.int32)
    serving_cell_keys = jax.random.split(jax.random.fold_in(seeds[4], 1), CELL_COUNT * USER_SLOTS // (CELLS_PER_PART * USER_SLOTS))
    serving_cell_turns = jax.random.permutation(jax.random.fold_in(seeds[4], 3), CELL_COUNT * USER_SLOTS // (CELLS_PER_PART * USER_SLOTS))
    serving_cell = jax.vmap(lambda own, number: shared_out(jax.random.fold_in(seeds[4], 2), own, number, CELLS_PER_PART * USER_SLOTS, CELL_COUNT, 1, CAP, 2))(serving_cell_keys, serving_cell_turns).reshape((CELL_COUNT, USER_SLOTS, 1))
    return {"channel": channel, "received": received, "noise_power": noise_power, "user_count": user_count, "serving_cell": serving_cell}


def adjoint_apply(matrix, vector):
    products = jnp.einsum('faku,fbsk->fabsu', matrix, vector, precision=lax.Precision.HIGHEST)
    return jnp.stack((products[:, 0, 0] + products[:, 1, 1], products[:, 0, 1] - products[:, 1, 0]), axis=1)


def apply_channel(matrix, vector):
    products = jnp.einsum('faku,fbsu->fabsk', matrix, vector, precision=lax.Precision.HIGHEST)
    return jnp.stack((products[:, 0, 0] - products[:, 1, 1], products[:, 0, 1] + products[:, 1, 0]), axis=1)


def round_half(values):
    return lax.optimization_barrier(values.astype(jnp.bfloat16)).astype(jnp.float32)


def user_sum(left, right):
    return jnp.sum(left * right, axis=(1, 3))


def widen(values):
    return values[:, None, :, None]


def detect_cell(inputs):
    channel, received, noise, counts = inputs
    matrix = channel.astype(jnp.float32)
    padded = jnp.pad(matrix, ((1, 1), (0, 0), (0, 0), (0, 0)))
    index = jnp.arange(SUBCARRIER_COUNT)
    weight = jnp.where((index == 0) | (index == SUBCARRIER_COUNT - 1), 0.75, 1.0).astype(jnp.float32)
    smooth = (0.25 * padded[:-2] + 0.5 * padded[1:-1] + 0.25 * padded[2:]) / weight[:, None, None, None]
    active = (jnp.arange(USER_SLOTS)[None, :] < counts[:, None]).astype(jnp.float32)
    smoothed = round_half(smooth * active[:, None, None, :])
    matched = adjoint_apply(smoothed, received.astype(jnp.float32))
    estimate = jnp.zeros_like(matched)
    residual = matched
    direction = matched
    norm_now = user_sum(residual, residual)
    for iteration in range(ITERS):
        column_image = round_half(apply_channel(smoothed, round_half(direction)))
        image = adjoint_apply(smoothed, column_image) + noise * direction
        alpha = norm_now / user_sum(direction, image)
        estimate = estimate + widen(alpha) * direction
        residual = residual - widen(alpha) * image
        norm_next = user_sum(residual, residual)
        direction = residual + widen(norm_next / norm_now) * direction
        norm_now = norm_next
    return estimate


def reference(channel, received, noise_power, user_count, serving_cell):
    counts = jnp.repeat(user_count, GRP, axis=1)
    estimate = lax.map(detect_cell, (channel, received, noise_power, counts))
    detected = estimate.astype(jnp.bfloat16)
    keys = serving_cell[:, :, 0].astype(jnp.int32)
    block_list = keys.reshape(N_CELL, CELLS_PER_PART * USER_SLOTS)
    position = jnp.arange(CELLS_PER_PART * USER_SLOTS)
    earlier = (block_list[:, :, None] == block_list[:, None, :]) & (position[None, None, :] < position[None, :, None])
    rank = jnp.sum(earlier.astype(jnp.int32), axis=2).reshape(-1).astype(jnp.int32)
    source = (jnp.arange(CELL_COUNT * USER_SLOTS) // (CELLS_PER_PART * USER_SLOTS)).astype(jnp.int32)
    target = (keys.reshape(-1) * SLOTS + source * CAP + rank).astype(jnp.int32)
    symbols = detected.transpose(0, 4, 2, 3, 1).reshape(CELL_COUNT * USER_SLOTS, 2, SYMBOL_COUNT, SUBCARRIER_COUNT)
    routed = jnp.zeros((CELL_COUNT * SLOTS, 2, SYMBOL_COUNT, SUBCARRIER_COUNT), jnp.bfloat16).at[target].set(symbols)
    return routed.reshape(CELL_COUNT, SLOTS, 2, SYMBOL_COUNT, SUBCARRIER_COUNT)
```

```python
import jax
import jax.numpy as jnp
from jax import lax
from jax.experimental import pallas as pl
from jax.experimental.pallas import tpu as pltpu
from jax.sharding import PartitionSpec as P

F32, BF16 = jnp.float32, jnp.bfloat16
SPAD = 16
VMEM_LIMIT = 40 << 20
CHUNKS = (3, 6, 6)
SWAP = [(0, 1), (1, 0)]

SMEM_SPEC = pl.BlockSpec(memory_space=pltpu.SMEM)
VMEM_SPEC = pl.BlockSpec(memory_space=pltpu.VMEM)
ANY_SPEC = pl.BlockSpec(memory_space=pl.ANY)


def prepare(below, here, above, samples, factor, mat, lhs):
    antennas, users = here.shape[1:]
    symbols = samples.shape[0]
    slab = 128
    for k in range(2):
        first = 2 * users + SPAD * k
        lhs[first : first + symbols, :] = samples[:, k, :]
        for row in range(0, antennas, slab):
            rows = pl.ds(row, slab)
            outer = below[k, rows, :].astype(F32) + above[k, rows, :].astype(F32)
            smooth = outer * 0.25 + here[k, rows, :].astype(F32) * 0.5
            value = (smooth * factor).astype(BF16)
            mat[rows, k * users : (k + 1) * users] = value
            lhs[k * users : (k + 1) * users, rows] = value.T


def gram(mat, lhs, out, users):
    product = jnp.dot(lhs[...], mat[...], preferred_element_type=F32)
    row = lax.broadcasted_iota(jnp.int32, (users, users), 0)
    col = lax.broadcasted_iota(jnp.int32, (users, users), 1)
    real = product[:users, :users] + product[users : 2 * users, users:]
    imag = product[:users, users:] - product[users : 2 * users, :users]
    out[:users, :] = jnp.where(row <= col, real, imag).astype(out.dtype)
    low, high = product[2 * users : 2 * users + SPAD], product[2 * users + SPAD :]
    out[users : users + SPAD, :] = (low[:, :users] + high[:, users:]).astype(out.dtype)
    out[users + SPAD :, :] = (high[:, :users] - low[:, users:]).astype(out.dtype)


def work_buffers(antennas, users):
    return [
        pltpu.VMEM((antennas, 2 * users), BF16),
        pltpu.VMEM((2 * users + 2 * SPAD, antennas), BF16),
    ]


def inner_gram(place, counts, channel, received, peer, first, number, dtype):
    cells, band, _, antennas, users = channel.shape
    symbols = received.shape[2]
    group = band // counts.shape[1]
    half = band // 2
    items = cells * number

    def kernel(place_ref, count_ref, chan, samp, out, win, ybuf, mat_a, lhs_a, mat_b, lhs_b, wsem, ysem):
        side = 1 - place_ref[0] if peer else place_ref[0]
        start = 1 + side * (half - 1) + first

        def fetch(c, i):
            return pltpu.make_async_copy(chan.at[c, start - 1 + i], win.at[c, i], wsem.at[c, i])

        def fetch_samples(c):
            return pltpu.make_async_copy(samp.at[c, pl.ds(start, number)], ybuf.at[c], ysem.at[c])

        for c in range(cells):
            fetch_samples(c).start()
            for i in range(number + 2):
                fetch(c, i).start()
        lhs_a[...] = jnp.zeros_like(lhs_a)
        lhs_b[...] = jnp.zeros_like(lhs_b)
        lane = lax.broadcasted_iota(jnp.int32, (1, users), 1)

        def wait(item):
            c, i = item // number, item % number

            @pl.when(item < items)
            def _():
                @pl.when(i == 0)
                def _():
                    fetch_samples(c).wait()
                    fetch(c, 0).wait()
                    fetch(c, 1).wait()

                fetch(c, i + 2).wait()

        def ready(item, mat, lhs):
            item = jnp.minimum(item, items - 1)
            c, i = item // number, item % number
            factor = (lane < count_ref[c, (start + i) // group]).astype(F32)
            prepare(win.at[c, i], win.at[c, i + 1], win.at[c, i + 2], ybuf.at[c, i], factor, mat, lhs)

        def multiply(item, mat, lhs):
            item = jnp.minimum(item, items - 1)
            gram(mat, lhs, out.at[item // number, item % number], users)

        wait(0)
        ready(0, mat_a, lhs_a)

        def step(t, carry):
            wait(2 * t + 1)
            wait(2 * t + 2)
            ready(2 * t + 1, mat_b, lhs_b)
            multiply(2 * t, mat_a, lhs_a)
            ready(2 * t + 2, mat_a, lhs_a)
            multiply(2 * t + 1, mat_b, lhs_b)
            return carry

        lax.fori_loop(0, (items + 1) // 2, step, 0)

    rows = users + 2 * SPAD
    return pl.pallas_call(
        kernel,
        in_specs=[SMEM_SPEC, SMEM_SPEC, ANY_SPEC, ANY_SPEC],
        out_specs=VMEM_SPEC,
        out_shape=jax.ShapeDtypeStruct((cells, number, rows, users), dtype),
        scratch_shapes=[
            pltpu.VMEM((cells, number + 2, 2, antennas, users), BF16),
            pltpu.VMEM((cells, number, symbols, 2, antennas), BF16),
            *work_buffers(antennas, users),
            *work_buffers(antennas, users),
            pltpu.SemaphoreType.DMA((cells, number + 2)),
            pltpu.SemaphoreType.DMA((cells,)),
        ],
        compiler_params=pltpu.CompilerParams(vmem_limit_bytes=VMEM_LIMIT),
        cost_estimate=pl.CostEstimate(
            flops=items * 4 * antennas * users * 2 * (users + SPAD),
            bytes_accessed=cells * (number + 2) * 4 * antennas * users,
            transcendentals=0,
        ),
    )(place, counts, channel, received)


def edge_gram(place, counts, channel, received, low, high):
    cells, band, _, antennas, users = channel.shape
    symbols = received.shape[2]
    group = band // counts.shape[1]

    def kernel(place_ref, count_ref, chan, samp, low_ref, high_ref, out_peer, out_own, win, ybuf, mat_a, lhs_a, mat_b, lhs_b, wsem, ysem):
        def sources(c):
            return (
                (low_ref.at[c, 0], chan.at[c, 0], chan.at[c, 1], samp.at[c, 0]),
                (chan.at[c, band - 2], chan.at[c, band - 1], high_ref.at[c, 0], samp.at[c, band - 1]),
            )

        copies = []
        for c in range(cells):
            for e in range(2):
                *blocks, samples = sources(c)[e]
                for i, block in enumerate(blocks):
                    copies.append(pltpu.make_async_copy(block, win.at[e, c, i], wsem.at[e, c, i]))
                copies.append(pltpu.make_async_copy(samples, ybuf.at[e, c], ysem.at[e, c]))
        for copy in copies:
            copy.start()
        lhs_a[...] = jnp.zeros_like(lhs_a)
        lhs_b[...] = jnp.zeros_like(lhs_b)
        lane = lax.broadcasted_iota(jnp.int32, (1, users), 1)
        for copy in copies:
            copy.wait()
        own = place_ref[0]

        def ready(e, c, mat, lhs):
            weight = jnp.where(place_ref[1 + e] == 1, 0.75, 1.0)
            count = count_ref[c, e * (band - 1) // group]
            factor = (lane < count).astype(F32) / jnp.full((1, users), weight, F32)
            prepare(win.at[e, c, 0], win.at[e, c, 1], win.at[e, c, 2], ybuf.at[e, c], factor, mat, lhs)

        for out, e in ((out_peer, 1 - own), (out_own, own)):
            for c in range(cells):
                mat, lhs = ((mat_a, lhs_a), (mat_b, lhs_b))[c % 2]
                ready(e, c, mat, lhs)
                gram(mat, lhs, out.at[c], users)

    rows = users + 2 * SPAD
    return pl.pallas_call(
        kernel,
        in_specs=[SMEM_SPEC, SMEM_SPEC, ANY_SPEC, ANY_SPEC, ANY_SPEC, ANY_SPEC],
        out_specs=[VMEM_SPEC, VMEM_SPEC],
        out_shape=[
            jax.ShapeDtypeStruct((cells, rows, users), BF16),
            jax.ShapeDtypeStruct((cells, rows, users), F32),
        ],
        scratch_shapes=[
            pltpu.VMEM((2, cells, 3, 2, antennas, users), BF16),
            pltpu.VMEM((2, cells, symbols, 2, antennas), BF16),
            *work_buffers(antennas, users),
            *work_buffers(antennas, users),
            pltpu.SemaphoreType.DMA((2, cells, 3)),
            pltpu.SemaphoreType.DMA((2, cells)),
        ],
        compiler_params=pltpu.CompilerParams(vmem_limit_bytes=VMEM_LIMIT),
        cost_estimate=pl.CostEstimate(
            flops=2 * cells * 4 * antennas * users * 2 * (users + SPAD),
            bytes_accessed=2 * cells * 12 * antennas * users,
            transcendentals=0,
        ),
    )(place, counts, channel, received, low, high)


def conjugate_gradient(sums, noise, users):
    row = lax.broadcasted_iota(jnp.int32, (users, users), 0)
    col = lax.broadcasted_iota(jnp.int32, (users, users), 1)
    upper = row <= col
    grams = []
    for value in sums:
        packed = value[:users]
        turned = packed.T
        real = jnp.where(upper, packed, turned)
        imag = jnp.where(row == col, 0.0, jnp.where(upper, -turned, packed))
        grams.append(jnp.concatenate([real, imag], axis=1).astype(BF16))

    def apply(matrix, vector):
        product = jnp.dot(vector.astype(BF16), matrix, preferred_element_type=F32)
        low, high = product[:SPAD], product[SPAD:]
        image = jnp.concatenate([low[:, :users] + high[:, users:], high[:, :users] - low[:, users:]], axis=0)
        return image + noise * vector

    def user_sum(left, right):
        total = jnp.sum(left * right, axis=1, keepdims=True)
        total = total[:SPAD] + total[SPAD:]
        return jnp.concatenate([total, total], axis=0)

    direction = [value[users:] for value in sums]
    norm = [user_sum(d, d) for d in direction]
    image = [apply(g, d) for g, d in zip(grams, direction)]
    alpha = [n / user_sum(d, i) for n, d, i in zip(norm, direction, image)]
    estimate = [a * d for a, d in zip(alpha, direction)]
    residual = [d - a * i for d, a, i in zip(direction, alpha, image)]
    norm_next = [user_sum(r, r) for r in residual]
    direction = [r + (m / n) * d for r, m, n, d in zip(residual, norm_next, norm, direction)]
    image = [apply(g, d) for g, d in zip(grams, direction)]
    alpha = [n / user_sum(d, i) for n, d, i in zip(norm_next, direction, image)]
    return [e + a * d for e, a, d in zip(estimate, alpha, direction)]


def inner_detect(place, noise_power, own, peers):
    cells, inner, rows, users = own.shape
    half = inner + 1
    batch = 3

    def kernel(place_ref, noise_ref, own_ref, *refs):
        *peer_refs, out = refs
        shift = 1 - place_ref[0]
        start = 0
        for peer_ref in peer_refs:
            number = peer_ref.shape[1]

            def step(t, carry, start=start, peer_ref=peer_ref, number=number):
                steps = number // batch
                c, base = t // steps, t % steps * batch
                sums = [own_ref[c, start + base + i] + peer_ref[c, base + i].astype(F32) for i in range(batch)]
                for i, value in enumerate(conjugate_gradient(sums, noise_ref[c], users)):
                    out[c, pl.ds(start + base + i + shift, 2 * SPAD, stride=half), :] = value
                return carry

            lax.fori_loop(0, cells * (number // batch), step, 0)
            start += number

    return pl.pallas_call(
        kernel,
        in_specs=[SMEM_SPEC, SMEM_SPEC, VMEM_SPEC] + [VMEM_SPEC] * len(peers),
        out_specs=VMEM_SPEC,
        out_shape=jax.ShapeDtypeStruct((cells, 2 * SPAD * half, users), F32),
        compiler_params=pltpu.CompilerParams(vmem_limit_bytes=VMEM_LIMIT),
        cost_estimate=pl.CostEstimate(
            flops=cells * inner * 2 * 2 * 2 * SPAD * users * 2 * users,
            bytes_accessed=cells * inner * rows * users * 6,
            transcendentals=0,
        ),
    )(place, noise_power, own, *peers)


def edge_detect(place, noise_power, own, peer, inner, onehot, symbols, rounds):
    cells, rows, users = own.shape
    half = inner.shape[1] // (2 * SPAD)
    width = onehot.shape[1] // rounds
    keep = symbols * half

    def kernel(place_ref, noise_ref, own_ref, peer_ref, inner_ref, hot_ref, *refs):
        *outs, state = refs
        state[...] = inner_ref[...]
        spot = place_ref[0] * (half - 1)
        for c in range(cells):
            (value,) = conjugate_gradient([own_ref[c] + peer_ref[c].astype(F32)], noise_ref[c], users)
            state[c, pl.ds(spot, 2 * SPAD, stride=half), :] = value
        blocks = [
            state[c, k * SPAD * half : k * SPAD * half + keep, :].astype(BF16) for k in range(2) for c in range(cells)
        ]
        lhs = jnp.concatenate(blocks, axis=1)
        placed = jnp.dot(lhs, hot_ref[...], preferred_element_type=F32).astype(BF16)
        for i, out in enumerate(outs):
            out[...] = placed[:, i * width : (i + 1) * width]

    return pl.pallas_call(
        kernel,
        in_specs=[SMEM_SPEC, SMEM_SPEC] + [VMEM_SPEC] * 4,
        out_specs=[VMEM_SPEC] * rounds,
        out_shape=[jax.ShapeDtypeStruct((keep, width), BF16)] * rounds,
        scratch_shapes=[pltpu.VMEM(inner.shape, F32)],
        compiler_params=pltpu.CompilerParams(vmem_limit_bytes=VMEM_LIMIT),
        cost_estimate=pl.CostEstimate(
            flops=2 * keep * onehot.shape[0] * onehot.shape[1], bytes_accessed=4 * inner.size, transcendentals=0
        ),
    )(place, noise_power, own, peer, inner, onehot)


def assemble(place, mine, theirs, sources, cells, per_device, symbols, half):
    total = len(sources) * 2 * half
    lanes = mine[0].shape[2]
    slots = cells * per_device

    def kernel(place_ref, source_ref, *refs):
        mine_refs, theirs_refs = refs[: len(mine)], refs[len(mine) : 2 * len(mine)]
        out, gathered, turned = refs[2 * len(mine) :]
        for side, group in ((place_ref[0], mine_refs), (1 - place_ref[0], theirs_refs)):
            number = 0
            for ref in group:
                for i in range(ref.shape[0]):
                    start = pl.multiple_of(source_ref[number] * (2 * half) + side * half, half)
                    for s in range(symbols):
                        gathered[s, pl.ds(start, half), :] = ref[i, s * half : (s + 1) * half, :]
                    number += 1
        for s in range(symbols):
            value = gathered[s].T.astype(F32)
            for k in range(2):
                for part in range(total // 128):
                    piece = value[k * slots : (k + 1) * slots, part * 128 : (part + 1) * 128]
                    turned[part, pl.ds(2 * s + k, slots, stride=2 * SPAD), :] = piece
        for slot in range(slots):
            for part in range(total // 128):
                value = turned[part, slot * 2 * SPAD : (slot + 1) * 2 * SPAD, :].astype(BF16)
                out[slot // per_device, slot % per_device, :, :, part * 128 : (part + 1) * 128] = value[
                    : 2 * symbols
                ].reshape(symbols, 2, 128)

    return pl.pallas_call(
        kernel,
        in_specs=[SMEM_SPEC, SMEM_SPEC] + [VMEM_SPEC] * (2 * len(mine)),
        out_specs=VMEM_SPEC,
        out_shape=jax.ShapeDtypeStruct((cells, per_device, symbols, 2, total), BF16),
        scratch_shapes=[
            pltpu.VMEM((symbols, total, lanes), BF16),
            pltpu.VMEM((total // 128, slots * 2 * SPAD, 128), F32),
        ],
        compiler_params=pltpu.CompilerParams(vmem_limit_bytes=VMEM_LIMIT),
    )(place, sources, *mine, *theirs)


def body(channel, received, noise_power, user_count, serving_cell):
    cells, band, _, antennas, users = channel.shape
    symbols = received.shape[3]
    half = band // 2
    n_sc, n_cell = lax.axis_size("sc"), lax.axis_size("cell")
    panel, sc, cell = lax.axis_index("panel"), lax.axis_index("sc"), lax.axis_index("cell")

    upward = [(i, i + 1) for i in range(n_sc - 1)]
    downward = [(i + 1, i) for i in range(n_sc - 1)]
    low = lax.ppermute(channel[:, band - 1 :], "sc", upward)
    high = lax.ppermute(channel[:, :1], "sc", downward)

    place = jnp.stack([panel, (sc == 0).astype(jnp.int32), (sc == n_sc - 1).astype(jnp.int32)]).astype(jnp.int32)
    samples = jnp.transpose(received, (0, 1, 3, 2, 4))

    peers, first = [], 0
    for number in CHUNKS:
        outgoing = inner_gram(place, user_count, channel, samples, True, first, number, BF16)
        peers.append(lax.ppermute(outgoing, "panel", SWAP))
        first += number
    own = inner_gram(place, user_count, channel, samples, False, 0, half - 1, F32)
    edge_out, edge_own = edge_gram(place, user_count, channel, samples, low, high)
    edge_peer = lax.ppermute(edge_out, "panel", SWAP)
    inner = inner_detect(place, noise_power, own, peers)

    capacity = cells * users // n_cell
    per_device = n_cell * capacity // n_sc
    reach = capacity // per_device
    rounds = n_cell * reach
    keys = serving_cell[:, :, 0].reshape(-1)
    position = lax.iota(jnp.int32, cells * users)
    earlier = (keys[:, None] == keys[None, :]) & (position[None, :] < position[:, None])
    rank = jnp.sum(earlier.astype(jnp.int32), axis=1)
    turn = (keys // cells - sc // reach) % n_cell * reach + (rank // per_device - sc % reach) % reach
    column = (turn * 2 * cells + keys % cells) * per_device + rank % per_device
    column = jnp.concatenate([column, column + cells * per_device])
    width = 2 * cells * per_device
    onehot = (column[:, None] == lax.iota(jnp.int32, rounds * width)[None, :]).astype(BF16)

    messages = edge_detect(place, noise_power, edge_own, edge_peer, inner, onehot, symbols, rounds)
    arrived, sources = [], []
    for a in range(n_cell):
        for b in range(reach):
            pairs = [
                (s * n_sc + j, (j // reach + a) % n_cell * n_sc + s * reach + (j % reach + b) % reach)
                for s in range(n_cell)
                for j in range(n_sc)
            ]
            arrived.append(lax.ppermute(messages[a * reach + b], ("cell", "sc"), pairs))
            sources.append((cell - a) % n_cell * reach + (sc % reach - b) % reach)
    sources = jnp.stack(sources).astype(jnp.int32)
    groups = [arrived[: rounds // 2], arrived[rounds // 2 :]]
    mine = [jnp.stack(group) for group in groups]
    theirs = [lax.ppermute(group, "panel", SWAP) for group in mine]
    routed = assemble(place, mine, theirs, sources, cells, per_device, symbols, half)
    return jnp.transpose(routed, (0, 1, 3, 2, 4))


def solution(mesh):
    return jax.shard_map(
        body,
        mesh=mesh,
        in_specs=(
            P("cell", "sc", None, "panel", None),
            P("cell", "sc", None, None, "panel"),
            P("cell"),
            P("cell", "sc"),
            P("cell", None, None),
        ),
        out_specs=P("cell", "sc", None, None, None),
        check_vma=False,
    )
```

```python
import jax
import jax.numpy as jnp
from jax import lax
from jax.experimental import pallas as pl
from jax.experimental.pallas import tpu as pltpu
from jax.sharding import PartitionSpec as P

F32, BF16 = jnp.float32, jnp.bfloat16
SPAD = 16
VMEM_LIMIT = 40 << 20
SWAP = [(0, 1), (1, 0)]

SMEM_SPEC = pl.BlockSpec(memory_space=pltpu.SMEM)
VMEM_SPEC = pl.BlockSpec(memory_space=pltpu.VMEM)
ANY_SPEC = pl.BlockSpec(memory_space=pl.ANY)


def prepare(below, here, above, samples, stretch, mat, lhs):
    antennas, users = here.shape[1:]
    symbols = samples.shape[0]
    slab = 128
    for k in range(2):
        first = 2 * users + SPAD * k
        lhs[first : first + symbols, :] = samples[:, k, :]
        for row in range(0, antennas, slab):
            rows = pl.ds(row, slab)
            outer = below[k, rows, :].astype(F32) + above[k, rows, :].astype(F32)
            middle = here[k, rows, :]
            value = outer + (middle + middle).astype(F32)
            value = (value if stretch is None else value * stretch).astype(BF16)
            mat[rows, k * users : (k + 1) * users] = value
            lhs[k * users : (k + 1) * users, rows] = value.T


def gram(mat, lhs, out, count, users):
    product = jnp.dot(lhs[...], mat[...], preferred_element_type=F32)
    row = lax.broadcasted_iota(jnp.int32, (users, users), 0)
    col = lax.broadcasted_iota(jnp.int32, (users, users), 1)
    real = product[:users, :users] + product[users : 2 * users, users:]
    imag = product[:users, users:] - product[users : 2 * users, :users]
    packed = jnp.where(row <= col, real, imag)
    out[:users, :] = jnp.where(jnp.maximum(row, col) < count, packed * 0.0625, 0.0).astype(out.dtype)
    lane = lax.broadcasted_iota(jnp.int32, (1, users), 1)
    scale = jnp.where(lane < count, 0.25, 0.0)
    low, high = product[2 * users : 2 * users + SPAD], product[2 * users + SPAD :]
    out[users : users + SPAD, :] = ((low[:, :users] + high[:, users:]) * scale).astype(out.dtype)
    out[users + SPAD :, :] = ((high[:, :users] - low[:, users:]) * scale).astype(out.dtype)


def work_buffers(antennas, users):
    return [
        pltpu.VMEM((antennas, 2 * users), BF16),
        pltpu.VMEM((2 * users + 2 * SPAD, antennas), BF16),
    ]


def inner_gram(place, counts, channel, received, peer, first, number, dtype):
    cells, band, _, antennas, users = channel.shape
    symbols = received.shape[2]
    group = band // counts.shape[1]
    half = band // 2
    items = cells * number

    def kernel(place_ref, count_ref, chan, samp, out, win, ybuf, mat_a, lhs_a, mat_b, lhs_b, wsem, ysem):
        side = 1 - place_ref[0] if peer else place_ref[0]
        start = 1 + side * (half - 1) + first

        def fetch(c, i):
            return pltpu.make_async_copy(chan.at[c, start - 1 + i], win.at[c, i], wsem.at[c, i])

        def fetch_samples(c):
            return pltpu.make_async_copy(samp.at[c, pl.ds(start, number)], ybuf.at[c], ysem.at[c])

        for c in range(cells):
            for i in range(number + 2):
                fetch(c, i).start()
                if i == min(2, number):
                    fetch_samples(c).start()
        lhs_a[...] = jnp.zeros_like(lhs_a)
        lhs_b[...] = jnp.zeros_like(lhs_b)

        def wait(item):
            c, i = item // number, item % number

            @pl.when(item < items)
            def _():
                @pl.when(i == 0)
                def _():
                    fetch_samples(c).wait()
                    fetch(c, 0).wait()
                    fetch(c, 1).wait()

                fetch(c, i + 2).wait()

        def ready(item, mat, lhs):
            item = jnp.minimum(item, items - 1)
            c, i = item // number, item % number
            prepare(win.at[c, i], win.at[c, i + 1], win.at[c, i + 2], ybuf.at[c, i], None, mat, lhs)

        def multiply(item, mat, lhs):
            item = jnp.minimum(item, items - 1)
            c, i = item // number, item % number
            gram(mat, lhs, out.at[c, i], count_ref[c, (start + i) // group], users)

        wait(0)
        ready(0, mat_a, lhs_a)

        def step(t, carry):
            wait(2 * t + 1)
            wait(2 * t + 2)
            ready(2 * t + 1, mat_b, lhs_b)
            multiply(2 * t, mat_a, lhs_a)
            ready(2 * t + 2, mat_a, lhs_a)
            multiply(2 * t + 1, mat_b, lhs_b)
            return carry

        lax.fori_loop(0, (items + 1) // 2, step, 0)

    rows = users + 2 * SPAD
    return pl.pallas_call(
        kernel,
        in_specs=[SMEM_SPEC, SMEM_SPEC, ANY_SPEC, ANY_SPEC],
        out_specs=VMEM_SPEC,
        out_shape=jax.ShapeDtypeStruct((cells, number, rows, users), dtype),
        scratch_shapes=[
            pltpu.VMEM((cells, number + 2, 2, antennas, users), BF16),
            pltpu.VMEM((cells, number, symbols, 2, antennas), BF16),
            *work_buffers(antennas, users),
            *work_buffers(antennas, users),
            pltpu.SemaphoreType.DMA((cells, number + 2)),
            pltpu.SemaphoreType.DMA((cells,)),
        ],
        compiler_params=pltpu.CompilerParams(vmem_limit_bytes=VMEM_LIMIT),
        cost_estimate=pl.CostEstimate(
            flops=items * 4 * antennas * users * 2 * (users + SPAD),
            bytes_accessed=cells * (number + 2) * 4 * antennas * users,
            transcendentals=0,
        ),
    )(place, counts, channel, received)


def edge_gram(place, counts, channel, received, low, high, peer, dtype):
    cells, band, _, antennas, users = channel.shape
    symbols = received.shape[2]
    group = band // counts.shape[1]

    def kernel(place_ref, count_ref, chan, samp, low_ref, high_ref, out, win, ybuf, mat_a, lhs_a, mat_b, lhs_b, wsem, ysem):
        side = 1 - place_ref[0] if peer else place_ref[0]

        def each_copy(act):
            def run(e):
                for c in range(cells):
                    blocks = (
                        (low_ref.at[c, 0], chan.at[c, 0], chan.at[c, 1]),
                        (chan.at[c, band - 2], chan.at[c, band - 1], high_ref.at[c, 0]),
                    )[e]
                    for i, block in enumerate(blocks):
                        act(pltpu.make_async_copy(block, win.at[c, i], wsem.at[c, i]))
                    act(pltpu.make_async_copy(samp.at[c, e * (band - 1)], ybuf.at[c], ysem.at[c]))

            @pl.when(side == 0)
            def _():
                run(0)

            @pl.when(side == 1)
            def _():
                run(1)

        each_copy(lambda copy: copy.start())
        lhs_a[...] = jnp.zeros_like(lhs_a)
        lhs_b[...] = jnp.zeros_like(lhs_b)
        each_copy(lambda copy: copy.wait())
        last = jnp.where(side == 0, place_ref[1], place_ref[2])
        stretch = jnp.where(jnp.full((1, users), last, jnp.int32) == 1, 1 / 0.75, 1.0)
        buffers = ((mat_a, lhs_a), (mat_b, lhs_b))
        for c in range(cells):
            mat, lhs = buffers[c % 2]
            prepare(win.at[c, 0], win.at[c, 1], win.at[c, 2], ybuf.at[c], stretch, mat, lhs)
        for c in range(cells):
            gram(*buffers[c % 2], out.at[c], count_ref[c, side * (band - 1) // group], users)

    rows = users + 2 * SPAD
    return pl.pallas_call(
        kernel,
        in_specs=[SMEM_SPEC, SMEM_SPEC, ANY_SPEC, ANY_SPEC, ANY_SPEC, ANY_SPEC],
        out_specs=VMEM_SPEC,
        out_shape=jax.ShapeDtypeStruct((cells, rows, users), dtype),
        scratch_shapes=[
            pltpu.VMEM((cells, 3, 2, antennas, users), BF16),
            pltpu.VMEM((cells, symbols, 2, antennas), BF16),
            *work_buffers(antennas, users),
            *work_buffers(antennas, users),
            pltpu.SemaphoreType.DMA((cells, 3)),
            pltpu.SemaphoreType.DMA((cells,)),
        ],
        compiler_params=pltpu.CompilerParams(vmem_limit_bytes=VMEM_LIMIT),
        cost_estimate=pl.CostEstimate(
            flops=cells * 4 * antennas * users * 2 * (users + SPAD),
            bytes_accessed=cells * 12 * antennas * users,
            transcendentals=0,
        ),
    )(place, counts, channel, received, low, high)


def conjugate_gradient(sums, noise, users):
    row = lax.broadcasted_iota(jnp.int32, (users, users), 0)
    col = lax.broadcasted_iota(jnp.int32, (users, users), 1)
    upper = row <= col
    grams = []
    for value in sums:
        packed = value[:users].astype(BF16)
        turned = packed.T
        real = jnp.where(upper, packed, turned)
        imag = jnp.where(row == col, jnp.zeros_like(packed), jnp.where(upper, -turned, packed))
        grams.append(jnp.concatenate([real, imag], axis=1))

    def apply(matrix, vector):
        product = jnp.dot(vector.astype(BF16), matrix, preferred_element_type=F32)
        low, high = product[:SPAD], product[SPAD:]
        image = jnp.concatenate([low[:, :users] + high[:, users:], high[:, :users] - low[:, users:]], axis=0)
        return image + noise * vector

    def user_sum(left, right):
        total = jnp.sum(left * right, axis=1, keepdims=True)
        total = total[:SPAD] + total[SPAD:]
        return jnp.concatenate([total, total], axis=0)

    direction = [value[users:] for value in sums]
    norm = [user_sum(d, d) for d in direction]
    image = [apply(g, d) for g, d in zip(grams, direction)]
    alpha = [n / user_sum(d, i) for n, d, i in zip(norm, direction, image)]
    estimate = [a * d for a, d in zip(alpha, direction)]
    residual = [d - a * i for d, a, i in zip(direction, alpha, image)]
    norm_next = [user_sum(r, r) for r in residual]
    direction = [r + (m / n) * d for r, m, n, d in zip(residual, norm_next, norm, direction)]
    image = [apply(g, d) for g, d in zip(grams, direction)]
    alpha = [n / user_sum(d, i) for n, d, i in zip(norm_next, direction, image)]
    return [e + a * d for e, a, d in zip(estimate, alpha, direction)]


def inner_detect(place, noise_power, own, peers):
    cells, inner, rows, users = own.shape
    half = inner + 1

    def kernel(place_ref, noise_ref, own_ref, *refs):
        *peer_refs, out = refs
        shift = 1 - place_ref[0]

        def step(c, carry):
            sums = []
            for peer_ref in peer_refs:
                for i in range(peer_ref.shape[1]):
                    sums.append(own_ref[c, len(sums)] + peer_ref[c, i].astype(F32))
            for i, value in enumerate(conjugate_gradient(sums, noise_ref[c], users)):
                out[c, pl.ds(i + shift, 2 * SPAD, stride=half), :] = value
            return carry

        lax.fori_loop(0, cells, step, 0)

    return pl.pallas_call(
        kernel,
        in_specs=[SMEM_SPEC, SMEM_SPEC, VMEM_SPEC] + [VMEM_SPEC] * len(peers),
        out_specs=VMEM_SPEC,
        out_shape=jax.ShapeDtypeStruct((cells, 2 * SPAD * half, users), F32),
        compiler_params=pltpu.CompilerParams(vmem_limit_bytes=VMEM_LIMIT),
        cost_estimate=pl.CostEstimate(
            flops=cells * inner * 2 * 2 * 2 * SPAD * users * 2 * users,
            bytes_accessed=cells * inner * rows * users * 6,
            transcendentals=0,
        ),
    )(place, noise_power, own, *peers)


def edge_detect(place, noise_power, own, peer, inner, onehot, symbols, rounds):
    cells, rows, users = own.shape
    half = inner.shape[1] // (2 * SPAD)
    width = onehot.shape[1] // rounds
    keep = symbols * half

    def kernel(place_ref, noise_ref, own_ref, peer_ref, inner_ref, hot_ref, *refs):
        *outs, state = refs
        state[...] = inner_ref[...]
        spot = place_ref[0] * (half - 1)
        for c in range(cells):
            (value,) = conjugate_gradient([own_ref[c] + peer_ref[c].astype(F32)], noise_ref[c], users)
            state[c, pl.ds(spot, 2 * SPAD, stride=half), :] = value
        blocks = [
            state[c, k * SPAD * half : k * SPAD * half + keep, :].astype(BF16) for k in range(2) for c in range(cells)
        ]
        lhs = jnp.concatenate(blocks, axis=1)
        placed = jnp.dot(lhs, hot_ref[...], preferred_element_type=F32).astype(BF16)
        for i, out in enumerate(outs):
            out[...] = placed[:, i * width : (i + 1) * width]

    return pl.pallas_call(
        kernel,
        in_specs=[SMEM_SPEC, SMEM_SPEC] + [VMEM_SPEC] * 4,
        out_specs=[VMEM_SPEC] * rounds,
        out_shape=[jax.ShapeDtypeStruct((keep, width), BF16)] * rounds,
        scratch_shapes=[pltpu.VMEM(inner.shape, F32)],
        compiler_params=pltpu.CompilerParams(vmem_limit_bytes=VMEM_LIMIT),
        cost_estimate=pl.CostEstimate(
            flops=2 * keep * onehot.shape[0] * onehot.shape[1], bytes_accessed=4 * inner.size, transcendentals=0
        ),
    )(place, noise_power, own, peer, inner, onehot)


def assemble(place, mine, theirs, sources, cells, per_device, symbols, half):
    total = len(sources) * 2 * half
    lanes = mine[0].shape[2]
    slots = cells * per_device

    def kernel(place_ref, source_ref, *refs):
        mine_refs, theirs_refs = refs[: len(mine)], refs[len(mine) : 2 * len(mine)]
        out, gathered, turned = refs[2 * len(mine) :]
        for side, group in ((place_ref[0], mine_refs), (1 - place_ref[0], theirs_refs)):
            number = 0
            for ref in group:
                for i in range(ref.shape[0]):
                    start = pl.multiple_of(source_ref[number] * (2 * half) + side * half, half)
                    for s in range(symbols):
                        gathered[s, pl.ds(start, half), :] = ref[i, s * half : (s + 1) * half, :]
                    number += 1
        for s in range(symbols):
            value = gathered[s].T.astype(F32)
            for k in range(2):
                for part in range(total // 128):
                    piece = value[k * slots : (k + 1) * slots, part * 128 : (part + 1) * 128]
                    turned[part, pl.ds(2 * s + k, slots, stride=2 * SPAD), :] = piece
        for slot in range(slots):
            for part in range(total // 128):
                value = turned[part, slot * 2 * SPAD : (slot + 1) * 2 * SPAD, :].astype(BF16)
                out[slot // per_device, slot % per_device, :, :, part * 128 : (part + 1) * 128] = value[
                    : 2 * symbols
                ].reshape(symbols, 2, 128)

    return pl.pallas_call(
        kernel,
        in_specs=[SMEM_SPEC, SMEM_SPEC] + [VMEM_SPEC] * (2 * len(mine)),
        out_specs=VMEM_SPEC,
        out_shape=jax.ShapeDtypeStruct((cells, per_device, symbols, 2, total), BF16),
        scratch_shapes=[
            pltpu.VMEM((symbols, total, lanes), BF16),
            pltpu.VMEM((total // 128, slots * 2 * SPAD, 128), F32),
        ],
        compiler_params=pltpu.CompilerParams(vmem_limit_bytes=VMEM_LIMIT),
    )(place, sources, *mine, *theirs)


def body(channel, received, noise_power, user_count, serving_cell):
    cells, band, _, antennas, users = channel.shape
    symbols = received.shape[3]
    half = band // 2
    n_sc, n_cell = lax.axis_size("sc"), lax.axis_size("cell")
    panel, sc, cell = lax.axis_index("panel"), lax.axis_index("sc"), lax.axis_index("cell")

    upward = [(i, i + 1) for i in range(n_sc - 1)]
    downward = [(i + 1, i) for i in range(n_sc - 1)]
    low = lax.ppermute(channel[:, band - 1 :], "sc", upward)
    high = lax.ppermute(channel[:, :1], "sc", downward)

    place = jnp.stack([panel, (sc == 0).astype(jnp.int32), (sc == n_sc - 1).astype(jnp.int32)]).astype(jnp.int32)
    samples = jnp.transpose(received, (0, 1, 3, 2, 4))

    peers, first = [], 0
    for number in (3, 6, half - 10):
        outgoing = inner_gram(place, user_count, channel, samples, True, first, number, BF16)
        peers.append(lax.ppermute(outgoing, "panel", SWAP))
        first += number
    own = inner_gram(place, user_count, channel, samples, False, 0, half - 1, F32)
    edge_out = edge_gram(place, user_count, channel, samples, low, high, True, BF16)
    edge_peer = lax.ppermute(edge_out, "panel", SWAP)
    edge_own = edge_gram(place, user_count, channel, samples, low, high, False, F32)
    inner = inner_detect(place, noise_power, own, peers)

    capacity = cells * users // n_cell
    per_device = n_cell * capacity // n_sc
    reach = capacity // per_device
    rounds = n_cell * reach
    keys = serving_cell[:, :, 0].reshape(-1)
    position = lax.iota(jnp.int32, cells * users)
    earlier = (keys[:, None] == keys[None, :]) & (position[None, :] < position[:, None])
    rank = jnp.sum(earlier.astype(jnp.int32), axis=1)
    turn = (keys // cells - sc // reach) % n_cell * reach + (rank // per_device - sc % reach) % reach
    column = (turn * 2 * cells + keys % cells) * per_device + rank % per_device
    column = jnp.concatenate([column, column + cells * per_device])
    width = 2 * cells * per_device
    onehot = (column[:, None] == lax.iota(jnp.int32, rounds * width)[None, :]).astype(BF16)

    messages = edge_detect(place, noise_power, edge_own, edge_peer, inner, onehot, symbols, rounds)
    arrived, sources = [], []
    for a in range(n_cell):
        for b in range(reach):
            pairs = [
                (s * n_sc + j, (j // reach + a) % n_cell * n_sc + s * reach + (j % reach + b) % reach)
                for s in range(n_cell)
                for j in range(n_sc)
            ]
            arrived.append(lax.ppermute(messages[a * reach + b], ("cell", "sc"), pairs))
            sources.append((cell - a) % n_cell * reach + (sc % reach - b) % reach)
    sources = jnp.stack(sources).astype(jnp.int32)
    groups = [arrived[: rounds // 2], arrived[rounds // 2 :]]
    mine = [jnp.stack(group) for group in groups]
    theirs = [lax.ppermute(group, "panel", SWAP) for group in mine]
    routed = assemble(place, mine, theirs, sources, cells, per_device, symbols, half)
    return jnp.transpose(routed, (0, 1, 3, 2, 4))


def solution(mesh):
    return jax.shard_map(
        body,
        mesh=mesh,
        in_specs=(
            P("cell", "sc", None, "panel", None),
            P("cell", "sc", None, None, "panel"),
            P("cell"),
            P("cell", "sc"),
            P("cell", None, None),
        ),
        out_specs=P("cell", "sc", None, None, None),
        check_vma=False,
    )
```

```python
import jax
import jax.numpy as jnp
from jax import lax
from jax.experimental import pallas as pl
from jax.experimental.pallas import tpu as pltpu
from jax.sharding import PartitionSpec as P

F32, BF16 = jnp.float32, jnp.bfloat16
GRP = 16
SPAD = 16
VMEM_LIMIT = 40 << 20
SWAP = [(0, 1), (1, 0)]

SMEM_SPEC = pl.BlockSpec(memory_space=pltpu.SMEM)
VMEM_SPEC = pl.BlockSpec(memory_space=pltpu.VMEM)
HBM_SPEC = pl.BlockSpec(memory_space=pltpu.HBM)


def cross(product, users):
    left, right = product[:, :users], product[:, users:]
    rows = product.shape[0]
    even = lax.broadcasted_iota(jnp.int32, left.shape, 0) % 2 == 0
    return left + jnp.where(even, pltpu.roll(right, rows - 1, 0), -pltpu.roll(right, 1, 0))


def prepare(below, here, above, samples, stretch, mat, lhs):
    antennas, users = here.shape[1:]
    symbols = samples.shape[0]
    slab = 128
    lhs[2 * users : 2 * (users + symbols), :] = samples[...].reshape(2 * symbols, antennas)
    for k in range(2):
        for row in range(0, antennas, slab):
            rows = pl.ds(row, slab)
            outer = below[k, rows, :].astype(F32) + above[k, rows, :].astype(F32)
            middle = here[k, rows, :]
            value = outer + (middle + middle).astype(F32)
            value = (value if stretch is None else value * stretch).astype(BF16)
            mat[rows, k * users : (k + 1) * users] = value
            lhs[k * users : (k + 1) * users, rows] = value.T


def gram(mat, lhs, out, count, users):
    product = jnp.dot(lhs[...], mat[...], preferred_element_type=F32)
    row = lax.broadcasted_iota(jnp.int32, (users, users), 0)
    col = lax.broadcasted_iota(jnp.int32, (users, users), 1)
    real = product[:users, :users] + product[users : 2 * users, users:]
    imag = product[:users, users:] - product[users : 2 * users, :users]
    packed = jnp.where(row <= col, real, imag)
    out[:users, :] = jnp.where(jnp.maximum(row, col) < count, packed * 0.0625, 0.0).astype(out.dtype)
    lane = lax.broadcasted_iota(jnp.int32, (1, users), 1)
    scale = jnp.where(lane < count, 0.25, 0.0)
    out[users:, :] = (cross(product[2 * users :], users) * scale).astype(out.dtype)


def work_buffers(antennas, users):
    return [
        pltpu.VMEM((antennas, 2 * users), BF16),
        pltpu.VMEM((2 * users + 2 * SPAD, antennas), BF16),
    ]


def inner_gram(control, channel, received, peer, first, number, dtype, halo=False):
    cells, band, _, antennas, users = channel.shape
    symbols = received.shape[2]
    group, groups = GRP, band // GRP
    half = band // 2
    items = cells * number

    def kernel(control_ref, chan, samp, out, *refs):
        ends, refs = (refs[:2], refs[2:]) if halo else ((), refs)
        win, ybuf, mat_a, lhs_a, mat_b, lhs_b, wsem, ysem, esem = refs
        edges = [
            pltpu.make_async_copy(chan.at[c, i * (band - 1)], ends[i].at[c, 0], esem.at[c, i])
            for c in range(cells)
            for i in range(len(ends))
        ]
        side = 1 - control_ref[0] if peer else control_ref[0]
        start = 1 + side * (half - 1) + first

        def fetch(c, i):
            return pltpu.make_async_copy(chan.at[c, start - 1 + i], win.at[c, i], wsem.at[c, i])

        def fetch_samples(c):
            return pltpu.make_async_copy(samp.at[c, pl.ds(start, number)], ybuf.at[c], ysem.at[c])

        for c in range(cells):
            for i in range(number + 2):
                fetch(c, i).start()
                if i == min(2, number):
                    fetch_samples(c).start()
        for copy in edges:
            copy.start()
        lhs_a[...] = jnp.zeros_like(lhs_a)
        lhs_b[...] = jnp.zeros_like(lhs_b)

        def wait(item):
            c, i = item // number, item % number

            @pl.when(item < items)
            def _():
                @pl.when(i == 0)
                def _():
                    fetch_samples(c).wait()
                    fetch(c, 0).wait()
                    fetch(c, 1).wait()

                fetch(c, i + 2).wait()

        def ready(item, mat, lhs):
            item = jnp.minimum(item, items - 1)
            c, i = item // number, item % number
            prepare(win.at[c, i], win.at[c, i + 1], win.at[c, i + 2], ybuf.at[c, i], None, mat, lhs)

        def multiply(item, mat, lhs):
            item = jnp.minimum(item, items - 1)
            c, i = item // number, item % number
            gram(mat, lhs, out.at[c, i], control_ref[3 + c * groups + (start + i) // group], users)

        wait(0)
        ready(0, mat_a, lhs_a)

        def step(t, carry):
            wait(2 * t + 1)
            wait(2 * t + 2)
            ready(2 * t + 1, mat_b, lhs_b)
            multiply(2 * t, mat_a, lhs_a)
            ready(2 * t + 2, mat_a, lhs_a)
            multiply(2 * t + 1, mat_b, lhs_b)
            return carry

        lax.fori_loop(0, (items + 1) // 2, step, 0)
        for copy in edges:
            copy.wait()

    rows = users + 2 * SPAD
    return pl.pallas_call(
        kernel,
        in_specs=[SMEM_SPEC, HBM_SPEC, HBM_SPEC],
        out_specs=[VMEM_SPEC] + [HBM_SPEC] * (2 * halo),
        out_shape=[jax.ShapeDtypeStruct((cells, number, rows, users), dtype)]
        + [jax.ShapeDtypeStruct((cells, 1, 2, antennas, users), BF16)] * (2 * halo),
        scratch_shapes=[
            pltpu.VMEM((cells, number + 2, 2, antennas, users), BF16),
            pltpu.VMEM((cells, number, symbols, 2, antennas), BF16),
            *work_buffers(antennas, users),
            *work_buffers(antennas, users),
            pltpu.SemaphoreType.DMA((cells, number + 2)),
            pltpu.SemaphoreType.DMA((cells,)),
            pltpu.SemaphoreType.DMA((cells, 2)),
        ],
        compiler_params=pltpu.CompilerParams(vmem_limit_bytes=VMEM_LIMIT),
        cost_estimate=pl.CostEstimate(
            flops=items * 4 * antennas * users * 2 * (users + SPAD),
            bytes_accessed=cells * (number + 2) * 4 * antennas * users,
            transcendentals=0,
        ),
    )(control, channel, received)


def edge_scratch(cells, symbols, antennas, users):
    return [
        pltpu.VMEM((cells, 3, 2, antennas, users), BF16),
        pltpu.VMEM((cells, symbols, 2, antennas), BF16),
        *work_buffers(antennas, users),
        *work_buffers(antennas, users),
        pltpu.SemaphoreType.DMA((cells, 3)),
        pltpu.SemaphoreType.DMA((cells,)),
    ]


def edge_work(side, control_ref, chan, samp, low_ref, high_ref, out, scratch):
    win, ybuf, mat_a, lhs_a, mat_b, lhs_b, wsem, ysem = scratch
    cells, band, _, _, users = chan.shape
    groups = band // GRP
    buffers = ((mat_a, lhs_a), (mat_b, lhs_b))

    def each_copy(act):
        def run(e):
            for c in range(cells):
                blocks = (
                    (low_ref.at[c, 0], chan.at[c, 0], chan.at[c, 1]),
                    (chan.at[c, band - 2], chan.at[c, band - 1], high_ref.at[c, 0]),
                )[e]
                for i, block in enumerate(blocks):
                    act(pltpu.make_async_copy(block, win.at[c, i], wsem.at[c, i]))
                act(pltpu.make_async_copy(samp.at[c, e * (band - 1)], ybuf.at[c], ysem.at[c]))

        @pl.when(side == 0)
        def _():
            run(0)

        @pl.when(side == 1)
        def _():
            run(1)

    def fetch():
        each_copy(lambda copy: copy.start())
        lhs_a[...] = jnp.zeros_like(lhs_a)
        lhs_b[...] = jnp.zeros_like(lhs_b)

    def work():
        each_copy(lambda copy: copy.wait())
        last = jnp.where(side == 0, control_ref[1], control_ref[2])
        stretch = jnp.where(jnp.full((1, users), last, jnp.int32) == 1, 1 / 0.75, 1.0)
        for c in range(cells):
            prepare(win.at[c, 0], win.at[c, 1], win.at[c, 2], ybuf.at[c], stretch, *buffers[c % 2])
        for c in range(cells):
            gram(*buffers[c % 2], out.at[c], control_ref[3 + c * groups + side * (band - 1) // GRP], users)

    return fetch, work


def edge_gram(control, channel, received, low, high):
    cells, _, _, antennas, users = channel.shape
    symbols = received.shape[2]

    def kernel(control_ref, chan, samp, low_ref, high_ref, out, *scratch):
        fetch, work = edge_work(1 - control_ref[0], control_ref, chan, samp, low_ref, high_ref, out, scratch)
        fetch()
        work()

    return pl.pallas_call(
        kernel,
        in_specs=[SMEM_SPEC] + [HBM_SPEC] * 4,
        out_specs=VMEM_SPEC,
        out_shape=jax.ShapeDtypeStruct((cells, users + 2 * SPAD, users), BF16),
        scratch_shapes=edge_scratch(cells, symbols, antennas, users),
        compiler_params=pltpu.CompilerParams(vmem_limit_bytes=VMEM_LIMIT),
        cost_estimate=pl.CostEstimate(
            flops=cells * 4 * antennas * users * 2 * (users + SPAD),
            bytes_accessed=cells * 12 * antennas * users,
            transcendentals=0,
        ),
    )(control, channel, received, low, high)


def conjugate_gradient(sums, noise, users):
    row = lax.broadcasted_iota(jnp.int32, (users, users), 0)
    col = lax.broadcasted_iota(jnp.int32, (users, users), 1)
    upper = row <= col
    grams = []
    for value in sums:
        packed = value[:users].astype(BF16)
        turned = packed.T
        real = jnp.where(upper, packed, turned)
        imag = jnp.where(row == col, jnp.zeros_like(packed), jnp.where(upper, -turned, packed))
        grams.append(jnp.concatenate([real, imag], axis=1))

    def apply(matrix, vector):
        product = jnp.dot(vector.astype(BF16), matrix, preferred_element_type=F32)
        return cross(product, users) + noise * vector

    def user_sum(left, right):
        total = left * right
        even = lax.broadcasted_iota(jnp.int32, total.shape, 0) % 2 == 0
        total = total + jnp.where(even, pltpu.roll(total, 2 * SPAD - 1, 0), pltpu.roll(total, 1, 0))
        return jnp.sum(total, axis=1, keepdims=True)

    direction = [value[users:] for value in sums]
    norm = [user_sum(d, d) for d in direction]
    image = [apply(g, d) for g, d in zip(grams, direction)]
    alpha = [n / user_sum(d, i) for n, d, i in zip(norm, direction, image)]
    estimate = [a * d for a, d in zip(alpha, direction)]
    residual = [d - a * i for d, a, i in zip(direction, alpha, image)]
    norm_next = [user_sum(r, r) for r in residual]
    direction = [r + (m / n) * d for r, m, n, d in zip(residual, norm_next, norm, direction)]
    image = [apply(g, d) for g, d in zip(grams, direction)]
    alpha = [n / user_sum(d, i) for n, d, i in zip(norm_next, direction, image)]
    return [e + a * d for e, a, d in zip(estimate, alpha, direction)]


def inner_detect(control, noise_power, own, peers, channel, received, low, high):
    cells, inner, rows, users = own.shape
    antennas, symbols = channel.shape[3], received.shape[2]
    half = inner + 1

    def kernel(control_ref, noise_ref, chan, samp, low_ref, high_ref, own_ref, *refs):
        peer_refs, (out, edge_out), scratch = refs[: len(peers)], refs[len(peers) : len(peers) + 2], refs[len(peers) + 2 :]
        fetch, work = edge_work(control_ref[0], control_ref, chan, samp, low_ref, high_ref, edge_out, scratch)
        fetch()
        shift = 1 - control_ref[0]

        def step(c, carry):
            sums = []
            for peer_ref in peer_refs:
                for i in range(peer_ref.shape[1]):
                    sums.append(own_ref[c, len(sums)] + peer_ref[c, i].astype(F32))
            for i, value in enumerate(conjugate_gradient(sums, noise_ref[c], users)):
                out[c, pl.ds(i + shift, 2 * SPAD, stride=half), :] = value
            return carry

        lax.fori_loop(0, cells, step, 0)
        work()

    return pl.pallas_call(
        kernel,
        in_specs=[SMEM_SPEC, SMEM_SPEC] + [HBM_SPEC] * 4 + [VMEM_SPEC] * (1 + len(peers)),
        out_specs=[VMEM_SPEC, VMEM_SPEC],
        out_shape=[
            jax.ShapeDtypeStruct((cells, 2 * SPAD * half, users), F32),
            jax.ShapeDtypeStruct((cells, rows, users), F32),
        ],
        scratch_shapes=edge_scratch(cells, symbols, antennas, users),
        compiler_params=pltpu.CompilerParams(vmem_limit_bytes=VMEM_LIMIT),
        cost_estimate=pl.CostEstimate(
            flops=cells * inner * 2 * 2 * 2 * SPAD * users * 2 * users,
            bytes_accessed=cells * inner * rows * users * 6,
            transcendentals=0,
        ),
    )(control, noise_power, channel, received, low, high, own, *peers)


def edge_detect(control, noise_power, own, peer, inner, onehot, symbols, rounds):
    cells, rows, users = own.shape
    half = inner.shape[1] // (2 * SPAD)
    width = onehot.shape[1] // rounds
    keep = symbols * half

    def kernel(control_ref, noise_ref, own_ref, peer_ref, inner_ref, hot_ref, *refs):
        *outs, state = refs
        state[...] = inner_ref[...]
        spot = control_ref[0] * (half - 1)
        for c in range(cells):
            (value,) = conjugate_gradient([own_ref[c] + peer_ref[c].astype(F32)], noise_ref[c], users)
            state[c, pl.ds(spot, 2 * SPAD, stride=half), :] = value
        values = state[...].astype(BF16)
        blocks = [
            jnp.concatenate([values[c, (2 * s + k) * half : (2 * s + k + 1) * half] for s in range(symbols)], axis=0)
            for k in range(2)
            for c in range(cells)
        ]
        lhs = jnp.concatenate(blocks, axis=1)
        placed = jnp.dot(lhs, hot_ref[...], preferred_element_type=F32).astype(BF16)
        for i, out in enumerate(outs):
            out[...] = placed[:, i * width : (i + 1) * width]

    return pl.pallas_call(
        kernel,
        in_specs=[SMEM_SPEC, SMEM_SPEC] + [VMEM_SPEC] * 4,
        out_specs=[VMEM_SPEC] * rounds,
        out_shape=[jax.ShapeDtypeStruct((keep, width), BF16)] * rounds,
        scratch_shapes=[pltpu.VMEM(inner.shape, F32)],
        compiler_params=pltpu.CompilerParams(vmem_limit_bytes=VMEM_LIMIT),
        cost_estimate=pl.CostEstimate(
            flops=2 * keep * onehot.shape[0] * onehot.shape[1], bytes_accessed=4 * inner.size, transcendentals=0
        ),
    )(control, noise_power, own, peer, inner, onehot)


def assemble(control, mine, theirs, sources, cells, per_device, symbols, half):
    total = len(sources) * 2 * half
    lanes = mine[0].shape[2]
    slots = cells * per_device

    def kernel(control_ref, source_ref, *refs):
        mine_refs, theirs_refs = refs[: len(mine)], refs[len(mine) : 2 * len(mine)]
        out, gathered, turned = refs[2 * len(mine) :]
        for side, group in ((control_ref[0], mine_refs), (1 - control_ref[0], theirs_refs)):
            number = 0
            for ref in group:
                for i in range(ref.shape[0]):
                    start = pl.multiple_of(source_ref[number] * (2 * half) + side * half, half)
                    for s in range(symbols):
                        gathered[s, pl.ds(start, half), :] = ref[i, s * half : (s + 1) * half, :]
                    number += 1
        for s in range(symbols):
            value = gathered[s].T.astype(F32)
            for k in range(2):
                for part in range(total // 128):
                    piece = value[k * slots : (k + 1) * slots, part * 128 : (part + 1) * 128]
                    turned[part, pl.ds(2 * s + k, slots, stride=2 * SPAD), :] = piece
        for slot in range(slots):
            for part in range(total // 128):
                value = turned[part, slot * 2 * SPAD : (slot + 1) * 2 * SPAD, :].astype(BF16)
                out[slot // per_device, slot % per_device, :, :, part * 128 : (part + 1) * 128] = value[
                    : 2 * symbols
                ].reshape(symbols, 2, 128)

    return pl.pallas_call(
        kernel,
        in_specs=[SMEM_SPEC, SMEM_SPEC] + [VMEM_SPEC] * (2 * len(mine)),
        out_specs=VMEM_SPEC,
        out_shape=jax.ShapeDtypeStruct((cells, per_device, symbols, 2, total), BF16),
        scratch_shapes=[
            pltpu.VMEM((symbols, total, lanes), BF16),
            pltpu.VMEM((total // 128, slots * 2 * SPAD, 128), F32),
        ],
        compiler_params=pltpu.CompilerParams(vmem_limit_bytes=VMEM_LIMIT),
    )(control, sources, *mine, *theirs)


def body(channel, received, noise_power, user_count, serving_cell):
    cells, band, _, antennas, users = channel.shape
    symbols = received.shape[3]
    half = band // 2
    n_sc, n_cell = lax.axis_size("sc"), lax.axis_size("cell")
    panel, sc, cell = lax.axis_index("panel"), lax.axis_index("sc"), lax.axis_index("cell")

    ends = jnp.stack([panel, (sc == 0).astype(jnp.int32), (sc == n_sc - 1).astype(jnp.int32)])
    control = jnp.concatenate([ends.astype(jnp.int32), user_count.reshape(-1)])
    samples = jnp.transpose(received, (0, 1, 3, 2, 4))

    inner = half - 1
    count = inner // 2
    outgoing, bottom, top = inner_gram(control, channel, samples, True, 0, count, BF16, halo=True)
    peers = [lax.ppermute(outgoing, "panel", SWAP)]
    low = lax.ppermute(top, "sc", [(i, i + 1) for i in range(n_sc - 1)])
    high = lax.ppermute(bottom, "sc", [(i + 1, i) for i in range(n_sc - 1)])
    (outgoing,) = inner_gram(control, channel, samples, True, count, inner - count, BF16)
    peers.append(lax.ppermute(outgoing, "panel", SWAP))
    (own,) = inner_gram(control, channel, samples, False, 0, inner, F32)
    edge_peer = lax.ppermute(edge_gram(control, channel, samples, low, high), "panel", SWAP)
    inner, edge_own = inner_detect(control, noise_power, own, peers, channel, samples, low, high)

    capacity = cells * users // n_cell
    per_device = n_cell * capacity // n_sc
    reach = capacity // per_device
    rounds = n_cell * reach
    keys = serving_cell[:, :, 0].reshape(-1)
    position = lax.iota(jnp.int32, cells * users)
    earlier = (keys[:, None] == keys[None, :]) & (position[None, :] < position[:, None])
    rank = jnp.sum(earlier.astype(jnp.int32), axis=1)
    turn = (keys // cells - sc // reach) % n_cell * reach + (rank // per_device - sc % reach) % reach
    column = (turn * 2 * cells + keys % cells) * per_device + rank % per_device
    column = jnp.concatenate([column, column + cells * per_device])
    width = 2 * cells * per_device
    onehot = (column[:, None] == lax.iota(jnp.int32, rounds * width)[None, :]).astype(BF16)

    messages = edge_detect(control, noise_power, edge_own, edge_peer, inner, onehot, symbols, rounds)
    arrived, sources = [], []
    for a in range(n_cell):
        if a == n_cell // 2:
            messages, arrived = lax.optimization_barrier((messages, arrived))
        for b in range(reach):
            pairs = [
                (s * n_sc + j, (j // reach + a) % n_cell * n_sc + s * reach + (j % reach + b) % reach)
                for s in range(n_cell)
                for j in range(n_sc)
            ]
            arrived.append(lax.ppermute(messages[a * reach + b], ("cell", "sc"), pairs))
            sources.append((cell - a) % n_cell * reach + (sc % reach - b) % reach)
    sources = jnp.stack(sources).astype(jnp.int32)
    groups = [arrived[: rounds // 2], arrived[rounds // 2 :]]
    mine = [jnp.stack(group) for group in groups]
    theirs = [lax.ppermute(group, "panel", SWAP) for group in mine]
    routed = assemble(control, mine, theirs, sources, cells, per_device, symbols, half)
    return jnp.transpose(routed, (0, 1, 3, 2, 4))


def solution(mesh):
    return jax.shard_map(
        body,
        mesh=mesh,
        in_specs=(
            P("cell", "sc", None, "panel", None),
            P("cell", "sc", None, None, "panel"),
            P("cell"),
            P("cell", "sc"),
            P("cell", None, None),
        ),
        out_specs=P("cell", "sc", None, None, None),
        check_vma=False,
    )
```

```python
import jax
import jax.numpy as jnp
from jax import lax
from jax.experimental import pallas as pl
from jax.experimental.pallas import tpu as pltpu
from jax.sharding import PartitionSpec as P

F32, BF16 = jnp.float32, jnp.bfloat16
GRP = 16
SPAD = 16
VMEM_LIMIT = 40 << 20
SWAP = [(0, 1), (1, 0)]

SMEM_SPEC = pl.BlockSpec(memory_space=pltpu.SMEM)
VMEM_SPEC = pl.BlockSpec(memory_space=pltpu.VMEM)
HBM_SPEC = pl.BlockSpec(memory_space=pltpu.HBM)


def cross(product, users):
    left, right = product[:, :users], product[:, users:]
    rows = product.shape[0]
    even = lax.broadcasted_iota(jnp.int32, left.shape, 0) % 2 == 0
    return left + jnp.where(even, pltpu.roll(right, rows - 1, 0), -pltpu.roll(right, 1, 0))


def prepare(below, here, above, samples, stretch, mat, lhs):
    antennas, users = here.shape[1:]
    symbols = samples.shape[0]
    slab = 128
    lhs[2 * users : 2 * (users + symbols), :] = samples[...].reshape(2 * symbols, antennas)
    for k in range(2):
        for row in range(0, antennas, slab):
            rows = pl.ds(row, slab)
            outer = below[k, rows, :].astype(F32) + above[k, rows, :].astype(F32)
            middle = here[k, rows, :]
            value = outer + (middle + middle).astype(F32)
            value = (value if stretch is None else value * stretch).astype(BF16)
            mat[rows, k * users : (k + 1) * users] = value
            lhs[k * users : (k + 1) * users, rows] = value.T


def gram(mat, lhs, out, count, users):
    product = jnp.dot(lhs[...], mat[...], preferred_element_type=F32)
    row = lax.broadcasted_iota(jnp.int32, (users, users), 0)
    col = lax.broadcasted_iota(jnp.int32, (users, users), 1)
    real = product[:users, :users] + product[users : 2 * users, users:]
    imag = product[:users, users:] - product[users : 2 * users, :users]
    packed = jnp.where(row <= col, real, imag)
    out[:users, :] = jnp.where(jnp.maximum(row, col) < count, packed * 0.0625, 0.0).astype(out.dtype)
    lane = lax.broadcasted_iota(jnp.int32, (1, users), 1)
    scale = jnp.where(lane < count, 0.25, 0.0)
    out[users:, :] = (cross(product[2 * users :], users) * scale).astype(out.dtype)


def work_buffers(antennas, users):
    return [
        pltpu.VMEM((antennas, 2 * users), BF16),
        pltpu.VMEM((2 * users + 2 * SPAD, antennas), BF16),
    ]


def inner_gram(counts, channel, received, peer, first, number, dtype, halo=False):
    cells, band, _, antennas, users = channel.shape
    symbols = received.shape[2]
    half = band // 2
    items = cells * number

    def kernel(counts_hbm, chan, samp, out, *refs):
        ends, refs = (refs[:2], refs[2:]) if halo else ((), refs)
        count_ref, win, ybuf, mat_a, lhs_a, mat_b, lhs_b, wsem, ysem, esem, csem = refs
        count_copy = pltpu.make_async_copy(counts_hbm, count_ref, csem)
        count_copy.start()
        edges = [
            pltpu.make_async_copy(chan.at[c, i * (band - 1)], ends[i].at[c, 0], esem.at[c, i])
            for c in range(cells)
            for i in range(len(ends))
        ]
        panel = lax.axis_index("panel")
        side = 1 - panel if peer else panel
        start = 1 + side * (half - 1) + first

        def fetch(c, i):
            return pltpu.make_async_copy(chan.at[c, start - 1 + i], win.at[c, i], wsem.at[c, i])

        def fetch_samples(c):
            return pltpu.make_async_copy(samp.at[c, pl.ds(start, number)], ybuf.at[c], ysem.at[c])

        for c in range(cells):
            for i in range(number + 2):
                fetch(c, i).start()
                if i == min(2, number):
                    fetch_samples(c).start()
        for copy in edges:
            copy.start()
        lhs_a[...] = jnp.zeros_like(lhs_a)
        lhs_b[...] = jnp.zeros_like(lhs_b)

        def wait(item):
            c, i = item // number, item % number

            @pl.when(item < items)
            def _():
                @pl.when(i == 0)
                def _():
                    fetch_samples(c).wait()
                    fetch(c, 0).wait()
                    fetch(c, 1).wait()

                fetch(c, i + 2).wait()

        def ready(item, mat, lhs):
            item = jnp.minimum(item, items - 1)
            c, i = item // number, item % number
            prepare(win.at[c, i], win.at[c, i + 1], win.at[c, i + 2], ybuf.at[c, i], None, mat, lhs)

        def multiply(item, mat, lhs):
            item = jnp.minimum(item, items - 1)
            c, i = item // number, item % number
            gram(mat, lhs, out.at[c, i], count_ref[c, (start + i) // GRP], users)

        count_copy.wait()
        wait(0)
        ready(0, mat_a, lhs_a)

        def step(t, carry):
            wait(2 * t + 1)
            wait(2 * t + 2)
            ready(2 * t + 1, mat_b, lhs_b)
            multiply(2 * t, mat_a, lhs_a)
            ready(2 * t + 2, mat_a, lhs_a)
            multiply(2 * t + 1, mat_b, lhs_b)
            return carry

        lax.fori_loop(0, (items + 1) // 2, step, 0)
        for copy in edges:
            copy.wait()

    rows = users + 2 * SPAD
    return pl.pallas_call(
        kernel,
        in_specs=[HBM_SPEC] * 3,
        out_specs=[VMEM_SPEC] * (1 + 2 * halo),
        out_shape=[jax.ShapeDtypeStruct((cells, number, rows, users), dtype)]
        + [jax.ShapeDtypeStruct((cells, 1, 2, antennas, users), BF16)] * (2 * halo),
        scratch_shapes=[
            pltpu.SMEM(counts.shape, jnp.int32),
            pltpu.VMEM((cells, number + 2, 2, antennas, users), BF16),
            pltpu.VMEM((cells, number, symbols, 2, antennas), BF16),
            *work_buffers(antennas, users),
            *work_buffers(antennas, users),
            pltpu.SemaphoreType.DMA((cells, number + 2)),
            pltpu.SemaphoreType.DMA((cells,)),
            pltpu.SemaphoreType.DMA((cells, 2)),
            pltpu.SemaphoreType.DMA,
        ],
        compiler_params=pltpu.CompilerParams(vmem_limit_bytes=VMEM_LIMIT),
        cost_estimate=pl.CostEstimate(
            flops=items * 4 * antennas * users * 2 * (users + SPAD),
            bytes_accessed=cells * (number + 2) * 4 * antennas * users,
            transcendentals=0,
        ),
    )(counts, channel, received)


def edge_scratch(counts, symbols, antennas, users):
    cells = counts.shape[0]
    return [
        pltpu.SMEM(counts.shape, jnp.int32),
        pltpu.VMEM((cells, 3, 2, antennas, users), BF16),
        pltpu.VMEM((cells, symbols, 2, antennas), BF16),
        *work_buffers(antennas, users),
        *work_buffers(antennas, users),
        pltpu.SemaphoreType.DMA((cells, 3)),
        pltpu.SemaphoreType.DMA((cells,)),
        pltpu.SemaphoreType.DMA,
    ]


def edge_work(side, counts_hbm, chan, samp, low_ref, high_ref, out, scratch):
    count_ref, win, ybuf, mat_a, lhs_a, mat_b, lhs_b, wsem, ysem, csem = scratch
    count_copy = pltpu.make_async_copy(counts_hbm, count_ref, csem)
    cells, band, _, _, users = chan.shape
    buffers = ((mat_a, lhs_a), (mat_b, lhs_b))

    def each_copy(act):
        def run(e):
            for c in range(cells):
                blocks = (
                    (low_ref.at[c, 0], chan.at[c, 0], chan.at[c, 1]),
                    (chan.at[c, band - 2], chan.at[c, band - 1], high_ref.at[c, 0]),
                )[e]
                for i, block in enumerate(blocks):
                    act(pltpu.make_async_copy(block, win.at[c, i], wsem.at[c, i]))
                act(pltpu.make_async_copy(samp.at[c, e * (band - 1)], ybuf.at[c], ysem.at[c]))

        @pl.when(side == 0)
        def _():
            run(0)

        @pl.when(side == 1)
        def _():
            run(1)

    def fetch():
        count_copy.start()
        each_copy(lambda copy: copy.start())
        lhs_a[...] = jnp.zeros_like(lhs_a)
        lhs_b[...] = jnp.zeros_like(lhs_b)

    def work():
        each_copy(lambda copy: copy.wait())
        count_copy.wait()
        last = lax.axis_index("sc") == side * (lax.axis_size("sc") - 1)
        stretch = jnp.where(jnp.full((1, users), last.astype(jnp.int32)) == 1, 1 / 0.75, 1.0)
        for c in range(cells):
            prepare(win.at[c, 0], win.at[c, 1], win.at[c, 2], ybuf.at[c], stretch, *buffers[c % 2])
        for c in range(cells):
            gram(*buffers[c % 2], out.at[c], count_ref[c, side * (band - 1) // GRP], users)

    return fetch, work


def edge_gram(counts, channel, received, low, high):
    cells, _, _, antennas, users = channel.shape
    symbols = received.shape[2]

    def kernel(counts_hbm, chan, samp, low_ref, high_ref, out, *scratch):
        fetch, work = edge_work(1 - lax.axis_index("panel"), counts_hbm, chan, samp, low_ref, high_ref, out, scratch)
        fetch()
        work()

    return pl.pallas_call(
        kernel,
        in_specs=[HBM_SPEC] * 5,
        out_specs=VMEM_SPEC,
        out_shape=jax.ShapeDtypeStruct((cells, users + 2 * SPAD, users), BF16),
        scratch_shapes=edge_scratch(counts, symbols, antennas, users),
        compiler_params=pltpu.CompilerParams(vmem_limit_bytes=VMEM_LIMIT),
        cost_estimate=pl.CostEstimate(
            flops=cells * 4 * antennas * users * 2 * (users + SPAD),
            bytes_accessed=cells * 12 * antennas * users,
            transcendentals=0,
        ),
    )(counts, channel, received, low, high)


def conjugate_gradient(sums, noise, users):
    row = lax.broadcasted_iota(jnp.int32, (users, users), 0)
    col = lax.broadcasted_iota(jnp.int32, (users, users), 1)
    upper = row <= col
    grams = []
    for value in sums:
        packed = value[:users].astype(BF16)
        turned = packed.T
        real = jnp.where(upper, packed, turned)
        imag = jnp.where(row == col, jnp.zeros_like(packed), jnp.where(upper, -turned, packed))
        grams.append(jnp.concatenate([real, imag], axis=1))

    def apply(matrix, vector):
        product = jnp.dot(vector.astype(BF16), matrix, preferred_element_type=F32)
        return cross(product, users) + noise * vector

    def user_sum(left, right):
        total = left * right
        even = lax.broadcasted_iota(jnp.int32, total.shape, 0) % 2 == 0
        total = total + jnp.where(even, pltpu.roll(total, 2 * SPAD - 1, 0), pltpu.roll(total, 1, 0))
        return jnp.sum(total, axis=1, keepdims=True)

    direction = [value[users:] for value in sums]
    norm = [user_sum(d, d) for d in direction]
    image = [apply(g, d) for g, d in zip(grams, direction)]
    alpha = [n / user_sum(d, i) for n, d, i in zip(norm, direction, image)]
    estimate = [a * d for a, d in zip(alpha, direction)]
    residual = [d - a * i for d, a, i in zip(direction, alpha, image)]
    norm_next = [user_sum(r, r) for r in residual]
    direction = [r + (m / n) * d for r, m, n, d in zip(residual, norm_next, norm, direction)]
    image = [apply(g, d) for g, d in zip(grams, direction)]
    alpha = [n / user_sum(d, i) for n, d, i in zip(norm_next, direction, image)]
    return [e + a * d for e, a, d in zip(estimate, alpha, direction)]


def inner_detect(counts, noise_power, own, peers, channel, received, low, high):
    cells, inner, rows, users = own.shape
    antennas, symbols = channel.shape[3], received.shape[2]
    half = inner + 1

    def kernel(noise_ref, counts_hbm, chan, samp, low_ref, high_ref, own_ref, *refs):
        panel = lax.axis_index("panel")
        peer_refs, (out, edge_out), scratch = refs[: len(peers)], refs[len(peers) : len(peers) + 2], refs[len(peers) + 2 :]
        fetch, work = edge_work(panel, counts_hbm, chan, samp, low_ref, high_ref, edge_out, scratch)
        fetch()
        shift = 1 - panel

        def step(c, carry):
            sums = []
            for peer_ref in peer_refs:
                for i in range(peer_ref.shape[1]):
                    sums.append(own_ref[c, len(sums)] + peer_ref[c, i].astype(F32))
            for i, value in enumerate(conjugate_gradient(sums, noise_ref[c], users)):
                out[c, pl.ds(i + shift, 2 * SPAD, stride=half), :] = value
            return carry

        lax.fori_loop(0, cells, step, 0)
        work()

    return pl.pallas_call(
        kernel,
        in_specs=[SMEM_SPEC] + [HBM_SPEC] * 5 + [VMEM_SPEC] * (1 + len(peers)),
        out_specs=[VMEM_SPEC, VMEM_SPEC],
        out_shape=[
            jax.ShapeDtypeStruct((cells, 2 * SPAD * half, users), F32),
            jax.ShapeDtypeStruct((cells, rows, users), F32),
        ],
        scratch_shapes=edge_scratch(counts, symbols, antennas, users),
        compiler_params=pltpu.CompilerParams(vmem_limit_bytes=VMEM_LIMIT),
        cost_estimate=pl.CostEstimate(
            flops=cells * inner * 2 * 2 * 2 * SPAD * users * 2 * users,
            bytes_accessed=cells * inner * rows * users * 6,
            transcendentals=0,
        ),
    )(noise_power, counts, channel, received, low, high, own, *peers)


def edge_detect(noise_power, own, peer, inner, onehot, symbols, rounds):
    cells, rows, users = own.shape
    half = inner.shape[1] // (2 * SPAD)
    width = onehot.shape[1] // (2 * rounds)
    keep = symbols * half

    def kernel(noise_ref, own_ref, peer_ref, inner_ref, hot_ref, *refs):
        *outs, state = refs
        state[...] = inner_ref[...]
        spot = lax.axis_index("panel") * (half - 1)
        for c in range(cells):
            (value,) = conjugate_gradient([own_ref[c] + peer_ref[c].astype(F32)], noise_ref[c], users)
            state[c, pl.ds(spot, 2 * SPAD, stride=half), :] = value
        values = state[...].astype(BF16)
        blocks = [
            jnp.concatenate([values[c, (2 * s + k) * half : (2 * s + k + 1) * half] for s in range(symbols)], axis=0)
            for k in range(2)
            for c in range(cells)
        ]
        lhs = jnp.concatenate(blocks, axis=1)
        placed = jnp.dot(lhs, hot_ref[...], preferred_element_type=F32).astype(BF16)
        for i, out in enumerate(outs):
            for side in range(2):
                first = (2 * i + side) * width
                out[side * keep : (side + 1) * keep, :] = placed[:, first : first + width]

    return pl.pallas_call(
        kernel,
        in_specs=[SMEM_SPEC] + [VMEM_SPEC] * 4,
        out_specs=[VMEM_SPEC] * rounds,
        out_shape=[jax.ShapeDtypeStruct((2 * keep, width), BF16)] * rounds,
        scratch_shapes=[pltpu.VMEM(inner.shape, F32)],
        compiler_params=pltpu.CompilerParams(vmem_limit_bytes=VMEM_LIMIT),
        cost_estimate=pl.CostEstimate(
            flops=2 * keep * onehot.shape[0] * onehot.shape[1], bytes_accessed=4 * inner.size, transcendentals=0
        ),
    )(noise_power, own, peer, inner, onehot)


def assemble(sources, mine, theirs, others, cells, per_device, symbols, half):
    rounds = sum(group.shape[0] for group in mine)
    total = 2 * rounds * 2 * half
    lanes = mine[0].shape[2]
    slots = cells * per_device
    keep = symbols * half
    number = len(mine)

    def kernel(source_ref, *refs):
        mine_refs, theirs_refs = refs[:number], refs[number : 2 * number]
        own_other, peer_others = refs[2 * number], refs[2 * number + 1 : 3 * number + 1]
        out, gathered, turned = refs[3 * number + 1 :]
        panel = lax.axis_index("panel")

        def place(ref, i, first, source, side):
            start = pl.multiple_of(source * (2 * half) + side * half, half)
            for s in range(symbols):
                gathered[s, pl.ds(start, half), :] = ref[i, first + s * half : first + (s + 1) * half, :]

        for side, group in ((panel, mine_refs), (1 - panel, theirs_refs)):
            n = 0
            for ref in group:
                for i in range(ref.shape[0]):
                    place(ref, i, keep, source_ref[n], side)
                    n += 1
        for side, group in ((panel, (own_other,)), (1 - panel, peer_others)):
            n = rounds
            for ref in group:
                for i in range(ref.shape[0]):
                    place(ref, i, 0, source_ref[n], side)
                    n += 1
        for s in range(symbols):
            value = gathered[s].T.astype(F32)
            for k in range(2):
                for part in range(total // 128):
                    piece = value[k * slots : (k + 1) * slots, part * 128 : (part + 1) * 128]
                    turned[part, pl.ds(2 * s + k, slots, stride=2 * SPAD), :] = piece
        for slot in range(slots):
            for part in range(total // 128):
                value = turned[part, slot * 2 * SPAD : (slot + 1) * 2 * SPAD, :].astype(BF16)
                out[slot // per_device, slot % per_device, :, :, part * 128 : (part + 1) * 128] = value[
                    : 2 * symbols
                ].reshape(symbols, 2, 128)

    return pl.pallas_call(
        kernel,
        in_specs=[SMEM_SPEC] + [VMEM_SPEC] * (3 * number + 1),
        out_specs=VMEM_SPEC,
        out_shape=jax.ShapeDtypeStruct((cells, per_device, symbols, 2, total), BF16),
        scratch_shapes=[
            pltpu.VMEM((symbols, total, lanes), BF16),
            pltpu.VMEM((total // 128, slots * 2 * SPAD, 128), F32),
        ],
        compiler_params=pltpu.CompilerParams(vmem_limit_bytes=VMEM_LIMIT),
    )(sources, *mine, *theirs, *others)


def body(channel, received, noise_power, user_count, serving_cell):
    cells, band, _, antennas, users = channel.shape
    symbols = received.shape[3]
    half = band // 2
    n_sc, n_cell = lax.axis_size("sc"), lax.axis_size("cell")
    panel, sc, cell = lax.axis_index("panel"), lax.axis_index("sc"), lax.axis_index("cell")

    samples = jnp.transpose(received, (0, 1, 3, 2, 4))

    inner = half - 1
    count = inner // 2
    outgoing, bottom, top = inner_gram(user_count, channel, samples, True, 0, count, BF16, halo=True)
    peers = [lax.ppermute(outgoing, "panel", SWAP)]
    low = lax.ppermute(top, "sc", [(i, i + 1) for i in range(n_sc - 1)])
    high = lax.ppermute(bottom, "sc", [(i + 1, i) for i in range(n_sc - 1)])
    (outgoing,) = inner_gram(user_count, channel, samples, True, count, inner - count, BF16)
    peers.append(lax.ppermute(outgoing, "panel", SWAP))
    (own,) = inner_gram(user_count, channel, samples, False, 0, inner, F32)
    low, high, own = lax.optimization_barrier((low, high, own))
    edge_peer = lax.ppermute(edge_gram(user_count, channel, samples, low, high), "panel", SWAP)
    inner, edge_own = inner_detect(user_count, noise_power, own, peers, channel, samples, low, high)

    capacity = cells * users // n_cell
    per_device = n_cell * capacity // n_sc
    reach = capacity // per_device
    keys = serving_cell[:, :, 0].reshape(-1)
    position = lax.iota(jnp.int32, cells * users)
    earlier = (keys[:, None] == keys[None, :]) & (position[None, :] < position[:, None])
    rank = jnp.sum(earlier.astype(jnp.int32), axis=1)
    turn = (rank // per_device - sc % reach) % reach * 2 + (keys // cells == sc // reach).astype(jnp.int32)
    column = (turn * 2 * cells + keys % cells) * per_device + rank % per_device
    column = jnp.concatenate([column, column + cells * per_device])
    width = 2 * cells * per_device
    onehot = (column[:, None] == lax.iota(jnp.int32, 2 * reach * width)[None, :]).astype(BF16)

    messages = edge_detect(noise_power, edge_own, edge_peer, inner, onehot, symbols, reach)
    arrived = []
    for b in range(reach):
        pairs = [
            (s * n_sc + j, j // reach * n_sc + s * reach + (j % reach + b) % reach)
            for s in range(n_cell)
            for j in range(n_sc)
        ]
        arrived.append(lax.ppermute(messages[b], ("cell", "sc"), pairs))
    turns = (sc % reach - lax.iota(jnp.int32, reach)) % reach
    sources = jnp.concatenate([cell * reach + turns, (1 - cell) * reach + turns])
    keep = symbols * half
    mine = [jnp.stack(arrived[: reach // 2]), jnp.stack(arrived[reach // 2 :])]
    theirs = [lax.ppermute(group, "panel", SWAP) for group in mine]
    others = [lax.ppermute(jnp.stack([block[:keep] for block in arrived]), "cell", SWAP)]
    others += [lax.ppermute(group[:, :keep], "cell", SWAP) for group in theirs]
    routed = assemble(sources, mine, theirs, others, cells, per_device, symbols, half)
    return jnp.transpose(routed, (0, 1, 3, 2, 4))


def solution(mesh):
    return jax.shard_map(
        body,
        mesh=mesh,
        in_specs=(
            P("cell", "sc", None, "panel", None),
            P("cell", "sc", None, None, "panel"),
            P("cell"),
            P("cell", "sc"),
            P("cell", None, None),
        ),
        out_specs=P("cell", "sc", None, None, None),
        check_vma=False,
    )
```

```python
import jax
import jax.numpy as jnp
from jax import lax
from jax.experimental import pallas as pl
from jax.experimental.pallas import tpu as pltpu
from jax.sharding import PartitionSpec as P

F32, BF16 = jnp.float32, jnp.bfloat16
GRP = 16
SPAD = 16
VMEM_LIMIT = 40 << 20
SWAP = [(0, 1), (1, 0)]

SMEM_SPEC = pl.BlockSpec(memory_space=pltpu.SMEM)
VMEM_SPEC = pl.BlockSpec(memory_space=pltpu.VMEM)
HBM_SPEC = pl.BlockSpec(memory_space=pltpu.HBM)


def cross(product, users):
    left, right = product[:, :users], product[:, users:]
    rows = product.shape[0]
    even = lax.broadcasted_iota(jnp.int32, left.shape, 0) % 2 == 0
    return left + jnp.where(even, pltpu.roll(right, rows - 1, 0), -pltpu.roll(right, 1, 0))


def prepare(below, here, above, samples, stretch, mat, lhs):
    antennas, users = here.shape[1:]
    symbols = samples.shape[0]
    slab = 128
    lhs[2 * users : 2 * (users + symbols), :] = samples[...].reshape(2 * symbols, antennas)
    for k in range(2):
        for row in range(0, antennas, slab):
            rows = pl.ds(row, slab)
            outer = below[k, rows, :].astype(F32) + above[k, rows, :].astype(F32)
            middle = here[k, rows, :]
            value = outer + (middle + middle).astype(F32)
            value = (value if stretch is None else value * stretch).astype(BF16)
            mat[rows, k * users : (k + 1) * users] = value
            lhs[k * users : (k + 1) * users, rows] = value.T


def gram(mat, lhs, out, count, users):
    product = jnp.dot(lhs[...], mat[...], preferred_element_type=F32)
    row = lax.broadcasted_iota(jnp.int32, (users, users), 0)
    col = lax.broadcasted_iota(jnp.int32, (users, users), 1)
    real = product[:users, :users] + product[users : 2 * users, users:]
    imag = product[:users, users:] - product[users : 2 * users, :users]
    packed = jnp.where(row <= col, real, imag)
    out[:users, :] = jnp.where(jnp.maximum(row, col) < count, packed * 0.0625, 0.0).astype(out.dtype)
    lane = lax.broadcasted_iota(jnp.int32, (1, users), 1)
    scale = jnp.where(lane < count, 0.25, 0.0)
    out[users:, :] = (cross(product[2 * users :], users) * scale).astype(out.dtype)


def work_buffers(antennas, users):
    return [
        pltpu.VMEM((antennas, 2 * users), BF16),
        pltpu.VMEM((2 * users + 2 * SPAD, antennas), BF16),
    ]


def inner_gram(counts, channel, received, peer, first, number, dtype, limit=VMEM_LIMIT):
    cells, band, _, antennas, users = channel.shape
    symbols = received.shape[2]
    half = band // 2
    items = cells * number

    def kernel(counts_hbm, chan, samp, out, count_ref, win, ybuf, mat_a, lhs_a, mat_b, lhs_b, wsem, ysem, csem):
        count_copy = pltpu.make_async_copy(counts_hbm, count_ref, csem)
        count_copy.start()
        panel = lax.axis_index("panel")
        side = 1 - panel if peer else panel
        start = 1 + side * (half - 1) + first

        def fetch(c, i):
            return pltpu.make_async_copy(chan.at[c, start - 1 + i], win.at[c, i], wsem.at[c, i])

        def fetch_samples(c):
            return pltpu.make_async_copy(samp.at[c, pl.ds(start, number)], ybuf.at[c], ysem.at[c])

        for c in range(cells):
            for i in range(number + 2):
                fetch(c, i).start()
                if i == min(2, number):
                    fetch_samples(c).start()
        lhs_a[...] = jnp.zeros_like(lhs_a)
        lhs_b[...] = jnp.zeros_like(lhs_b)

        def wait(item):
            c, i = item // number, item % number

            @pl.when(item < items)
            def _():
                @pl.when(i == 0)
                def _():
                    fetch_samples(c).wait()
                    fetch(c, 0).wait()
                    fetch(c, 1).wait()

                fetch(c, i + 2).wait()

        def ready(item, mat, lhs):
            item = jnp.minimum(item, items - 1)
            c, i = item // number, item % number
            prepare(win.at[c, i], win.at[c, i + 1], win.at[c, i + 2], ybuf.at[c, i], None, mat, lhs)

        def multiply(item, mat, lhs):
            item = jnp.minimum(item, items - 1)
            c, i = item // number, item % number
            gram(mat, lhs, out.at[c, i], count_ref[c, (start + i) // GRP], users)

        count_copy.wait()
        wait(0)
        ready(0, mat_a, lhs_a)

        def step(t, carry):
            wait(2 * t + 1)
            wait(2 * t + 2)
            ready(2 * t + 1, mat_b, lhs_b)
            multiply(2 * t, mat_a, lhs_a)
            ready(2 * t + 2, mat_a, lhs_a)
            multiply(2 * t + 1, mat_b, lhs_b)
            return carry

        lax.fori_loop(0, (items + 1) // 2, step, 0)

    rows = users + 2 * SPAD
    return pl.pallas_call(
        kernel,
        in_specs=[HBM_SPEC] * 3,
        out_specs=VMEM_SPEC,
        out_shape=jax.ShapeDtypeStruct((cells, number, rows, users), dtype),
        scratch_shapes=[
            pltpu.SMEM(counts.shape, jnp.int32),
            pltpu.VMEM((cells, number + 2, 2, antennas, users), BF16),
            pltpu.VMEM((cells, number, symbols, 2, antennas), BF16),
            *work_buffers(antennas, users),
            *work_buffers(antennas, users),
            pltpu.SemaphoreType.DMA((cells, number + 2)),
            pltpu.SemaphoreType.DMA((cells,)),
            pltpu.SemaphoreType.DMA,
        ],
        compiler_params=pltpu.CompilerParams(vmem_limit_bytes=limit),
        cost_estimate=pl.CostEstimate(
            flops=items * 4 * antennas * users * 2 * (users + SPAD),
            bytes_accessed=cells * (number + 2) * 4 * antennas * users,
            transcendentals=0,
        ),
    )(counts, channel, received)


def band_ends(channel, after):
    cells, band, _, antennas, users = channel.shape

    def kernel(chan, after_ref, *refs):
        *ends, sems = refs
        copies = [
            pltpu.make_async_copy(chan.at[c, i * (band - 1)], ends[i].at[c, 0], sems.at[c, i])
            for c in range(cells)
            for i in range(2)
        ]
        for copy in copies:
            copy.start()
        for copy in copies:
            copy.wait()

    return pl.pallas_call(
        kernel,
        in_specs=[HBM_SPEC] * 2,
        out_specs=[VMEM_SPEC] * 2,
        out_shape=[jax.ShapeDtypeStruct((cells, 1, 2, antennas, users), BF16)] * 2,
        scratch_shapes=[pltpu.SemaphoreType.DMA((cells, 2))],
        compiler_params=pltpu.CompilerParams(vmem_limit_bytes=VMEM_LIMIT),
        cost_estimate=pl.CostEstimate(flops=0, bytes_accessed=cells * 16 * antennas * users, transcendentals=0),
    )(channel, after)


def edge_scratch(counts, symbols, antennas, users):
    cells = counts.shape[0]
    return [
        pltpu.SMEM(counts.shape, jnp.int32),
        pltpu.VMEM((cells, 3, 2, antennas, users), BF16),
        pltpu.VMEM((cells, symbols, 2, antennas), BF16),
        *work_buffers(antennas, users),
        *work_buffers(antennas, users),
        pltpu.SemaphoreType.DMA((cells, 3)),
        pltpu.SemaphoreType.DMA((cells,)),
        pltpu.SemaphoreType.DMA,
    ]


def edge_work(side, counts_hbm, chan, samp, low_ref, high_ref, out, scratch):
    count_ref, win, ybuf, mat_a, lhs_a, mat_b, lhs_b, wsem, ysem, csem = scratch
    count_copy = pltpu.make_async_copy(counts_hbm, count_ref, csem)
    cells, band, _, _, users = chan.shape
    buffers = ((mat_a, lhs_a), (mat_b, lhs_b))

    def each_copy(act):
        def run(e):
            for c in range(cells):
                blocks = (
                    (low_ref.at[c, 0], chan.at[c, 0], chan.at[c, 1]),
                    (chan.at[c, band - 2], chan.at[c, band - 1], high_ref.at[c, 0]),
                )[e]
                for i, block in enumerate(blocks):
                    act(pltpu.make_async_copy(block, win.at[c, i], wsem.at[c, i]))
                act(pltpu.make_async_copy(samp.at[c, e * (band - 1)], ybuf.at[c], ysem.at[c]))

        @pl.when(side == 0)
        def _():
            run(0)

        @pl.when(side == 1)
        def _():
            run(1)

    def fetch():
        count_copy.start()
        each_copy(lambda copy: copy.start())
        lhs_a[...] = jnp.zeros_like(lhs_a)
        lhs_b[...] = jnp.zeros_like(lhs_b)

    def work():
        each_copy(lambda copy: copy.wait())
        count_copy.wait()
        last = lax.axis_index("sc") == side * (lax.axis_size("sc") - 1)
        stretch = jnp.where(jnp.full((1, users), last.astype(jnp.int32)) == 1, 1 / 0.75, 1.0)
        for c in range(cells):
            prepare(win.at[c, 0], win.at[c, 1], win.at[c, 2], ybuf.at[c], stretch, *buffers[c % 2])
        for c in range(cells):
            gram(*buffers[c % 2], out.at[c], count_ref[c, side * (band - 1) // GRP], users)

    return fetch, work


def edge_gram(counts, channel, received, low, high):
    cells, _, _, antennas, users = channel.shape
    symbols = received.shape[2]

    def kernel(counts_hbm, chan, samp, low_ref, high_ref, out, *scratch):
        fetch, work = edge_work(1 - lax.axis_index("panel"), counts_hbm, chan, samp, low_ref, high_ref, out, scratch)
        fetch()
        work()

    return pl.pallas_call(
        kernel,
        in_specs=[HBM_SPEC] * 5,
        out_specs=VMEM_SPEC,
        out_shape=jax.ShapeDtypeStruct((cells, users + 2 * SPAD, users), BF16),
        scratch_shapes=edge_scratch(counts, symbols, antennas, users),
        compiler_params=pltpu.CompilerParams(vmem_limit_bytes=VMEM_LIMIT),
        cost_estimate=pl.CostEstimate(
            flops=cells * 4 * antennas * users * 2 * (users + SPAD),
            bytes_accessed=cells * 12 * antennas * users,
            transcendentals=0,
        ),
    )(counts, channel, received, low, high)


def conjugate_gradient(sums, noises, users):
    row = lax.broadcasted_iota(jnp.int32, (users, users), 0)
    col = lax.broadcasted_iota(jnp.int32, (users, users), 1)
    upper = row <= col
    grams = []
    for value in sums:
        packed = value[:users].astype(BF16)
        turned = packed.T
        real = jnp.where(upper, packed, turned)
        imag = jnp.where(row == col, jnp.zeros_like(packed), jnp.where(upper, -turned, packed))
        grams.append(jnp.concatenate([real, imag], axis=1))

    def apply(matrix, vector, noise):
        product = jnp.dot(vector.astype(BF16), matrix, preferred_element_type=F32)
        return cross(product, users) + noise * vector

    def user_sum(left, right):
        total = left * right
        even = lax.broadcasted_iota(jnp.int32, total.shape, 0) % 2 == 0
        total = total + jnp.where(even, pltpu.roll(total, 2 * SPAD - 1, 0), pltpu.roll(total, 1, 0))
        return jnp.sum(total, axis=1, keepdims=True)

    direction = [value[users:] for value in sums]
    norm = [user_sum(d, d) for d in direction]
    image = [apply(*terms) for terms in zip(grams, direction, noises)]
    alpha = [n / user_sum(d, i) for n, d, i in zip(norm, direction, image)]
    estimate = [a * d for a, d in zip(alpha, direction)]
    residual = [d - a * i for d, a, i in zip(direction, alpha, image)]
    norm_next = [user_sum(r, r) for r in residual]
    direction = [r + (m / n) * d for r, m, n, d in zip(residual, norm_next, norm, direction)]
    image = [apply(*terms) for terms in zip(grams, direction, noises)]
    alpha = [n / user_sum(d, i) for n, d, i in zip(norm_next, direction, image)]
    return [e + a * d for e, a, d in zip(estimate, alpha, direction)]


def detect_first(counts, noise_power, own, peer, channel, received, low, high):
    cells, inner, rows, users = own.shape
    antennas, symbols = channel.shape[3], received.shape[2]
    half, number = inner + 1, peer.shape[1]

    def kernel(noise_ref, counts_hbm, chan, samp, low_ref, high_ref, own_ref, peer_ref, out, edge_out, *scratch):
        panel = lax.axis_index("panel")
        fetch, work = edge_work(panel, counts_hbm, chan, samp, low_ref, high_ref, edge_out, scratch)
        fetch()
        spots = [(c, i) for c in range(cells) for i in range(number)]
        sums = [own_ref[c, i] + peer_ref[c, i].astype(F32) for c, i in spots]
        values = conjugate_gradient(sums, [noise_ref[c] for c, _ in spots], users)
        for (c, i), value in zip(spots, values):
            out[c, pl.ds(i + 1 - panel, 2 * SPAD, stride=half), :] = value
        work()

    return pl.pallas_call(
        kernel,
        in_specs=[SMEM_SPEC] + [HBM_SPEC] * 5 + [VMEM_SPEC] * 2,
        out_specs=[VMEM_SPEC, VMEM_SPEC],
        out_shape=[
            jax.ShapeDtypeStruct((cells, 2 * SPAD * half, users), F32),
            jax.ShapeDtypeStruct((cells, rows, users), F32),
        ],
        scratch_shapes=edge_scratch(counts, symbols, antennas, users),
        compiler_params=pltpu.CompilerParams(vmem_limit_bytes=VMEM_LIMIT),
        cost_estimate=pl.CostEstimate(
            flops=cells * number * 2 * 2 * 2 * SPAD * users * 2 * users,
            bytes_accessed=cells * inner * rows * users * 6,
            transcendentals=0,
        ),
    )(noise_power, counts, channel, received, low, high, own, peer)


def detect_last(noise_power, own, peer, edge_own, edge_peer, state, onehot, symbols, rounds):
    cells, inner, rows, users = own.shape
    half, number = inner + 1, peer.shape[1]
    width = onehot.shape[1] // (2 * rounds)
    keep = symbols * half

    def kernel(noise_ref, own_ref, peer_ref, edge_own_ref, edge_peer_ref, hot_ref, state_ref, *refs):
        *outs, full = refs
        panel = lax.axis_index("panel")
        full[...] = state_ref[...]
        first = inner - number
        spots = [(c, i) for c in range(cells) for i in range(number)]
        sums = [own_ref[c, first + i] + peer_ref[c, i].astype(F32) for c, i in spots]
        places = [(c, first + i + 1 - panel) for c, i in spots]
        sums += [edge_own_ref[c] + edge_peer_ref[c].astype(F32) for c in range(cells)]
        places += [(c, panel * (half - 1)) for c in range(cells)]
        values = conjugate_gradient(sums, [noise_ref[c] for c, _ in places], users)
        for (c, place), value in zip(places, values):
            full[c, pl.ds(place, 2 * SPAD, stride=half), :] = value
        found = full[...].astype(BF16)
        blocks = [
            jnp.concatenate([found[c, (2 * s + k) * half : (2 * s + k + 1) * half] for s in range(symbols)], axis=0)
            for k in range(2)
            for c in range(cells)
        ]
        lhs = jnp.concatenate(blocks, axis=1)
        placed = jnp.dot(lhs, hot_ref[...], preferred_element_type=F32).astype(BF16)
        for i, out in enumerate(outs):
            for side in range(2):
                start = (2 * i + side) * width
                out[side * keep : (side + 1) * keep, :] = placed[:, start : start + width]

    return pl.pallas_call(
        kernel,
        in_specs=[SMEM_SPEC] + [VMEM_SPEC] * 6,
        out_specs=[VMEM_SPEC] * rounds,
        out_shape=[jax.ShapeDtypeStruct((2 * keep, width), BF16)] * rounds,
        scratch_shapes=[pltpu.VMEM(state.shape, F32)],
        compiler_params=pltpu.CompilerParams(vmem_limit_bytes=VMEM_LIMIT),
        cost_estimate=pl.CostEstimate(
            flops=2 * keep * onehot.shape[0] * onehot.shape[1], bytes_accessed=4 * state.size, transcendentals=0
        ),
    )(noise_power, own, peer, edge_own, edge_peer, onehot, state)


def assemble(sources, mine, theirs, others, cells, per_device, symbols, half):
    rounds = sum(group.shape[0] for group in mine)
    total = 2 * rounds * 2 * half
    lanes = mine[0].shape[2]
    keep = symbols * half
    number = len(mine)

    def kernel(source_ref, *refs):
        mine_refs, theirs_refs = refs[:number], refs[number : 2 * number]
        own_other, peer_others = refs[2 * number], refs[2 * number + 1 : 3 * number + 1]
        out, gathered = refs[3 * number + 1 :]
        panel = lax.axis_index("panel")

        def place(ref, i, first, source, side):
            start = pl.multiple_of(source * (2 * half) + side * half, half)
            for s in range(symbols):
                gathered[s, pl.ds(start, half), :] = ref[i, first + s * half : first + (s + 1) * half, :]

        for side, group in ((panel, mine_refs), (1 - panel, theirs_refs)):
            n = 0
            for ref in group:
                for i in range(ref.shape[0]):
                    place(ref, i, keep, source_ref[n], side)
                    n += 1
        for side, group in ((panel, (own_other,)), (1 - panel, peer_others)):
            n = rounds
            for ref in group:
                for i in range(ref.shape[0]):
                    place(ref, i, 0, source_ref[n], side)
                    n += 1
        for s in range(symbols):
            out[:, :, s] = gathered[s].T.reshape(cells, per_device, 2, total)

    return pl.pallas_call(
        kernel,
        in_specs=[SMEM_SPEC] + [VMEM_SPEC] * (3 * number + 1),
        out_specs=VMEM_SPEC,
        out_shape=jax.ShapeDtypeStruct((cells, per_device, symbols, 2, total), BF16),
        scratch_shapes=[pltpu.VMEM((symbols, total, lanes), BF16)],
        compiler_params=pltpu.CompilerParams(vmem_limit_bytes=VMEM_LIMIT),
    )(sources, *mine, *theirs, *others)


def body(channel, received, noise_power, user_count, serving_cell):
    cells, band, _, antennas, users = channel.shape
    symbols = received.shape[3]
    half = band // 2
    n_sc, n_cell = lax.axis_size("sc"), lax.axis_size("cell")
    panel, sc, cell = lax.axis_index("panel"), lax.axis_index("sc"), lax.axis_index("cell")

    samples = jnp.transpose(received, (0, 1, 3, 2, 4))

    inner = half - 1
    count = inner * 2 // 5
    first = inner_gram(user_count, channel, samples, True, 0, count, BF16, limit=56 << 20)
    first_peer = lax.ppermute(first, "panel", SWAP)
    bottom, top = band_ends(channel, first)
    low = lax.ppermute(top, "sc", [(i, i + 1) for i in range(n_sc - 1)])
    high = lax.ppermute(bottom, "sc", [(i + 1, i) for i in range(n_sc - 1)])
    second = inner_gram(user_count, channel, samples, True, count, inner - count, BF16)
    second_peer = lax.ppermute(second, "panel", SWAP)
    own = inner_gram(user_count, channel, samples, False, 0, inner, F32)
    low, high, own = lax.optimization_barrier((low, high, own))
    edge_peer = lax.ppermute(edge_gram(user_count, channel, samples, low, high), "panel", SWAP)
    state, edge_own = detect_first(user_count, noise_power, own, first_peer, channel, samples, low, high)

    capacity = cells * users // n_cell
    per_device = n_cell * capacity // n_sc
    reach = capacity // per_device
    keys = serving_cell[:, :, 0].reshape(-1)
    position = lax.iota(jnp.int32, cells * users)
    earlier = (keys[:, None] == keys[None, :]) & (position[None, :] < position[:, None])
    rank = jnp.sum(earlier.astype(jnp.int32), axis=1)
    turn = (rank // per_device - sc % reach) % reach * 2 + (keys // cells == sc // reach).astype(jnp.int32)
    column = ((turn * cells + keys % cells) * per_device + rank % per_device) * 2
    column = jnp.concatenate([column, column + 1])
    width = 2 * cells * per_device
    onehot = (column[:, None] == lax.iota(jnp.int32, 2 * reach * width)[None, :]).astype(BF16)

    messages = detect_last(noise_power, own, second_peer, edge_own, edge_peer, state, onehot, symbols, reach)
    arrived = []
    for b in range(reach):
        pairs = [
            (s * n_sc + j, j // reach * n_sc + s * reach + (j % reach + b) % reach)
            for s in range(n_cell)
            for j in range(n_sc)
        ]
        arrived.append(lax.ppermute(messages[b], ("cell", "sc"), pairs))
    turns = (sc % reach - lax.iota(jnp.int32, reach)) % reach
    sources = jnp.concatenate([cell * reach + turns, (1 - cell) * reach + turns])
    keep = symbols * half
    mine = [jnp.stack(arrived[: reach // 2]), jnp.stack(arrived[reach // 2 :])]
    theirs = [lax.ppermute(group, "panel", SWAP) for group in mine]
    others = [lax.ppermute(jnp.stack([block[:keep] for block in arrived]), "cell", SWAP)]
    others += [lax.ppermute(group[:, :keep], "cell", SWAP) for group in theirs]
    routed = assemble(sources, mine, theirs, others, cells, per_device, symbols, half)
    return jnp.transpose(routed, (0, 1, 3, 2, 4))


def solution(mesh):
    return jax.shard_map(
        body,
        mesh=mesh,
        in_specs=(
            P("cell", "sc", None, "panel", None),
            P("cell", "sc", None, None, "panel"),
            P("cell"),
            P("cell", "sc"),
            P("cell", None, None),
        ),
        out_specs=P("cell", "sc", None, None, None),
        check_vma=False,
    )
```

```python
import jax
import jax.numpy as jnp
from jax import lax
from jax.experimental import pallas as pl
from jax.experimental.pallas import tpu as pltpu
from jax.sharding import PartitionSpec as P

F32, BF16 = jnp.float32, jnp.bfloat16
GRP = 16
SPAD = 16
VMEM_LIMIT = 40 << 20
SWAP = [(0, 1), (1, 0)]

SMEM_SPEC = pl.BlockSpec(memory_space=pltpu.SMEM)
VMEM_SPEC = pl.BlockSpec(memory_space=pltpu.VMEM)
HBM_SPEC = pl.BlockSpec(memory_space=pltpu.HBM)


def cross(product, users):
    left, right = product[:, :users], product[:, users:]
    rows = product.shape[0]
    even = lax.broadcasted_iota(jnp.int32, left.shape, 0) % 2 == 0
    return left + jnp.where(even, pltpu.roll(right, rows - 1, 0), -pltpu.roll(right, 1, 0))


def prepare(below, here, above, samples, stretch, mat, lhs):
    antennas, users = here.shape[1:]
    symbols = samples.shape[0]
    slab = 128
    lhs[2 * users : 2 * (users + symbols), :] = samples[...].reshape(2 * symbols, antennas)
    for k in range(2):
        for row in range(0, antennas, slab):
            rows = pl.ds(row, slab)
            outer = below[k, rows, :].astype(F32) + above[k, rows, :].astype(F32)
            middle = here[k, rows, :]
            value = outer + (middle + middle).astype(F32)
            value = (value if stretch is None else value * stretch).astype(BF16)
            mat[rows, k * users : (k + 1) * users] = value
            lhs[k * users : (k + 1) * users, rows] = value.T


def gram(mat, lhs, out, count, users):
    product = jnp.dot(lhs[...], mat[...], preferred_element_type=F32)
    row = lax.broadcasted_iota(jnp.int32, (users, users), 0)
    col = lax.broadcasted_iota(jnp.int32, (users, users), 1)
    real = product[:users, :users] + product[users : 2 * users, users:]
    imag = product[:users, users:] - product[users : 2 * users, :users]
    packed = jnp.where(row <= col, real, imag)
    out[:users, :] = jnp.where(jnp.maximum(row, col) < count, packed * 0.0625, 0.0).astype(out.dtype)
    lane = lax.broadcasted_iota(jnp.int32, (1, users), 1)
    scale = jnp.where(lane < count, 0.25, 0.0)
    out[users:, :] = (cross(product[2 * users :], users) * scale).astype(out.dtype)


def work_buffers(antennas, users):
    return [
        pltpu.VMEM((antennas, 2 * users), BF16),
        pltpu.VMEM((2 * users + 2 * SPAD, antennas), BF16),
    ]


def inner_gram(counts, channel, received, peer, firsts, number, dtype, limit=VMEM_LIMIT, ends=False):
    cells, band, _, antennas, users = channel.shape
    symbols = received.shape[2]
    items = cells * number

    def kernel(counts_hbm, chan, samp, out, *refs):
        end_refs, refs = (refs[:2], refs[2:]) if ends else ((), refs)
        count_ref, win, ybuf, mat_a, lhs_a, mat_b, lhs_b, wsem, ysem, csem, esem = refs
        count_copy = pltpu.make_async_copy(counts_hbm, count_ref, csem)
        count_copy.start()
        panel = lax.axis_index("panel")
        side = 1 - panel if peer else panel
        start = jnp.where(side == 0, firsts[0], firsts[1])
        end_copies = [
            pltpu.make_async_copy(chan.at[c, i * (band - 1)], end_ref.at[c, 0], esem.at[c, i])
            for c in range(cells)
            for i, end_ref in enumerate(end_refs)
        ]

        def fetch(c, i):
            return pltpu.make_async_copy(chan.at[c, start - 1 + i], win.at[c, i], wsem.at[c, i])

        def fetch_samples(c):
            return pltpu.make_async_copy(samp.at[c, pl.ds(start, number)], ybuf.at[c], ysem.at[c])

        for c in range(cells):
            for i in range(number + 2):
                fetch(c, i).start()
                if i == min(2, number):
                    fetch_samples(c).start()
        for copy in end_copies:
            copy.start()
        lhs_a[...] = jnp.zeros_like(lhs_a)
        lhs_b[...] = jnp.zeros_like(lhs_b)

        def wait(item):
            c, i = item // number, item % number

            @pl.when(item < items)
            def _():
                @pl.when(i == 0)
                def _():
                    fetch_samples(c).wait()
                    fetch(c, 0).wait()
                    fetch(c, 1).wait()

                fetch(c, i + 2).wait()

        def ready(item, mat, lhs):
            item = jnp.minimum(item, items - 1)
            c, i = item // number, item % number
            prepare(win.at[c, i], win.at[c, i + 1], win.at[c, i + 2], ybuf.at[c, i], None, mat, lhs)

        def multiply(item, mat, lhs):
            item = jnp.minimum(item, items - 1)
            c, i = item // number, item % number
            gram(mat, lhs, out.at[c, i], count_ref[c, (start + i) // GRP], users)

        count_copy.wait()
        wait(0)
        ready(0, mat_a, lhs_a)

        def step(t, carry):
            wait(2 * t + 1)
            wait(2 * t + 2)
            ready(2 * t + 1, mat_b, lhs_b)
            multiply(2 * t, mat_a, lhs_a)
            ready(2 * t + 2, mat_a, lhs_a)
            multiply(2 * t + 1, mat_b, lhs_b)
            return carry

        lax.fori_loop(0, (items + 1) // 2, step, 0)
        for copy in end_copies:
            copy.wait()

    rows = users + 2 * SPAD
    return pl.pallas_call(
        kernel,
        in_specs=[HBM_SPEC] * 3,
        out_specs=[VMEM_SPEC] * (1 + 2 * ends),
        out_shape=[jax.ShapeDtypeStruct((cells, number, rows, users), dtype)]
        + [jax.ShapeDtypeStruct((cells, 1, 2, antennas, users), BF16)] * (2 * ends),
        scratch_shapes=[
            pltpu.SMEM(counts.shape, jnp.int32),
            pltpu.VMEM((cells, number + 2, 2, antennas, users), BF16),
            pltpu.VMEM((cells, number, symbols, 2, antennas), BF16),
            *work_buffers(antennas, users),
            *work_buffers(antennas, users),
            pltpu.SemaphoreType.DMA((cells, number + 2)),
            pltpu.SemaphoreType.DMA((cells,)),
            pltpu.SemaphoreType.DMA,
            pltpu.SemaphoreType.DMA((cells, 2)),
        ],
        compiler_params=pltpu.CompilerParams(vmem_limit_bytes=limit),
        cost_estimate=pl.CostEstimate(
            flops=items * 4 * antennas * users * 2 * (users + SPAD),
            bytes_accessed=cells * (number + 2) * 4 * antennas * users,
            transcendentals=0,
        ),
    )(counts, channel, received)


def hand_on(arrays):
    def kernel(*refs):
        refs[-1][0] = 0

    return pl.pallas_call(
        kernel,
        in_specs=[HBM_SPEC] * len(arrays),
        out_specs=[HBM_SPEC] * len(arrays),
        out_shape=[jax.ShapeDtypeStruct(a.shape, a.dtype) for a in arrays],
        scratch_shapes=[pltpu.SMEM((1,), jnp.int32)],
        input_output_aliases={i: i for i in range(len(arrays))},
    )(*arrays)


def edge_scratch(counts, symbols, antennas, users):
    cells = counts.shape[0]
    return [
        pltpu.SMEM(counts.shape, jnp.int32),
        pltpu.VMEM((cells, 3, 2, antennas, users), BF16),
        pltpu.VMEM((cells, symbols, 2, antennas), BF16),
        *work_buffers(antennas, users),
        *work_buffers(antennas, users),
        pltpu.SemaphoreType.DMA((cells, 3)),
        pltpu.SemaphoreType.DMA((cells,)),
        pltpu.SemaphoreType.DMA,
    ]


def edge_work(side, counts_hbm, chan, samp, low_ref, high_ref, out, scratch):
    count_ref, win, ybuf, mat_a, lhs_a, mat_b, lhs_b, wsem, ysem, csem = scratch
    count_copy = pltpu.make_async_copy(counts_hbm, count_ref, csem)
    cells, band, _, _, users = chan.shape
    buffers = ((mat_a, lhs_a), (mat_b, lhs_b))

    def each_copy(act):
        def run(e):
            for c in range(cells):
                blocks = (
                    (low_ref.at[c, 0], chan.at[c, 0], chan.at[c, 1]),
                    (chan.at[c, band - 2], chan.at[c, band - 1], high_ref.at[c, 0]),
                )[e]
                for i, block in enumerate(blocks):
                    act(pltpu.make_async_copy(block, win.at[c, i], wsem.at[c, i]))
                act(pltpu.make_async_copy(samp.at[c, e * (band - 1)], ybuf.at[c], ysem.at[c]))

        @pl.when(side == 0)
        def _():
            run(0)

        @pl.when(side == 1)
        def _():
            run(1)

    def fetch():
        count_copy.start()
        each_copy(lambda copy: copy.start())
        lhs_a[...] = jnp.zeros_like(lhs_a)
        lhs_b[...] = jnp.zeros_like(lhs_b)

    def work():
        each_copy(lambda copy: copy.wait())
        count_copy.wait()
        last = lax.axis_index("sc") == side * (lax.axis_size("sc") - 1)
        stretch = jnp.where(jnp.full((1, users), last.astype(jnp.int32)) == 1, 1 / 0.75, 1.0)
        for c in range(cells):
            prepare(win.at[c, 0], win.at[c, 1], win.at[c, 2], ybuf.at[c], stretch, *buffers[c % 2])
        for c in range(cells):
            gram(*buffers[c % 2], out.at[c], count_ref[c, side * (band - 1) // GRP], users)

    return fetch, work


def edge_gram(counts, channel, received, low, high, peer, dtype):
    cells, _, _, antennas, users = channel.shape
    symbols = received.shape[2]

    def kernel(counts_hbm, chan, samp, low_ref, high_ref, out, *scratch):
        panel = lax.axis_index("panel")
        fetch, work = edge_work(1 - panel if peer else panel, counts_hbm, chan, samp, low_ref, high_ref, out, scratch)
        fetch()
        work()

    return pl.pallas_call(
        kernel,
        in_specs=[HBM_SPEC] * 5,
        out_specs=VMEM_SPEC,
        out_shape=jax.ShapeDtypeStruct((cells, users + 2 * SPAD, users), dtype),
        scratch_shapes=edge_scratch(counts, symbols, antennas, users),
        compiler_params=pltpu.CompilerParams(vmem_limit_bytes=VMEM_LIMIT),
        cost_estimate=pl.CostEstimate(
            flops=cells * 4 * antennas * users * 2 * (users + SPAD),
            bytes_accessed=cells * 12 * antennas * users,
            transcendentals=0,
        ),
    )(counts, channel, received, low, high)


def conjugate_gradient(sums, noises, users):
    row = lax.broadcasted_iota(jnp.int32, (users, users), 0)
    col = lax.broadcasted_iota(jnp.int32, (users, users), 1)
    upper = row <= col
    grams = []
    for value in sums:
        packed = value[:users].astype(BF16)
        turned = packed.T
        real = jnp.where(upper, packed, turned)
        imag = jnp.where(row == col, jnp.zeros_like(packed), jnp.where(upper, -turned, packed))
        grams.append(jnp.concatenate([real, imag], axis=1))

    def apply(matrix, vector, noise):
        product = jnp.dot(vector.astype(BF16), matrix, preferred_element_type=F32)
        return cross(product, users) + noise * vector

    def user_sum(left, right):
        total = left * right
        even = lax.broadcasted_iota(jnp.int32, total.shape, 0) % 2 == 0
        total = total + jnp.where(even, pltpu.roll(total, 2 * SPAD - 1, 0), pltpu.roll(total, 1, 0))
        return jnp.sum(total, axis=1, keepdims=True)

    direction = [value[users:] for value in sums]
    norm = [user_sum(d, d) for d in direction]
    image = [apply(*terms) for terms in zip(grams, direction, noises)]
    alpha = [n / user_sum(d, i) for n, d, i in zip(norm, direction, image)]
    estimate = [a * d for a, d in zip(alpha, direction)]
    residual = [d - a * i for d, a, i in zip(direction, alpha, image)]
    norm_next = [user_sum(r, r) for r in residual]
    direction = [r + (m / n) * d for r, m, n, d in zip(residual, norm_next, norm, direction)]
    image = [apply(*terms) for terms in zip(grams, direction, noises)]
    alpha = [n / user_sum(d, i) for n, d, i in zip(norm_next, direction, image)]
    return [e + a * d for e, a, d in zip(estimate, alpha, direction)]


def detect(noise_power, own, own_firsts, peer, edges, onehot, symbols, rounds):
    cells, _, rows, users = own.shape
    number = peer.shape[1]
    half = number + (len(edges) > 0)
    width = onehot.shape[1] // (2 * rounds)
    keep = symbols * half

    def kernel(noise_ref, own_ref, peer_ref, hot_ref, *refs):
        edge_refs, outs, full = refs[: len(edges)], refs[len(edges) : -1], refs[-1]
        panel = lax.axis_index("panel")
        first = jnp.where(panel == 0, own_firsts[0], own_firsts[1])
        spots = [(c, i) for c in range(cells) for i in range(number)]
        sums = [own_ref[c, first + i] + peer_ref[c, i].astype(F32) for c, i in spots]
        places = [(c, i + 1 - panel if edges else i) for c, i in spots]
        if edges:
            edge_own_ref, edge_peer_ref = edge_refs
            sums += [edge_own_ref[c] + edge_peer_ref[c].astype(F32) for c in range(cells)]
            places += [(c, panel * (half - 1)) for c in range(cells)]
        values = conjugate_gradient(sums, [noise_ref[c] for c, _ in places], users)
        for (c, place), value in zip(places, values):
            full[c, pl.ds(place, 2 * SPAD, stride=half), :] = value
        blocks = [
            jnp.concatenate([full[c, (2 * s + k) * half : (2 * s + k + 1) * half] for s in range(symbols)], axis=0)
            for k in range(2)
            for c in range(cells)
        ]
        lhs = jnp.concatenate(blocks, axis=1).astype(BF16)
        placed = jnp.dot(lhs, hot_ref[...], preferred_element_type=F32).astype(BF16)
        for i, out in enumerate(outs):
            for side in range(2):
                start = (2 * i + side) * width
                out[side * keep : (side + 1) * keep, :] = placed[:, start : start + width]

    return pl.pallas_call(
        kernel,
        in_specs=[SMEM_SPEC] + [VMEM_SPEC] * (3 + len(edges)),
        out_specs=[VMEM_SPEC] * rounds,
        out_shape=[jax.ShapeDtypeStruct((2 * keep, width), BF16)] * rounds,
        scratch_shapes=[pltpu.VMEM((cells, 2 * SPAD * half, users), F32)],
        compiler_params=pltpu.CompilerParams(vmem_limit_bytes=VMEM_LIMIT),
        cost_estimate=pl.CostEstimate(
            flops=2 * keep * onehot.shape[0] * onehot.shape[1], bytes_accessed=4 * own.size, transcendentals=0
        ),
    )(noise_power, own, peer, onehot, *edges)


def assemble(sources, parts, cells, per_device, symbols, half):
    rounds = parts[0][0].shape[0]
    total = 2 * rounds * 2 * half
    lanes = parts[0][0].shape[2]
    keep = symbols * half // 2

    def kernel(source_ref, *refs):
        out, gathered = refs[4 * len(parts) :]
        panel = lax.axis_index("panel")
        for n in range(len(parts)):
            for r in range(4):
                ref = refs[4 * n + r]
                side = panel if r % 2 == 0 else 1 - panel
                inside = side * half + (1 - side if n == 0 else side) * (half // 2)
                for i in range(rounds):
                    source = source_ref[i if r < 2 else rounds + i]
                    start = pl.multiple_of(source * (2 * half) + inside, half // 2)
                    block = ref[i, keep if r < 2 else 0 : 2 * keep if r < 2 else keep, :].astype(F32)
                    for s in range(symbols):
                        gathered[s, pl.ds(start, half // 2), :] = block[s * (half // 2) : (s + 1) * (half // 2)]
        for s in range(symbols):
            out[:, :, s] = gathered[s].astype(BF16).T.reshape(cells, per_device, 2, total)

    return pl.pallas_call(
        kernel,
        in_specs=[SMEM_SPEC] + [VMEM_SPEC] * (4 * len(parts)),
        out_specs=VMEM_SPEC,
        out_shape=jax.ShapeDtypeStruct((cells, per_device, symbols, 2, total), BF16),
        scratch_shapes=[pltpu.VMEM((symbols, total, lanes), F32)],
        compiler_params=pltpu.CompilerParams(vmem_limit_bytes=VMEM_LIMIT),
    )(sources, *[array for part in parts for array in part])


def body(channel, received, noise_power, user_count, serving_cell):
    cells, band, _, antennas, users = channel.shape
    symbols = received.shape[3]
    half = band // 2
    n_sc, n_cell = lax.axis_size("sc"), lax.axis_size("cell")
    panel, sc, cell = lax.axis_index("panel"), lax.axis_index("sc"), lax.axis_index("cell")

    samples = jnp.transpose(received, (0, 1, 3, 2, 4))

    part = half // 2
    middle, outer = (part, half), (1, band - part)
    first, bottom, top = inner_gram(
        user_count, channel, samples, True, middle, part, BF16, limit=56 << 20, ends=True
    )
    first_peer = lax.ppermute(first, "panel", SWAP)
    bottom, top = hand_on([bottom, top])
    low = lax.ppermute(top, "sc", [(i, i + 1) for i in range(n_sc - 1)])
    high = lax.ppermute(bottom, "sc", [(i + 1, i) for i in range(n_sc - 1)])
    (second,) = inner_gram(user_count, channel, samples, True, outer, part - 1, BF16, limit=56 << 20)
    second_peer = lax.ppermute(second, "panel", SWAP)
    (own,) = inner_gram(user_count, channel, samples, False, (1, half), half - 1, F32)

    capacity = cells * users // n_cell
    per_device = n_cell * capacity // n_sc
    reach = capacity // per_device
    keys = serving_cell[:, :, 0].reshape(-1)
    position = lax.iota(jnp.int32, cells * users)
    earlier = (keys[:, None] == keys[None, :]) & (position[None, :] < position[:, None])
    rank = jnp.sum(earlier.astype(jnp.int32), axis=1)
    turn = (rank // per_device - sc % reach) % reach * 2 + (keys // cells == sc // reach).astype(jnp.int32)
    column = ((turn * cells + keys % cells) * per_device + rank % per_device) * 2
    column = jnp.concatenate([column, column + 1])
    width = 2 * cells * per_device
    onehot = (column[:, None] == lax.iota(jnp.int32, 2 * reach * width)[None, :]).astype(BF16)

    def travel(messages):
        arrived = []
        for b in range(reach):
            pairs = [
                (s * n_sc + j, j // reach * n_sc + s * reach + (j % reach + b) % reach)
                for s in range(n_cell)
                for j in range(n_sc)
            ]
            arrived.append(lax.ppermute(messages[b], ("cell", "sc"), pairs))
        return arrived

    keep = symbols * part
    messages = detect(noise_power, own, (part - 1, 0), first_peer, (), onehot, symbols, reach)
    arrived_1 = travel(messages)
    low, high, arrived_1[: reach // 2] = lax.optimization_barrier((low, high, arrived_1[: reach // 2]))
    mine_1 = jnp.stack(arrived_1)
    theirs_1 = lax.ppermute(mine_1, "panel", SWAP)
    edge_peer = lax.ppermute(edge_gram(user_count, channel, samples, low, high, True, BF16), "panel", SWAP)
    edge_own = edge_gram(user_count, channel, samples, low, high, False, F32)
    second_peer, mine_1 = lax.optimization_barrier((second_peer, mine_1))
    messages = detect(noise_power, own, (0, part), second_peer, (edge_own, edge_peer), onehot, symbols, reach)
    mine_2 = jnp.stack(travel(messages))
    theirs_2 = lax.ppermute(mine_2, "panel", SWAP)
    gifts = lax.ppermute(jnp.stack([mine_1[:, :keep], theirs_1[:, :keep], mine_2[:, :keep]]), "cell", SWAP)
    last = lax.ppermute(theirs_2[:, :keep], "cell", SWAP)
    turns = (sc % reach - lax.iota(jnp.int32, reach)) % reach
    sources = jnp.concatenate([cell * reach + turns, (1 - cell) * reach + turns])
    parts = ((mine_1, theirs_1, gifts[0], gifts[1]), (mine_2, theirs_2, gifts[2], last))
    routed = assemble(sources, parts, cells, per_device, symbols, half)
    return jnp.transpose(routed, (0, 1, 3, 2, 4))


def solution(mesh):
    return jax.shard_map(
        body,
        mesh=mesh,
        in_specs=(
            P("cell", "sc", None, "panel", None),
            P("cell", "sc", None, None, "panel"),
            P("cell"),
            P("cell", "sc"),
            P("cell", None, None),
        ),
        out_specs=P("cell", "sc", None, None, None),
        check_vma=False,
    )
```

```python
import jax
import jax.numpy as jnp
from jax import lax
from jax.experimental import pallas as pl
from jax.experimental.pallas import tpu as pltpu
from jax.sharding import PartitionSpec as P

F32, BF16 = jnp.float32, jnp.bfloat16
GRP = 16
SPAD = 16
VMEM_LIMIT = 40 << 20
SWAP = [(0, 1), (1, 0)]

SMEM_SPEC = pl.BlockSpec(memory_space=pltpu.SMEM)
VMEM_SPEC = pl.BlockSpec(memory_space=pltpu.VMEM)
HBM_SPEC = pl.BlockSpec(memory_space=pltpu.HBM)


def cross(product, users):
    left, right = product[:, :users], product[:, users:]
    rows = product.shape[0]
    even = lax.broadcasted_iota(jnp.int32, left.shape, 0) % 2 == 0
    return left + jnp.where(even, pltpu.roll(right, rows - 1, 0), -pltpu.roll(right, 1, 0))


def prepare(below, here, above, samples, stretch, mat, lhs):
    antennas, users = here.shape[1:]
    symbols = samples.shape[0]
    slab = 128
    lhs[2 * users : 2 * (users + symbols), :] = samples[...].reshape(2 * symbols, antennas)
    for k in range(2):
        for row in range(0, antennas, slab):
            rows = pl.ds(row, slab)
            outer = below[k, rows, :].astype(F32) + above[k, rows, :].astype(F32)
            middle = here[k, rows, :]
            value = outer + (middle + middle).astype(F32)
            value = (value if stretch is None else value * stretch).astype(BF16)
            mat[rows, k * users : (k + 1) * users] = value
            lhs[k * users : (k + 1) * users, rows] = value.T


def gram(mat, lhs, out, count, users):
    product = jnp.dot(lhs[...], mat[...], preferred_element_type=F32)
    row = lax.broadcasted_iota(jnp.int32, (users, users), 0)
    col = lax.broadcasted_iota(jnp.int32, (users, users), 1)
    real = product[:users, :users] + product[users : 2 * users, users:]
    imag = product[:users, users:] - product[users : 2 * users, :users]
    packed = jnp.where(row <= col, real, imag)
    out[:users, :] = jnp.where(jnp.maximum(row, col) < count, packed * 0.0625, 0.0).astype(out.dtype)
    lane = lax.broadcasted_iota(jnp.int32, (1, users), 1)
    scale = jnp.where(lane < count, 0.25, 0.0)
    out[users:, :] = (cross(product[2 * users :], users) * scale).astype(out.dtype)


def work_buffers(antennas, users):
    return [
        pltpu.VMEM((antennas, 2 * users), BF16),
        pltpu.VMEM((2 * users + 2 * SPAD, antennas), BF16),
    ]


def inner_gram(counts, channel, received, peer, firsts, number, dtype, limit=VMEM_LIMIT, ends=False):
    cells, band, _, antennas, users = channel.shape
    symbols = received.shape[2]
    items = cells * number

    def kernel(counts_hbm, chan, samp, out, *refs):
        end_refs, refs = (refs[:2], refs[2:]) if ends else ((), refs)
        count_ref, win, ybuf, mat_a, lhs_a, mat_b, lhs_b, wsem, ysem, csem, esem = refs
        count_copy = pltpu.make_async_copy(counts_hbm, count_ref, csem)
        count_copy.start()
        panel = lax.axis_index("panel")
        side = 1 - panel if peer else panel
        start = jnp.where(side == 0, firsts[0], firsts[1])
        end_copies = [
            pltpu.make_async_copy(chan.at[c, i * (band - 1)], end_ref.at[c, 0], esem.at[c, i])
            for c in range(cells)
            for i, end_ref in enumerate(end_refs)
        ]

        def fetch(c, i):
            return pltpu.make_async_copy(chan.at[c, start - 1 + i], win.at[c, i], wsem.at[c, i])

        def fetch_samples(c):
            return pltpu.make_async_copy(samp.at[c, pl.ds(start, number)], ybuf.at[c], ysem.at[c])

        for c in range(cells):
            for i in range(number + 2):
                fetch(c, i).start()
                if i == min(2, number):
                    fetch_samples(c).start()
        for copy in end_copies:
            copy.start()
        lhs_a[...] = jnp.zeros_like(lhs_a)
        lhs_b[...] = jnp.zeros_like(lhs_b)

        def wait(item):
            c, i = item // number, item % number

            @pl.when(item < items)
            def _():
                @pl.when(i == 0)
                def _():
                    fetch_samples(c).wait()
                    fetch(c, 0).wait()
                    fetch(c, 1).wait()

                fetch(c, i + 2).wait()

        def ready(item, mat, lhs):
            item = jnp.minimum(item, items - 1)
            c, i = item // number, item % number
            prepare(win.at[c, i], win.at[c, i + 1], win.at[c, i + 2], ybuf.at[c, i], None, mat, lhs)

        def multiply(item, mat, lhs):
            item = jnp.minimum(item, items - 1)
            c, i = item // number, item % number
            gram(mat, lhs, out.at[c, i], count_ref[c, (start + i) // GRP], users)

        count_copy.wait()
        wait(0)
        ready(0, mat_a, lhs_a)

        def step(t, carry):
            wait(2 * t + 1)
            wait(2 * t + 2)
            ready(2 * t + 1, mat_b, lhs_b)
            multiply(2 * t, mat_a, lhs_a)
            ready(2 * t + 2, mat_a, lhs_a)
            multiply(2 * t + 1, mat_b, lhs_b)
            return carry

        lax.fori_loop(0, (items + 1) // 2, step, 0)
        for copy in end_copies:
            copy.wait()

    rows = users + 2 * SPAD
    return pl.pallas_call(
        kernel,
        in_specs=[HBM_SPEC] * 3,
        out_specs=[VMEM_SPEC] * (1 + 2 * ends),
        out_shape=[jax.ShapeDtypeStruct((cells, number, rows, users), dtype)]
        + [jax.ShapeDtypeStruct((cells, 1, 2, antennas, users), BF16)] * (2 * ends),
        scratch_shapes=[
            pltpu.SMEM(counts.shape, jnp.int32),
            pltpu.VMEM((cells, number + 2, 2, antennas, users), BF16),
            pltpu.VMEM((cells, number, symbols, 2, antennas), BF16),
            *work_buffers(antennas, users),
            *work_buffers(antennas, users),
            pltpu.SemaphoreType.DMA((cells, number + 2)),
            pltpu.SemaphoreType.DMA((cells,)),
            pltpu.SemaphoreType.DMA,
            pltpu.SemaphoreType.DMA((cells, 2)),
        ],
        compiler_params=pltpu.CompilerParams(vmem_limit_bytes=limit),
        cost_estimate=pl.CostEstimate(
            flops=items * 4 * antennas * users * 2 * (users + SPAD) // (1 if peer else 16),
            bytes_accessed=cells * (number + 2) * 4 * antennas * users // (1 if peer else 16),
            transcendentals=0,
        ),
    )(counts, channel, received)


def hand_on(arrays):
    def kernel(*refs):
        refs[-1][0] = 0

    return pl.pallas_call(
        kernel,
        in_specs=[HBM_SPEC] * len(arrays),
        out_specs=[HBM_SPEC] * len(arrays),
        out_shape=[jax.ShapeDtypeStruct(a.shape, a.dtype) for a in arrays],
        scratch_shapes=[pltpu.SMEM((1,), jnp.int32)],
        input_output_aliases={i: i for i in range(len(arrays))},
        cost_estimate=pl.CostEstimate(flops=0, bytes_accessed=8 * arrays[0].size, transcendentals=0),
    )(*arrays)


def edge_scratch(counts, symbols, antennas, users):
    cells = counts.shape[0]
    return [
        pltpu.SMEM(counts.shape, jnp.int32),
        pltpu.VMEM((cells, 3, 2, antennas, users), BF16),
        pltpu.VMEM((cells, symbols, 2, antennas), BF16),
        *work_buffers(antennas, users),
        *work_buffers(antennas, users),
        pltpu.SemaphoreType.DMA((cells, 3)),
        pltpu.SemaphoreType.DMA((cells,)),
        pltpu.SemaphoreType.DMA,
    ]


def edge_work(side, counts_hbm, chan, samp, low_ref, high_ref, out, scratch):
    count_ref, win, ybuf, mat_a, lhs_a, mat_b, lhs_b, wsem, ysem, csem = scratch
    count_copy = pltpu.make_async_copy(counts_hbm, count_ref, csem)
    cells, band, _, _, users = chan.shape
    buffers = ((mat_a, lhs_a), (mat_b, lhs_b))

    def each_copy(act):
        def run(e):
            for c in range(cells):
                blocks = (
                    (low_ref.at[c, 0], chan.at[c, 0], chan.at[c, 1]),
                    (chan.at[c, band - 2], chan.at[c, band - 1], high_ref.at[c, 0]),
                )[e]
                for i, block in enumerate(blocks):
                    act(pltpu.make_async_copy(block, win.at[c, i], wsem.at[c, i]))
                act(pltpu.make_async_copy(samp.at[c, e * (band - 1)], ybuf.at[c], ysem.at[c]))

        @pl.when(side == 0)
        def _():
            run(0)

        @pl.when(side == 1)
        def _():
            run(1)

    def fetch():
        count_copy.start()
        each_copy(lambda copy: copy.start())
        lhs_a[...] = jnp.zeros_like(lhs_a)
        lhs_b[...] = jnp.zeros_like(lhs_b)

    def work():
        each_copy(lambda copy: copy.wait())
        count_copy.wait()
        last = lax.axis_index("sc") == side * (lax.axis_size("sc") - 1)
        stretch = jnp.where(jnp.full((1, users), last.astype(jnp.int32)) == 1, 1 / 0.75, 1.0)
        for c in range(cells):
            prepare(win.at[c, 0], win.at[c, 1], win.at[c, 2], ybuf.at[c], stretch, *buffers[c % 2])
        for c in range(cells):
            gram(*buffers[c % 2], out.at[c], count_ref[c, side * (band - 1) // GRP], users)

    return fetch, work


def edge_gram(counts, channel, received, low, high, peer, dtype):
    cells, _, _, antennas, users = channel.shape
    symbols = received.shape[2]

    def kernel(counts_hbm, chan, samp, low_ref, high_ref, out, *scratch):
        panel = lax.axis_index("panel")
        fetch, work = edge_work(1 - panel if peer else panel, counts_hbm, chan, samp, low_ref, high_ref, out, scratch)
        fetch()
        work()

    return pl.pallas_call(
        kernel,
        in_specs=[HBM_SPEC] * 5,
        out_specs=VMEM_SPEC,
        out_shape=jax.ShapeDtypeStruct((cells, users + 2 * SPAD, users), dtype),
        scratch_shapes=edge_scratch(counts, symbols, antennas, users),
        compiler_params=pltpu.CompilerParams(vmem_limit_bytes=VMEM_LIMIT),
        cost_estimate=pl.CostEstimate(
            flops=cells * 4 * antennas * users * 2 * (users + SPAD),
            bytes_accessed=cells * 12 * antennas * users,
            transcendentals=0,
        ),
    )(counts, channel, received, low, high)


def conjugate_gradient(sums, noises, users):
    row = lax.broadcasted_iota(jnp.int32, (users, users), 0)
    col = lax.broadcasted_iota(jnp.int32, (users, users), 1)
    upper = row <= col
    grams = []
    for value in sums:
        packed = value[:users].astype(BF16)
        turned = packed.T
        real = jnp.where(upper, packed, turned)
        imag = jnp.where(row == col, jnp.zeros_like(packed), jnp.where(upper, -turned, packed))
        grams.append(jnp.concatenate([real, imag], axis=1))

    def apply(matrix, vector, noise):
        product = jnp.dot(vector.astype(BF16), matrix, preferred_element_type=F32)
        return cross(product, users) + noise * vector

    def user_sum(left, right):
        total = left * right
        even = lax.broadcasted_iota(jnp.int32, total.shape, 0) % 2 == 0
        total = total + jnp.where(even, pltpu.roll(total, 2 * SPAD - 1, 0), pltpu.roll(total, 1, 0))
        return jnp.sum(total, axis=1, keepdims=True)

    direction = [value[users:] for value in sums]
    norm = [user_sum(d, d) for d in direction]
    image = [apply(*terms) for terms in zip(grams, direction, noises)]
    alpha = [n / user_sum(d, i) for n, d, i in zip(norm, direction, image)]
    estimate = [a * d for a, d in zip(alpha, direction)]
    residual = [d - a * i for d, a, i in zip(direction, alpha, image)]
    norm_next = [user_sum(r, r) for r in residual]
    direction = [r + (m / n) * d for r, m, n, d in zip(residual, norm_next, norm, direction)]
    image = [apply(*terms) for terms in zip(grams, direction, noises)]
    alpha = [n / user_sum(d, i) for n, d, i in zip(norm_next, direction, image)]
    return [e + a * d for e, a, d in zip(estimate, alpha, direction)]


def detect_first(noise_power, own, peer):
    cells, inner, rows, users = own.shape
    half, number = inner + 1, peer.shape[1]

    def kernel(noise_ref, own_ref, peer_ref, out):
        panel = lax.axis_index("panel")
        spots = [(c, i) for c in range(cells) for i in range(number)]
        sums = [own_ref[c, i] + peer_ref[c, i].astype(F32) for c, i in spots]
        values = conjugate_gradient(sums, [noise_ref[c] for c, _ in spots], users)
        for (c, i), value in zip(spots, values):
            out[c, pl.ds(i + 1 - panel, 2 * SPAD, stride=half), :] = value

    return pl.pallas_call(
        kernel,
        in_specs=[SMEM_SPEC] + [VMEM_SPEC] * 2,
        out_specs=VMEM_SPEC,
        out_shape=jax.ShapeDtypeStruct((cells, 2 * SPAD * half, users), F32),
        compiler_params=pltpu.CompilerParams(vmem_limit_bytes=VMEM_LIMIT),
        cost_estimate=pl.CostEstimate(
            flops=cells * number * 2 * 2 * 2 * SPAD * users * 2 * users,
            bytes_accessed=cells * inner * rows * users * 6,
            transcendentals=0,
        ),
    )(noise_power, own, peer)


def detect_last(noise_power, own, peer, edge_own, edge_peer, state, onehot, symbols, rounds):
    cells, inner, rows, users = own.shape
    half, number = inner + 1, peer.shape[1]
    width = onehot.shape[1] // (2 * rounds)
    keep = symbols * half

    def kernel(noise_ref, own_ref, peer_ref, edge_own_ref, edge_peer_ref, hot_ref, state_ref, *refs):
        *outs, full = refs
        panel = lax.axis_index("panel")
        full[...] = state_ref[...]
        first = inner - number
        spots = [(c, i) for c in range(cells) for i in range(number)]
        sums = [own_ref[c, first + i] + peer_ref[c, i].astype(F32) for c, i in spots]
        places = [(c, first + i + 1 - panel) for c, i in spots]
        sums += [edge_own_ref[c] + edge_peer_ref[c].astype(F32) for c in range(cells)]
        places += [(c, panel * (half - 1)) for c in range(cells)]
        values = conjugate_gradient(sums, [noise_ref[c] for c, _ in places], users)
        for (c, place), value in zip(places, values):
            full[c, pl.ds(place, 2 * SPAD, stride=half), :] = value
        found = full[...].astype(BF16)
        blocks = [
            jnp.concatenate([found[c, (2 * s + k) * half : (2 * s + k + 1) * half] for s in range(symbols)], axis=0)
            for k in range(2)
            for c in range(cells)
        ]
        lhs = jnp.concatenate(blocks, axis=1)
        placed = jnp.dot(lhs, hot_ref[...], preferred_element_type=F32).astype(BF16)
        for i, out in enumerate(outs):
            for side in range(2):
                start = (2 * i + side) * width
                out[side * keep : (side + 1) * keep, :] = placed[:, start : start + width]

    return pl.pallas_call(
        kernel,
        in_specs=[SMEM_SPEC] + [VMEM_SPEC] * 6,
        out_specs=[VMEM_SPEC] * rounds,
        out_shape=[jax.ShapeDtypeStruct((2 * keep, width), BF16)] * rounds,
        scratch_shapes=[pltpu.VMEM(state.shape, F32)],
        compiler_params=pltpu.CompilerParams(vmem_limit_bytes=VMEM_LIMIT),
        cost_estimate=pl.CostEstimate(
            flops=2 * keep * onehot.shape[0] * onehot.shape[1], bytes_accessed=4 * state.size, transcendentals=0
        ),
    )(noise_power, own, peer, edge_own, edge_peer, onehot, state)


def assemble(sources, mine, theirs, others, cells, per_device, symbols, half):
    rounds = sum(group.shape[0] for group in mine)
    total = 2 * rounds * 2 * half
    lanes = mine[0].shape[2]
    keep = symbols * half
    number = len(mine)

    def kernel(source_ref, *refs):
        mine_refs, theirs_refs = refs[:number], refs[number : 2 * number]
        own_other, peer_others = refs[2 * number], refs[2 * number + 1 : 3 * number + 1]
        out, gathered = refs[3 * number + 1 :]
        panel = lax.axis_index("panel")

        def place(ref, i, first, source, side):
            start = pl.multiple_of(source * (2 * half) + side * half, half)
            for s in range(symbols):
                gathered[s, pl.ds(start, half), :] = ref[i, first + s * half : first + (s + 1) * half, :]

        for side, group in ((panel, mine_refs), (1 - panel, theirs_refs)):
            n = 0
            for ref in group:
                for i in range(ref.shape[0]):
                    place(ref, i, keep, source_ref[n], side)
                    n += 1
        for side, group in ((panel, (own_other,)), (1 - panel, peer_others)):
            n = rounds
            for ref in group:
                for i in range(ref.shape[0]):
                    place(ref, i, 0, source_ref[n], side)
                    n += 1
        for s in range(symbols):
            out[:, :, s] = gathered[s].T.reshape(cells, per_device, 2, total)

    return pl.pallas_call(
        kernel,
        in_specs=[SMEM_SPEC] + [VMEM_SPEC] * (3 * number + 1),
        out_specs=VMEM_SPEC,
        out_shape=jax.ShapeDtypeStruct((cells, per_device, symbols, 2, total), BF16),
        scratch_shapes=[pltpu.VMEM((symbols, total, lanes), BF16)],
        compiler_params=pltpu.CompilerParams(vmem_limit_bytes=VMEM_LIMIT),
    )(sources, *mine, *theirs, *others)


def body(channel, received, noise_power, user_count, serving_cell):
    cells, band, _, antennas, users = channel.shape
    symbols = received.shape[3]
    half = band // 2
    n_sc, n_cell = lax.axis_size("sc"), lax.axis_size("cell")
    panel, sc, cell = lax.axis_index("panel"), lax.axis_index("sc"), lax.axis_index("cell")

    samples = jnp.transpose(received, (0, 1, 3, 2, 4))

    inner = half - 1
    count = inner * 2 // 5
    first, bottom, top = inner_gram(
        user_count, channel, samples, True, (1, half), count, BF16, limit=56 << 20, ends=True
    )
    first_peer = lax.ppermute(first, "panel", SWAP)
    bottom, top = hand_on([bottom, top])
    low = lax.ppermute(top, "sc", [(i, i + 1) for i in range(n_sc - 1)])
    high = lax.ppermute(bottom, "sc", [(i + 1, i) for i in range(n_sc - 1)])
    (second,) = inner_gram(
        user_count, channel, samples, True, (1 + count, half + count), inner - count, BF16, limit=56 << 20
    )
    second_peer = lax.ppermute(second, "panel", SWAP)
    counts, first_peer = lax.optimization_barrier((user_count, first_peer))
    (own,) = inner_gram(counts, channel, samples, False, (1, half), inner, F32)
    state = detect_first(noise_power, own, first_peer)
    low, high, state = lax.optimization_barrier((low, high, state))
    edge_peer = lax.ppermute(edge_gram(user_count, channel, samples, low, high, True, BF16), "panel", SWAP)
    edge_own = edge_gram(user_count, channel, samples, low, high, False, F32)

    capacity = cells * users // n_cell
    per_device = n_cell * capacity // n_sc
    reach = capacity // per_device
    keys = serving_cell[:, :, 0].reshape(-1)
    position = lax.iota(jnp.int32, cells * users)
    earlier = (keys[:, None] == keys[None, :]) & (position[None, :] < position[:, None])
    rank = jnp.sum(earlier.astype(jnp.int32), axis=1)
    turn = (rank // per_device - sc % reach) % reach * 2 + (keys // cells == sc // reach).astype(jnp.int32)
    column = ((turn * cells + keys % cells) * per_device + rank % per_device) * 2
    column = jnp.concatenate([column, column + 1])
    width = 2 * cells * per_device
    onehot = (column[:, None] == lax.iota(jnp.int32, 2 * reach * width)[None, :]).astype(BF16)

    messages = detect_last(noise_power, own, second_peer, edge_own, edge_peer, state, onehot, symbols, reach)
    arrived = []
    for b in range(reach):
        pairs = [
            (s * n_sc + j, j // reach * n_sc + s * reach + (j % reach + b) % reach)
            for s in range(n_cell)
            for j in range(n_sc)
        ]
        arrived.append(lax.ppermute(messages[b], ("cell", "sc"), pairs))
    turns = (sc % reach - lax.iota(jnp.int32, reach)) % reach
    sources = jnp.concatenate([cell * reach + turns, (1 - cell) * reach + turns])
    keep = symbols * half
    mine = [jnp.stack(arrived[: reach // 2]), jnp.stack(arrived[reach // 2 :])]
    theirs = [lax.ppermute(group, "panel", SWAP) for group in mine]
    others = [lax.ppermute(jnp.stack([block[:keep] for block in arrived]), "cell", SWAP)]
    others += [lax.ppermute(group[:, :keep], "cell", SWAP) for group in theirs]
    routed = assemble(sources, mine, theirs, others, cells, per_device, symbols, half)
    return jnp.transpose(routed, (0, 1, 3, 2, 4))


def solution(mesh):
    return jax.shard_map(
        body,
        mesh=mesh,
        in_specs=(
            P("cell", "sc", None, "panel", None),
            P("cell", "sc", None, None, "panel"),
            P("cell"),
            P("cell", "sc"),
            P("cell", None, None),
        ),
        out_specs=P("cell", "sc", None, None, None),
        check_vma=False,
    )
```

```python
import jax
import jax.numpy as jnp
from jax import lax
from jax.experimental import pallas as pl
from jax.experimental.pallas import tpu as pltpu
from jax.sharding import PartitionSpec as P

F32, BF16 = jnp.float32, jnp.bfloat16
GRP = 16
SPAD = 16
VMEM_LIMIT = 40 << 20
SWAP = [(0, 1), (1, 0)]

SMEM_SPEC = pl.BlockSpec(memory_space=pltpu.SMEM)
VMEM_SPEC = pl.BlockSpec(memory_space=pltpu.VMEM)
HBM_SPEC = pl.BlockSpec(memory_space=pltpu.HBM)


def cross(product, users):
    left, right = product[:, :users], product[:, users:]
    rows = product.shape[0]
    even = lax.broadcasted_iota(jnp.int32, left.shape, 0) % 2 == 0
    return left + jnp.where(even, pltpu.roll(right, rows - 1, 0), -pltpu.roll(right, 1, 0))


def prepare(below, here, above, samples, stretch, mat, lhs):
    antennas, users = here.shape[1:]
    symbols = samples.shape[0]
    slab = 128
    lhs[2 * users : 2 * (users + symbols), :] = samples[...].reshape(2 * symbols, antennas)
    for k in range(2):
        for row in range(0, antennas, slab):
            rows = pl.ds(row, slab)
            outer = below[k, rows, :].astype(F32) + above[k, rows, :].astype(F32)
            middle = here[k, rows, :]
            value = outer + (middle + middle).astype(F32)
            value = (value if stretch is None else value * stretch).astype(BF16)
            mat[rows, k * users : (k + 1) * users] = value
            lhs[k * users : (k + 1) * users, rows] = value.T


def gram(mat, lhs, out, count, users):
    product = jnp.dot(lhs[...], mat[...], preferred_element_type=F32)
    row = lax.broadcasted_iota(jnp.int32, (users, users), 0)
    col = lax.broadcasted_iota(jnp.int32, (users, users), 1)
    real = product[:users, :users] + product[users : 2 * users, users:]
    imag = product[:users, users:] - product[users : 2 * users, :users]
    packed = jnp.where(row <= col, real, imag)
    out[:users, :] = jnp.where(jnp.maximum(row, col) < count, packed * 0.0625, 0.0).astype(out.dtype)
    lane = lax.broadcasted_iota(jnp.int32, (1, users), 1)
    scale = jnp.where(lane < count, 0.25, 0.0)
    out[users:, :] = (cross(product[2 * users :], users) * scale).astype(out.dtype)


def work_buffers(antennas, users):
    return [
        pltpu.VMEM((antennas, 2 * users), BF16),
        pltpu.VMEM((2 * users + 2 * SPAD, antennas), BF16),
    ]


def inner_gram(counts, channel, received, peer, firsts, number, dtype, limit=VMEM_LIMIT, ends=False):
    cells, band, _, antennas, users = channel.shape
    symbols = received.shape[2]
    items = cells * number

    def kernel(counts_hbm, chan, samp, out, *refs):
        end_refs, refs = (refs[:2], refs[2:]) if ends else ((), refs)
        count_ref, win, ybuf, mat_a, lhs_a, mat_b, lhs_b, wsem, ysem, csem, esem = refs
        count_copy = pltpu.make_async_copy(counts_hbm, count_ref, csem)
        count_copy.start()
        panel = lax.axis_index("panel")
        side = 1 - panel if peer else panel
        start = jnp.where(side == 0, firsts[0], firsts[1])
        end_copies = [
            pltpu.make_async_copy(chan.at[c, i * (band - 1)], end_ref.at[c, 0], esem.at[c, i])
            for c in range(cells)
            for i, end_ref in enumerate(end_refs)
        ]

        def fetch(c, i):
            return pltpu.make_async_copy(chan.at[c, start - 1 + i], win.at[c, i], wsem.at[c, i])

        def fetch_samples(c):
            return pltpu.make_async_copy(samp.at[c, pl.ds(start, number)], ybuf.at[c], ysem.at[c])

        for c in range(cells):
            for i in range(number + 2):
                fetch(c, i).start()
                if i == min(2, number):
                    fetch_samples(c).start()
        for copy in end_copies:
            copy.start()
        lhs_a[...] = jnp.zeros_like(lhs_a)
        lhs_b[...] = jnp.zeros_like(lhs_b)

        def wait(item):
            c, i = item // number, item % number

            @pl.when(item < items)
            def _():
                @pl.when(i == 0)
                def _():
                    fetch_samples(c).wait()
                    fetch(c, 0).wait()
                    fetch(c, 1).wait()

                fetch(c, i + 2).wait()

        def ready(item, mat, lhs):
            item = jnp.minimum(item, items - 1)
            c, i = item // number, item % number
            prepare(win.at[c, i], win.at[c, i + 1], win.at[c, i + 2], ybuf.at[c, i], None, mat, lhs)

        def multiply(item, mat, lhs):
            item = jnp.minimum(item, items - 1)
            c, i = item // number, item % number
            gram(mat, lhs, out.at[c, i], count_ref[c, (start + i) // GRP], users)

        count_copy.wait()
        wait(0)
        ready(0, mat_a, lhs_a)

        def step(t, carry):
            wait(2 * t + 1)
            wait(2 * t + 2)
            ready(2 * t + 1, mat_b, lhs_b)
            multiply(2 * t, mat_a, lhs_a)
            ready(2 * t + 2, mat_a, lhs_a)
            multiply(2 * t + 1, mat_b, lhs_b)
            return carry

        lax.fori_loop(0, (items + 1) // 2, step, 0)
        for copy in end_copies:
            copy.wait()

    rows = users + 2 * SPAD
    return pl.pallas_call(
        kernel,
        in_specs=[HBM_SPEC] * 3,
        out_specs=[VMEM_SPEC] * (1 + 2 * ends),
        out_shape=[jax.ShapeDtypeStruct((cells, number, rows, users), dtype)]
        + [jax.ShapeDtypeStruct((cells, 1, 2, antennas, users), BF16)] * (2 * ends),
        scratch_shapes=[
            pltpu.SMEM(counts.shape, jnp.int32),
            pltpu.VMEM((cells, number + 2, 2, antennas, users), BF16),
            pltpu.VMEM((cells, number, symbols, 2, antennas), BF16),
            *work_buffers(antennas, users),
            *work_buffers(antennas, users),
            pltpu.SemaphoreType.DMA((cells, number + 2)),
            pltpu.SemaphoreType.DMA((cells,)),
            pltpu.SemaphoreType.DMA,
            pltpu.SemaphoreType.DMA((cells, 2)),
        ],
        compiler_params=pltpu.CompilerParams(vmem_limit_bytes=limit),
        cost_estimate=pl.CostEstimate(
            flops=items * 4 * antennas * users * 2 * (users + SPAD) // (1 if peer else 16),
            bytes_accessed=cells * (number + 2) * 4 * antennas * users // (1 if peer else 16),
            transcendentals=0,
        ),
    )(counts, channel, received)


def hand_on(arrays):
    def kernel(*refs):
        refs[-1][0] = 0

    return pl.pallas_call(
        kernel,
        in_specs=[HBM_SPEC] * len(arrays),
        out_specs=[HBM_SPEC] * len(arrays),
        out_shape=[jax.ShapeDtypeStruct(a.shape, a.dtype) for a in arrays],
        scratch_shapes=[pltpu.SMEM((1,), jnp.int32)],
        input_output_aliases={i: i for i in range(len(arrays))},
        cost_estimate=pl.CostEstimate(flops=0, bytes_accessed=8 * arrays[0].size, transcendentals=0),
    )(*arrays)


def edge_scratch(counts, symbols, antennas, users):
    cells = counts.shape[0]
    return [
        pltpu.SMEM(counts.shape, jnp.int32),
        pltpu.VMEM((cells, 3, 2, antennas, users), BF16),
        pltpu.VMEM((cells, symbols, 2, antennas), BF16),
        *work_buffers(antennas, users),
        *work_buffers(antennas, users),
        pltpu.SemaphoreType.DMA((cells, 3)),
        pltpu.SemaphoreType.DMA((cells,)),
        pltpu.SemaphoreType.DMA,
    ]


def edge_work(side, counts_hbm, chan, samp, low_ref, high_ref, out, scratch):
    count_ref, win, ybuf, mat_a, lhs_a, mat_b, lhs_b, wsem, ysem, csem = scratch
    count_copy = pltpu.make_async_copy(counts_hbm, count_ref, csem)
    cells, band, _, _, users = chan.shape
    buffers = ((mat_a, lhs_a), (mat_b, lhs_b))

    def each_copy(act):
        def run(e):
            for c in range(cells):
                blocks = (
                    (low_ref.at[c, 0], chan.at[c, 0], chan.at[c, 1]),
                    (chan.at[c, band - 2], chan.at[c, band - 1], high_ref.at[c, 0]),
                )[e]
                for i, block in enumerate(blocks):
                    act(pltpu.make_async_copy(block, win.at[c, i], wsem.at[c, i]))
                act(pltpu.make_async_copy(samp.at[c, e * (band - 1)], ybuf.at[c], ysem.at[c]))

        @pl.when(side == 0)
        def _():
            run(0)

        @pl.when(side == 1)
        def _():
            run(1)

    def fetch():
        count_copy.start()
        each_copy(lambda copy: copy.start())
        lhs_a[...] = jnp.zeros_like(lhs_a)
        lhs_b[...] = jnp.zeros_like(lhs_b)

    def work():
        each_copy(lambda copy: copy.wait())
        count_copy.wait()
        last = lax.axis_index("sc") == side * (lax.axis_size("sc") - 1)
        stretch = jnp.where(jnp.full((1, users), last.astype(jnp.int32)) == 1, 1 / 0.75, 1.0)
        for c in range(cells):
            prepare(win.at[c, 0], win.at[c, 1], win.at[c, 2], ybuf.at[c], stretch, *buffers[c % 2])
        for c in range(cells):
            gram(*buffers[c % 2], out.at[c], count_ref[c, side * (band - 1) // GRP], users)

    return fetch, work


def edge_gram(counts, channel, received, low, high, peer, dtype):
    cells, _, _, antennas, users = channel.shape
    symbols = received.shape[2]

    def kernel(counts_hbm, chan, samp, low_ref, high_ref, out, *scratch):
        panel = lax.axis_index("panel")
        fetch, work = edge_work(1 - panel if peer else panel, counts_hbm, chan, samp, low_ref, high_ref, out, scratch)
        fetch()
        work()

    return pl.pallas_call(
        kernel,
        in_specs=[HBM_SPEC] * 5,
        out_specs=VMEM_SPEC,
        out_shape=jax.ShapeDtypeStruct((cells, users + 2 * SPAD, users), dtype),
        scratch_shapes=edge_scratch(counts, symbols, antennas, users),
        compiler_params=pltpu.CompilerParams(vmem_limit_bytes=VMEM_LIMIT),
        cost_estimate=pl.CostEstimate(
            flops=cells * 4 * antennas * users * 2 * (users + SPAD),
            bytes_accessed=cells * 12 * antennas * users,
            transcendentals=0,
        ),
    )(counts, channel, received, low, high)


def conjugate_gradient(sums, noises, users):
    row = lax.broadcasted_iota(jnp.int32, (users, users), 0)
    col = lax.broadcasted_iota(jnp.int32, (users, users), 1)
    upper = row <= col
    grams = []
    for value in sums:
        packed = value[:users].astype(BF16)
        turned = packed.T
        real = jnp.where(upper, packed, turned)
        imag = jnp.where(row == col, jnp.zeros_like(packed), jnp.where(upper, -turned, packed))
        grams.append(jnp.concatenate([real, imag], axis=1))

    def apply(matrix, vector, noise):
        product = jnp.dot(vector.astype(BF16), matrix, preferred_element_type=F32)
        return cross(product, users) + noise * vector

    def user_sum(left, right):
        total = left * right
        even = lax.broadcasted_iota(jnp.int32, total.shape, 0) % 2 == 0
        total = total + jnp.where(even, pltpu.roll(total, 2 * SPAD - 1, 0), pltpu.roll(total, 1, 0))
        return jnp.sum(total, axis=1, keepdims=True)

    direction = [value[users:] for value in sums]
    norm = [user_sum(d, d) for d in direction]
    image = [apply(*terms) for terms in zip(grams, direction, noises)]
    alpha = [n / user_sum(d, i) for n, d, i in zip(norm, direction, image)]
    estimate = [a * d for a, d in zip(alpha, direction)]
    residual = [d - a * i for d, a, i in zip(direction, alpha, image)]
    norm_next = [user_sum(r, r) for r in residual]
    direction = [r + (m / n) * d for r, m, n, d in zip(residual, norm_next, norm, direction)]
    image = [apply(*terms) for terms in zip(grams, direction, noises)]
    alpha = [n / user_sum(d, i) for n, d, i in zip(norm_next, direction, image)]
    return [e + a * d for e, a, d in zip(estimate, alpha, direction)]


def detect(noise_power, own, own_firsts, peer, edges, symbols):
    cells, _, rows, users = own.shape
    number = peer.shape[1]
    half = number + (len(edges) > 0)
    keep = symbols * half

    def kernel(noise_ref, own_ref, peer_ref, *refs):
        edge_refs, (out, full) = refs[: len(edges)], refs[len(edges) :]
        panel = lax.axis_index("panel")
        first = jnp.where(panel == 0, own_firsts[0], own_firsts[1])
        spots = [(c, i) for c in range(cells) for i in range(number)]
        sums = [own_ref[c, first + i] + peer_ref[c, i].astype(F32) for c, i in spots]
        places = [(c, i + 1 - panel if edges else i) for c, i in spots]
        if edges:
            edge_own_ref, edge_peer_ref = edge_refs
            sums += [edge_own_ref[c] + edge_peer_ref[c].astype(F32) for c in range(cells)]
            places += [(c, panel * (half - 1)) for c in range(cells)]
        values = conjugate_gradient(sums, [noise_ref[c] for c, _ in places], users)
        for (c, place), value in zip(places, values):
            full[c, pl.ds(place, 2 * SPAD, stride=half), :] = value
        for k in range(2):
            for c in range(cells):
                rows_k = [full[c, (2 * s + k) * half : (2 * s + k + 1) * half] for s in range(symbols)]
                first_lane = (k * cells + c) * users
                out[:, first_lane : first_lane + users] = jnp.concatenate(rows_k, axis=0).astype(BF16)

    return pl.pallas_call(
        kernel,
        in_specs=[SMEM_SPEC] + [VMEM_SPEC] * (2 + len(edges)),
        out_specs=VMEM_SPEC,
        out_shape=jax.ShapeDtypeStruct((keep, 2 * cells * users), BF16),
        scratch_shapes=[pltpu.VMEM((cells, 2 * SPAD * half, users), F32)],
        compiler_params=pltpu.CompilerParams(vmem_limit_bytes=VMEM_LIMIT),
        cost_estimate=pl.CostEstimate(
            flops=cells * half * 2 * 2 * 2 * SPAD * users * 2 * users, bytes_accessed=4 * own.size, transcendentals=0
        ),
    )(noise_power, own, peer, *edges)


def place(crossed, founds, received, onehot, reach):
    keep = founds[0].shape[0]
    width = onehot.shape[1] // (2 * reach)

    def kernel(crossed_ref, *refs):
        found_refs, received_refs, hot_ref, outs = refs[:2], refs[2:4], refs[4], refs[5:]
        cross = jnp.full((1, founds[0].shape[1]), crossed_ref[0]) == 1
        lhs = jnp.concatenate([jnp.where(cross, r[...], f[...]) for f, r in zip(found_refs, received_refs)], axis=0)
        placed = jnp.dot(lhs, hot_ref[...], preferred_element_type=F32).astype(BF16)
        for i, out in enumerate(outs):
            for side in range(2):
                start = (2 * i + side) * width
                out[side * 2 * keep : (side + 1) * 2 * keep, :] = placed[:, start : start + width]

    return pl.pallas_call(
        kernel,
        in_specs=[SMEM_SPEC] + [VMEM_SPEC] * 5,
        out_specs=[VMEM_SPEC] * reach,
        out_shape=[jax.ShapeDtypeStruct((4 * keep, width), BF16)] * reach,
        compiler_params=pltpu.CompilerParams(vmem_limit_bytes=VMEM_LIMIT),
        cost_estimate=pl.CostEstimate(
            flops=4 * keep * onehot.shape[0] * onehot.shape[1], bytes_accessed=4 * onehot.size, transcendentals=0
        ),
    )(crossed, *founds, *received, onehot)


def assemble(sources, mine, theirs, others, cells, per_device, symbols, half):
    rounds = sum(group.shape[0] for group in mine)
    total = 2 * rounds * 2 * half
    lanes = mine[0].shape[2]
    keep = symbols * half
    groups = [mine, theirs, others[0], others[1]]
    part = half // 2

    def kernel(source_ref, *refs):
        out, gathered = refs[-2:]
        panel = lax.axis_index("panel")
        at = 0
        for r, group in enumerate(groups):
            side = panel if r % 2 == 0 else 1 - panel
            n = 0 if r < 2 else rounds
            for array in group:
                ref, at = refs[at], at + 1
                for i in range(array.shape[0]):
                    block = ref[i, keep if r < 2 else 0 : 2 * keep if r < 2 else keep, :].astype(F32)
                    for h in range(2):
                        inside = side * half + (1 - side if h == 0 else side) * part
                        start = pl.multiple_of(source_ref[n] * (2 * half) + inside, part)
                        for s in range(symbols):
                            row = (h * symbols + s) * part
                            gathered[s, pl.ds(start, part), :] = block[row : row + part]
                    n += 1
        for s in range(symbols):
            out[:, :, s] = gathered[s].astype(BF16).T.reshape(cells, per_device, 2, total)

    arrays = [array for group in groups for array in group]
    return pl.pallas_call(
        kernel,
        in_specs=[SMEM_SPEC] + [VMEM_SPEC] * len(arrays),
        out_specs=VMEM_SPEC,
        out_shape=jax.ShapeDtypeStruct((cells, per_device, symbols, 2, total), BF16),
        scratch_shapes=[pltpu.VMEM((symbols, total, lanes), F32)],
        compiler_params=pltpu.CompilerParams(vmem_limit_bytes=VMEM_LIMIT),
    )(sources, *arrays)


def body(channel, received, noise_power, user_count, serving_cell):
    cells, band, _, antennas, users = channel.shape
    symbols = received.shape[3]
    half = band // 2
    n_sc, n_cell = lax.axis_size("sc"), lax.axis_size("cell")
    panel, sc, cell = lax.axis_index("panel"), lax.axis_index("sc"), lax.axis_index("cell")

    samples = jnp.transpose(received, (0, 1, 3, 2, 4))

    part = half // 2
    middle, outer = (part, half), (1, band - part)
    first, bottom, top = inner_gram(
        user_count, channel, samples, True, middle, part, BF16, limit=56 << 20, ends=True
    )
    first_peer = lax.ppermute(first, "panel", SWAP)
    bottom, top = hand_on([bottom, top])
    low = lax.ppermute(top, "sc", [(i, i + 1) for i in range(n_sc - 1)])
    high = lax.ppermute(bottom, "sc", [(i + 1, i) for i in range(n_sc - 1)])
    (second,) = inner_gram(user_count, channel, samples, True, outer, part - 1, BF16, limit=56 << 20)
    second_peer = lax.ppermute(second, "panel", SWAP)
    own_keys = serving_cell[:, :, 0].reshape(-1)
    other_keys = lax.ppermute(own_keys, "cell", SWAP)
    counts, first_peer, other_keys = lax.optimization_barrier((user_count, first_peer, other_keys))
    (own,) = inner_gram(counts, channel, samples, False, (1, half), half - 1, F32)
    found_1 = detect(noise_power, own, (part - 1, 0), first_peer, (), symbols)
    low, high, found_1 = lax.optimization_barrier((low, high, found_1))
    edge_peer = lax.ppermute(edge_gram(user_count, channel, samples, low, high, True, BF16), "panel", SWAP)
    edge_own = edge_gram(user_count, channel, samples, low, high, False, F32)

    reach = n_sc // n_cell
    mirror = [
        (s * n_sc + h * reach + j, h * n_sc + s * reach + j)
        for s in range(n_cell)
        for h in range(n_cell)
        for j in range(reach)
        if s != h
    ]
    found_2 = detect(noise_power, own, (0, part), second_peer, (edge_own, edge_peer), symbols)
    founds = (found_1, found_2)
    received_founds = [lax.ppermute(found, ("cell", "sc"), mirror) for found in founds]

    capacity = cells * users // n_cell
    per_device = n_cell * capacity // n_sc
    crossed = cell != sc // reach
    keys = jnp.where(crossed, other_keys, own_keys)
    position = lax.iota(jnp.int32, cells * users)
    earlier = (keys[:, None] == keys[None, :]) & (position[None, :] < position[:, None])
    rank = jnp.sum(earlier.astype(jnp.int32), axis=1)
    turn = (rank // per_device - sc % reach) % reach * 2 + (keys // cells == cell).astype(jnp.int32)
    column = ((turn * cells + keys % cells) * per_device + rank % per_device) * 2
    column = jnp.concatenate([column, column + 1])
    width = 2 * cells * per_device
    onehot = (column[:, None] == lax.iota(jnp.int32, 2 * reach * width)[None, :]).astype(BF16)

    messages = place(crossed.astype(jnp.int32).reshape(1), founds, received_founds, onehot, reach)
    arrived = [messages[0]]
    for b in range(1, reach):
        pairs = [
            (s * n_sc + j, s * n_sc + j // reach * reach + (j % reach + b) % reach)
            for s in range(n_cell)
            for j in range(n_sc)
        ]
        arrived.append(lax.ppermute(messages[b], ("cell", "sc"), pairs))
    keep = symbols * half
    cuts = (0, 1, reach // 2, reach)
    mine = [jnp.stack(arrived[i:j]) for i, j in zip(cuts, cuts[1:])]
    theirs = [lax.ppermute(group, "panel", SWAP) for group in mine]
    gifts = [group[:, :keep] for group in mine + theirs[:-1]]
    gifts = lax.ppermute(jnp.concatenate(gifts), "cell", SWAP)
    last = lax.ppermute(theirs[-1][:, :keep], "cell", SWAP)
    others = ([gifts[:reach]], [gifts[reach:], last])
    turns = (sc % reach - lax.iota(jnp.int32, reach)) % reach
    sources = jnp.concatenate([cell * reach + turns, (1 - cell) * reach + turns])
    routed = assemble(sources, mine, theirs, others, cells, per_device, symbols, half)
    return jnp.transpose(routed, (0, 1, 3, 2, 4))


def solution(mesh):
    return jax.shard_map(
        body,
        mesh=mesh,
        in_specs=(
            P("cell", "sc", None, "panel", None),
            P("cell", "sc", None, None, "panel"),
            P("cell"),
            P("cell", "sc"),
            P("cell", None, None),
        ),
        out_specs=P("cell", "sc", None, None, None),
        check_vma=False,
    )
```

```python
import jax
import jax.numpy as jnp
from jax import lax
from jax.experimental import pallas as pl
from jax.experimental.pallas import tpu as pltpu
from jax.sharding import PartitionSpec as P

F32, BF16 = jnp.float32, jnp.bfloat16
GRP = 16
SPAD = 16
VMEM_LIMIT = 40 << 20
SWAP = [(0, 1), (1, 0)]

SMEM_SPEC = pl.BlockSpec(memory_space=pltpu.SMEM)
VMEM_SPEC = pl.BlockSpec(memory_space=pltpu.VMEM)
HBM_SPEC = pl.BlockSpec(memory_space=pltpu.HBM)


def cross(product, users):
    left, right = product[:, :users], product[:, users:]
    rows = product.shape[0]
    even = lax.broadcasted_iota(jnp.int32, left.shape, 0) % 2 == 0
    return left + jnp.where(even, pltpu.roll(right, rows - 1, 0), -pltpu.roll(right, 1, 0))


def prepare(below, here, above, samples, stretch, mat, lhs):
    antennas, users = here.shape[1:]
    symbols = samples.shape[0]
    slab = 128
    lhs[2 * users : 2 * (users + symbols), :] = samples[...].reshape(2 * symbols, antennas)
    for k in range(2):
        for row in range(0, antennas, slab):
            rows = pl.ds(row, slab)
            outer = below[k, rows, :].astype(F32) + above[k, rows, :].astype(F32)
            middle = here[k, rows, :]
            value = outer + (middle + middle).astype(F32)
            value = (value if stretch is None else value * stretch).astype(BF16)
            mat[rows, k * users : (k + 1) * users] = value
            lhs[k * users : (k + 1) * users, rows] = value.T


def gram(mat, lhs, out, count, users):
    product = jnp.dot(lhs[...], mat[...], preferred_element_type=F32)
    row = lax.broadcasted_iota(jnp.int32, (users, users), 0)
    col = lax.broadcasted_iota(jnp.int32, (users, users), 1)
    real = product[:users, :users] + product[users : 2 * users, users:]
    imag = product[:users, users:] - product[users : 2 * users, :users]
    packed = jnp.where(row <= col, real, imag)
    out[:users, :] = jnp.where(jnp.maximum(row, col) < count, packed * 0.0625, 0.0).astype(out.dtype)
    lane = lax.broadcasted_iota(jnp.int32, (1, users), 1)
    scale = jnp.where(lane < count, 0.25, 0.0)
    out[users:, :] = (cross(product[2 * users :], users) * scale).astype(out.dtype)


def work_buffers(antennas, users):
    return [
        pltpu.VMEM((antennas, 2 * users), BF16),
        pltpu.VMEM((2 * users + 2 * SPAD, antennas), BF16),
    ]


def inner_gram(counts, channel, received, peer, firsts, number, dtype, limit=VMEM_LIMIT, ends=False):
    cells, band, _, antennas, users = channel.shape
    symbols = received.shape[2]
    items = cells * number

    def kernel(counts_hbm, chan, samp, out, *refs):
        end_refs, refs = (refs[:2], refs[2:]) if ends else ((), refs)
        count_ref, win, ybuf, mat_a, lhs_a, mat_b, lhs_b, wsem, ysem, csem, esem = refs
        count_copy = pltpu.make_async_copy(counts_hbm, count_ref, csem)
        count_copy.start()
        panel = lax.axis_index("panel")
        side = 1 - panel if peer else panel
        start = jnp.where(side == 0, firsts[0], firsts[1])
        end_copies = [
            pltpu.make_async_copy(chan.at[c, i * (band - 1)], end_ref.at[c, 0], esem.at[c, i])
            for c in range(cells)
            for i, end_ref in enumerate(end_refs)
        ]

        def fetch(c, i):
            return pltpu.make_async_copy(chan.at[c, start - 1 + i], win.at[c, i], wsem.at[c, i])

        def fetch_samples(c):
            return pltpu.make_async_copy(samp.at[c, pl.ds(start, number)], ybuf.at[c], ysem.at[c])

        for c in range(cells):
            for i in range(number + 2):
                fetch(c, i).start()
                if i == min(2, number):
                    fetch_samples(c).start()
        for copy in end_copies:
            copy.start()
        lhs_a[...] = jnp.zeros_like(lhs_a)
        lhs_b[...] = jnp.zeros_like(lhs_b)

        def wait(item):
            c, i = item // number, item % number

            @pl.when(item < items)
            def _():
                @pl.when(i == 0)
                def _():
                    fetch_samples(c).wait()
                    fetch(c, 0).wait()
                    fetch(c, 1).wait()

                fetch(c, i + 2).wait()

        def ready(item, mat, lhs):
            item = jnp.minimum(item, items - 1)
            c, i = item // number, item % number
            prepare(win.at[c, i], win.at[c, i + 1], win.at[c, i + 2], ybuf.at[c, i], None, mat, lhs)

        def multiply(item, mat, lhs):
            item = jnp.minimum(item, items - 1)
            c, i = item // number, item % number
            gram(mat, lhs, out.at[c, i], count_ref[c, (start + i) // GRP], users)

        count_copy.wait()
        wait(0)
        ready(0, mat_a, lhs_a)

        def step(t, carry):
            wait(2 * t + 1)
            wait(2 * t + 2)
            ready(2 * t + 1, mat_b, lhs_b)
            multiply(2 * t, mat_a, lhs_a)
            ready(2 * t + 2, mat_a, lhs_a)
            multiply(2 * t + 1, mat_b, lhs_b)
            return carry

        lax.fori_loop(0, (items + 1) // 2, step, 0)
        for copy in end_copies:
            copy.wait()

    rows = users + 2 * SPAD
    return pl.pallas_call(
        kernel,
        in_specs=[HBM_SPEC] * 3,
        out_specs=[VMEM_SPEC] * (1 + 2 * ends),
        out_shape=[jax.ShapeDtypeStruct((cells, number, rows, users), dtype)]
        + [jax.ShapeDtypeStruct((cells, 1, 2, antennas, users), BF16)] * (2 * ends),
        scratch_shapes=[
            pltpu.SMEM(counts.shape, jnp.int32),
            pltpu.VMEM((cells, number + 2, 2, antennas, users), BF16),
            pltpu.VMEM((cells, number, symbols, 2, antennas), BF16),
            *work_buffers(antennas, users),
            *work_buffers(antennas, users),
            pltpu.SemaphoreType.DMA((cells, number + 2)),
            pltpu.SemaphoreType.DMA((cells,)),
            pltpu.SemaphoreType.DMA,
            pltpu.SemaphoreType.DMA((cells, 2)),
        ],
        compiler_params=pltpu.CompilerParams(vmem_limit_bytes=limit),
        cost_estimate=pl.CostEstimate(
            flops=items * 4 * antennas * users * 2 * (users + SPAD) // (1 if peer else 16),
            bytes_accessed=cells * (number + 2) * 4 * antennas * users // (1 if peer else 16),
            transcendentals=0,
        ),
    )(counts, channel, received)


def hand_on(arrays):
    def kernel(*refs):
        refs[-1][0] = 0

    return pl.pallas_call(
        kernel,
        in_specs=[HBM_SPEC] * len(arrays),
        out_specs=[HBM_SPEC] * len(arrays),
        out_shape=[jax.ShapeDtypeStruct(a.shape, a.dtype) for a in arrays],
        scratch_shapes=[pltpu.SMEM((1,), jnp.int32)],
        input_output_aliases={i: i for i in range(len(arrays))},
        cost_estimate=pl.CostEstimate(flops=0, bytes_accessed=8 * arrays[0].size, transcendentals=0),
    )(*arrays)


def edge_scratch(counts, symbols, antennas, users):
    cells = counts.shape[0]
    return [
        pltpu.SMEM(counts.shape, jnp.int32),
        pltpu.VMEM((cells, 3, 2, antennas, users), BF16),
        pltpu.VMEM((cells, symbols, 2, antennas), BF16),
        *work_buffers(antennas, users),
        *work_buffers(antennas, users),
        pltpu.SemaphoreType.DMA((cells, 3)),
        pltpu.SemaphoreType.DMA((cells,)),
        pltpu.SemaphoreType.DMA,
    ]


def edge_work(side, counts_hbm, chan, samp, low_ref, high_ref, out, scratch):
    count_ref, win, ybuf, mat_a, lhs_a, mat_b, lhs_b, wsem, ysem, csem = scratch
    count_copy = pltpu.make_async_copy(counts_hbm, count_ref, csem)
    cells, band, _, _, users = chan.shape
    buffers = ((mat_a, lhs_a), (mat_b, lhs_b))

    def each_copy(act):
        def run(e):
            for c in range(cells):
                blocks = (
                    (low_ref.at[c, 0], chan.at[c, 0], chan.at[c, 1]),
                    (chan.at[c, band - 2], chan.at[c, band - 1], high_ref.at[c, 0]),
                )[e]
                for i, block in enumerate(blocks):
                    act(pltpu.make_async_copy(block, win.at[c, i], wsem.at[c, i]))
                act(pltpu.make_async_copy(samp.at[c, e * (band - 1)], ybuf.at[c], ysem.at[c]))

        @pl.when(side == 0)
        def _():
            run(0)

        @pl.when(side == 1)
        def _():
            run(1)

    def fetch():
        count_copy.start()
        each_copy(lambda copy: copy.start())
        lhs_a[...] = jnp.zeros_like(lhs_a)
        lhs_b[...] = jnp.zeros_like(lhs_b)

    def work():
        each_copy(lambda copy: copy.wait())
        count_copy.wait()
        last = lax.axis_index("sc") == side * (lax.axis_size("sc") - 1)
        stretch = jnp.where(jnp.full((1, users), last.astype(jnp.int32)) == 1, 1 / 0.75, 1.0)
        for c in range(cells):
            prepare(win.at[c, 0], win.at[c, 1], win.at[c, 2], ybuf.at[c], stretch, *buffers[c % 2])
        for c in range(cells):
            gram(*buffers[c % 2], out.at[c], count_ref[c, side * (band - 1) // GRP], users)

    return fetch, work


def edge_gram(counts, channel, received, low, high, peer, dtype):
    cells, _, _, antennas, users = channel.shape
    symbols = received.shape[2]

    def kernel(counts_hbm, chan, samp, low_ref, high_ref, out, *scratch):
        panel = lax.axis_index("panel")
        fetch, work = edge_work(1 - panel if peer else panel, counts_hbm, chan, samp, low_ref, high_ref, out, scratch)
        fetch()
        work()

    return pl.pallas_call(
        kernel,
        in_specs=[HBM_SPEC] * 5,
        out_specs=VMEM_SPEC,
        out_shape=jax.ShapeDtypeStruct((cells, users + 2 * SPAD, users), dtype),
        scratch_shapes=edge_scratch(counts, symbols, antennas, users),
        compiler_params=pltpu.CompilerParams(vmem_limit_bytes=VMEM_LIMIT),
        cost_estimate=pl.CostEstimate(
            flops=cells * 4 * antennas * users * 2 * (users + SPAD),
            bytes_accessed=cells * 12 * antennas * users,
            transcendentals=0,
        ),
    )(counts, channel, received, low, high)


def conjugate_gradient(sums, noises, users):
    row = lax.broadcasted_iota(jnp.int32, (users, users), 0)
    col = lax.broadcasted_iota(jnp.int32, (users, users), 1)
    upper = row <= col
    grams = []
    for value in sums:
        packed = value[:users].astype(BF16)
        turned = packed.T
        real = jnp.where(upper, packed, turned)
        imag = jnp.where(row == col, jnp.zeros_like(packed), jnp.where(upper, -turned, packed))
        grams.append(jnp.concatenate([real, imag], axis=1))

    def apply(matrix, vector, noise):
        product = jnp.dot(vector.astype(BF16), matrix, preferred_element_type=F32)
        return cross(product, users) + noise * vector

    def user_sum(left, right):
        total = left * right
        even = lax.broadcasted_iota(jnp.int32, total.shape, 0) % 2 == 0
        total = total + jnp.where(even, pltpu.roll(total, 2 * SPAD - 1, 0), pltpu.roll(total, 1, 0))
        return jnp.sum(total, axis=1, keepdims=True)

    direction = [value[users:] for value in sums]
    norm = [user_sum(d, d) for d in direction]
    image = [apply(*terms) for terms in zip(grams, direction, noises)]
    alpha = [n / user_sum(d, i) for n, d, i in zip(norm, direction, image)]
    estimate = [a * d for a, d in zip(alpha, direction)]
    residual = [d - a * i for d, a, i in zip(direction, alpha, image)]
    norm_next = [user_sum(r, r) for r in residual]
    direction = [r + (m / n) * d for r, m, n, d in zip(residual, norm_next, norm, direction)]
    image = [apply(*terms) for terms in zip(grams, direction, noises)]
    alpha = [n / user_sum(d, i) for n, d, i in zip(norm_next, direction, image)]
    return [e + a * d for e, a, d in zip(estimate, alpha, direction)]


def detect(noise_power, own, own_firsts, peer, edges, symbols):
    cells, _, rows, users = own.shape
    number = peer.shape[1]
    half = number + (len(edges) > 0)
    keep = symbols * half

    def kernel(noise_ref, own_ref, peer_ref, *refs):
        edge_refs, (out, full) = refs[: len(edges)], refs[len(edges) :]
        panel = lax.axis_index("panel")
        first = jnp.where(panel == 0, own_firsts[0], own_firsts[1])
        spots = [(c, i) for c in range(cells) for i in range(number)]
        sums = [own_ref[c, first + i] + peer_ref[c, i].astype(F32) for c, i in spots]
        places = [(c, i + 1 - panel if edges else i) for c, i in spots]
        if edges:
            edge_own_ref, edge_peer_ref = edge_refs
            sums += [edge_own_ref[c] + edge_peer_ref[c].astype(F32) for c in range(cells)]
            places += [(c, panel * (half - 1)) for c in range(cells)]
        values = conjugate_gradient(sums, [noise_ref[c] for c, _ in places], users)
        for (c, place), value in zip(places, values):
            full[c, pl.ds(place, 2 * SPAD, stride=half), :] = value
        for k in range(2):
            for c in range(cells):
                rows_k = [full[c, (2 * s + k) * half : (2 * s + k + 1) * half] for s in range(symbols)]
                first_lane = (k * cells + c) * users
                out[:, first_lane : first_lane + users] = jnp.concatenate(rows_k, axis=0).astype(BF16)

    return pl.pallas_call(
        kernel,
        in_specs=[SMEM_SPEC] + [VMEM_SPEC] * (2 + len(edges)),
        out_specs=VMEM_SPEC,
        out_shape=jax.ShapeDtypeStruct((keep, 2 * cells * users), BF16),
        scratch_shapes=[pltpu.VMEM((cells, 2 * SPAD * half, users), F32)],
        compiler_params=pltpu.CompilerParams(vmem_limit_bytes=VMEM_LIMIT),
        cost_estimate=pl.CostEstimate(
            flops=cells * half * 2 * 2 * 2 * SPAD * users * 2 * users, bytes_accessed=4 * own.size, transcendentals=0
        ),
    )(noise_power, own, peer, *edges)


def place(crossed, founds, mirrored, turned, onehot, reach):
    keep = founds[0].shape[0]
    width = onehot.shape[1] // reach

    def kernel(crossed_ref, *refs):
        found_refs, mirrored_refs, turned_refs, hot_ref, outs = refs[:2], refs[2:4], refs[4:6], refs[6], refs[7:]
        cross = jnp.full((1, founds[0].shape[1]), crossed_ref[0]) == 1
        same = [jnp.where(cross, t[...], f[...]) for f, t in zip(found_refs, turned_refs)]
        far = [jnp.where(cross, m[...], t[...]) for m, t in zip(mirrored_refs, turned_refs)]
        lhs = jnp.concatenate(same + far, axis=0)
        placed = jnp.dot(lhs, hot_ref[...], preferred_element_type=F32).astype(BF16)
        for i, out in enumerate(outs):
            out[...] = placed[:, i * width : (i + 1) * width]

    return pl.pallas_call(
        kernel,
        in_specs=[SMEM_SPEC] + [VMEM_SPEC] * 7,
        out_specs=[VMEM_SPEC] * reach,
        out_shape=[jax.ShapeDtypeStruct((4 * keep, width), BF16)] * reach,
        compiler_params=pltpu.CompilerParams(vmem_limit_bytes=VMEM_LIMIT),
        cost_estimate=pl.CostEstimate(
            flops=8 * keep * onehot.shape[0] * onehot.shape[1], bytes_accessed=4 * onehot.size, transcendentals=0
        ),
    )(crossed, *founds, *mirrored, *turned, onehot)


def assemble(sources, mine, theirs, cells, per_device, symbols, half):
    rounds = sum(group.shape[0] for group in mine)
    total = 2 * rounds * 2 * half
    lanes = mine[0].shape[2]
    part = half // 2

    def kernel(source_ref, *refs):
        out, gathered = refs[-2:]
        panel = lax.axis_index("panel")
        at = 0
        for side, group in ((panel, mine), (1 - panel, theirs)):
            n = 0
            for array in group:
                ref, at = refs[at], at + 1
                for i in range(array.shape[0]):
                    block = ref[i].astype(F32)
                    for far in range(2):
                        for h in range(2):
                            inside = side * half + (1 - side if h == 0 else side) * part
                            start = pl.multiple_of(source_ref[far * rounds + n] * (2 * half) + inside, part)
                            for s in range(symbols):
                                row = ((2 * far + h) * symbols + s) * part
                                gathered[s, pl.ds(start, part), :] = block[row : row + part]
                    n += 1
        for s in range(symbols):
            out[:, :, s] = gathered[s].astype(BF16).T.reshape(cells, per_device, 2, total)

    return pl.pallas_call(
        kernel,
        in_specs=[SMEM_SPEC] + [VMEM_SPEC] * (2 * len(mine)),
        out_specs=VMEM_SPEC,
        out_shape=jax.ShapeDtypeStruct((cells, per_device, symbols, 2, total), BF16),
        scratch_shapes=[pltpu.VMEM((symbols, total, lanes), F32)],
        compiler_params=pltpu.CompilerParams(vmem_limit_bytes=VMEM_LIMIT),
    )(sources, *mine, *theirs)


def body(channel, received, noise_power, user_count, serving_cell):
    cells, band, _, antennas, users = channel.shape
    symbols = received.shape[3]
    half = band // 2
    n_sc, n_cell = lax.axis_size("sc"), lax.axis_size("cell")
    panel, sc, cell = lax.axis_index("panel"), lax.axis_index("sc"), lax.axis_index("cell")

    samples = jnp.transpose(received, (0, 1, 3, 2, 4))

    part = half // 2
    middle, outer = (part, half), (1, band - part)
    first, bottom, top = inner_gram(
        user_count, channel, samples, True, middle, part, BF16, limit=56 << 20, ends=True
    )
    first_peer = lax.ppermute(first, "panel", SWAP)
    bottom, top = hand_on([bottom, top])
    low = lax.ppermute(top, "sc", [(i, i + 1) for i in range(n_sc - 1)])
    high = lax.ppermute(bottom, "sc", [(i + 1, i) for i in range(n_sc - 1)])
    (second,) = inner_gram(user_count, channel, samples, True, outer, part - 1, BF16, limit=56 << 20)
    second_peer = lax.ppermute(second, "panel", SWAP)
    own_keys = serving_cell[:, :, 0].reshape(-1)
    other_keys = lax.ppermute(own_keys, "cell", SWAP)
    counts, first_peer, other_keys = lax.optimization_barrier((user_count, first_peer, other_keys))
    (own,) = inner_gram(counts, channel, samples, False, (1, half), half - 1, F32)
    found_1 = detect(noise_power, own, (part - 1, 0), first_peer, (), symbols)
    low, high, found_1 = lax.optimization_barrier((low, high, found_1))
    edge_out = edge_gram(user_count, channel, samples, low, high, True, BF16)
    edge_peer = lax.ppermute(edge_out, "panel", SWAP)
    edge_out, found_1 = lax.optimization_barrier((edge_out, found_1))
    edge_own = edge_gram(user_count, channel, samples, low, high, False, F32)

    reach = n_sc // n_cell
    mirror = [
        (s * n_sc + h * reach + j, h * n_sc + s * reach + j)
        for s in range(n_cell)
        for h in range(n_cell)
        for j in range(reach)
        if s != h
    ]
    found_2 = detect(noise_power, own, (0, part), second_peer, (edge_own, edge_peer), symbols)
    turn = [
        (s * n_sc + h * reach + j, (n_cell - 1 - s if s == h else s) * n_sc + s * reach + j)
        for s in range(n_cell)
        for h in range(n_cell)
        for j in range(reach)
    ]
    founds = (found_1, found_2)
    mirrored = [lax.ppermute(found, ("cell", "sc"), mirror) for found in founds]
    turned = [lax.ppermute(found, ("cell", "sc"), turn) for found in founds]

    capacity = cells * users // n_cell
    per_device = n_cell * capacity // n_sc
    crossed = cell != sc // reach
    keys = jnp.where(crossed, other_keys, own_keys)
    position = lax.iota(jnp.int32, cells * users)
    earlier = (keys[:, None] == keys[None, :]) & (position[None, :] < position[:, None])
    rank = jnp.sum(earlier.astype(jnp.int32), axis=1)
    turn = (rank // per_device - sc % reach) % reach
    column = ((turn * cells + keys % cells) * per_device + rank % per_device) * 2
    column = jnp.where(keys // cells == cell, column, -2)
    column = jnp.concatenate([column, column + 1])
    width = 2 * cells * per_device
    onehot = (column[:, None] == lax.iota(jnp.int32, reach * width)[None, :]).astype(BF16)

    messages = place(crossed.astype(jnp.int32).reshape(1), founds, mirrored, turned, onehot, reach)
    arrived = [messages[0]]
    for b in range(1, reach):
        pairs = [
            (s * n_sc + j, s * n_sc + j // reach * reach + (j % reach + b) % reach)
            for s in range(n_cell)
            for j in range(n_sc)
        ]
        arrived.append(lax.ppermute(messages[b], ("cell", "sc"), pairs))
    cuts = (0, 1, reach // 2, reach)
    mine = [jnp.stack(arrived[i:j]) for i, j in zip(cuts, cuts[1:])]
    theirs = []
    for n, group in enumerate(mine):
        if n == 2:
            group, theirs[0] = lax.optimization_barrier((group, theirs[0]))
        theirs.append(lax.ppermute(group, "panel", SWAP))
    turns = (sc % reach - lax.iota(jnp.int32, reach)) % reach
    here = sc // reach
    sources = jnp.concatenate([here * reach + turns, (1 - here) * reach + turns])
    routed = assemble(sources, mine, theirs, cells, per_device, symbols, half)
    return jnp.transpose(routed, (0, 1, 3, 2, 4))


def solution(mesh):
    return jax.shard_map(
        body,
        mesh=mesh,
        in_specs=(
            P("cell", "sc", None, "panel", None),
            P("cell", "sc", None, None, "panel"),
            P("cell"),
            P("cell", "sc"),
            P("cell", None, None),
        ),
        out_specs=P("cell", "sc", None, None, None),
        check_vma=False,
    )
```

```python
import jax
import jax.numpy as jnp
from jax import lax
from jax.experimental import pallas as pl
from jax.experimental.pallas import tpu as pltpu
from jax.sharding import PartitionSpec as P

F32, BF16 = jnp.float32, jnp.bfloat16
GRP = 16
SPAD = 16
VMEM_LIMIT = 40 << 20
SWAP = [(0, 1), (1, 0)]

SMEM_SPEC = pl.BlockSpec(memory_space=pltpu.SMEM)
VMEM_SPEC = pl.BlockSpec(memory_space=pltpu.VMEM)
HBM_SPEC = pl.BlockSpec(memory_space=pltpu.HBM)


def cross(product, users):
    left, right = product[:, :users], product[:, users:]
    rows = product.shape[0]
    even = lax.broadcasted_iota(jnp.int32, left.shape, 0) % 2 == 0
    return left + jnp.where(even, pltpu.roll(right, rows - 1, 0), -pltpu.roll(right, 1, 0))


def prepare(below, here, above, samples, stretch, mat, lhs):
    antennas, users = here.shape[1:]
    symbols = samples.shape[0]
    slab = 128
    lhs[2 * users : 2 * (users + symbols), :] = samples[...].reshape(2 * symbols, antennas)
    for k in range(2):
        for row in range(0, antennas, slab):
            rows = pl.ds(row, slab)
            outer = below[k, rows, :].astype(F32) + above[k, rows, :].astype(F32)
            middle = here[k, rows, :]
            value = outer + (middle + middle).astype(F32)
            value = (value if stretch is None else value * stretch).astype(BF16)
            mat[rows, k * users : (k + 1) * users] = value
            lhs[k * users : (k + 1) * users, rows] = value.T


def gram(mat, lhs, out, count, users):
    product = jnp.dot(lhs[...], mat[...], preferred_element_type=F32)
    row = lax.broadcasted_iota(jnp.int32, (users, users), 0)
    col = lax.broadcasted_iota(jnp.int32, (users, users), 1)
    real = product[:users, :users] + product[users : 2 * users, users:]
    imag = product[:users, users:] - product[users : 2 * users, :users]
    packed = jnp.where(row <= col, real, imag)
    out[:users, :] = jnp.where(jnp.maximum(row, col) < count, packed * 0.0625, 0.0).astype(out.dtype)
    lane = lax.broadcasted_iota(jnp.int32, (1, users), 1)
    scale = jnp.where(lane < count, 0.25, 0.0)
    out[users:, :] = (cross(product[2 * users :], users) * scale).astype(out.dtype)


def work_buffers(antennas, users):
    return [
        pltpu.VMEM((antennas, 2 * users), BF16),
        pltpu.VMEM((2 * users + 2 * SPAD, antennas), BF16),
    ]


def inner_gram(counts, channel, received, peer, firsts, number, dtype, limit=VMEM_LIMIT, ends=False):
    cells, band, _, antennas, users = channel.shape
    symbols = received.shape[2]
    items = cells * number

    def kernel(counts_hbm, chan, samp, out, *refs):
        end_outs, refs = (refs[:2], refs[2:]) if ends else ((), refs)
        end_refs, refs = (refs[:2], refs[2:]) if ends else ((), refs)
        count_ref, win, ybuf, mat_a, lhs_a, mat_b, lhs_b, wsem, ysem, csem, esem, osem = refs
        count_copy = pltpu.make_async_copy(counts_hbm, count_ref, csem)
        count_copy.start()
        panel = lax.axis_index("panel")
        side = 1 - panel if peer else panel
        start = jnp.where(side == 0, firsts[0], firsts[1])
        end_copies = [
            pltpu.make_async_copy(chan.at[c, i * (band - 1)], end_ref.at[c], esem.at[c, i])
            for c in range(cells)
            for i, end_ref in enumerate(end_refs)
        ]
        end_writes = [
            pltpu.make_async_copy(end_ref.at[c], end_out.at[c, 0], osem.at[c, i])
            for c in range(cells)
            for i, (end_ref, end_out) in enumerate(zip(end_refs, end_outs))
        ]

        def fetch(c, i):
            return pltpu.make_async_copy(chan.at[c, start - 1 + i], win.at[c, i], wsem.at[c, i])

        def fetch_samples(c, i):
            return pltpu.make_async_copy(samp.at[c, start + i], ybuf.at[c, i], ysem.at[c, i])

        for c in range(cells):
            for i in range(number + 2):
                fetch(c, i).start()
                if i >= 2:
                    fetch_samples(c, i - 2).start()
        for copy in end_copies:
            copy.start()
        lhs_a[...] = jnp.zeros_like(lhs_a)
        lhs_b[...] = jnp.zeros_like(lhs_b)

        def wait(item):
            c, i = item // number, item % number

            @pl.when(item < items)
            def _():
                @pl.when(i == 0)
                def _():
                    fetch(c, 0).wait()
                    fetch(c, 1).wait()

                fetch(c, i + 2).wait()
                fetch_samples(c, i).wait()

        def ready(item, mat, lhs):
            item = jnp.minimum(item, items - 1)
            c, i = item // number, item % number
            prepare(win.at[c, i], win.at[c, i + 1], win.at[c, i + 2], ybuf.at[c, i], None, mat, lhs)

        def multiply(item, mat, lhs):
            item = jnp.minimum(item, items - 1)
            c, i = item // number, item % number
            gram(mat, lhs, out.at[c, i], count_ref[c, (start + i) // GRP], users)

        count_copy.wait()
        wait(0)
        ready(0, mat_a, lhs_a)

        def step(t, carry):
            wait(2 * t + 1)
            wait(2 * t + 2)
            ready(2 * t + 1, mat_b, lhs_b)
            multiply(2 * t, mat_a, lhs_a)
            ready(2 * t + 2, mat_a, lhs_a)
            multiply(2 * t + 1, mat_b, lhs_b)
            return carry

        steps = (items + 1) // 2
        lax.fori_loop(0, steps // 2, step, 0)
        for copy, write in zip(end_copies, end_writes):
            copy.wait()
            write.start()
        lax.fori_loop(steps // 2, steps, step, 0)
        for write in end_writes:
            write.wait()

    rows = users + 2 * SPAD
    return pl.pallas_call(
        kernel,
        in_specs=[HBM_SPEC] * 3,
        out_specs=[VMEM_SPEC] + [HBM_SPEC] * (2 * ends),
        out_shape=[jax.ShapeDtypeStruct((cells, number, rows, users), dtype)]
        + [jax.ShapeDtypeStruct((cells, 1, 2, antennas, users), BF16)] * (2 * ends),
        scratch_shapes=[pltpu.VMEM((cells, 2, antennas, users), BF16)] * (2 * ends)
        + [
            pltpu.SMEM(counts.shape, jnp.int32),
            pltpu.VMEM((cells, number + 2, 2, antennas, users), BF16),
            pltpu.VMEM((cells, number, symbols, 2, antennas), BF16),
            *work_buffers(antennas, users),
            *work_buffers(antennas, users),
            pltpu.SemaphoreType.DMA((cells, number + 2)),
            pltpu.SemaphoreType.DMA((cells, number)),
            pltpu.SemaphoreType.DMA,
            pltpu.SemaphoreType.DMA((cells, 2)),
            pltpu.SemaphoreType.DMA((cells, 2)),
        ],
        compiler_params=pltpu.CompilerParams(vmem_limit_bytes=limit),
        cost_estimate=pl.CostEstimate(
            flops=items * 4 * antennas * users * 2 * (users + SPAD) // (1 if peer else 16),
            bytes_accessed=cells * (number + 2) * 4 * antennas * users // (1 if peer else 16),
            transcendentals=0,
        ),
    )(counts, channel, received)


def hand_on(arrays):
    def kernel(*refs):
        refs[-1][0] = 0

    return pl.pallas_call(
        kernel,
        in_specs=[HBM_SPEC] * len(arrays),
        out_specs=[HBM_SPEC] * len(arrays),
        out_shape=[jax.ShapeDtypeStruct(a.shape, a.dtype) for a in arrays],
        scratch_shapes=[pltpu.SMEM((1,), jnp.int32)],
        input_output_aliases={i: i for i in range(len(arrays))},
        cost_estimate=pl.CostEstimate(flops=0, bytes_accessed=8 * arrays[0].size, transcendentals=0),
    )(*arrays)


def edge_scratch(counts, symbols, antennas, users):
    cells = counts.shape[0]
    return [
        pltpu.SMEM(counts.shape, jnp.int32),
        pltpu.VMEM((cells, 3, 2, antennas, users), BF16),
        pltpu.VMEM((cells, symbols, 2, antennas), BF16),
        *work_buffers(antennas, users),
        *work_buffers(antennas, users),
        pltpu.SemaphoreType.DMA((cells, 3)),
        pltpu.SemaphoreType.DMA((cells,)),
        pltpu.SemaphoreType.DMA,
    ]


def edge_work(side, counts_hbm, chan, samp, low_ref, high_ref, out, scratch):
    count_ref, win, ybuf, mat_a, lhs_a, mat_b, lhs_b, wsem, ysem, csem = scratch
    count_copy = pltpu.make_async_copy(counts_hbm, count_ref, csem)
    cells, band, _, _, users = chan.shape
    buffers = ((mat_a, lhs_a), (mat_b, lhs_b))

    def each_copy(act):
        def run(e):
            for c in range(cells):
                blocks = (
                    (low_ref.at[c, 0], chan.at[c, 0], chan.at[c, 1]),
                    (chan.at[c, band - 2], chan.at[c, band - 1], high_ref.at[c, 0]),
                )[e]
                for i, block in enumerate(blocks):
                    act(pltpu.make_async_copy(block, win.at[c, i], wsem.at[c, i]))
                act(pltpu.make_async_copy(samp.at[c, e * (band - 1)], ybuf.at[c], ysem.at[c]))

        @pl.when(side == 0)
        def _():
            run(0)

        @pl.when(side == 1)
        def _():
            run(1)

    def fetch():
        count_copy.start()
        each_copy(lambda copy: copy.start())
        lhs_a[...] = jnp.zeros_like(lhs_a)
        lhs_b[...] = jnp.zeros_like(lhs_b)

    def work():
        each_copy(lambda copy: copy.wait())
        count_copy.wait()
        last = lax.axis_index("sc") == side * (lax.axis_size("sc") - 1)
        stretch = jnp.where(jnp.full((1, users), last.astype(jnp.int32)) == 1, 1 / 0.75, 1.0)
        for c in range(cells):
            prepare(win.at[c, 0], win.at[c, 1], win.at[c, 2], ybuf.at[c], stretch, *buffers[c % 2])
        for c in range(cells):
            gram(*buffers[c % 2], out.at[c], count_ref[c, side * (band - 1) // GRP], users)

    return fetch, work


def edge_gram(counts, channel, received, low, high, peer, dtype):
    cells, _, _, antennas, users = channel.shape
    symbols = received.shape[2]

    def kernel(counts_hbm, chan, samp, low_ref, high_ref, out, *scratch):
        panel = lax.axis_index("panel")
        fetch, work = edge_work(1 - panel if peer else panel, counts_hbm, chan, samp, low_ref, high_ref, out, scratch)
        fetch()
        work()

    return pl.pallas_call(
        kernel,
        in_specs=[HBM_SPEC] * 5,
        out_specs=VMEM_SPEC,
        out_shape=jax.ShapeDtypeStruct((cells, users + 2 * SPAD, users), dtype),
        scratch_shapes=edge_scratch(counts, symbols, antennas, users),
        compiler_params=pltpu.CompilerParams(vmem_limit_bytes=VMEM_LIMIT),
        cost_estimate=pl.CostEstimate(
            flops=cells * 4 * antennas * users * 2 * (users + SPAD),
            bytes_accessed=cells * 12 * antennas * users,
            transcendentals=0,
        ),
    )(counts, channel, received, low, high)


def conjugate_gradient(sums, noises, users):
    row = lax.broadcasted_iota(jnp.int32, (users, users), 0)
    col = lax.broadcasted_iota(jnp.int32, (users, users), 1)
    upper = row <= col
    grams = []
    for value in sums:
        packed = value[:users].astype(BF16)
        turned = packed.T
        real = jnp.where(upper, packed, turned)
        imag = jnp.where(row == col, jnp.zeros_like(packed), jnp.where(upper, -turned, packed))
        grams.append(jnp.concatenate([real, imag], axis=1))

    def apply(matrix, vector, noise):
        product = jnp.dot(vector.astype(BF16), matrix, preferred_element_type=F32)
        return cross(product, users) + noise * vector

    def user_sum(left, right):
        total = left * right
        even = lax.broadcasted_iota(jnp.int32, total.shape, 0) % 2 == 0
        total = total + jnp.where(even, pltpu.roll(total, 2 * SPAD - 1, 0), pltpu.roll(total, 1, 0))
        return jnp.sum(total, axis=1, keepdims=True)

    direction = [value[users:] for value in sums]
    norm = [user_sum(d, d) for d in direction]
    image = [apply(*terms) for terms in zip(grams, direction, noises)]
    alpha = [n / user_sum(d, i) for n, d, i in zip(norm, direction, image)]
    estimate = [a * d for a, d in zip(alpha, direction)]
    residual = [d - a * i for d, a, i in zip(direction, alpha, image)]
    norm_next = [user_sum(r, r) for r in residual]
    direction = [r + (m / n) * d for r, m, n, d in zip(residual, norm_next, norm, direction)]
    image = [apply(*terms) for terms in zip(grams, direction, noises)]
    alpha = [n / user_sum(d, i) for n, d, i in zip(norm_next, direction, image)]
    return [e + a * d for e, a, d in zip(estimate, alpha, direction)]


def detect_first(noise_power, own, peer):
    cells, inner, rows, users = own.shape
    half, number = inner + 1, peer.shape[1]

    def kernel(noise_ref, own_ref, peer_ref, out):
        panel = lax.axis_index("panel")
        spots = [(c, i) for c in range(cells) for i in range(number)]
        sums = [own_ref[c, i] + peer_ref[c, i].astype(F32) for c, i in spots]
        values = conjugate_gradient(sums, [noise_ref[c] for c, _ in spots], users)
        for (c, i), value in zip(spots, values):
            out[c, pl.ds(i + 1 - panel, 2 * SPAD, stride=half), :] = value

    return pl.pallas_call(
        kernel,
        in_specs=[SMEM_SPEC] + [VMEM_SPEC] * 2,
        out_specs=VMEM_SPEC,
        out_shape=jax.ShapeDtypeStruct((cells, 2 * SPAD * half, users), F32),
        compiler_params=pltpu.CompilerParams(vmem_limit_bytes=VMEM_LIMIT),
        cost_estimate=pl.CostEstimate(
            flops=cells * number * 2 * 2 * 2 * SPAD * users * 2 * users,
            bytes_accessed=cells * inner * rows * users * 6,
            transcendentals=0,
        ),
    )(noise_power, own, peer)


def detect_last(noise_power, own, peer, edge_own, edge_peer, state, onehot, symbols, rounds):
    cells, inner, rows, users = own.shape
    half, number = inner + 1, peer.shape[1]
    width = onehot.shape[1] // (2 * rounds)
    keep = symbols * half

    def kernel(noise_ref, own_ref, peer_ref, edge_own_ref, edge_peer_ref, hot_ref, state_ref, *refs):
        *outs, full = refs
        panel = lax.axis_index("panel")
        full[...] = state_ref[...]
        first = inner - number
        spots = [(c, i) for c in range(cells) for i in range(number)]
        sums = [own_ref[c, first + i] + peer_ref[c, i].astype(F32) for c, i in spots]
        places = [(c, first + i + 1 - panel) for c, i in spots]
        sums += [edge_own_ref[c] + edge_peer_ref[c].astype(F32) for c in range(cells)]
        places += [(c, panel * (half - 1)) for c in range(cells)]
        values = conjugate_gradient(sums, [noise_ref[c] for c, _ in places], users)
        for (c, place), value in zip(places, values):
            full[c, pl.ds(place, 2 * SPAD, stride=half), :] = value
        found = full[...].astype(BF16)
        blocks = [
            jnp.concatenate([found[c, (2 * s + k) * half : (2 * s + k + 1) * half] for s in range(symbols)], axis=0)
            for k in range(2)
            for c in range(cells)
        ]
        lhs = jnp.concatenate(blocks, axis=1)
        placed = jnp.dot(lhs, hot_ref[...], preferred_element_type=F32).astype(BF16)
        for i, out in enumerate(outs):
            for side in range(2):
                start = (2 * i + side) * width
                out[side * keep : (side + 1) * keep, :] = placed[:, start : start + width]

    return pl.pallas_call(
        kernel,
        in_specs=[SMEM_SPEC] + [VMEM_SPEC] * 6,
        out_specs=[VMEM_SPEC] * rounds,
        out_shape=[jax.ShapeDtypeStruct((2 * keep, width), BF16)] * rounds,
        scratch_shapes=[pltpu.VMEM(state.shape, F32)],
        compiler_params=pltpu.CompilerParams(vmem_limit_bytes=VMEM_LIMIT),
        cost_estimate=pl.CostEstimate(
            flops=2 * keep * onehot.shape[0] * onehot.shape[1], bytes_accessed=4 * state.size, transcendentals=0
        ),
    )(noise_power, own, peer, edge_own, edge_peer, onehot, state)


def assemble(sources, mine, theirs, others, cells, per_device, symbols, half):
    rounds = sum(group.shape[0] for group in mine)
    total = 2 * rounds * 2 * half
    lanes = mine[0].shape[2]
    keep = symbols * half
    number = len(mine)

    def kernel(source_ref, *refs):
        mine_refs, theirs_refs = refs[:number], refs[number : 2 * number]
        own_other, peer_others = refs[2 * number], refs[2 * number + 1 : 3 * number + 1]
        out, gathered = refs[3 * number + 1 :]
        panel = lax.axis_index("panel")

        def place(ref, i, first, source, side):
            start = pl.multiple_of(source * (2 * half) + side * half, half)
            for s in range(symbols):
                gathered[s, pl.ds(start, half), :] = ref[i, first + s * half : first + (s + 1) * half, :]

        for side, group in ((panel, mine_refs), (1 - panel, theirs_refs)):
            n = 0
            for ref in group:
                for i in range(ref.shape[0]):
                    place(ref, i, keep, source_ref[n], side)
                    n += 1
        for side, group in ((panel, (own_other,)), (1 - panel, peer_others)):
            n = rounds
            for ref in group:
                for i in range(ref.shape[0]):
                    place(ref, i, 0, source_ref[n], side)
                    n += 1
        for s in range(symbols):
            out[:, :, s] = gathered[s].T.reshape(cells, per_device, 2, total)

    return pl.pallas_call(
        kernel,
        in_specs=[SMEM_SPEC] + [VMEM_SPEC] * (3 * number + 1),
        out_specs=VMEM_SPEC,
        out_shape=jax.ShapeDtypeStruct((cells, per_device, symbols, 2, total), BF16),
        scratch_shapes=[pltpu.VMEM((symbols, total, lanes), BF16)],
        compiler_params=pltpu.CompilerParams(vmem_limit_bytes=VMEM_LIMIT),
    )(sources, *mine, *theirs, *others)


def body(channel, received, noise_power, user_count, serving_cell):
    cells, band, _, antennas, users = channel.shape
    symbols = received.shape[3]
    half = band // 2
    n_sc, n_cell = lax.axis_size("sc"), lax.axis_size("cell")
    panel, sc, cell = lax.axis_index("panel"), lax.axis_index("sc"), lax.axis_index("cell")

    samples = jnp.transpose(received, (0, 1, 3, 2, 4))

    inner = half - 1
    count = inner // 2
    first, bottom, top = inner_gram(
        user_count, channel, samples, True, (1, half), count, BF16, limit=56 << 20, ends=True
    )
    first_peer = lax.ppermute(first, "panel", SWAP)
    bottom, top = hand_on([bottom, top])
    low = lax.ppermute(top, "sc", [(i, i + 1) for i in range(n_sc - 1)])
    high = lax.ppermute(bottom, "sc", [(i + 1, i) for i in range(n_sc - 1)])
    (second,) = inner_gram(
        user_count, channel, samples, True, (1 + count, half + count), inner - count, BF16, limit=56 << 20
    )
    second_peer = lax.ppermute(second, "panel", SWAP)
    counts, first_peer = lax.optimization_barrier((user_count, first_peer))
    (own,) = inner_gram(counts, channel, samples, False, (1, half), inner, F32)
    state = detect_first(noise_power, own, first_peer)
    low, high, state = lax.optimization_barrier((low, high, state))
    edge_peer = lax.ppermute(edge_gram(user_count, channel, samples, low, high, True, BF16), "panel", SWAP)
    edge_own = edge_gram(user_count, channel, samples, low, high, False, F32)

    capacity = cells * users // n_cell
    per_device = n_cell * capacity // n_sc
    reach = capacity // per_device
    keys = serving_cell[:, :, 0].reshape(-1)
    position = lax.iota(jnp.int32, cells * users)
    earlier = (keys[:, None] == keys[None, :]) & (position[None, :] < position[:, None])
    rank = jnp.sum(earlier.astype(jnp.int32), axis=1)
    turn = (rank // per_device - sc % reach) % reach * 2 + (keys // cells == sc // reach).astype(jnp.int32)
    column = ((turn * cells + keys % cells) * per_device + rank % per_device) * 2
    column = jnp.concatenate([column, column + 1])
    width = 2 * cells * per_device
    onehot = (column[:, None] == lax.iota(jnp.int32, 2 * reach * width)[None, :]).astype(BF16)

    messages = detect_last(noise_power, own, second_peer, edge_own, edge_peer, state, onehot, symbols, reach)
    arrived = []
    for b in range(reach):
        pairs = [
            (s * n_sc + j, j // reach * n_sc + s * reach + (j % reach + b) % reach)
            for s in range(n_cell)
            for j in range(n_sc)
        ]
        arrived.append(lax.ppermute(messages[b], ("cell", "sc"), pairs))
    turns = (sc % reach - lax.iota(jnp.int32, reach)) % reach
    sources = jnp.concatenate([cell * reach + turns, (1 - cell) * reach + turns])
    keep = symbols * half
    mine = [jnp.stack(arrived[: reach // 2]), jnp.stack(arrived[reach // 2 :])]
    theirs = [lax.ppermute(group, "panel", SWAP) for group in mine]
    others = [lax.ppermute(jnp.stack([block[:keep] for block in arrived]), "cell", SWAP)]
    others += [lax.ppermute(group[:, :keep], "cell", SWAP) for group in theirs]
    routed = assemble(sources, mine, theirs, others, cells, per_device, symbols, half)
    return jnp.transpose(routed, (0, 1, 3, 2, 4))


def solution(mesh):
    return jax.shard_map(
        body,
        mesh=mesh,
        in_specs=(
            P("cell", "sc", None, "panel", None),
            P("cell", "sc", None, None, "panel"),
            P("cell"),
            P("cell", "sc"),
            P("cell", None, None),
        ),
        out_specs=P("cell", "sc", None, None, None),
        check_vma=False,
    )
```

```python
import jax
import jax.numpy as jnp
from jax import lax
from jax.experimental import pallas as pl
from jax.experimental.pallas import tpu as pltpu
from jax.sharding import PartitionSpec as P

F32, BF16 = jnp.float32, jnp.bfloat16
GRP = 16
SPAD = 16
VMEM_LIMIT = 40 << 20
SWAP = [(0, 1), (1, 0)]

SMEM_SPEC = pl.BlockSpec(memory_space=pltpu.SMEM)
VMEM_SPEC = pl.BlockSpec(memory_space=pltpu.VMEM)
HBM_SPEC = pl.BlockSpec(memory_space=pltpu.HBM)


def cross(product, users):
    left, right = product[:, :users], product[:, users:]
    rows = product.shape[0]
    even = lax.broadcasted_iota(jnp.int32, left.shape, 0) % 2 == 0
    return left + jnp.where(even, pltpu.roll(right, rows - 1, 0), -pltpu.roll(right, 1, 0))


def prepare(below, here, above, samples, stretch, mat, lhs):
    antennas, users = here.shape[1:]
    symbols = samples.shape[0]
    slab = 128
    lhs[2 * users : 2 * (users + symbols), :] = samples[...].reshape(2 * symbols, antennas)
    for k in range(2):
        for row in range(0, antennas, slab):
            rows = pl.ds(row, slab)
            outer = below[k, rows, :].astype(F32) + above[k, rows, :].astype(F32)
            middle = here[k, rows, :]
            value = outer + (middle + middle).astype(F32)
            value = (value if stretch is None else value * stretch).astype(BF16)
            mat[rows, k * users : (k + 1) * users] = value
            lhs[k * users : (k + 1) * users, rows] = value.T


def gram(mat, lhs, out, count, users):
    product = jnp.dot(lhs[...], mat[...], preferred_element_type=F32)
    row = lax.broadcasted_iota(jnp.int32, (users, users), 0)
    col = lax.broadcasted_iota(jnp.int32, (users, users), 1)
    real = product[:users, :users] + product[users : 2 * users, users:]
    imag = product[:users, users:] - product[users : 2 * users, :users]
    packed = jnp.where(row <= col, real, imag)
    out[:users, :] = jnp.where(jnp.maximum(row, col) < count, packed * 0.0625, 0.0).astype(out.dtype)
    lane = lax.broadcasted_iota(jnp.int32, (1, users), 1)
    scale = jnp.where(lane < count, 0.25, 0.0)
    out[users:, :] = (cross(product[2 * users :], users) * scale).astype(out.dtype)


def work_buffers(antennas, users):
    return [
        pltpu.VMEM((antennas, 2 * users), BF16),
        pltpu.VMEM((2 * users + 2 * SPAD, antennas), BF16),
    ]


def inner_gram(counts, channel, received, peer, firsts, number, dtype, limit=VMEM_LIMIT, ends=False):
    cells, band, _, antennas, users = channel.shape
    symbols = received.shape[2]
    items = cells * number

    def kernel(counts_hbm, chan, samp, out, *refs):
        end_outs, refs = (refs[:2], refs[2:]) if ends else ((), refs)
        end_refs, refs = (refs[:2], refs[2:]) if ends else ((), refs)
        count_ref, win, ybuf, mat_a, lhs_a, mat_b, lhs_b, wsem, ysem, csem, esem, osem = refs
        count_copy = pltpu.make_async_copy(counts_hbm, count_ref, csem)
        count_copy.start()
        panel, sc = lax.axis_index("panel"), lax.axis_index("sc")
        side = 1 - panel if peer else panel
        start = jnp.where(side == 0, firsts[0], firsts[1])
        end_copies = [
            pltpu.make_async_copy(chan.at[c, (band - 1) * ((sc + i + 1) % 2)], end_ref.at[c], esem.at[c, i])
            for c in range(cells)
            for i, end_ref in enumerate(end_refs)
        ]
        end_writes = [
            pltpu.make_async_copy(end_ref.at[c], end_out.at[c, 0], osem.at[c, i])
            for c in range(cells)
            for i, (end_ref, end_out) in enumerate(zip(end_refs, end_outs))
        ]

        def fetch(c, i):
            return pltpu.make_async_copy(chan.at[c, start - 1 + i], win.at[c, i], wsem.at[c, i])

        def fetch_samples(c, i):
            return pltpu.make_async_copy(samp.at[c, start + i], ybuf.at[c, i], ysem.at[c, i])

        for c in range(cells):
            for i in range(number + 2):
                fetch(c, i).start()
                if i >= 2:
                    fetch_samples(c, i - 2).start()
        for copy in end_copies:
            copy.start()
        lhs_a[...] = jnp.zeros_like(lhs_a)
        lhs_b[...] = jnp.zeros_like(lhs_b)

        def wait(item):
            c, i = item // number, item % number

            @pl.when(item < items)
            def _():
                @pl.when(i == 0)
                def _():
                    fetch(c, 0).wait()
                    fetch(c, 1).wait()

                fetch(c, i + 2).wait()
                fetch_samples(c, i).wait()

        def ready(item, mat, lhs):
            item = jnp.minimum(item, items - 1)
            c, i = item // number, item % number
            prepare(win.at[c, i], win.at[c, i + 1], win.at[c, i + 2], ybuf.at[c, i], None, mat, lhs)

        def multiply(item, mat, lhs):
            item = jnp.minimum(item, items - 1)
            c, i = item // number, item % number
            gram(mat, lhs, out.at[c, i], count_ref[c, (start + i) // GRP], users)

        count_copy.wait()
        wait(0)
        ready(0, mat_a, lhs_a)

        def step(t, carry):
            wait(2 * t + 1)
            wait(2 * t + 2)
            ready(2 * t + 1, mat_b, lhs_b)
            multiply(2 * t, mat_a, lhs_a)
            ready(2 * t + 2, mat_a, lhs_a)
            multiply(2 * t + 1, mat_b, lhs_b)
            return carry

        steps = (items + 1) // 2
        lax.fori_loop(0, steps // 2, step, 0)
        for copy, write in zip(end_copies, end_writes):
            copy.wait()
            write.start()
        lax.fori_loop(steps // 2, steps, step, 0)
        for write in end_writes:
            write.wait()

    rows = users + 2 * SPAD
    return pl.pallas_call(
        kernel,
        in_specs=[HBM_SPEC] * 3,
        out_specs=[VMEM_SPEC] + [HBM_SPEC] * (2 * ends),
        out_shape=[jax.ShapeDtypeStruct((cells, number, rows, users), dtype)]
        + [jax.ShapeDtypeStruct((cells, 1, 2, antennas, users), BF16)] * (2 * ends),
        scratch_shapes=[pltpu.VMEM((cells, 2, antennas, users), BF16)] * (2 * ends)
        + [
            pltpu.SMEM(counts.shape, jnp.int32),
            pltpu.VMEM((cells, number + 2, 2, antennas, users), BF16),
            pltpu.VMEM((cells, number, symbols, 2, antennas), BF16),
            *work_buffers(antennas, users),
            *work_buffers(antennas, users),
            pltpu.SemaphoreType.DMA((cells, number + 2)),
            pltpu.SemaphoreType.DMA((cells, number)),
            pltpu.SemaphoreType.DMA,
            pltpu.SemaphoreType.DMA((cells, 2)),
            pltpu.SemaphoreType.DMA((cells, 2)),
        ],
        compiler_params=pltpu.CompilerParams(vmem_limit_bytes=limit),
        cost_estimate=pl.CostEstimate(
            flops=items * 4 * antennas * users * 2 * (users + SPAD) // (1 if peer else 16),
            bytes_accessed=cells * (number + 2) * 4 * antennas * users // (1 if peer else 16),
            transcendentals=0,
        ),
    )(counts, channel, received)


def hand_on(arrays):
    def kernel(*refs):
        refs[-1][0] = 0

    return pl.pallas_call(
        kernel,
        in_specs=[HBM_SPEC] * len(arrays),
        out_specs=[HBM_SPEC] * len(arrays),
        out_shape=[jax.ShapeDtypeStruct(a.shape, a.dtype) for a in arrays],
        scratch_shapes=[pltpu.SMEM((1,), jnp.int32)],
        input_output_aliases={i: i for i in range(len(arrays))},
        cost_estimate=pl.CostEstimate(flops=0, bytes_accessed=8 * arrays[0].size, transcendentals=0),
    )(*arrays)


def edge_scratch(counts, symbols, antennas, users):
    cells = counts.shape[0]
    return [
        pltpu.SMEM(counts.shape, jnp.int32),
        pltpu.VMEM((cells, 3, 2, antennas, users), BF16),
        pltpu.VMEM((cells, symbols, 2, antennas), BF16),
        *work_buffers(antennas, users),
        *work_buffers(antennas, users),
        pltpu.SemaphoreType.DMA((cells, 3)),
        pltpu.SemaphoreType.DMA((cells,)),
        pltpu.SemaphoreType.DMA,
    ]


def edge_work(side, counts_hbm, chan, samp, near_ref, far_ref, out, scratch):
    count_ref, win, ybuf, mat_a, lhs_a, mat_b, lhs_b, wsem, ysem, csem = scratch
    count_copy = pltpu.make_async_copy(counts_hbm, count_ref, csem)
    cells, band, _, _, users = chan.shape
    buffers = ((mat_a, lhs_a), (mat_b, lhs_b))

    def each_copy(act):
        def run(e, halo_ref):
            for c in range(cells):
                blocks = (
                    (halo_ref.at[c, 0], chan.at[c, 0], chan.at[c, 1]),
                    (chan.at[c, band - 2], chan.at[c, band - 1], halo_ref.at[c, 0]),
                )[e]
                for i, block in enumerate(blocks):
                    act(pltpu.make_async_copy(block, win.at[c, i], wsem.at[c, i]))
                act(pltpu.make_async_copy(samp.at[c, e * (band - 1)], ybuf.at[c], ysem.at[c]))

        odd = lax.axis_index("sc") % 2
        for e in range(2):
            @pl.when((side == e) & (odd != e))
            def _(e=e):
                run(e, near_ref)

            @pl.when((side == e) & (odd == e))
            def _(e=e):
                run(e, far_ref)

    def fetch():
        count_copy.start()
        each_copy(lambda copy: copy.start())
        lhs_a[...] = jnp.zeros_like(lhs_a)
        lhs_b[...] = jnp.zeros_like(lhs_b)

    def work():
        each_copy(lambda copy: copy.wait())
        count_copy.wait()
        last = lax.axis_index("sc") == side * (lax.axis_size("sc") - 1)
        stretch = jnp.where(jnp.full((1, users), last.astype(jnp.int32)) == 1, 1 / 0.75, 1.0)
        for c in range(cells):
            prepare(win.at[c, 0], win.at[c, 1], win.at[c, 2], ybuf.at[c], stretch, *buffers[c % 2])
        for c in range(cells):
            gram(*buffers[c % 2], out.at[c], count_ref[c, side * (band - 1) // GRP], users)

    return fetch, work


def edge_gram(counts, channel, received, near, far, peer, dtype):
    cells, _, _, antennas, users = channel.shape
    symbols = received.shape[2]

    def kernel(counts_hbm, chan, samp, near_ref, far_ref, out, *scratch):
        panel = lax.axis_index("panel")
        fetch, work = edge_work(1 - panel if peer else panel, counts_hbm, chan, samp, near_ref, far_ref, out, scratch)
        fetch()
        work()

    return pl.pallas_call(
        kernel,
        in_specs=[HBM_SPEC] * 5,
        out_specs=VMEM_SPEC,
        out_shape=jax.ShapeDtypeStruct((cells, users + 2 * SPAD, users), dtype),
        scratch_shapes=edge_scratch(counts, symbols, antennas, users),
        compiler_params=pltpu.CompilerParams(vmem_limit_bytes=VMEM_LIMIT),
        cost_estimate=pl.CostEstimate(
            flops=cells * 4 * antennas * users * 2 * (users + SPAD),
            bytes_accessed=cells * 12 * antennas * users,
            transcendentals=0,
        ),
    )(counts, channel, received, near, far)


def conjugate_gradient(sums, noises, users):
    row = lax.broadcasted_iota(jnp.int32, (users, users), 0)
    col = lax.broadcasted_iota(jnp.int32, (users, users), 1)
    upper = row <= col
    grams = []
    for value in sums:
        packed = value[:users].astype(BF16)
        turned = packed.T
        real = jnp.where(upper, packed, turned)
        imag = jnp.where(row == col, jnp.zeros_like(packed), jnp.where(upper, -turned, packed))
        grams.append(jnp.concatenate([real, imag], axis=1))

    def apply(matrix, vector, noise):
        product = jnp.dot(vector.astype(BF16), matrix, preferred_element_type=F32)
        return cross(product, users) + noise * vector

    def user_sum(left, right):
        total = left * right
        even = lax.broadcasted_iota(jnp.int32, total.shape, 0) % 2 == 0
        total = total + jnp.where(even, pltpu.roll(total, 2 * SPAD - 1, 0), pltpu.roll(total, 1, 0))
        return jnp.sum(total, axis=1, keepdims=True)

    direction = [value[users:] for value in sums]
    norm = [user_sum(d, d) for d in direction]
    image = [apply(*terms) for terms in zip(grams, direction, noises)]
    alpha = [n / user_sum(d, i) for n, d, i in zip(norm, direction, image)]
    estimate = [a * d for a, d in zip(alpha, direction)]
    residual = [d - a * i for d, a, i in zip(direction, alpha, image)]
    norm_next = [user_sum(r, r) for r in residual]
    direction = [r + (m / n) * d for r, m, n, d in zip(residual, norm_next, norm, direction)]
    image = [apply(*terms) for terms in zip(grams, direction, noises)]
    alpha = [n / user_sum(d, i) for n, d, i in zip(norm_next, direction, image)]
    return [e + a * d for e, a, d in zip(estimate, alpha, direction)]


def detect_first(noise_power, own, peer):
    cells, inner, rows, users = own.shape
    half, number = inner + 1, peer.shape[1]

    def kernel(noise_ref, own_ref, peer_ref, out):
        panel = lax.axis_index("panel")
        spots = [(c, i) for c in range(cells) for i in range(number)]
        sums = [own_ref[c, i] + peer_ref[c, i].astype(F32) for c, i in spots]
        values = conjugate_gradient(sums, [noise_ref[c] for c, _ in spots], users)
        for (c, i), value in zip(spots, values):
            out[c, pl.ds(i + 1 - panel, 2 * SPAD, stride=half), :] = value

    return pl.pallas_call(
        kernel,
        in_specs=[SMEM_SPEC] + [VMEM_SPEC] * 2,
        out_specs=VMEM_SPEC,
        out_shape=jax.ShapeDtypeStruct((cells, 2 * SPAD * half, users), F32),
        compiler_params=pltpu.CompilerParams(vmem_limit_bytes=VMEM_LIMIT),
        cost_estimate=pl.CostEstimate(
            flops=cells * number * 2 * 2 * 2 * SPAD * users * 2 * users,
            bytes_accessed=cells * inner * rows * users * 6,
            transcendentals=0,
        ),
    )(noise_power, own, peer)


def detect_last(noise_power, own, peer, edge_own, edge_peer, state, onehot, symbols, rounds):
    cells, inner, rows, users = own.shape
    half, number = inner + 1, peer.shape[1]
    width = onehot.shape[1] // (2 * rounds)
    keep = symbols * half

    def kernel(noise_ref, own_ref, peer_ref, edge_own_ref, edge_peer_ref, hot_ref, state_ref, *refs):
        *outs, full = refs
        panel = lax.axis_index("panel")
        full[...] = state_ref[...]
        first = inner - number
        spots = [(c, i) for c in range(cells) for i in range(number)]
        sums = [own_ref[c, first + i] + peer_ref[c, i].astype(F32) for c, i in spots]
        places = [(c, first + i + 1 - panel) for c, i in spots]
        sums += [edge_own_ref[c] + edge_peer_ref[c].astype(F32) for c in range(cells)]
        places += [(c, panel * (half - 1)) for c in range(cells)]
        values = conjugate_gradient(sums, [noise_ref[c] for c, _ in places], users)
        for (c, place), value in zip(places, values):
            full[c, pl.ds(place, 2 * SPAD, stride=half), :] = value
        found = full[...].astype(BF16)
        blocks = [
            jnp.concatenate([found[c, (2 * s + k) * half : (2 * s + k + 1) * half] for s in range(symbols)], axis=0)
            for k in range(2)
            for c in range(cells)
        ]
        lhs = jnp.concatenate(blocks, axis=1)
        placed = jnp.dot(lhs, hot_ref[...], preferred_element_type=F32).astype(BF16)
        for i, out in enumerate(outs):
            for side in range(2):
                start = (2 * i + side) * width
                out[side * keep : (side + 1) * keep, :] = placed[:, start : start + width]

    return pl.pallas_call(
        kernel,
        in_specs=[SMEM_SPEC] + [VMEM_SPEC] * 6,
        out_specs=[VMEM_SPEC] * rounds,
        out_shape=[jax.ShapeDtypeStruct((2 * keep, width), BF16)] * rounds,
        scratch_shapes=[pltpu.VMEM(state.shape, F32)],
        compiler_params=pltpu.CompilerParams(vmem_limit_bytes=VMEM_LIMIT),
        cost_estimate=pl.CostEstimate(
            flops=2 * keep * onehot.shape[0] * onehot.shape[1], bytes_accessed=4 * state.size, transcendentals=0
        ),
    )(noise_power, own, peer, edge_own, edge_peer, onehot, state)


def assemble(sources, mine, theirs, others, cells, per_device, symbols, half):
    rounds = sum(group.shape[0] for group in mine)
    total = 2 * rounds * 2 * half
    lanes = mine[0].shape[2]
    keep = symbols * half
    number = len(mine)

    def kernel(source_ref, *refs):
        mine_refs, theirs_refs = refs[:number], refs[number : 2 * number]
        own_other, peer_others = refs[2 * number], refs[2 * number + 1 : 3 * number + 1]
        out, gathered = refs[3 * number + 1 :]
        panel = lax.axis_index("panel")

        def place(ref, i, first, source, side):
            start = pl.multiple_of(source * (2 * half) + side * half, half)
            for s in range(symbols):
                gathered[s, pl.ds(start, half), :] = ref[i, first + s * half : first + (s + 1) * half, :]

        for side, group in ((panel, mine_refs), (1 - panel, theirs_refs)):
            n = 0
            for ref in group:
                for i in range(ref.shape[0]):
                    place(ref, i, keep, source_ref[n], side)
                    n += 1
        for side, group in ((panel, (own_other,)), (1 - panel, peer_others)):
            n = rounds
            for ref in group:
                for i in range(ref.shape[0]):
                    place(ref, i, 0, source_ref[n], side)
                    n += 1
        for s in range(symbols):
            out[:, :, s] = gathered[s].T.reshape(cells, per_device, 2, total)

    return pl.pallas_call(
        kernel,
        in_specs=[SMEM_SPEC] + [VMEM_SPEC] * (3 * number + 1),
        out_specs=VMEM_SPEC,
        out_shape=jax.ShapeDtypeStruct((cells, per_device, symbols, 2, total), BF16),
        scratch_shapes=[pltpu.VMEM((symbols, total, lanes), BF16)],
        compiler_params=pltpu.CompilerParams(vmem_limit_bytes=VMEM_LIMIT),
    )(sources, *mine, *theirs, *others)


def body(channel, received, noise_power, user_count, serving_cell):
    cells, band, _, antennas, users = channel.shape
    symbols = received.shape[3]
    half = band // 2
    n_sc, n_cell = lax.axis_size("sc"), lax.axis_size("cell")
    panel, sc, cell = lax.axis_index("panel"), lax.axis_index("sc"), lax.axis_index("cell")

    samples = jnp.transpose(received, (0, 1, 3, 2, 4))

    inner = half - 1
    count = inner * 2 // 5
    first, near, far = inner_gram(
        user_count, channel, samples, True, (1, half), count, BF16, limit=56 << 20, ends=True
    )
    first_peer = lax.ppermute(first, "panel", SWAP)
    near, far = hand_on([near, far])
    near = lax.ppermute(near, "sc", [(i, i ^ 1) for i in range(n_sc)])
    far = lax.ppermute(far, "sc", [(i, ((i - 1) ^ 1) + 1) for i in range(1, n_sc - 1)])
    (second,) = inner_gram(
        user_count, channel, samples, True, (1 + count, half + count), inner - count, BF16, limit=56 << 20
    )
    second_peer = lax.ppermute(second, "panel", SWAP)
    counts, first_peer = lax.optimization_barrier((user_count, first_peer))
    (own,) = inner_gram(counts, channel, samples, False, (1, half), inner, F32)
    state = detect_first(noise_power, own, first_peer)
    near, far, state = lax.optimization_barrier((near, far, state))
    edge_peer = lax.ppermute(edge_gram(user_count, channel, samples, near, far, True, BF16), "panel", SWAP)
    edge_own = edge_gram(user_count, channel, samples, near, far, False, F32)

    capacity = cells * users // n_cell
    per_device = n_cell * capacity // n_sc
    reach = capacity // per_device
    keys = serving_cell[:, :, 0].reshape(-1)
    position = lax.iota(jnp.int32, cells * users)
    earlier = (keys[:, None] == keys[None, :]) & (position[None, :] < position[:, None])
    rank = jnp.sum(earlier.astype(jnp.int32), axis=1)
    turn = (rank // per_device - sc % reach) % reach * 2 + (keys // cells == sc // reach).astype(jnp.int32)
    column = ((turn * cells + keys % cells) * per_device + rank % per_device) * 2
    column = jnp.concatenate([column, column + 1])
    width = 2 * cells * per_device
    onehot = (column[:, None] == lax.iota(jnp.int32, 2 * reach * width)[None, :]).astype(BF16)

    messages = detect_last(noise_power, own, second_peer, edge_own, edge_peer, state, onehot, symbols, reach)
    arrived = []
    for b in range(reach):
        pairs = [
            (s * n_sc + j, j // reach * n_sc + s * reach + (j % reach + b) % reach)
            for s in range(n_cell)
            for j in range(n_sc)
        ]
        arrived.append(lax.ppermute(messages[b], ("cell", "sc"), pairs))
    turns = (sc % reach - lax.iota(jnp.int32, reach)) % reach
    sources = jnp.concatenate([cell * reach + turns, (1 - cell) * reach + turns])
    keep = symbols * half
    mine = [jnp.stack(arrived[: reach // 2]), jnp.stack(arrived[reach // 2 :])]
    theirs = [lax.ppermute(group, "panel", SWAP) for group in mine]
    others = [lax.ppermute(jnp.stack([block[:keep] for block in arrived]), "cell", SWAP)]
    others += [lax.ppermute(group[:, :keep], "cell", SWAP) for group in theirs]
    routed = assemble(sources, mine, theirs, others, cells, per_device, symbols, half)
    return jnp.transpose(routed, (0, 1, 3, 2, 4))


def solution(mesh):
    return jax.shard_map(
        body,
        mesh=mesh,
        in_specs=(
            P("cell", "sc", None, "panel", None),
            P("cell", "sc", None, None, "panel"),
            P("cell"),
            P("cell", "sc"),
            P("cell", None, None),
        ),
        out_specs=P("cell", "sc", None, None, None),
        check_vma=False,
    )
```

```python
import jax
import jax.numpy as jnp
from jax import lax
from jax.experimental import pallas as pl
from jax.experimental.pallas import tpu as pltpu
from jax.sharding import PartitionSpec as P

F32, BF16 = jnp.float32, jnp.bfloat16
GRP = 16
SPAD = 16
VMEM_LIMIT = 40 << 20
SWAP = [(0, 1), (1, 0)]

SMEM_SPEC = pl.BlockSpec(memory_space=pltpu.SMEM)
VMEM_SPEC = pl.BlockSpec(memory_space=pltpu.VMEM)
HBM_SPEC = pl.BlockSpec(memory_space=pltpu.HBM)


def cross(product, users):
    left, right = product[:, :users], product[:, users:]
    rows = product.shape[0]
    even = lax.broadcasted_iota(jnp.int32, left.shape, 0) % 2 == 0
    return left + jnp.where(even, pltpu.roll(right, rows - 1, 0), -pltpu.roll(right, 1, 0))


def prepare(below, here, above, samples, stretch, mat, lhs):
    antennas, users = here.shape[1:]
    symbols = samples.shape[0]
    slab = 128
    lhs[2 * users : 2 * (users + symbols), :] = samples[...].reshape(2 * symbols, antennas)
    for k in range(2):
        for row in range(0, antennas, slab):
            rows = pl.ds(row, slab)
            outer = below[k, rows, :].astype(F32) + above[k, rows, :].astype(F32)
            middle = here[k, rows, :]
            value = outer + (middle + middle).astype(F32)
            value = (value if stretch is None else value * stretch).astype(BF16)
            mat[rows, k * users : (k + 1) * users] = value
            lhs[k * users : (k + 1) * users, rows] = value.T


def gram(mat, lhs, out, count, users):
    product = jnp.dot(lhs[...], mat[...], preferred_element_type=F32)
    row = lax.broadcasted_iota(jnp.int32, (users, users), 0)
    col = lax.broadcasted_iota(jnp.int32, (users, users), 1)
    real = product[:users, :users] + product[users : 2 * users, users:]
    imag = product[:users, users:] - product[users : 2 * users, :users]
    packed = jnp.where(row <= col, real, imag)
    out[:users, :] = jnp.where(jnp.maximum(row, col) < count, packed * 0.0625, 0.0).astype(out.dtype)
    lane = lax.broadcasted_iota(jnp.int32, (1, users), 1)
    scale = jnp.where(lane < count, 0.25, 0.0)
    out[users:, :] = (cross(product[2 * users :], users) * scale).astype(out.dtype)


def work_buffers(antennas, users):
    return [
        pltpu.VMEM((antennas, 2 * users), BF16),
        pltpu.VMEM((2 * users + 2 * SPAD, antennas), BF16),
    ]


def inner_gram(counts, channel, received, peer, firsts, number, dtype, limit=VMEM_LIMIT, ends=False):
    cells, band, _, antennas, users = channel.shape
    symbols = received.shape[2]
    items = cells * number

    def kernel(counts_hbm, chan, samp, out, *refs):
        end_outs, refs = (refs[:2], refs[2:]) if ends else ((), refs)
        end_refs, refs = (refs[:2], refs[2:]) if ends else ((), refs)
        count_ref, win, ybuf, mat_a, lhs_a, mat_b, lhs_b, wsem, ysem, csem, esem, osem = refs
        count_copy = pltpu.make_async_copy(counts_hbm, count_ref, csem)
        count_copy.start()
        panel, sc = lax.axis_index("panel"), lax.axis_index("sc")
        side = 1 - panel if peer else panel
        start = jnp.where(side == 0, firsts[0], firsts[1])
        end_copies = [
            pltpu.make_async_copy(chan.at[c, (band - 1) * ((sc + i + 1) % 2)], end_ref.at[c], esem.at[c, i])
            for c in range(cells)
            for i, end_ref in enumerate(end_refs)
        ]
        end_writes = [
            pltpu.make_async_copy(end_ref.at[c], end_out.at[c, 0], osem.at[c, i])
            for c in range(cells)
            for i, (end_ref, end_out) in enumerate(zip(end_refs, end_outs))
        ]

        def fetch(c, i):
            return pltpu.make_async_copy(chan.at[c, start - 1 + i], win.at[c, i], wsem.at[c, i])

        def fetch_samples(c, i):
            return pltpu.make_async_copy(samp.at[c, start + i], ybuf.at[c, i], ysem.at[c, i])

        for c in range(cells):
            for i in range(number + 2):
                fetch(c, i).start()
                if i >= 2:
                    fetch_samples(c, i - 2).start()
        for copy in end_copies:
            copy.start()
        lhs_a[...] = jnp.zeros_like(lhs_a)
        lhs_b[...] = jnp.zeros_like(lhs_b)

        def wait(item):
            c, i = item // number, item % number

            @pl.when(item < items)
            def _():
                @pl.when(i == 0)
                def _():
                    fetch(c, 0).wait()
                    fetch(c, 1).wait()

                fetch(c, i + 2).wait()
                fetch_samples(c, i).wait()

        def ready(item, mat, lhs):
            item = jnp.minimum(item, items - 1)
            c, i = item // number, item % number
            prepare(win.at[c, i], win.at[c, i + 1], win.at[c, i + 2], ybuf.at[c, i], None, mat, lhs)

        def multiply(item, mat, lhs):
            item = jnp.minimum(item, items - 1)
            c, i = item // number, item % number
            gram(mat, lhs, out.at[c, i], count_ref[c, (start + i) // GRP], users)

        count_copy.wait()
        wait(0)
        ready(0, mat_a, lhs_a)

        def step(t, carry):
            wait(2 * t + 1)
            wait(2 * t + 2)
            ready(2 * t + 1, mat_b, lhs_b)
            multiply(2 * t, mat_a, lhs_a)
            ready(2 * t + 2, mat_a, lhs_a)
            multiply(2 * t + 1, mat_b, lhs_b)
            return carry

        steps = (items + 1) // 2
        lax.fori_loop(0, steps // 2, step, 0)
        for copy, write in zip(end_copies, end_writes):
            copy.wait()
            write.start()
        lax.fori_loop(steps // 2, steps, step, 0)
        for write in end_writes:
            write.wait()

    rows = users + 2 * SPAD
    return pl.pallas_call(
        kernel,
        in_specs=[HBM_SPEC] * 3,
        out_specs=[VMEM_SPEC] + [HBM_SPEC] * (2 * ends),
        out_shape=[jax.ShapeDtypeStruct((cells, number, rows, users), dtype)]
        + [jax.ShapeDtypeStruct((cells, 1, 2, antennas, users), BF16)] * (2 * ends),
        scratch_shapes=[pltpu.VMEM((cells, 2, antennas, users), BF16)] * (2 * ends)
        + [
            pltpu.SMEM(counts.shape, jnp.int32),
            pltpu.VMEM((cells, number + 2, 2, antennas, users), BF16),
            pltpu.VMEM((cells, number, symbols, 2, antennas), BF16),
            *work_buffers(antennas, users),
            *work_buffers(antennas, users),
            pltpu.SemaphoreType.DMA((cells, number + 2)),
            pltpu.SemaphoreType.DMA((cells, number)),
            pltpu.SemaphoreType.DMA,
            pltpu.SemaphoreType.DMA((cells, 2)),
            pltpu.SemaphoreType.DMA((cells, 2)),
        ],
        compiler_params=pltpu.CompilerParams(vmem_limit_bytes=limit),
        cost_estimate=pl.CostEstimate(
            flops=items * 4 * antennas * users * 2 * (users + SPAD) // (1 if peer else 16),
            bytes_accessed=cells * (number + 2) * 4 * antennas * users // (1 if peer else 16),
            transcendentals=0,
        ),
    )(counts, channel, received)


def hand_on(arrays):
    def kernel(*refs):
        refs[-1][0] = 0

    return pl.pallas_call(
        kernel,
        in_specs=[HBM_SPEC] * len(arrays),
        out_specs=[HBM_SPEC] * len(arrays),
        out_shape=[jax.ShapeDtypeStruct(a.shape, a.dtype) for a in arrays],
        scratch_shapes=[pltpu.SMEM((1,), jnp.int32)],
        input_output_aliases={i: i for i in range(len(arrays))},
        cost_estimate=pl.CostEstimate(flops=0, bytes_accessed=8 * arrays[0].size, transcendentals=0),
    )(*arrays)


def edge_scratch(counts, symbols, antennas, users):
    cells = counts.shape[0]
    return [
        pltpu.SMEM(counts.shape, jnp.int32),
        pltpu.VMEM((cells, 3, 2, antennas, users), BF16),
        pltpu.VMEM((cells, symbols, 2, antennas), BF16),
        *work_buffers(antennas, users),
        *work_buffers(antennas, users),
        pltpu.SemaphoreType.DMA((cells, 3)),
        pltpu.SemaphoreType.DMA((cells,)),
        pltpu.SemaphoreType.DMA,
    ]


def edge_work(side, counts_hbm, chan, samp, near_ref, far_ref, out, scratch):
    count_ref, win, ybuf, mat_a, lhs_a, mat_b, lhs_b, wsem, ysem, csem = scratch
    count_copy = pltpu.make_async_copy(counts_hbm, count_ref, csem)
    cells, band, _, _, users = chan.shape
    buffers = ((mat_a, lhs_a), (mat_b, lhs_b))

    def each_copy(act, chosen):
        def run(e, halo_ref):
            for c in chosen:
                blocks = (
                    (halo_ref.at[c, 0], chan.at[c, 0], chan.at[c, 1]),
                    (chan.at[c, band - 2], chan.at[c, band - 1], halo_ref.at[c, 0]),
                )[e]
                for i, block in enumerate(blocks):
                    act(pltpu.make_async_copy(block, win.at[c, i], wsem.at[c, i]))
                act(pltpu.make_async_copy(samp.at[c, e * (band - 1)], ybuf.at[c], ysem.at[c]))

        odd = lax.axis_index("sc") % 2
        for e in range(2):
            @pl.when((side == e) & (odd != e))
            def _(e=e):
                run(e, near_ref)

            @pl.when((side == e) & (odd == e))
            def _(e=e):
                run(e, far_ref)

    def fetch():
        count_copy.start()
        each_copy(lambda copy: copy.start(), range(cells))
        lhs_a[...] = jnp.zeros_like(lhs_a)
        lhs_b[...] = jnp.zeros_like(lhs_b)

    def work():
        count_copy.wait()
        last = lax.axis_index("sc") == side * (lax.axis_size("sc") - 1)
        stretch = jnp.where(jnp.full((1, users), last.astype(jnp.int32)) == 1, 1 / 0.75, 1.0)
        for c in range(cells):
            each_copy(lambda copy: copy.wait(), (c,))
            prepare(win.at[c, 0], win.at[c, 1], win.at[c, 2], ybuf.at[c], stretch, *buffers[c % 2])
            gram(*buffers[c % 2], out.at[c], count_ref[c, side * (band - 1) // GRP], users)

    return fetch, work


def edge_gram(counts, channel, received, near, far, peer, dtype):
    cells, _, _, antennas, users = channel.shape
    symbols = received.shape[2]

    def kernel(counts_hbm, chan, samp, near_ref, far_ref, out, *scratch):
        panel = lax.axis_index("panel")
        fetch, work = edge_work(1 - panel if peer else panel, counts_hbm, chan, samp, near_ref, far_ref, out, scratch)
        fetch()
        work()

    return pl.pallas_call(
        kernel,
        in_specs=[HBM_SPEC] * 5,
        out_specs=VMEM_SPEC,
        out_shape=jax.ShapeDtypeStruct((cells, users + 2 * SPAD, users), dtype),
        scratch_shapes=edge_scratch(counts, symbols, antennas, users),
        compiler_params=pltpu.CompilerParams(vmem_limit_bytes=VMEM_LIMIT),
        cost_estimate=pl.CostEstimate(
            flops=cells * 4 * antennas * users * 2 * (users + SPAD),
            bytes_accessed=cells * 12 * antennas * users,
            transcendentals=0,
        ),
    )(counts, channel, received, near, far)


def conjugate_gradient(sums, noises, users):
    row = lax.broadcasted_iota(jnp.int32, (users, users), 0)
    col = lax.broadcasted_iota(jnp.int32, (users, users), 1)
    upper = row <= col
    grams = []
    for value in sums:
        packed = value[:users].astype(BF16)
        turned = packed.T
        real = jnp.where(upper, packed, turned)
        imag = jnp.where(row == col, jnp.zeros_like(packed), jnp.where(upper, -turned, packed))
        grams.append(jnp.concatenate([real, imag], axis=1))

    def apply(matrix, vector, noise):
        product = jnp.dot(vector.astype(BF16), matrix, preferred_element_type=F32)
        return cross(product, users) + noise * vector

    def user_sum(left, right):
        total = left * right
        even = lax.broadcasted_iota(jnp.int32, total.shape, 0) % 2 == 0
        total = total + jnp.where(even, pltpu.roll(total, 2 * SPAD - 1, 0), pltpu.roll(total, 1, 0))
        return jnp.sum(total, axis=1, keepdims=True)

    direction = [value[users:] for value in sums]
    norm = [user_sum(d, d) for d in direction]
    image = [apply(*terms) for terms in zip(grams, direction, noises)]
    alpha = [n / user_sum(d, i) for n, d, i in zip(norm, direction, image)]
    estimate = [a * d for a, d in zip(alpha, direction)]
    residual = [d - a * i for d, a, i in zip(direction, alpha, image)]
    norm_next = [user_sum(r, r) for r in residual]
    direction = [r + (m / n) * d for r, m, n, d in zip(residual, norm_next, norm, direction)]
    image = [apply(*terms) for terms in zip(grams, direction, noises)]
    alpha = [n / user_sum(d, i) for n, d, i in zip(norm_next, direction, image)]
    return [e + a * d for e, a, d in zip(estimate, alpha, direction)]


def detect_inner(noise_power, own, peer, first, state):
    cells, inner, rows, users = own.shape
    half, number = inner + 1, peer.shape[1]

    def kernel(noise_ref, own_ref, peer_ref, *refs):
        out = refs[-1]
        if state:
            out[...] = refs[0][...]
        panel = lax.axis_index("panel")
        spots = [(c, i) for c in range(cells) for i in range(number)]
        sums = [own_ref[c, first + i] + peer_ref[c, i].astype(F32) for c, i in spots]
        values = conjugate_gradient(sums, [noise_ref[c] for c, _ in spots], users)
        for (c, i), value in zip(spots, values):
            out[c, pl.ds(first + i + 1 - panel, 2 * SPAD, stride=half), :] = value

    return pl.pallas_call(
        kernel,
        in_specs=[SMEM_SPEC] + [VMEM_SPEC] * (2 + len(state)),
        out_specs=VMEM_SPEC,
        out_shape=jax.ShapeDtypeStruct((cells, 2 * SPAD * half, users), F32),
        compiler_params=pltpu.CompilerParams(vmem_limit_bytes=VMEM_LIMIT),
        cost_estimate=pl.CostEstimate(
            flops=cells * number * 2 * 2 * 2 * SPAD * users * 2 * users,
            bytes_accessed=cells * inner * rows * users * 6,
            transcendentals=0,
        ),
    )(noise_power, own, peer, *state)


def detect_edge(noise_power, edge_own, edge_peer, state, onehot, symbols, rounds):
    cells, _, users = edge_own.shape
    half = state.shape[1] // (2 * SPAD)
    width = onehot.shape[1] // (2 * rounds)
    keep = symbols * half

    def kernel(noise_ref, edge_own_ref, edge_peer_ref, hot_ref, state_ref, *refs):
        *outs, full = refs
        full[...] = state_ref[...]
        sums = [edge_own_ref[c] + edge_peer_ref[c].astype(F32) for c in range(cells)]
        values = conjugate_gradient(sums, [noise_ref[c] for c in range(cells)], users)
        place = lax.axis_index("panel") * (half - 1)
        for c, value in enumerate(values):
            full[c, pl.ds(place, 2 * SPAD, stride=half), :] = value
        found = full[...].astype(BF16)
        blocks = [
            jnp.concatenate([found[c, (2 * s + k) * half : (2 * s + k + 1) * half] for s in range(symbols)], axis=0)
            for k in range(2)
            for c in range(cells)
        ]
        lhs = jnp.concatenate(blocks, axis=1)
        placed = jnp.dot(lhs, hot_ref[...], preferred_element_type=F32).astype(BF16)
        for i, out in enumerate(outs):
            for side in range(2):
                start = (2 * i + side) * width
                out[side * keep : (side + 1) * keep, :] = placed[:, start : start + width]

    return pl.pallas_call(
        kernel,
        in_specs=[SMEM_SPEC] + [VMEM_SPEC] * 4,
        out_specs=[VMEM_SPEC] * rounds,
        out_shape=[jax.ShapeDtypeStruct((2 * keep, width), BF16)] * rounds,
        scratch_shapes=[pltpu.VMEM(state.shape, F32)],
        compiler_params=pltpu.CompilerParams(vmem_limit_bytes=VMEM_LIMIT),
        cost_estimate=pl.CostEstimate(
            flops=2 * keep * onehot.shape[0] * onehot.shape[1], bytes_accessed=4 * state.size, transcendentals=0
        ),
    )(noise_power, edge_own, edge_peer, onehot, state)


def assemble(sources, mine, theirs, others, cells, per_device, symbols, half):
    rounds = sum(group.shape[0] for group in mine)
    total = 2 * rounds * 2 * half
    lanes = mine[0].shape[2]
    keep = symbols * half
    number = len(mine)

    def kernel(source_ref, *refs):
        mine_refs, theirs_refs = refs[:number], refs[number : 2 * number]
        own_other, peer_others = refs[2 * number], refs[2 * number + 1 : 3 * number + 1]
        out, gathered = refs[3 * number + 1 :]
        panel = lax.axis_index("panel")

        def place(ref, i, first, source, side):
            start = pl.multiple_of(source * (2 * half) + side * half, half)
            for s in range(symbols):
                gathered[s, pl.ds(start, half), :] = ref[i, first + s * half : first + (s + 1) * half, :]

        for side, group in ((panel, mine_refs), (1 - panel, theirs_refs)):
            n = 0
            for ref in group:
                for i in range(ref.shape[0]):
                    place(ref, i, keep, source_ref[n], side)
                    n += 1
        for side, group in ((panel, (own_other,)), (1 - panel, peer_others)):
            n = rounds
            for ref in group:
                for i in range(ref.shape[0]):
                    place(ref, i, 0, source_ref[n], side)
                    n += 1
        for s in range(symbols):
            out[:, :, s] = gathered[s].T.reshape(cells, per_device, 2, total)

    return pl.pallas_call(
        kernel,
        in_specs=[SMEM_SPEC] + [VMEM_SPEC] * (3 * number + 1),
        out_specs=VMEM_SPEC,
        out_shape=jax.ShapeDtypeStruct((cells, per_device, symbols, 2, total), BF16),
        scratch_shapes=[pltpu.VMEM((symbols, total, lanes), BF16)],
        compiler_params=pltpu.CompilerParams(vmem_limit_bytes=VMEM_LIMIT),
    )(sources, *mine, *theirs, *others)


def body(channel, received, noise_power, user_count, serving_cell):
    cells, band, _, antennas, users = channel.shape
    symbols = received.shape[3]
    half = band // 2
    n_sc, n_cell = lax.axis_size("sc"), lax.axis_size("cell")
    panel, sc, cell = lax.axis_index("panel"), lax.axis_index("sc"), lax.axis_index("cell")

    samples = jnp.transpose(received, (0, 1, 3, 2, 4))

    inner = half - 1
    count = inner * 2 // 5
    first, near, far = inner_gram(
        user_count, channel, samples, True, (1, half), count, BF16, limit=56 << 20, ends=True
    )
    first_peer = lax.ppermute(first, "panel", SWAP)
    near, far = hand_on([near, far])
    near = lax.ppermute(near, "sc", [(i, i ^ 1) for i in range(n_sc)])
    far = lax.ppermute(far, "sc", [(i, ((i - 1) ^ 1) + 1) for i in range(1, n_sc - 1)])
    (second,) = inner_gram(
        user_count, channel, samples, True, (1 + count, half + count), inner - count, BF16, limit=56 << 20
    )
    second_peer = lax.ppermute(second, "panel", SWAP)
    counts, first_peer = lax.optimization_barrier((user_count, first_peer))
    (own,) = inner_gram(counts, channel, samples, False, (1, half), inner, F32)
    state = detect_inner(noise_power, own, first_peer, 0, ())
    near, far, state = lax.optimization_barrier((near, far, state))
    edge_peer = lax.ppermute(edge_gram(user_count, channel, samples, near, far, True, BF16), "panel", SWAP)
    edge_own = edge_gram(user_count, channel, samples, near, far, False, F32)
    edge_own, second_peer = lax.optimization_barrier((edge_own, second_peer))
    state = detect_inner(noise_power, own, second_peer, count, (state,))

    capacity = cells * users // n_cell
    per_device = n_cell * capacity // n_sc
    reach = capacity // per_device
    keys = serving_cell[:, :, 0].reshape(-1)
    position = lax.iota(jnp.int32, cells * users)
    earlier = (keys[:, None] == keys[None, :]) & (position[None, :] < position[:, None])
    rank = jnp.sum(earlier.astype(jnp.int32), axis=1)
    turn = (rank // per_device - sc % reach) % reach * 2 + (keys // cells == sc // reach).astype(jnp.int32)
    column = ((turn * cells + keys % cells) * per_device + rank % per_device) * 2
    column = jnp.concatenate([column, column + 1])
    width = 2 * cells * per_device
    onehot = (column[:, None] == lax.iota(jnp.int32, 2 * reach * width)[None, :]).astype(BF16)

    messages = detect_edge(noise_power, edge_own, edge_peer, state, onehot, symbols, reach)
    arrived = []
    for b in range(reach):
        pairs = [
            (s * n_sc + j, j // reach * n_sc + s * reach + (j % reach + b) % reach)
            for s in range(n_cell)
            for j in range(n_sc)
        ]
        arrived.append(lax.ppermute(messages[b], ("cell", "sc"), pairs))
    turns = (sc % reach - lax.iota(jnp.int32, reach)) % reach
    sources = jnp.concatenate([cell * reach + turns, (1 - cell) * reach + turns])
    keep = symbols * half
    mine = [jnp.stack(arrived[: reach // 2]), jnp.stack(arrived[reach // 2 :])]
    theirs = [lax.ppermute(group, "panel", SWAP) for group in mine]
    others = [lax.ppermute(jnp.stack([block[:keep] for block in arrived]), "cell", SWAP)]
    others += [lax.ppermute(group[:, :keep], "cell", SWAP) for group in theirs]
    routed = assemble(sources, mine, theirs, others, cells, per_device, symbols, half)
    return jnp.transpose(routed, (0, 1, 3, 2, 4))


def solution(mesh):
    return jax.shard_map(
        body,
        mesh=mesh,
        in_specs=(
            P("cell", "sc", None, "panel", None),
            P("cell", "sc", None, None, "panel"),
            P("cell"),
            P("cell", "sc"),
            P("cell", None, None),
        ),
        out_specs=P("cell", "sc", None, None, None),
        check_vma=False,
    )
```

```python
import jax
import jax.numpy as jnp
from jax import lax
from jax.experimental import pallas as pl
from jax.experimental.pallas import tpu as pltpu
from jax.sharding import PartitionSpec as P

F32, BF16 = jnp.float32, jnp.bfloat16
GRP = 16
SPAD = 16
VMEM_LIMIT = 40 << 20
SWAP = [(0, 1), (1, 0)]

SMEM_SPEC = pl.BlockSpec(memory_space=pltpu.SMEM)
VMEM_SPEC = pl.BlockSpec(memory_space=pltpu.VMEM)
HBM_SPEC = pl.BlockSpec(memory_space=pltpu.HBM)


def cross(product, users):
    left, right = product[:, :users], product[:, users:]
    rows = product.shape[0]
    even = lax.broadcasted_iota(jnp.int32, left.shape, 0) % 2 == 0
    return left + jnp.where(even, pltpu.roll(right, rows - 1, 0), -pltpu.roll(right, 1, 0))


def prepare(below, here, above, samples, stretch, mat, lhs):
    antennas, users = here.shape[1:]
    symbols = samples.shape[0]
    slab = 128
    lhs[2 * users : 2 * (users + symbols), :] = samples[...].reshape(2 * symbols, antennas)
    for k in range(2):
        for row in range(0, antennas, slab):
            rows = pl.ds(row, slab)
            outer = below[k, rows, :].astype(F32) + above[k, rows, :].astype(F32)
            middle = here[k, rows, :]
            value = outer + (middle + middle).astype(F32)
            value = (value if stretch is None else value * stretch).astype(BF16)
            mat[rows, k * users : (k + 1) * users] = value
            lhs[k * users : (k + 1) * users, rows] = value.T


def gram(mat, lhs, out, count, users):
    product = jnp.dot(lhs[...], mat[...], preferred_element_type=F32)
    row = lax.broadcasted_iota(jnp.int32, (users, users), 0)
    col = lax.broadcasted_iota(jnp.int32, (users, users), 1)
    real = product[:users, :users] + product[users : 2 * users, users:]
    imag = product[:users, users:] - product[users : 2 * users, :users]
    packed = jnp.where(row <= col, real, imag)
    out[:users, :] = jnp.where(jnp.maximum(row, col) < count, packed * 0.0625, 0.0).astype(out.dtype)
    lane = lax.broadcasted_iota(jnp.int32, (1, users), 1)
    scale = jnp.where(lane < count, 0.25, 0.0)
    out[users:, :] = (cross(product[2 * users :], users) * scale).astype(out.dtype)


def work_buffers(antennas, users):
    return [
        pltpu.VMEM((antennas, 2 * users), BF16),
        pltpu.VMEM((2 * users + 2 * SPAD, antennas), BF16),
    ]


def inner_gram(counts, channel, received, peer, firsts, number, dtype, limit=VMEM_LIMIT, ends=False):
    cells, band, _, antennas, users = channel.shape
    symbols = received.shape[2]
    items = cells * number

    def kernel(counts_hbm, chan, samp, out, *refs):
        end_outs, refs = (refs[:2], refs[2:]) if ends else ((), refs)
        end_refs, refs = (refs[:2], refs[2:]) if ends else ((), refs)
        count_ref, win, ybuf, mat_a, lhs_a, mat_b, lhs_b, wsem, ysem, csem, esem, osem = refs
        count_copy = pltpu.make_async_copy(counts_hbm, count_ref, csem)
        count_copy.start()
        panel, sc = lax.axis_index("panel"), lax.axis_index("sc")
        side = 1 - panel if peer else panel
        start = jnp.where(side == 0, firsts[0], firsts[1])
        end_copies = [
            pltpu.make_async_copy(chan.at[c, (band - 1) * ((sc + i + 1) % 2)], end_ref.at[c], esem.at[c, i])
            for c in range(cells)
            for i, end_ref in enumerate(end_refs)
        ]
        end_writes = [
            pltpu.make_async_copy(end_ref.at[c], end_out.at[c, 0], osem.at[c, i])
            for c in range(cells)
            for i, (end_ref, end_out) in enumerate(zip(end_refs, end_outs))
        ]

        def fetch(c, i):
            return pltpu.make_async_copy(chan.at[c, start - 1 + i], win.at[c, i], wsem.at[c, i])

        def fetch_samples(c, i):
            return pltpu.make_async_copy(samp.at[c, start + i], ybuf.at[c, i], ysem.at[c, i])

        for c in range(cells):
            for i in range(number + 2):
                fetch(c, i).start()
                if i >= 2:
                    fetch_samples(c, i - 2).start()
        for copy in end_copies:
            copy.start()
        lhs_a[...] = jnp.zeros_like(lhs_a)
        lhs_b[...] = jnp.zeros_like(lhs_b)

        def wait(item):
            c, i = item // number, item % number

            @pl.when(item < items)
            def _():
                @pl.when(i == 0)
                def _():
                    fetch(c, 0).wait()
                    fetch(c, 1).wait()

                fetch(c, i + 2).wait()
                fetch_samples(c, i).wait()

        def ready(item, mat, lhs):
            item = jnp.minimum(item, items - 1)
            c, i = item // number, item % number
            prepare(win.at[c, i], win.at[c, i + 1], win.at[c, i + 2], ybuf.at[c, i], None, mat, lhs)

        def multiply(item, mat, lhs):
            item = jnp.minimum(item, items - 1)
            c, i = item // number, item % number
            gram(mat, lhs, out.at[c, i], count_ref[c, (start + i) // GRP], users)

        count_copy.wait()
        wait(0)
        ready(0, mat_a, lhs_a)

        def step(t, carry):
            wait(2 * t + 1)
            wait(2 * t + 2)
            ready(2 * t + 1, mat_b, lhs_b)
            multiply(2 * t, mat_a, lhs_a)
            ready(2 * t + 2, mat_a, lhs_a)
            multiply(2 * t + 1, mat_b, lhs_b)
            return carry

        steps = (items + 1) // 2
        lax.fori_loop(0, steps // 2, step, 0)
        for copy, write in zip(end_copies, end_writes):
            copy.wait()
            write.start()
        lax.fori_loop(steps // 2, steps, step, 0)
        for write in end_writes:
            write.wait()

    rows = users + 2 * SPAD
    return pl.pallas_call(
        kernel,
        in_specs=[HBM_SPEC] * 3,
        out_specs=[VMEM_SPEC] + [HBM_SPEC] * (2 * ends),
        out_shape=[jax.ShapeDtypeStruct((cells, number, rows, users), dtype)]
        + [jax.ShapeDtypeStruct((cells, 1, 2, antennas, users), BF16)] * (2 * ends),
        scratch_shapes=[pltpu.VMEM((cells, 2, antennas, users), BF16)] * (2 * ends)
        + [
            pltpu.SMEM(counts.shape, jnp.int32),
            pltpu.VMEM((cells, number + 2, 2, antennas, users), BF16),
            pltpu.VMEM((cells, number, symbols, 2, antennas), BF16),
            *work_buffers(antennas, users),
            *work_buffers(antennas, users),
            pltpu.SemaphoreType.DMA((cells, number + 2)),
            pltpu.SemaphoreType.DMA((cells, number)),
            pltpu.SemaphoreType.DMA,
            pltpu.SemaphoreType.DMA((cells, 2)),
            pltpu.SemaphoreType.DMA((cells, 2)),
        ],
        compiler_params=pltpu.CompilerParams(vmem_limit_bytes=limit),
        cost_estimate=pl.CostEstimate(
            flops=items * 4 * antennas * users * 2 * (users + SPAD) // (1 if peer else 16),
            bytes_accessed=cells * (number + 2) * 4 * antennas * users // (1 if peer else 16),
            transcendentals=0,
        ),
    )(counts, channel, received)


def hand_on(arrays):
    def kernel(*refs):
        refs[-1][0] = 0

    return pl.pallas_call(
        kernel,
        in_specs=[HBM_SPEC] * len(arrays),
        out_specs=[HBM_SPEC] * len(arrays),
        out_shape=[jax.ShapeDtypeStruct(a.shape, a.dtype) for a in arrays],
        scratch_shapes=[pltpu.SMEM((1,), jnp.int32)],
        input_output_aliases={i: i for i in range(len(arrays))},
        cost_estimate=pl.CostEstimate(flops=0, bytes_accessed=8 * arrays[0].size, transcendentals=0),
    )(*arrays)


def edge_scratch(counts, symbols, antennas, users):
    cells = counts.shape[0]
    return [
        pltpu.SMEM(counts.shape, jnp.int32),
        pltpu.VMEM((cells, 3, 2, antennas, users), BF16),
        pltpu.VMEM((cells, symbols, 2, antennas), BF16),
        *work_buffers(antennas, users),
        *work_buffers(antennas, users),
        pltpu.SemaphoreType.DMA((cells, 3)),
        pltpu.SemaphoreType.DMA((cells,)),
        pltpu.SemaphoreType.DMA,
    ]


def edge_work(side, counts_hbm, chan, samp, near_ref, far_ref, out, scratch):
    count_ref, win, ybuf, mat_a, lhs_a, mat_b, lhs_b, wsem, ysem, csem = scratch
    count_copy = pltpu.make_async_copy(counts_hbm, count_ref, csem)
    cells, band, _, _, users = chan.shape
    buffers = ((mat_a, lhs_a), (mat_b, lhs_b))

    def each_copy(act, chosen):
        def run(e, halo_ref):
            for c in chosen:
                blocks = (
                    (halo_ref.at[c, 0], chan.at[c, 0], chan.at[c, 1]),
                    (chan.at[c, band - 2], chan.at[c, band - 1], halo_ref.at[c, 0]),
                )[e]
                for i, block in enumerate(blocks):
                    act(pltpu.make_async_copy(block, win.at[c, i], wsem.at[c, i]))
                act(pltpu.make_async_copy(samp.at[c, e * (band - 1)], ybuf.at[c], ysem.at[c]))

        odd = lax.axis_index("sc") % 2
        for e in range(2):
            @pl.when((side == e) & (odd != e))
            def _(e=e):
                run(e, near_ref)

            @pl.when((side == e) & (odd == e))
            def _(e=e):
                run(e, far_ref)

    def fetch():
        count_copy.start()
        each_copy(lambda copy: copy.start(), range(cells))
        lhs_a[...] = jnp.zeros_like(lhs_a)
        lhs_b[...] = jnp.zeros_like(lhs_b)

    def work():
        count_copy.wait()
        last = lax.axis_index("sc") == side * (lax.axis_size("sc") - 1)
        stretch = jnp.where(jnp.full((1, users), last.astype(jnp.int32)) == 1, 1 / 0.75, 1.0)
        for c in range(cells):
            each_copy(lambda copy: copy.wait(), (c,))
            prepare(win.at[c, 0], win.at[c, 1], win.at[c, 2], ybuf.at[c], stretch, *buffers[c % 2])
            gram(*buffers[c % 2], out.at[c], count_ref[c, side * (band - 1) // GRP], users)

    return fetch, work


def edge_gram(counts, channel, received, near, far):
    cells, _, _, antennas, users = channel.shape
    symbols = received.shape[2]

    def kernel(counts_hbm, chan, samp, near_ref, far_ref, out, *scratch):
        panel = lax.axis_index("panel")
        fetch, work = edge_work(1 - panel, counts_hbm, chan, samp, near_ref, far_ref, out, scratch)
        fetch()
        work()

    return pl.pallas_call(
        kernel,
        in_specs=[HBM_SPEC] * 5,
        out_specs=VMEM_SPEC,
        out_shape=jax.ShapeDtypeStruct((cells, users + 2 * SPAD, users), BF16),
        scratch_shapes=edge_scratch(counts, symbols, antennas, users),
        compiler_params=pltpu.CompilerParams(vmem_limit_bytes=VMEM_LIMIT),
        cost_estimate=pl.CostEstimate(
            flops=cells * 4 * antennas * users * 2 * (users + SPAD),
            bytes_accessed=cells * 12 * antennas * users,
            transcendentals=0,
        ),
    )(counts, channel, received, near, far)


def conjugate_gradient(sums, noises, users):
    row = lax.broadcasted_iota(jnp.int32, (users, users), 0)
    col = lax.broadcasted_iota(jnp.int32, (users, users), 1)
    upper = row <= col
    grams = []
    for value in sums:
        packed = value[:users].astype(BF16)
        turned = packed.T
        real = jnp.where(upper, packed, turned)
        imag = jnp.where(row == col, jnp.zeros_like(packed), jnp.where(upper, -turned, packed))
        grams.append(jnp.concatenate([real, imag], axis=1))

    def apply(matrix, vector, noise):
        product = jnp.dot(vector.astype(BF16), matrix, preferred_element_type=F32)
        return cross(product, users) + noise * vector

    def user_sum(left, right):
        total = left * right
        even = lax.broadcasted_iota(jnp.int32, total.shape, 0) % 2 == 0
        total = total + jnp.where(even, pltpu.roll(total, 2 * SPAD - 1, 0), pltpu.roll(total, 1, 0))
        return jnp.sum(total, axis=1, keepdims=True)

    direction = [value[users:] for value in sums]
    norm = [user_sum(d, d) for d in direction]
    image = [apply(*terms) for terms in zip(grams, direction, noises)]
    alpha = [n / user_sum(d, i) for n, d, i in zip(norm, direction, image)]
    estimate = [a * d for a, d in zip(alpha, direction)]
    residual = [d - a * i for d, a, i in zip(direction, alpha, image)]
    norm_next = [user_sum(r, r) for r in residual]
    direction = [r + (m / n) * d for r, m, n, d in zip(residual, norm_next, norm, direction)]
    image = [apply(*terms) for terms in zip(grams, direction, noises)]
    alpha = [n / user_sum(d, i) for n, d, i in zip(norm_next, direction, image)]
    return [e + a * d for e, a, d in zip(estimate, alpha, direction)]


def detect_inner(noise_power, own, peer, first, state, edge):
    cells, inner, rows, users = own.shape
    half, number = inner + 1, peer.shape[1]

    def kernel(noise_ref, own_ref, peer_ref, *refs):
        panel = lax.axis_index("panel")
        state_refs, edge_refs = refs[: len(state)], refs[len(state) : len(state) + len(edge)]
        out, *refs = refs[len(state) + len(edge) :]
        if edge:
            fetch, work = edge_work(panel, *edge_refs, refs[0], refs[1:])
            fetch()
        if state:
            out[...] = state_refs[0][...]
        spots = [(c, i) for c in range(cells) for i in range(number)]
        sums = [own_ref[c, first + i] + peer_ref[c, i].astype(F32) for c, i in spots]
        values = conjugate_gradient(sums, [noise_ref[c] for c, _ in spots], users)
        for (c, i), value in zip(spots, values):
            out[c, pl.ds(first + i + 1 - panel, 2 * SPAD, stride=half), :] = value
        if edge:
            work()

    outs = [jax.ShapeDtypeStruct((cells, 2 * SPAD * half, users), F32)]
    scratch = []
    if edge:
        outs.append(jax.ShapeDtypeStruct((cells, rows, users), F32))
        scratch = edge_scratch(edge[0], edge[2].shape[2], edge[1].shape[3], users)
    return pl.pallas_call(
        kernel,
        in_specs=[SMEM_SPEC] + [VMEM_SPEC] * (2 + len(state)) + [HBM_SPEC] * len(edge),
        out_specs=[VMEM_SPEC] * len(outs),
        out_shape=outs,
        scratch_shapes=scratch,
        compiler_params=pltpu.CompilerParams(vmem_limit_bytes=VMEM_LIMIT),
        cost_estimate=pl.CostEstimate(
            flops=cells * number * 2 * 2 * 2 * SPAD * users * 2 * users,
            bytes_accessed=cells * inner * rows * users * 6,
            transcendentals=0,
        ),
    )(noise_power, own, peer, *state, *edge)


def detect_edge(noise_power, edge_own, edge_peer, state, onehot, symbols, rounds):
    cells, _, users = edge_own.shape
    half = state.shape[1] // (2 * SPAD)
    width = onehot.shape[1] // (2 * rounds)
    keep = symbols * half

    def kernel(noise_ref, edge_own_ref, edge_peer_ref, hot_ref, state_ref, *refs):
        *outs, full = refs
        full[...] = state_ref[...]
        sums = [edge_own_ref[c] + edge_peer_ref[c].astype(F32) for c in range(cells)]
        values = conjugate_gradient(sums, [noise_ref[c] for c in range(cells)], users)
        place = lax.axis_index("panel") * (half - 1)
        for c, value in enumerate(values):
            full[c, pl.ds(place, 2 * SPAD, stride=half), :] = value
        found = full[...].astype(BF16)
        blocks = [
            jnp.concatenate([found[c, (2 * s + k) * half : (2 * s + k + 1) * half] for s in range(symbols)], axis=0)
            for k in range(2)
            for c in range(cells)
        ]
        lhs = jnp.concatenate(blocks, axis=1)
        placed = jnp.dot(lhs, hot_ref[...], preferred_element_type=F32).astype(BF16)
        for i, out in enumerate(outs):
            for side in range(2):
                start = (2 * i + side) * width
                out[side * keep : (side + 1) * keep, :] = placed[:, start : start + width]

    return pl.pallas_call(
        kernel,
        in_specs=[SMEM_SPEC] + [VMEM_SPEC] * 4,
        out_specs=[VMEM_SPEC] * rounds,
        out_shape=[jax.ShapeDtypeStruct((2 * keep, width), BF16)] * rounds,
        scratch_shapes=[pltpu.VMEM(state.shape, F32)],
        compiler_params=pltpu.CompilerParams(vmem_limit_bytes=VMEM_LIMIT),
        cost_estimate=pl.CostEstimate(
            flops=2 * keep * onehot.shape[0] * onehot.shape[1], bytes_accessed=4 * state.size, transcendentals=0
        ),
    )(noise_power, edge_own, edge_peer, onehot, state)


def assemble(sources, mine, theirs, others, cells, per_device, symbols, half):
    rounds = sum(group.shape[0] for group in mine)
    total = 2 * rounds * 2 * half
    lanes = mine[0].shape[2]
    keep = symbols * half
    number = len(mine)

    def kernel(source_ref, *refs):
        mine_refs, theirs_refs = refs[:number], refs[number : 2 * number]
        own_other, peer_others = refs[2 * number], refs[2 * number + 1 : 3 * number + 1]
        out, gathered = refs[3 * number + 1 :]
        panel = lax.axis_index("panel")

        def place(ref, i, first, source, side):
            start = pl.multiple_of(source * (2 * half) + side * half, half)
            for s in range(symbols):
                gathered[s, pl.ds(start, half), :] = ref[i, first + s * half : first + (s + 1) * half, :]

        for side, group in ((panel, mine_refs), (1 - panel, theirs_refs)):
            n = 0
            for ref in group:
                for i in range(ref.shape[0]):
                    place(ref, i, keep, source_ref[n], side)
                    n += 1
        for side, group in ((panel, (own_other,)), (1 - panel, peer_others)):
            n = rounds
            for ref in group:
                for i in range(ref.shape[0]):
                    place(ref, i, 0, source_ref[n], side)
                    n += 1
        for s in range(symbols):
            out[:, :, s] = gathered[s].T.reshape(cells, per_device, 2, total)

    return pl.pallas_call(
        kernel,
        in_specs=[SMEM_SPEC] + [VMEM_SPEC] * (3 * number + 1),
        out_specs=VMEM_SPEC,
        out_shape=jax.ShapeDtypeStruct((cells, per_device, symbols, 2, total), BF16),
        scratch_shapes=[pltpu.VMEM((symbols, total, lanes), BF16)],
        compiler_params=pltpu.CompilerParams(vmem_limit_bytes=VMEM_LIMIT),
    )(sources, *mine, *theirs, *others)


def body(channel, received, noise_power, user_count, serving_cell):
    cells, band, _, antennas, users = channel.shape
    symbols = received.shape[3]
    half = band // 2
    n_sc, n_cell = lax.axis_size("sc"), lax.axis_size("cell")
    panel, sc, cell = lax.axis_index("panel"), lax.axis_index("sc"), lax.axis_index("cell")

    samples = jnp.transpose(received, (0, 1, 3, 2, 4))

    inner = half - 1
    count = inner * 2 // 5
    first, near, far = inner_gram(
        user_count, channel, samples, True, (1, half), count, BF16, limit=56 << 20, ends=True
    )
    first_peer = lax.ppermute(first, "panel", SWAP)
    near, far = hand_on([near, far])
    near = lax.ppermute(near, "sc", [(i, i ^ 1) for i in range(n_sc)])
    far = lax.ppermute(far, "sc", [(i, ((i - 1) ^ 1) + 1) for i in range(1, n_sc - 1)])
    (second,) = inner_gram(
        user_count, channel, samples, True, (1 + count, half + count), inner - count, BF16, limit=56 << 20
    )
    second_peer = lax.ppermute(second, "panel", SWAP)
    counts, first_peer = lax.optimization_barrier((user_count, first_peer))
    (own,) = inner_gram(counts, channel, samples, False, (1, half), inner, F32)
    (state,) = detect_inner(noise_power, own, first_peer, 0, (), ())
    near, far, state = lax.optimization_barrier((near, far, state))
    edge_peer = lax.ppermute(edge_gram(user_count, channel, samples, near, far), "panel", SWAP)
    edge_inputs = (user_count, channel, samples, near, far)
    state, edge_own = detect_inner(noise_power, own, second_peer, count, (state,), edge_inputs)

    capacity = cells * users // n_cell
    per_device = n_cell * capacity // n_sc
    reach = capacity // per_device
    keys = serving_cell[:, :, 0].reshape(-1)
    position = lax.iota(jnp.int32, cells * users)
    earlier = (keys[:, None] == keys[None, :]) & (position[None, :] < position[:, None])
    rank = jnp.sum(earlier.astype(jnp.int32), axis=1)
    turn = (rank // per_device - sc % reach - reach // 2) % reach * 2 + (keys // cells == sc // reach).astype(jnp.int32)
    column = ((turn * cells + keys % cells) * per_device + rank % per_device) * 2
    column = jnp.concatenate([column, column + 1])
    width = 2 * cells * per_device
    onehot = (column[:, None] == lax.iota(jnp.int32, 2 * reach * width)[None, :]).astype(BF16)

    messages = detect_edge(noise_power, edge_own, edge_peer, state, onehot, symbols, reach)
    arrived = []
    for b in [(n + reach // 2) % reach for n in range(reach)]:
        pairs = [
            (s * n_sc + j, j // reach * n_sc + s * reach + (j % reach + b) % reach)
            for s in range(n_cell)
            for j in range(n_sc)
        ]
        arrived.append(lax.ppermute(messages[len(arrived)], ("cell", "sc"), pairs))
    turns = (sc % reach - lax.iota(jnp.int32, reach) - reach // 2) % reach
    sources = jnp.concatenate([cell * reach + turns, (1 - cell) * reach + turns])
    keep = symbols * half
    mine = [jnp.stack(arrived[: reach // 2]), jnp.stack(arrived[reach // 2 :])]
    theirs = [lax.ppermute(group, "panel", SWAP) for group in mine]
    others = [lax.ppermute(jnp.stack([block[:keep] for block in arrived]), "cell", SWAP)]
    others += [lax.ppermute(group[:, :keep], "cell", SWAP) for group in theirs]
    routed = assemble(sources, mine, theirs, others, cells, per_device, symbols, half)
    return jnp.transpose(routed, (0, 1, 3, 2, 4))


def solution(mesh):
    return jax.shard_map(
        body,
        mesh=mesh,
        in_specs=(
            P("cell", "sc", None, "panel", None),
            P("cell", "sc", None, None, "panel"),
            P("cell"),
            P("cell", "sc"),
            P("cell", None, None),
        ),
        out_specs=P("cell", "sc", None, None, None),
        check_vma=False,
    )
```

```python
import jax
import jax.numpy as jnp
from jax import lax
from jax.experimental import pallas as pl
from jax.experimental.pallas import tpu as pltpu
from jax.sharding import PartitionSpec as P

F32, BF16 = jnp.float32, jnp.bfloat16
GRP = 16
SPAD = 16
VMEM_LIMIT = 40 << 20
SWAP = [(0, 1), (1, 0)]

SMEM_SPEC = pl.BlockSpec(memory_space=pltpu.SMEM)
VMEM_SPEC = pl.BlockSpec(memory_space=pltpu.VMEM)
HBM_SPEC = pl.BlockSpec(memory_space=pltpu.HBM)


def cross(product, users):
    left, right = product[:, :users], product[:, users:]
    rows = product.shape[0]
    even = lax.broadcasted_iota(jnp.int32, left.shape, 0) % 2 == 0
    return left + jnp.where(even, pltpu.roll(right, rows - 1, 0), -pltpu.roll(right, 1, 0))


def prepare(below, here, above, samples, stretch, mat, lhs):
    antennas, users = here.shape[1:]
    symbols = samples.shape[0]
    slab = 128
    lhs[2 * users : 2 * (users + symbols), :] = samples[...].reshape(2 * symbols, antennas)
    for k in range(2):
        for row in range(0, antennas, slab):
            rows = pl.ds(row, slab)
            outer = below[k, rows, :].astype(F32) + above[k, rows, :].astype(F32)
            middle = here[k, rows, :]
            value = outer + (middle + middle).astype(F32)
            value = (value if stretch is None else value * stretch).astype(BF16)
            mat[rows, k * users : (k + 1) * users] = value
            lhs[k * users : (k + 1) * users, rows] = value.T


def gram(mat, lhs, out, count, users):
    product = jnp.dot(lhs[...], mat[...], preferred_element_type=F32)
    row = lax.broadcasted_iota(jnp.int32, (users, users), 0)
    col = lax.broadcasted_iota(jnp.int32, (users, users), 1)
    real = product[:users, :users] + product[users : 2 * users, users:]
    imag = product[:users, users:] - product[users : 2 * users, :users]
    packed = jnp.where(row <= col, real, imag)
    out[:users, :] = jnp.where(jnp.maximum(row, col) < count, packed * 0.0625, 0.0).astype(out.dtype)
    lane = lax.broadcasted_iota(jnp.int32, (1, users), 1)
    scale = jnp.where(lane < count, 0.25, 0.0)
    out[users:, :] = (cross(product[2 * users :], users) * scale).astype(out.dtype)


def work_buffers(antennas, users):
    return [
        pltpu.VMEM((antennas, 2 * users), BF16),
        pltpu.VMEM((2 * users + 2 * SPAD, antennas), BF16),
    ]


def inner_gram(counts, channel, received, peer, firsts, number, dtype, limit=VMEM_LIMIT, ends=False):
    cells, band, _, antennas, users = channel.shape
    symbols = received.shape[2]
    items = cells * number

    def kernel(counts_hbm, chan, samp, out, *refs):
        end_outs, refs = (refs[:2], refs[2:]) if ends else ((), refs)
        end_refs, refs = (refs[:2], refs[2:]) if ends else ((), refs)
        count_ref, win, ybuf, mat_a, lhs_a, mat_b, lhs_b, wsem, ysem, csem, esem, osem = refs
        count_copy = pltpu.make_async_copy(counts_hbm, count_ref, csem)
        count_copy.start()
        panel, sc = lax.axis_index("panel"), lax.axis_index("sc")
        side = 1 - panel if peer else panel
        start = jnp.where(side == 0, firsts[0], firsts[1])
        end_copies = [
            pltpu.make_async_copy(chan.at[c, (band - 1) * ((sc + i + 1) % 2)], end_ref.at[c], esem.at[c, i])
            for c in range(cells)
            for i, end_ref in enumerate(end_refs)
        ]
        end_writes = [
            pltpu.make_async_copy(end_ref.at[c], end_out.at[c, 0], osem.at[c, i])
            for c in range(cells)
            for i, (end_ref, end_out) in enumerate(zip(end_refs, end_outs))
        ]

        def fetch(c, i):
            return pltpu.make_async_copy(chan.at[c, start - 1 + i], win.at[c, i], wsem.at[c, i])

        def fetch_samples(c, i):
            return pltpu.make_async_copy(samp.at[c, start + i], ybuf.at[c, i], ysem.at[c, i])

        for c in range(cells):
            for i in range(number + 2):
                fetch(c, i).start()
                if i >= 2:
                    fetch_samples(c, i - 2).start()
        for copy in end_copies:
            copy.start()
        lhs_a[...] = jnp.zeros_like(lhs_a)
        lhs_b[...] = jnp.zeros_like(lhs_b)

        def wait(item):
            c, i = item // number, item % number

            @pl.when(item < items)
            def _():
                @pl.when(i == 0)
                def _():
                    fetch(c, 0).wait()
                    fetch(c, 1).wait()

                fetch(c, i + 2).wait()
                fetch_samples(c, i).wait()

        def ready(item, mat, lhs):
            item = jnp.minimum(item, items - 1)
            c, i = item // number, item % number
            prepare(win.at[c, i], win.at[c, i + 1], win.at[c, i + 2], ybuf.at[c, i], None, mat, lhs)

        def multiply(item, mat, lhs):
            item = jnp.minimum(item, items - 1)
            c, i = item // number, item % number
            gram(mat, lhs, out.at[c, i], count_ref[c, (start + i) // GRP], users)

        count_copy.wait()
        wait(0)
        ready(0, mat_a, lhs_a)

        def step(t, carry):
            wait(2 * t + 1)
            wait(2 * t + 2)
            ready(2 * t + 1, mat_b, lhs_b)
            multiply(2 * t, mat_a, lhs_a)
            ready(2 * t + 2, mat_a, lhs_a)
            multiply(2 * t + 1, mat_b, lhs_b)
            return carry

        steps = (items + 1) // 2
        lax.fori_loop(0, steps // 2, step, 0)
        for copy, write in zip(end_copies, end_writes):
            copy.wait()
            write.start()
        lax.fori_loop(steps // 2, steps, step, 0)
        for write in end_writes:
            write.wait()

    rows = users + 2 * SPAD
    return pl.pallas_call(
        kernel,
        in_specs=[HBM_SPEC] * 3,
        out_specs=[VMEM_SPEC] + [HBM_SPEC] * (2 * ends),
        out_shape=[jax.ShapeDtypeStruct((cells, number, rows, users), dtype)]
        + [jax.ShapeDtypeStruct((cells, 1, 2, antennas, users), BF16)] * (2 * ends),
        scratch_shapes=[pltpu.VMEM((cells, 2, antennas, users), BF16)] * (2 * ends)
        + [
            pltpu.SMEM(counts.shape, jnp.int32),
            pltpu.VMEM((cells, number + 2, 2, antennas, users), BF16),
            pltpu.VMEM((cells, number, symbols, 2, antennas), BF16),
            *work_buffers(antennas, users),
            *work_buffers(antennas, users),
            pltpu.SemaphoreType.DMA((cells, number + 2)),
            pltpu.SemaphoreType.DMA((cells, number)),
            pltpu.SemaphoreType.DMA,
            pltpu.SemaphoreType.DMA((cells, 2)),
            pltpu.SemaphoreType.DMA((cells, 2)),
        ],
        compiler_params=pltpu.CompilerParams(vmem_limit_bytes=limit),
        cost_estimate=pl.CostEstimate(
            flops=items * 4 * antennas * users * 2 * (users + SPAD) // (1 if peer else 16),
            bytes_accessed=cells * (number + 2) * 4 * antennas * users // (1 if peer else 16),
            transcendentals=0,
        ),
    )(counts, channel, received)


def hand_on(arrays):
    def kernel(*refs):
        refs[-1][0] = 0

    return pl.pallas_call(
        kernel,
        in_specs=[HBM_SPEC] * len(arrays),
        out_specs=[HBM_SPEC] * len(arrays),
        out_shape=[jax.ShapeDtypeStruct(a.shape, a.dtype) for a in arrays],
        scratch_shapes=[pltpu.SMEM((1,), jnp.int32)],
        input_output_aliases={i: i for i in range(len(arrays))},
        cost_estimate=pl.CostEstimate(flops=0, bytes_accessed=8 * arrays[0].size, transcendentals=0),
    )(*arrays)


def edge_scratch(counts, symbols, antennas, users):
    cells = counts.shape[0]
    return [
        pltpu.SMEM(counts.shape, jnp.int32),
        pltpu.VMEM((cells, 3, 2, antennas, users), BF16),
        pltpu.VMEM((cells, symbols, 2, antennas), BF16),
        *work_buffers(antennas, users),
        *work_buffers(antennas, users),
        pltpu.SemaphoreType.DMA((cells, 3)),
        pltpu.SemaphoreType.DMA((cells,)),
        pltpu.SemaphoreType.DMA,
    ]


def edge_work(side, counts_hbm, chan, samp, near_ref, far_ref, out, scratch):
    count_ref, win, ybuf, mat_a, lhs_a, mat_b, lhs_b, wsem, ysem, csem = scratch
    count_copy = pltpu.make_async_copy(counts_hbm, count_ref, csem)
    cells, band, _, _, users = chan.shape
    buffers = ((mat_a, lhs_a), (mat_b, lhs_b))

    def each_copy(act, chosen):
        def run(e, halo_ref):
            for c in chosen:
                blocks = (
                    (halo_ref.at[c, 0], chan.at[c, 0], chan.at[c, 1]),
                    (chan.at[c, band - 2], chan.at[c, band - 1], halo_ref.at[c, 0]),
                )[e]
                for i, block in enumerate(blocks):
                    act(pltpu.make_async_copy(block, win.at[c, i], wsem.at[c, i]))
                act(pltpu.make_async_copy(samp.at[c, e * (band - 1)], ybuf.at[c], ysem.at[c]))

        odd = lax.axis_index("sc") % 2
        for e in range(2):
            @pl.when((side == e) & (odd != e))
            def _(e=e):
                run(e, near_ref)

            @pl.when((side == e) & (odd == e))
            def _(e=e):
                run(e, far_ref)

    def fetch():
        count_copy.start()
        each_copy(lambda copy: copy.start(), range(cells))
        lhs_a[...] = jnp.zeros_like(lhs_a)
        lhs_b[...] = jnp.zeros_like(lhs_b)

    def work():
        count_copy.wait()
        last = lax.axis_index("sc") == side * (lax.axis_size("sc") - 1)
        stretch = jnp.where(jnp.full((1, users), last.astype(jnp.int32)) == 1, 1 / 0.75, 1.0)
        for c in range(cells):
            each_copy(lambda copy: copy.wait(), (c,))
            prepare(win.at[c, 0], win.at[c, 1], win.at[c, 2], ybuf.at[c], stretch, *buffers[c % 2])
            gram(*buffers[c % 2], out.at[c], count_ref[c, side * (band - 1) // GRP], users)

    return fetch, work


def edge_gram(counts, channel, received, near, far, peer, dtype):
    cells, _, _, antennas, users = channel.shape
    symbols = received.shape[2]

    def kernel(counts_hbm, chan, samp, near_ref, far_ref, out, *scratch):
        panel = lax.axis_index("panel")
        fetch, work = edge_work(1 - panel if peer else panel, counts_hbm, chan, samp, near_ref, far_ref, out, scratch)
        fetch()
        work()

    return pl.pallas_call(
        kernel,
        in_specs=[HBM_SPEC] * 5,
        out_specs=VMEM_SPEC,
        out_shape=jax.ShapeDtypeStruct((cells, users + 2 * SPAD, users), dtype),
        scratch_shapes=edge_scratch(counts, symbols, antennas, users),
        compiler_params=pltpu.CompilerParams(vmem_limit_bytes=VMEM_LIMIT),
        cost_estimate=pl.CostEstimate(
            flops=cells * 4 * antennas * users * 2 * (users + SPAD),
            bytes_accessed=cells * 12 * antennas * users,
            transcendentals=0,
        ),
    )(counts, channel, received, near, far)


def conjugate_gradient(sums, noises, users):
    row = lax.broadcasted_iota(jnp.int32, (users, users), 0)
    col = lax.broadcasted_iota(jnp.int32, (users, users), 1)
    upper = row <= col
    grams = []
    for value in sums:
        packed = value[:users].astype(BF16)
        turned = packed.T
        real = jnp.where(upper, packed, turned)
        imag = jnp.where(row == col, jnp.zeros_like(packed), jnp.where(upper, -turned, packed))
        grams.append(jnp.concatenate([real, imag], axis=1))

    def apply(matrix, vector, noise):
        product = jnp.dot(vector.astype(BF16), matrix, preferred_element_type=F32)
        return cross(product, users) + noise * vector

    def user_sum(left, right):
        total = left * right
        even = lax.broadcasted_iota(jnp.int32, total.shape, 0) % 2 == 0
        total = total + jnp.where(even, pltpu.roll(total, 2 * SPAD - 1, 0), pltpu.roll(total, 1, 0))
        return jnp.sum(total, axis=1, keepdims=True)

    direction = [value[users:] for value in sums]
    norm = [user_sum(d, d) for d in direction]
    image = [apply(*terms) for terms in zip(grams, direction, noises)]
    alpha = [n / user_sum(d, i) for n, d, i in zip(norm, direction, image)]
    estimate = [a * d for a, d in zip(alpha, direction)]
    residual = [d - a * i for d, a, i in zip(direction, alpha, image)]
    norm_next = [user_sum(r, r) for r in residual]
    direction = [r + (m / n) * d for r, m, n, d in zip(residual, norm_next, norm, direction)]
    image = [apply(*terms) for terms in zip(grams, direction, noises)]
    alpha = [n / user_sum(d, i) for n, d, i in zip(norm_next, direction, image)]
    return [e + a * d for e, a, d in zip(estimate, alpha, direction)]


def detect_inner(noise_power, own, peer, first, state):
    cells, inner, rows, users = own.shape
    half, number = inner + 1, peer.shape[1]

    def kernel(noise_ref, own_ref, peer_ref, *refs):
        out = refs[-1]
        if state:
            out[...] = refs[0][...]
        panel = lax.axis_index("panel")
        spots = [(c, i) for c in range(cells) for i in range(number)]
        sums = [own_ref[c, first + i] + peer_ref[c, i].astype(F32) for c, i in spots]
        values = conjugate_gradient(sums, [noise_ref[c] for c, _ in spots], users)
        for (c, i), value in zip(spots, values):
            out[c, pl.ds(first + i + 1 - panel, 2 * SPAD, stride=half), :] = value

    return pl.pallas_call(
        kernel,
        in_specs=[SMEM_SPEC] + [VMEM_SPEC] * (2 + len(state)),
        out_specs=VMEM_SPEC,
        out_shape=jax.ShapeDtypeStruct((cells, 2 * SPAD * half, users), F32),
        compiler_params=pltpu.CompilerParams(vmem_limit_bytes=VMEM_LIMIT),
        cost_estimate=pl.CostEstimate(
            flops=cells * number * 2 * 2 * 2 * SPAD * users * 2 * users,
            bytes_accessed=cells * inner * rows * users * 6,
            transcendentals=0,
        ),
    )(noise_power, own, peer, *state)


def detect_edge(noise_power, edge_own, edge_peer, state, onehot, symbols, rounds):
    cells, _, users = edge_own.shape
    half = state.shape[1] // (2 * SPAD)
    width = onehot.shape[1] // (2 * rounds)
    keep = symbols * half

    def kernel(noise_ref, edge_own_ref, edge_peer_ref, hot_ref, state_ref, *refs):
        *outs, full = refs
        full[...] = state_ref[...]
        sums = [edge_own_ref[c] + edge_peer_ref[c].astype(F32) for c in range(cells)]
        values = conjugate_gradient(sums, [noise_ref[c] for c in range(cells)], users)
        place = lax.axis_index("panel") * (half - 1)
        for c, value in enumerate(values):
            full[c, pl.ds(place, 2 * SPAD, stride=half), :] = value
        found = full[...].astype(BF16)
        blocks = [
            jnp.concatenate([found[c, (2 * s + k) * half : (2 * s + k + 1) * half] for s in range(symbols)], axis=0)
            for k in range(2)
            for c in range(cells)
        ]
        lhs = jnp.concatenate(blocks, axis=1)
        placed = jnp.dot(lhs, hot_ref[...], preferred_element_type=F32).astype(BF16)
        for i, out in enumerate(outs):
            for side in range(2):
                start = (2 * i + side) * width
                out[side * keep : (side + 1) * keep, :] = placed[:, start : start + width]

    return pl.pallas_call(
        kernel,
        in_specs=[SMEM_SPEC] + [VMEM_SPEC] * 4,
        out_specs=[VMEM_SPEC] * rounds,
        out_shape=[jax.ShapeDtypeStruct((2 * keep, width), BF16)] * rounds,
        scratch_shapes=[pltpu.VMEM(state.shape, F32)],
        compiler_params=pltpu.CompilerParams(vmem_limit_bytes=VMEM_LIMIT),
        cost_estimate=pl.CostEstimate(
            flops=2 * keep * onehot.shape[0] * onehot.shape[1], bytes_accessed=4 * state.size, transcendentals=0
        ),
    )(noise_power, edge_own, edge_peer, onehot, state)


def assemble(sources, mine, theirs, others, cells, per_device, symbols, half):
    rounds = sum(group.shape[0] for group in mine)
    total = 2 * rounds * 2 * half
    lanes = mine[0].shape[2]
    keep = symbols * half
    number = len(mine)

    def kernel(source_ref, *refs):
        mine_refs, theirs_refs = refs[:number], refs[number : 2 * number]
        own_other, peer_others = refs[2 * number], refs[2 * number + 1 : 3 * number + 1]
        out, gathered = refs[3 * number + 1 :]
        panel = lax.axis_index("panel")

        def place(ref, i, first, source, side):
            start = pl.multiple_of(source * (2 * half) + side * half, half)
            for s in range(symbols):
                gathered[s, pl.ds(start, half), :] = ref[i, first + s * half : first + (s + 1) * half, :]

        for side, group in ((panel, mine_refs), (1 - panel, theirs_refs)):
            n = 0
            for ref in group:
                for i in range(ref.shape[0]):
                    place(ref, i, keep, source_ref[n], side)
                    n += 1
        for side, group in ((panel, (own_other,)), (1 - panel, peer_others)):
            n = rounds
            for ref in group:
                for i in range(ref.shape[0]):
                    place(ref, i, 0, source_ref[n], side)
                    n += 1
        for s in range(symbols):
            out[:, :, s] = gathered[s].T.reshape(cells, per_device, 2, total)

    return pl.pallas_call(
        kernel,
        in_specs=[SMEM_SPEC] + [VMEM_SPEC] * (3 * number + 1),
        out_specs=VMEM_SPEC,
        out_shape=jax.ShapeDtypeStruct((cells, per_device, symbols, 2, total), BF16),
        scratch_shapes=[pltpu.VMEM((symbols, total, lanes), BF16)],
        compiler_params=pltpu.CompilerParams(vmem_limit_bytes=VMEM_LIMIT),
    )(sources, *mine, *theirs, *others)


def body(channel, received, noise_power, user_count, serving_cell):
    cells, band, _, antennas, users = channel.shape
    symbols = received.shape[3]
    half = band // 2
    n_sc, n_cell = lax.axis_size("sc"), lax.axis_size("cell")
    panel, sc, cell = lax.axis_index("panel"), lax.axis_index("sc"), lax.axis_index("cell")

    samples = jnp.transpose(received, (0, 1, 3, 2, 4))

    inner = half - 1
    count = inner // 2
    first, near, far = inner_gram(
        user_count, channel, samples, True, (1, half), count, BF16, limit=56 << 20, ends=True
    )
    first_peer = lax.ppermute(first, "panel", SWAP)
    near, far = hand_on([near, far])
    near = lax.ppermute(near, "sc", [(i, i ^ 1) for i in range(n_sc)])
    far = lax.ppermute(far, "sc", [(i, ((i - 1) ^ 1) + 1) for i in range(1, n_sc - 1)])
    (second,) = inner_gram(
        user_count, channel, samples, True, (1 + count, half + count), inner - count, BF16, limit=56 << 20
    )
    second_peer = lax.ppermute(second, "panel", SWAP)
    counts, first_peer = lax.optimization_barrier((user_count, first_peer))
    (own,) = inner_gram(counts, channel, samples, False, (1, half), inner, F32)
    state = detect_inner(noise_power, own, first_peer, 0, ())
    near, far, state = lax.optimization_barrier((near, far, state))
    edge_peer = lax.ppermute(edge_gram(user_count, channel, samples, near, far, True, BF16), "panel", SWAP)
    edge_own = edge_gram(user_count, channel, samples, near, far, False, F32)
    edge_own, second_peer = lax.optimization_barrier((edge_own, second_peer))
    state = detect_inner(noise_power, own, second_peer, count, (state,))

    capacity = cells * users // n_cell
    per_device = n_cell * capacity // n_sc
    reach = capacity // per_device
    keys = serving_cell[:, :, 0].reshape(-1)
    position = lax.iota(jnp.int32, cells * users)
    earlier = (keys[:, None] == keys[None, :]) & (position[None, :] < position[:, None])
    rank = jnp.sum(earlier.astype(jnp.int32), axis=1)
    turn = (rank // per_device - sc % reach - reach // 2) % reach * 2 + (keys // cells == sc // reach).astype(jnp.int32)
    column = ((turn * cells + keys % cells) * per_device + rank % per_device) * 2
    column = jnp.concatenate([column, column + 1])
    width = 2 * cells * per_device
    onehot = (column[:, None] == lax.iota(jnp.int32, 2 * reach * width)[None, :]).astype(BF16)

    messages = detect_edge(noise_power, edge_own, edge_peer, state, onehot, symbols, reach)
    arrived = []
    for b in [(n + reach // 2) % reach for n in range(reach)]:
        pairs = [
            (s * n_sc + j, j // reach * n_sc + s * reach + (j % reach + b) % reach)
            for s in range(n_cell)
            for j in range(n_sc)
        ]
        arrived.append(lax.ppermute(messages[len(arrived)], ("cell", "sc"), pairs))
    turns = (sc % reach - lax.iota(jnp.int32, reach) - reach // 2) % reach
    sources = jnp.concatenate([cell * reach + turns, (1 - cell) * reach + turns])
    keep = symbols * half
    mine = [jnp.stack(arrived[: reach // 2]), jnp.stack(arrived[reach // 2 :])]
    theirs = [lax.ppermute(group, "panel", SWAP) for group in mine]
    others = [lax.ppermute(jnp.stack([block[:keep] for block in arrived]), "cell", SWAP)]
    others += [lax.ppermute(group[:, :keep], "cell", SWAP) for group in theirs]
    routed = assemble(sources, mine, theirs, others, cells, per_device, symbols, half)
    return jnp.transpose(routed, (0, 1, 3, 2, 4))


def solution(mesh):
    return jax.shard_map(
        body,
        mesh=mesh,
        in_specs=(
            P("cell", "sc", None, "panel", None),
            P("cell", "sc", None, None, "panel"),
            P("cell"),
            P("cell", "sc"),
            P("cell", None, None),
        ),
        out_specs=P("cell", "sc", None, None, None),
        check_vma=False,
    )
```

```python
import jax
import jax.numpy as jnp
from jax import lax
from jax.experimental import pallas as pl
from jax.experimental.pallas import tpu as pltpu
from jax.sharding import PartitionSpec as P

F32, BF16 = jnp.float32, jnp.bfloat16
GRP = 16
SPAD = 16
VMEM_LIMIT = 40 << 20
SWAP = [(0, 1), (1, 0)]

SMEM_SPEC = pl.BlockSpec(memory_space=pltpu.SMEM)
VMEM_SPEC = pl.BlockSpec(memory_space=pltpu.VMEM)
HBM_SPEC = pl.BlockSpec(memory_space=pltpu.HBM)


def cross(product, users):
    left, right = product[:, :users], product[:, users:]
    rows = product.shape[0]
    even = lax.broadcasted_iota(jnp.int32, left.shape, 0) % 2 == 0
    return left + jnp.where(even, pltpu.roll(right, rows - 1, 0), -pltpu.roll(right, 1, 0))


def prepare(below, here, above, samples, stretch, mat, lhs):
    antennas, users = here.shape[1:]
    symbols = samples.shape[0]
    slab = 128
    lhs[2 * users : 2 * (users + symbols), :] = samples[...].reshape(2 * symbols, antennas)
    for k in range(2):
        for row in range(0, antennas, slab):
            rows = pl.ds(row, slab)
            outer = below[k, rows, :].astype(F32) + above[k, rows, :].astype(F32)
            middle = here[k, rows, :]
            value = outer + (middle + middle).astype(F32)
            value = (value if stretch is None else value * stretch).astype(BF16)
            mat[rows, k * users : (k + 1) * users] = value
            lhs[k * users : (k + 1) * users, rows] = value.T


def gram(mat, lhs, out, count, users):
    product = jnp.dot(lhs[...], mat[...], preferred_element_type=F32)
    row = lax.broadcasted_iota(jnp.int32, (users, users), 0)
    col = lax.broadcasted_iota(jnp.int32, (users, users), 1)
    real = product[:users, :users] + product[users : 2 * users, users:]
    imag = product[:users, users:] - product[users : 2 * users, :users]
    packed = jnp.where(row <= col, real, imag)
    out[:users, :] = jnp.where(jnp.maximum(row, col) < count, packed * 0.0625, 0.0).astype(out.dtype)
    lane = lax.broadcasted_iota(jnp.int32, (1, users), 1)
    scale = jnp.where(lane < count, 0.25, 0.0)
    out[users:, :] = (cross(product[2 * users :], users) * scale).astype(out.dtype)


def work_buffers(antennas, users):
    return [
        pltpu.VMEM((antennas, 2 * users), BF16),
        pltpu.VMEM((2 * users + 2 * SPAD, antennas), BF16),
    ]


def inner_gram(counts, channel, received, peer, firsts, number, dtype, limit=VMEM_LIMIT, ends=False):
    cells, band, _, antennas, users = channel.shape
    symbols = received.shape[2]
    items = cells * number

    def kernel(counts_hbm, chan, samp, out, *refs):
        end_outs, refs = (refs[:2], refs[2:]) if ends else ((), refs)
        end_refs, refs = (refs[:2], refs[2:]) if ends else ((), refs)
        count_ref, win, ybuf, mat_a, lhs_a, mat_b, lhs_b, wsem, ysem, csem, esem, osem = refs
        count_copy = pltpu.make_async_copy(counts_hbm, count_ref, csem)
        count_copy.start()
        panel, sc = lax.axis_index("panel"), lax.axis_index("sc")
        side = 1 - panel if peer else panel
        start = jnp.where(side == 0, firsts[0], firsts[1])
        end_copies = [
            pltpu.make_async_copy(chan.at[c, (band - 1) * ((sc + i + 1) % 2)], end_ref.at[c], esem.at[c, i])
            for c in range(cells)
            for i, end_ref in enumerate(end_refs)
        ]
        end_writes = [
            pltpu.make_async_copy(end_ref.at[c], end_out.at[c, 0], osem.at[c, i])
            for c in range(cells)
            for i, (end_ref, end_out) in enumerate(zip(end_refs, end_outs))
        ]

        def fetch(c, i):
            return pltpu.make_async_copy(chan.at[c, start - 1 + i], win.at[c, i], wsem.at[c, i])

        def fetch_samples(c, i):
            return pltpu.make_async_copy(samp.at[c, start + i], ybuf.at[c, i], ysem.at[c, i])

        for c in range(cells):
            for i in range(number + 2):
                fetch(c, i).start()
                if i >= 2:
                    fetch_samples(c, i - 2).start()
        for copy in end_copies:
            copy.start()
        lhs_a[...] = jnp.zeros_like(lhs_a)
        lhs_b[...] = jnp.zeros_like(lhs_b)

        def wait(item):
            c, i = item // number, item % number

            @pl.when(item < items)
            def _():
                @pl.when(i == 0)
                def _():
                    fetch(c, 0).wait()
                    fetch(c, 1).wait()

                fetch(c, i + 2).wait()
                fetch_samples(c, i).wait()

        def ready(item, mat, lhs):
            item = jnp.minimum(item, items - 1)
            c, i = item // number, item % number
            prepare(win.at[c, i], win.at[c, i + 1], win.at[c, i + 2], ybuf.at[c, i], None, mat, lhs)

        def multiply(item, mat, lhs):
            item = jnp.minimum(item, items - 1)
            c, i = item // number, item % number
            gram(mat, lhs, out.at[c, i], count_ref[c, (start + i) // GRP], users)

        count_copy.wait()
        wait(0)
        ready(0, mat_a, lhs_a)

        def step(t, carry):
            wait(2 * t + 1)
            wait(2 * t + 2)
            ready(2 * t + 1, mat_b, lhs_b)
            multiply(2 * t, mat_a, lhs_a)
            ready(2 * t + 2, mat_a, lhs_a)
            multiply(2 * t + 1, mat_b, lhs_b)
            return carry

        steps = (items + 1) // 2
        lax.fori_loop(0, steps // 2, step, 0)
        for copy, write in zip(end_copies, end_writes):
            copy.wait()
            write.start()
        lax.fori_loop(steps // 2, steps, step, 0)
        for write in end_writes:
            write.wait()

    rows = users + 2 * SPAD
    return pl.pallas_call(
        kernel,
        in_specs=[HBM_SPEC] * 3,
        out_specs=[VMEM_SPEC] + [HBM_SPEC] * (2 * ends),
        out_shape=[jax.ShapeDtypeStruct((cells, number, rows, users), dtype)]
        + [jax.ShapeDtypeStruct((cells, 1, 2, antennas, users), BF16)] * (2 * ends),
        scratch_shapes=[pltpu.VMEM((cells, 2, antennas, users), BF16)] * (2 * ends)
        + [
            pltpu.SMEM(counts.shape, jnp.int32),
            pltpu.VMEM((cells, number + 2, 2, antennas, users), BF16),
            pltpu.VMEM((cells, number, symbols, 2, antennas), BF16),
            *work_buffers(antennas, users),
            *work_buffers(antennas, users),
            pltpu.SemaphoreType.DMA((cells, number + 2)),
            pltpu.SemaphoreType.DMA((cells, number)),
            pltpu.SemaphoreType.DMA,
            pltpu.SemaphoreType.DMA((cells, 2)),
            pltpu.SemaphoreType.DMA((cells, 2)),
        ],
        compiler_params=pltpu.CompilerParams(vmem_limit_bytes=limit),
        cost_estimate=pl.CostEstimate(
            flops=items * 4 * antennas * users * 2 * (users + SPAD) // (1 if peer else 16),
            bytes_accessed=cells * (number + 2) * 4 * antennas * users // (1 if peer else 16),
            transcendentals=0,
        ),
    )(counts, channel, received)


def hand_on(arrays):
    def kernel(*refs):
        refs[-1][0] = 0

    return pl.pallas_call(
        kernel,
        in_specs=[HBM_SPEC] * len(arrays),
        out_specs=[HBM_SPEC] * len(arrays),
        out_shape=[jax.ShapeDtypeStruct(a.shape, a.dtype) for a in arrays],
        scratch_shapes=[pltpu.SMEM((1,), jnp.int32)],
        input_output_aliases={i: i for i in range(len(arrays))},
        cost_estimate=pl.CostEstimate(flops=0, bytes_accessed=8 * arrays[0].size, transcendentals=0),
    )(*arrays)


def edge_scratch(counts, symbols, antennas, users):
    cells = counts.shape[0]
    return [
        pltpu.SMEM(counts.shape, jnp.int32),
        pltpu.VMEM((cells, 3, 2, antennas, users), BF16),
        pltpu.VMEM((cells, symbols, 2, antennas), BF16),
        *work_buffers(antennas, users),
        *work_buffers(antennas, users),
        pltpu.SemaphoreType.DMA((cells, 3)),
        pltpu.SemaphoreType.DMA((cells,)),
        pltpu.SemaphoreType.DMA,
    ]


def edge_work(side, counts_hbm, chan, samp, near_ref, far_ref, out, scratch):
    count_ref, win, ybuf, mat_a, lhs_a, mat_b, lhs_b, wsem, ysem, csem = scratch
    count_copy = pltpu.make_async_copy(counts_hbm, count_ref, csem)
    cells, band, _, _, users = chan.shape
    buffers = ((mat_a, lhs_a), (mat_b, lhs_b))

    def each_copy(act, chosen):
        def run(e, halo_ref):
            for c in chosen:
                blocks = (
                    (halo_ref.at[c, 0], chan.at[c, 0], chan.at[c, 1]),
                    (chan.at[c, band - 2], chan.at[c, band - 1], halo_ref.at[c, 0]),
                )[e]
                for i, block in enumerate(blocks):
                    act(pltpu.make_async_copy(block, win.at[c, i], wsem.at[c, i]))
                act(pltpu.make_async_copy(samp.at[c, e * (band - 1)], ybuf.at[c], ysem.at[c]))

        odd = lax.axis_index("sc") % 2
        for e in range(2):
            @pl.when((side == e) & (odd != e))
            def _(e=e):
                run(e, near_ref)

            @pl.when((side == e) & (odd == e))
            def _(e=e):
                run(e, far_ref)

    def fetch():
        count_copy.start()
        each_copy(lambda copy: copy.start(), range(cells))
        lhs_a[...] = jnp.zeros_like(lhs_a)
        lhs_b[...] = jnp.zeros_like(lhs_b)

    def work():
        count_copy.wait()
        last = lax.axis_index("sc") == side * (lax.axis_size("sc") - 1)
        stretch = jnp.where(jnp.full((1, users), last.astype(jnp.int32)) == 1, 1 / 0.75, 1.0)
        for c in range(cells):
            each_copy(lambda copy: copy.wait(), (c,))
            prepare(win.at[c, 0], win.at[c, 1], win.at[c, 2], ybuf.at[c], stretch, *buffers[c % 2])
            gram(*buffers[c % 2], out.at[c], count_ref[c, side * (band - 1) // GRP], users)

    return fetch, work


def edge_gram(counts, channel, received, near, far, peer, dtype):
    cells, _, _, antennas, users = channel.shape
    symbols = received.shape[2]

    def kernel(counts_hbm, chan, samp, near_ref, far_ref, out, *scratch):
        panel = lax.axis_index("panel")
        fetch, work = edge_work(1 - panel if peer else panel, counts_hbm, chan, samp, near_ref, far_ref, out, scratch)
        fetch()
        work()

    return pl.pallas_call(
        kernel,
        in_specs=[HBM_SPEC] * 5,
        out_specs=VMEM_SPEC,
        out_shape=jax.ShapeDtypeStruct((cells, users + 2 * SPAD, users), dtype),
        scratch_shapes=edge_scratch(counts, symbols, antennas, users),
        compiler_params=pltpu.CompilerParams(vmem_limit_bytes=VMEM_LIMIT),
        cost_estimate=pl.CostEstimate(
            flops=cells * 4 * antennas * users * 2 * (users + SPAD),
            bytes_accessed=cells * 12 * antennas * users,
            transcendentals=0,
        ),
    )(counts, channel, received, near, far)


def conjugate_gradient(sums, noises, users):
    row = lax.broadcasted_iota(jnp.int32, (users, users), 0)
    col = lax.broadcasted_iota(jnp.int32, (users, users), 1)
    upper = row <= col
    grams = []
    for value in sums:
        packed = value[:users].astype(BF16)
        turned = packed.T
        real = jnp.where(upper, packed, turned)
        imag = jnp.where(row == col, jnp.zeros_like(packed), jnp.where(upper, -turned, packed))
        grams.append(jnp.concatenate([real, imag], axis=1))

    def apply(matrix, vector, noise):
        product = jnp.dot(vector.astype(BF16), matrix, preferred_element_type=F32)
        return cross(product, users) + noise * vector

    def user_sum(left, right):
        total = left * right
        even = lax.broadcasted_iota(jnp.int32, total.shape, 0) % 2 == 0
        total = total + jnp.where(even, pltpu.roll(total, 2 * SPAD - 1, 0), pltpu.roll(total, 1, 0))
        return jnp.sum(total, axis=1, keepdims=True)

    direction = [value[users:] for value in sums]
    norm = [user_sum(d, d) for d in direction]
    image = [apply(*terms) for terms in zip(grams, direction, noises)]
    alpha = [n / user_sum(d, i) for n, d, i in zip(norm, direction, image)]
    estimate = [a * d for a, d in zip(alpha, direction)]
    residual = [d - a * i for d, a, i in zip(direction, alpha, image)]
    norm_next = [user_sum(r, r) for r in residual]
    direction = [r + (m / n) * d for r, m, n, d in zip(residual, norm_next, norm, direction)]
    image = [apply(*terms) for terms in zip(grams, direction, noises)]
    alpha = [n / user_sum(d, i) for n, d, i in zip(norm_next, direction, image)]
    return [e + a * d for e, a, d in zip(estimate, alpha, direction)]


def detect_inner(noise_power, own, peer, first, state):
    cells, inner, rows, users = own.shape
    half, number = inner + 1, peer.shape[1]

    def kernel(noise_ref, own_ref, peer_ref, *refs):
        out = refs[-1]
        if state:
            out[...] = refs[0][...]
        panel = lax.axis_index("panel")
        spots = [(c, i) for c in range(cells) for i in range(number)]
        sums = [own_ref[c, first + i] + peer_ref[c, i].astype(F32) for c, i in spots]
        values = conjugate_gradient(sums, [noise_ref[c] for c, _ in spots], users)
        for (c, i), value in zip(spots, values):
            out[c, pl.ds(first + i + 1 - panel, 2 * SPAD, stride=half), :] = value

    return pl.pallas_call(
        kernel,
        in_specs=[SMEM_SPEC] + [VMEM_SPEC] * (2 + len(state)),
        out_specs=VMEM_SPEC,
        out_shape=jax.ShapeDtypeStruct((cells, 2 * SPAD * half, users), F32),
        compiler_params=pltpu.CompilerParams(vmem_limit_bytes=VMEM_LIMIT),
        cost_estimate=pl.CostEstimate(
            flops=cells * number * 2 * 2 * 2 * SPAD * users * 2 * users,
            bytes_accessed=cells * inner * rows * users * 6,
            transcendentals=0,
        ),
    )(noise_power, own, peer, *state)


def detect_edge(noise_power, edge_own, edge_peer, state, onehot, symbols, rounds):
    cells, _, users = edge_own.shape
    half = state.shape[1] // (2 * SPAD)
    width = onehot.shape[1] // (2 * rounds)
    keep = symbols * half

    def kernel(noise_ref, edge_own_ref, edge_peer_ref, hot_ref, state_ref, *refs):
        *outs, full = refs
        full[...] = state_ref[...]
        sums = [edge_own_ref[c] + edge_peer_ref[c].astype(F32) for c in range(cells)]
        values = conjugate_gradient(sums, [noise_ref[c] for c in range(cells)], users)
        place = lax.axis_index("panel") * (half - 1)
        for c, value in enumerate(values):
            full[c, pl.ds(place, 2 * SPAD, stride=half), :] = value
        found = full[...].astype(BF16)
        blocks = [
            jnp.concatenate([found[c, (2 * s + k) * half : (2 * s + k + 1) * half] for s in range(symbols)], axis=0)
            for k in range(2)
            for c in range(cells)
        ]
        lhs = jnp.concatenate(blocks, axis=1)
        placed = jnp.dot(lhs, hot_ref[...], preferred_element_type=F32).astype(BF16)
        for i, out in enumerate(outs):
            for side in range(2):
                start = (2 * i + side) * width
                out[side * keep : (side + 1) * keep, :] = placed[:, start : start + width]

    return pl.pallas_call(
        kernel,
        in_specs=[SMEM_SPEC] + [VMEM_SPEC] * 4,
        out_specs=[VMEM_SPEC] * rounds,
        out_shape=[jax.ShapeDtypeStruct((2 * keep, width), BF16)] * rounds,
        scratch_shapes=[pltpu.VMEM(state.shape, F32)],
        compiler_params=pltpu.CompilerParams(vmem_limit_bytes=VMEM_LIMIT),
        cost_estimate=pl.CostEstimate(
            flops=2 * keep * onehot.shape[0] * onehot.shape[1], bytes_accessed=4 * state.size, transcendentals=0
        ),
    )(noise_power, edge_own, edge_peer, onehot, state)


def assemble(sources, mine, theirs, others, cells, per_device, symbols, half):
    rounds = sum(group.shape[0] for group in mine)
    total = 2 * rounds * 2 * half
    lanes = mine[0].shape[2]
    keep = symbols * half
    number = len(mine)

    def kernel(source_ref, *refs):
        mine_refs, theirs_refs = refs[:number], refs[number : 2 * number]
        own_other, peer_others = refs[2 * number], refs[2 * number + 1 : 3 * number + 1]
        out, gathered = refs[3 * number + 1 :]
        panel = lax.axis_index("panel")

        def place(ref, i, first, source, side):
            start = pl.multiple_of(source * (2 * half) + side * half, half)
            for s in range(symbols):
                gathered[s, pl.ds(start, half), :] = ref[i, first + s * half : first + (s + 1) * half, :]

        for side, group in ((panel, mine_refs), (1 - panel, theirs_refs)):
            n = 0
            for ref in group:
                for i in range(ref.shape[0]):
                    place(ref, i, keep, source_ref[n], side)
                    n += 1
        for side, group in ((panel, (own_other,)), (1 - panel, peer_others)):
            n = rounds
            for ref in group:
                for i in range(ref.shape[0]):
                    place(ref, i, 0, source_ref[n], side)
                    n += 1
        for s in range(symbols):
            out[:, :, s] = gathered[s].T.reshape(cells, per_device, 2, total)

    return pl.pallas_call(
        kernel,
        in_specs=[SMEM_SPEC] + [VMEM_SPEC] * (3 * number + 1),
        out_specs=VMEM_SPEC,
        out_shape=jax.ShapeDtypeStruct((cells, per_device, symbols, 2, total), BF16),
        scratch_shapes=[pltpu.VMEM((symbols, total, lanes), BF16)],
        compiler_params=pltpu.CompilerParams(vmem_limit_bytes=VMEM_LIMIT),
    )(sources, *mine, *theirs, *others)


def body(channel, received, noise_power, user_count, serving_cell):
    cells, band, _, antennas, users = channel.shape
    symbols = received.shape[3]
    half = band // 2
    n_sc, n_cell = lax.axis_size("sc"), lax.axis_size("cell")
    panel, sc, cell = lax.axis_index("panel"), lax.axis_index("sc"), lax.axis_index("cell")

    samples = jnp.transpose(received, (0, 1, 3, 2, 4))

    inner = half - 1
    count = inner * 2 // 5
    first, near, far = inner_gram(
        user_count, channel, samples, True, (1, half), count, BF16, limit=56 << 20, ends=True
    )
    first_peer = lax.ppermute(first, "panel", SWAP)
    near, far = hand_on([near, far])
    near = lax.ppermute(near, "sc", [(i, i ^ 1) for i in range(n_sc)])
    far = lax.ppermute(far, "sc", [(i, ((i - 1) ^ 1) + 1) for i in range(1, n_sc - 1)])
    (second,) = inner_gram(
        user_count, channel, samples, True, (1 + count, half + count), inner - count, BF16, limit=56 << 20
    )
    second_peer = lax.ppermute(second, "panel", SWAP)
    counts, first_peer = lax.optimization_barrier((user_count, first_peer))
    (own,) = inner_gram(counts, channel, samples, False, (1, half), inner, F32)
    state = detect_inner(noise_power, own, first_peer, 0, ())
    near, far, state = lax.optimization_barrier((near, far, state))
    edge_peer = lax.ppermute(edge_gram(user_count, channel, samples, near, far, True, BF16), "panel", SWAP)
    edge_own = edge_gram(user_count, channel, samples, near, far, False, F32)
    edge_own, second_peer = lax.optimization_barrier((edge_own, second_peer))
    state = detect_inner(noise_power, own, second_peer, count, (state,))

    capacity = cells * users // n_cell
    per_device = n_cell * capacity // n_sc
    reach = capacity // per_device
    keys = serving_cell[:, :, 0].reshape(-1)
    position = lax.iota(jnp.int32, cells * users)
    earlier = (keys[:, None] == keys[None, :]) & (position[None, :] < position[:, None])
    rank = jnp.sum(earlier.astype(jnp.int32), axis=1)
    turn = (rank // per_device - sc % reach - reach // 2) % reach * 2 + (keys // cells == sc // reach).astype(jnp.int32)
    column = ((turn * cells + keys % cells) * per_device + rank % per_device) * 2
    column = jnp.concatenate([column, column + 1])
    width = 2 * cells * per_device
    onehot = (column[:, None] == lax.iota(jnp.int32, 2 * reach * width)[None, :]).astype(BF16)

    messages = detect_edge(noise_power, edge_own, edge_peer, state, onehot, symbols, reach)
    arrived = []
    for b in [(n + reach // 2) % reach for n in range(reach)]:
        pairs = [
            (s * n_sc + j, j // reach * n_sc + s * reach + (j % reach + b) % reach)
            for s in range(n_cell)
            for j in range(n_sc)
        ]
        arrived.append(lax.ppermute(messages[len(arrived)], ("cell", "sc"), pairs))
    turns = (sc % reach - lax.iota(jnp.int32, reach) - reach // 2) % reach
    sources = jnp.concatenate([cell * reach + turns, (1 - cell) * reach + turns])
    keep = symbols * half
    mine = [jnp.stack(arrived[: reach // 2]), jnp.stack(arrived[reach // 2 :])]
    theirs = [lax.ppermute(group, "panel", SWAP) for group in mine]
    others = [lax.ppermute(jnp.stack([block[:keep] for block in arrived]), "cell", SWAP)]
    others += [lax.ppermute(group[:, :keep], "cell", SWAP) for group in theirs]
    routed = assemble(sources, mine, theirs, others, cells, per_device, symbols, half)
    return jnp.transpose(routed, (0, 1, 3, 2, 4))


def solution(mesh):
    return jax.shard_map(
        body,
        mesh=mesh,
        in_specs=(
            P("cell", "sc", None, "panel", None),
            P("cell", "sc", None, None, "panel"),
            P("cell"),
            P("cell", "sc"),
            P("cell", None, None),
        ),
        out_specs=P("cell", "sc", None, None, None),
        check_vma=False,
    )
```

```python
import jax
import jax.numpy as jnp
from jax import lax
from jax.experimental import pallas as pl
from jax.experimental.pallas import tpu as pltpu
from jax.sharding import PartitionSpec as P

F32, BF16 = jnp.float32, jnp.bfloat16
GRP = 16
SPAD = 16
VMEM_LIMIT = 40 << 20
SWAP = [(0, 1), (1, 0)]

SMEM_SPEC = pl.BlockSpec(memory_space=pltpu.SMEM)
VMEM_SPEC = pl.BlockSpec(memory_space=pltpu.VMEM)
HBM_SPEC = pl.BlockSpec(memory_space=pltpu.HBM)


def cross(product, users):
    left, right = product[:, :users], product[:, users:]
    rows = product.shape[0]
    even = lax.broadcasted_iota(jnp.int32, left.shape, 0) % 2 == 0
    return left + jnp.where(even, pltpu.roll(right, rows - 1, 0), -pltpu.roll(right, 1, 0))


def prepare(below, here, above, samples, stretch, mat, lhs):
    antennas, users = here.shape[1:]
    symbols = samples.shape[0]
    slab = 128
    lhs[2 * users : 2 * (users + symbols), :] = samples[...].reshape(2 * symbols, antennas)
    for k in range(2):
        for row in range(0, antennas, slab):
            rows = pl.ds(row, slab)
            outer = below[k, rows, :].astype(F32) + above[k, rows, :].astype(F32)
            middle = here[k, rows, :]
            value = outer + (middle + middle).astype(F32)
            value = (value if stretch is None else value * stretch).astype(BF16)
            mat[rows, k * users : (k + 1) * users] = value
            lhs[k * users : (k + 1) * users, rows] = value.T


def gram(mat, lhs, out, count, users):
    product = jnp.dot(lhs[...], mat[...], preferred_element_type=F32)
    row = lax.broadcasted_iota(jnp.int32, (users, users), 0)
    col = lax.broadcasted_iota(jnp.int32, (users, users), 1)
    real = product[:users, :users] + product[users : 2 * users, users:]
    imag = product[:users, users:] - product[users : 2 * users, :users]
    packed = jnp.where(row <= col, real, imag)
    out[:users, :] = jnp.where(jnp.maximum(row, col) < count, packed * 0.0625, 0.0).astype(out.dtype)
    lane = lax.broadcasted_iota(jnp.int32, (1, users), 1)
    scale = jnp.where(lane < count, 0.25, 0.0)
    out[users:, :] = (cross(product[2 * users :], users) * scale).astype(out.dtype)


def work_buffers(antennas, users):
    return [
        pltpu.VMEM((antennas, 2 * users), BF16),
        pltpu.VMEM((2 * users + 2 * SPAD, antennas), BF16),
    ]


def inner_gram(counts, channel, received, peer, firsts, number, dtype, limit=VMEM_LIMIT, ends=False):
    cells, band, _, antennas, users = channel.shape
    symbols = received.shape[2]
    items = cells * number

    def kernel(counts_hbm, chan, samp, out, *refs):
        end_outs, refs = (refs[:2], refs[2:]) if ends else ((), refs)
        end_refs, refs = (refs[:2], refs[2:]) if ends else ((), refs)
        count_ref, win, ybuf, mat_a, lhs_a, mat_b, lhs_b, wsem, ysem, csem, esem, osem = refs
        count_copy = pltpu.make_async_copy(counts_hbm, count_ref, csem)
        count_copy.start()
        panel, sc = lax.axis_index("panel"), lax.axis_index("sc")
        side = 1 - panel if peer else panel
        start = jnp.where(side == 0, firsts[0], firsts[1])
        end_copies = [
            pltpu.make_async_copy(chan.at[c, (band - 1) * ((sc + i + 1) % 2)], end_ref.at[c], esem.at[c, i])
            for c in range(cells)
            for i, end_ref in enumerate(end_refs)
        ]
        end_writes = [
            pltpu.make_async_copy(end_ref.at[c], end_out.at[c, 0], osem.at[c, i])
            for c in range(cells)
            for i, (end_ref, end_out) in enumerate(zip(end_refs, end_outs))
        ]

        def fetch(c, i):
            return pltpu.make_async_copy(chan.at[c, start - 1 + i], win.at[c, i], wsem.at[c, i])

        def fetch_samples(c, i):
            return pltpu.make_async_copy(samp.at[c, start + i], ybuf.at[c, i], ysem.at[c, i])

        for c in range(cells):
            for i in range(number + 2):
                fetch(c, i).start()
                if i >= 2:
                    fetch_samples(c, i - 2).start()
        for copy in end_copies:
            copy.start()
        lhs_a[...] = jnp.zeros_like(lhs_a)
        lhs_b[...] = jnp.zeros_like(lhs_b)

        def wait(item):
            c, i = item // number, item % number

            @pl.when(item < items)
            def _():
                @pl.when(i == 0)
                def _():
                    fetch(c, 0).wait()
                    fetch(c, 1).wait()

                fetch(c, i + 2).wait()
                fetch_samples(c, i).wait()

        def ready(item, mat, lhs):
            item = jnp.minimum(item, items - 1)
            c, i = item // number, item % number
            prepare(win.at[c, i], win.at[c, i + 1], win.at[c, i + 2], ybuf.at[c, i], None, mat, lhs)

        def multiply(item, mat, lhs):
            item = jnp.minimum(item, items - 1)
            c, i = item // number, item % number
            gram(mat, lhs, out.at[c, i], count_ref[c, (start + i) // GRP], users)

        count_copy.wait()
        wait(0)
        ready(0, mat_a, lhs_a)

        def step(t, carry):
            wait(2 * t + 1)
            wait(2 * t + 2)
            ready(2 * t + 1, mat_b, lhs_b)
            multiply(2 * t, mat_a, lhs_a)
            ready(2 * t + 2, mat_a, lhs_a)
            multiply(2 * t + 1, mat_b, lhs_b)
            return carry

        steps = (items + 1) // 2
        lax.fori_loop(0, steps // 2, step, 0)
        for copy, write in zip(end_copies, end_writes):
            copy.wait()
            write.start()
        lax.fori_loop(steps // 2, steps, step, 0)
        for write in end_writes:
            write.wait()

    rows = users + 2 * SPAD
    return pl.pallas_call(
        kernel,
        in_specs=[HBM_SPEC] * 3,
        out_specs=[VMEM_SPEC] + [HBM_SPEC] * (2 * ends),
        out_shape=[jax.ShapeDtypeStruct((cells, number, rows, users), dtype)]
        + [jax.ShapeDtypeStruct((cells, 1, 2, antennas, users), BF16)] * (2 * ends),
        scratch_shapes=[pltpu.VMEM((cells, 2, antennas, users), BF16)] * (2 * ends)
        + [
            pltpu.SMEM(counts.shape, jnp.int32),
            pltpu.VMEM((cells, number + 2, 2, antennas, users), BF16),
            pltpu.VMEM((cells, number, symbols, 2, antennas), BF16),
            *work_buffers(antennas, users),
            *work_buffers(antennas, users),
            pltpu.SemaphoreType.DMA((cells, number + 2)),
            pltpu.SemaphoreType.DMA((cells, number)),
            pltpu.SemaphoreType.DMA,
            pltpu.SemaphoreType.DMA((cells, 2)),
            pltpu.SemaphoreType.DMA((cells, 2)),
        ],
        compiler_params=pltpu.CompilerParams(vmem_limit_bytes=limit),
        cost_estimate=pl.CostEstimate(
            flops=items * 4 * antennas * users * 2 * (users + SPAD) // (1 if peer else 16),
            bytes_accessed=cells * (number + 2) * 4 * antennas * users // (1 if peer else 16),
            transcendentals=0,
        ),
    )(counts, channel, received)


def hand_on(arrays):
    def kernel(*refs):
        refs[-1][0] = 0

    return pl.pallas_call(
        kernel,
        in_specs=[HBM_SPEC] * len(arrays),
        out_specs=[HBM_SPEC] * len(arrays),
        out_shape=[jax.ShapeDtypeStruct(a.shape, a.dtype) for a in arrays],
        scratch_shapes=[pltpu.SMEM((1,), jnp.int32)],
        input_output_aliases={i: i for i in range(len(arrays))},
        cost_estimate=pl.CostEstimate(flops=0, bytes_accessed=8 * arrays[0].size, transcendentals=0),
    )(*arrays)


def edge_scratch(counts, symbols, antennas, users):
    cells = counts.shape[0]
    return [
        pltpu.SMEM(counts.shape, jnp.int32),
        pltpu.VMEM((cells, 3, 2, antennas, users), BF16),
        pltpu.VMEM((cells, symbols, 2, antennas), BF16),
        *work_buffers(antennas, users),
        *work_buffers(antennas, users),
        pltpu.SemaphoreType.DMA((cells, 3)),
        pltpu.SemaphoreType.DMA((cells,)),
        pltpu.SemaphoreType.DMA,
    ]


def edge_work(side, counts_hbm, chan, samp, near_ref, far_ref, out, scratch):
    count_ref, win, ybuf, mat_a, lhs_a, mat_b, lhs_b, wsem, ysem, csem = scratch
    count_copy = pltpu.make_async_copy(counts_hbm, count_ref, csem)
    cells, band, _, _, users = chan.shape
    buffers = ((mat_a, lhs_a), (mat_b, lhs_b))

    def each_copy(act, chosen):
        def run(e, halo_ref):
            for c in chosen:
                blocks = (
                    (halo_ref.at[c, 0], chan.at[c, 0], chan.at[c, 1]),
                    (chan.at[c, band - 2], chan.at[c, band - 1], halo_ref.at[c, 0]),
                )[e]
                for i, block in enumerate(blocks):
                    act(pltpu.make_async_copy(block, win.at[c, i], wsem.at[c, i]))
                act(pltpu.make_async_copy(samp.at[c, e * (band - 1)], ybuf.at[c], ysem.at[c]))

        odd = lax.axis_index("sc") % 2
        for e in range(2):
            @pl.when((side == e) & (odd != e))
            def _(e=e):
                run(e, near_ref)

            @pl.when((side == e) & (odd == e))
            def _(e=e):
                run(e, far_ref)

    def fetch():
        count_copy.start()
        each_copy(lambda copy: copy.start(), range(cells))
        lhs_a[...] = jnp.zeros_like(lhs_a)
        lhs_b[...] = jnp.zeros_like(lhs_b)

    def work():
        count_copy.wait()
        last = lax.axis_index("sc") == side * (lax.axis_size("sc") - 1)
        stretch = jnp.where(jnp.full((1, users), last.astype(jnp.int32)) == 1, 1 / 0.75, 1.0)
        for c in range(cells):
            each_copy(lambda copy: copy.wait(), (c,))
            prepare(win.at[c, 0], win.at[c, 1], win.at[c, 2], ybuf.at[c], stretch, *buffers[c % 2])
            gram(*buffers[c % 2], out.at[c], count_ref[c, side * (band - 1) // GRP], users)

    return fetch, work


def edge_gram(counts, channel, received, near, far, peer, dtype):
    cells, _, _, antennas, users = channel.shape
    symbols = received.shape[2]

    def kernel(counts_hbm, chan, samp, near_ref, far_ref, out, *scratch):
        panel = lax.axis_index("panel")
        fetch, work = edge_work(1 - panel if peer else panel, counts_hbm, chan, samp, near_ref, far_ref, out, scratch)
        fetch()
        work()

    return pl.pallas_call(
        kernel,
        in_specs=[HBM_SPEC] * 5,
        out_specs=VMEM_SPEC,
        out_shape=jax.ShapeDtypeStruct((cells, users + 2 * SPAD, users), dtype),
        scratch_shapes=edge_scratch(counts, symbols, antennas, users),
        compiler_params=pltpu.CompilerParams(vmem_limit_bytes=VMEM_LIMIT),
        cost_estimate=pl.CostEstimate(
            flops=cells * 4 * antennas * users * 2 * (users + SPAD),
            bytes_accessed=cells * 12 * antennas * users,
            transcendentals=0,
        ),
    )(counts, channel, received, near, far)


def conjugate_gradient(sums, noises, users):
    row = lax.broadcasted_iota(jnp.int32, (users, users), 0)
    col = lax.broadcasted_iota(jnp.int32, (users, users), 1)
    upper = row <= col
    grams = []
    for value in sums:
        packed = value[:users].astype(BF16)
        turned = packed.T
        real = jnp.where(upper, packed, turned)
        imag = jnp.where(row == col, jnp.zeros_like(packed), jnp.where(upper, -turned, packed))
        grams.append(jnp.concatenate([real, imag], axis=1))

    def apply(matrix, vector, noise):
        product = jnp.dot(vector.astype(BF16), matrix, preferred_element_type=F32)
        return cross(product, users) + noise * vector

    def user_sum(left, right):
        total = left * right
        even = lax.broadcasted_iota(jnp.int32, total.shape, 0) % 2 == 0
        total = total + jnp.where(even, pltpu.roll(total, 2 * SPAD - 1, 0), pltpu.roll(total, 1, 0))
        return jnp.sum(total, axis=1, keepdims=True)

    direction = [value[users:] for value in sums]
    norm = [user_sum(d, d) for d in direction]
    image = [apply(*terms) for terms in zip(grams, direction, noises)]
    alpha = [n / user_sum(d, i) for n, d, i in zip(norm, direction, image)]
    estimate = [a * d for a, d in zip(alpha, direction)]
    residual = [d - a * i for d, a, i in zip(direction, alpha, image)]
    norm_next = [user_sum(r, r) for r in residual]
    direction = [r + (m / n) * d for r, m, n, d in zip(residual, norm_next, norm, direction)]
    image = [apply(*terms) for terms in zip(grams, direction, noises)]
    alpha = [n / user_sum(d, i) for n, d, i in zip(norm_next, direction, image)]
    return [e + a * d for e, a, d in zip(estimate, alpha, direction)]


def detect_inner(noise_power, own, peer, first, state):
    cells, inner, rows, users = own.shape
    half, number = inner + 1, peer.shape[1]

    def kernel(noise_ref, own_ref, peer_ref, *refs):
        out = refs[-1]
        if state:
            out[...] = refs[0][...]
        panel = lax.axis_index("panel")
        spots = [(c, i) for c in range(cells) for i in range(number)]
        sums = [own_ref[c, first + i] + peer_ref[c, i].astype(F32) for c, i in spots]
        values = conjugate_gradient(sums, [noise_ref[c] for c, _ in spots], users)
        for (c, i), value in zip(spots, values):
            out[c, pl.ds(first + i + 1 - panel, 2 * SPAD, stride=half), :] = value

    return pl.pallas_call(
        kernel,
        in_specs=[SMEM_SPEC] + [VMEM_SPEC] * (2 + len(state)),
        out_specs=VMEM_SPEC,
        out_shape=jax.ShapeDtypeStruct((cells, 2 * SPAD * half, users), F32),
        compiler_params=pltpu.CompilerParams(vmem_limit_bytes=VMEM_LIMIT),
        cost_estimate=pl.CostEstimate(
            flops=cells * number * 2 * 2 * 2 * SPAD * users * 2 * users,
            bytes_accessed=cells * inner * rows * users * 6,
            transcendentals=0,
        ),
    )(noise_power, own, peer, *state)


def detect_edge(noise_power, edge_own, edge_peer, state, onehot, symbols, rounds):
    cells, _, users = edge_own.shape
    half = state.shape[1] // (2 * SPAD)
    width = onehot.shape[1] // (2 * rounds)
    keep = symbols * half

    def kernel(noise_ref, edge_own_ref, edge_peer_ref, hot_ref, state_ref, *refs):
        *outs, full = refs
        full[...] = state_ref[...]
        sums = [edge_own_ref[c] + edge_peer_ref[c].astype(F32) for c in range(cells)]
        values = conjugate_gradient(sums, [noise_ref[c] for c in range(cells)], users)
        place = lax.axis_index("panel") * (half - 1)
        for c, value in enumerate(values):
            full[c, pl.ds(place, 2 * SPAD, stride=half), :] = value
        found = full[...].astype(BF16)
        blocks = [
            jnp.concatenate([found[c, (2 * s + k) * half : (2 * s + k + 1) * half] for s in range(symbols)], axis=0)
            for k in range(2)
            for c in range(cells)
        ]
        lhs = jnp.concatenate(blocks, axis=1)
        placed = jnp.dot(lhs, hot_ref[...], preferred_element_type=F32).astype(BF16)
        for i, out in enumerate(outs):
            for side in range(2):
                start = (2 * i + side) * width
                out[side * keep : (side + 1) * keep, :] = placed[:, start : start + width]

    return pl.pallas_call(
        kernel,
        in_specs=[SMEM_SPEC] + [VMEM_SPEC] * 4,
        out_specs=[VMEM_SPEC] * rounds,
        out_shape=[jax.ShapeDtypeStruct((2 * keep, width), BF16)] * rounds,
        scratch_shapes=[pltpu.VMEM(state.shape, F32)],
        compiler_params=pltpu.CompilerParams(vmem_limit_bytes=VMEM_LIMIT),
        cost_estimate=pl.CostEstimate(
            flops=2 * keep * onehot.shape[0] * onehot.shape[1], bytes_accessed=4 * state.size, transcendentals=0
        ),
    )(noise_power, edge_own, edge_peer, onehot, state)


def assemble(sources, mine, theirs, others, cells, per_device, symbols, half):
    rounds = sum(group.shape[0] for group in mine)
    total = 2 * rounds * 2 * half
    lanes = mine[0].shape[2]
    keep = symbols * half
    number = len(mine)

    def kernel(source_ref, *refs):
        mine_refs, theirs_refs = refs[:number], refs[number : 2 * number]
        own_other, peer_others = refs[2 * number], refs[2 * number + 1 : 3 * number + 1]
        out, gathered = refs[3 * number + 1 :]
        panel = lax.axis_index("panel")

        def place(ref, i, first, source, side):
            start = pl.multiple_of(source * (2 * half) + side * half, half)
            for s in range(symbols):
                gathered[s, pl.ds(start, half), :] = ref[i, first + s * half : first + (s + 1) * half, :]

        for side, group in ((panel, mine_refs), (1 - panel, theirs_refs)):
            n = 0
            for ref in group:
                for i in range(ref.shape[0]):
                    place(ref, i, keep, source_ref[n], side)
                    n += 1
        for side, group in ((panel, (own_other,)), (1 - panel, peer_others)):
            n = rounds
            for ref in group:
                for i in range(ref.shape[0]):
                    place(ref, i, 0, source_ref[n], side)
                    n += 1
        for s in range(symbols):
            out[:, :, s] = gathered[s].T.reshape(cells, per_device, 2, total)

    return pl.pallas_call(
        kernel,
        in_specs=[SMEM_SPEC] + [VMEM_SPEC] * (3 * number + 1),
        out_specs=VMEM_SPEC,
        out_shape=jax.ShapeDtypeStruct((cells, per_device, symbols, 2, total), BF16),
        scratch_shapes=[pltpu.VMEM((symbols, total, lanes), BF16)],
        compiler_params=pltpu.CompilerParams(vmem_limit_bytes=VMEM_LIMIT),
    )(sources, *mine, *theirs, *others)


def body(channel, received, noise_power, user_count, serving_cell):
    cells, band, _, antennas, users = channel.shape
    symbols = received.shape[3]
    half = band // 2
    n_sc, n_cell = lax.axis_size("sc"), lax.axis_size("cell")
    panel, sc, cell = lax.axis_index("panel"), lax.axis_index("sc"), lax.axis_index("cell")

    samples = jnp.transpose(received, (0, 1, 3, 2, 4))

    inner = half - 1
    count = inner * 2 // 5
    first, near, far = inner_gram(
        user_count, channel, samples, True, (1, half), count, BF16, limit=56 << 20, ends=True
    )
    first_peer = lax.ppermute(first, "panel", SWAP)
    near, far = hand_on([near, far])
    near = lax.ppermute(near, "sc", [(i, i ^ 1) for i in range(n_sc)])
    far = lax.ppermute(far, "sc", [(i, ((i - 1) ^ 1) + 1) for i in range(1, n_sc - 1)])
    (second,) = inner_gram(
        user_count, channel, samples, True, (1 + count, half + count), inner - count, BF16, limit=56 << 20
    )
    second_peer = lax.ppermute(second, "panel", SWAP)
    counts, first_peer = lax.optimization_barrier((user_count, first_peer))
    (own,) = inner_gram(counts, channel, samples, False, (1, half), inner, F32)
    state = detect_inner(noise_power, own, first_peer, 0, ())
    near, far, state = lax.optimization_barrier((near, far, state))
    edge_peer = lax.ppermute(edge_gram(user_count, channel, samples, near, far, True, BF16), "panel", SWAP)
    edge_own = edge_gram(user_count, channel, samples, near, far, False, F32)
    edge_own, second_peer = lax.optimization_barrier((edge_own, second_peer))
    state = detect_inner(noise_power, own, second_peer, count, (state,))

    capacity = cells * users // n_cell
    per_device = n_cell * capacity // n_sc
    reach = capacity // per_device
    keys = serving_cell[:, :, 0].reshape(-1)
    position = lax.iota(jnp.int32, cells * users)
    earlier = (keys[:, None] == keys[None, :]) & (position[None, :] < position[:, None])
    rank = jnp.sum(earlier.astype(jnp.int32), axis=1)
    turn = (rank // per_device - sc % reach) % reach * 2 + (keys // cells == sc // reach).astype(jnp.int32)
    column = ((turn * cells + keys % cells) * per_device + rank % per_device) * 2
    column = jnp.concatenate([column, column + 1])
    width = 2 * cells * per_device
    onehot = (column[:, None] == lax.iota(jnp.int32, 2 * reach * width)[None, :]).astype(BF16)

    messages = detect_edge(noise_power, edge_own, edge_peer, state, onehot, symbols, reach)
    arrived = []
    for b in range(reach):
        pairs = [
            (s * n_sc + j, j // reach * n_sc + s * reach + (j % reach + b) % reach)
            for s in range(n_cell)
            for j in range(n_sc)
        ]
        message, before = messages[b], b - reach // 2
        if before >= 0:
            message, arrived[before] = lax.optimization_barrier((message, arrived[before]))
        arrived.append(lax.ppermute(message, ("cell", "sc"), pairs))
    turns = (sc % reach - lax.iota(jnp.int32, reach)) % reach
    sources = jnp.concatenate([cell * reach + turns, (1 - cell) * reach + turns])
    keep = symbols * half
    mine = [jnp.stack(arrived[: reach // 2]), jnp.stack(arrived[reach // 2 :])]
    theirs = [lax.ppermute(group, "panel", SWAP) for group in mine]
    others = [lax.ppermute(jnp.stack([block[:keep] for block in arrived]), "cell", SWAP)]
    others += [lax.ppermute(group[:, :keep], "cell", SWAP) for group in theirs]
    routed = assemble(sources, mine, theirs, others, cells, per_device, symbols, half)
    return jnp.transpose(routed, (0, 1, 3, 2, 4))


def solution(mesh):
    return jax.shard_map(
        body,
        mesh=mesh,
        in_specs=(
            P("cell", "sc", None, "panel", None),
            P("cell", "sc", None, None, "panel"),
            P("cell"),
            P("cell", "sc"),
            P("cell", None, None),
        ),
        out_specs=P("cell", "sc", None, None, None),
        check_vma=False,
    )
```

```python
import jax
import jax.numpy as jnp
from jax import lax
from jax.experimental import pallas as pl
from jax.experimental.pallas import tpu as pltpu
from jax.sharding import PartitionSpec as P

F32, BF16 = jnp.float32, jnp.bfloat16
GRP = 16
SPAD = 16
VMEM_LIMIT = 40 << 20
SWAP = [(0, 1), (1, 0)]

SMEM_SPEC = pl.BlockSpec(memory_space=pltpu.SMEM)
VMEM_SPEC = pl.BlockSpec(memory_space=pltpu.VMEM)
HBM_SPEC = pl.BlockSpec(memory_space=pltpu.HBM)


def cross(product, users):
    left, right = product[:, :users], product[:, users:]
    rows = product.shape[0]
    even = lax.broadcasted_iota(jnp.int32, left.shape, 0) % 2 == 0
    return left + jnp.where(even, pltpu.roll(right, rows - 1, 0), -pltpu.roll(right, 1, 0))


def prepare(below, here, above, samples, stretch, mat, lhs):
    antennas, users = here.shape[1:]
    symbols = samples.shape[0]
    slab = 128
    lhs[2 * users : 2 * (users + symbols), :] = samples[...].reshape(2 * symbols, antennas)
    for k in range(2):
        for row in range(0, antennas, slab):
            rows = pl.ds(row, slab)
            outer = below[k, rows, :].astype(F32) + above[k, rows, :].astype(F32)
            middle = here[k, rows, :]
            value = outer + (middle + middle).astype(F32)
            value = (value if stretch is None else value * stretch).astype(BF16)
            mat[rows, k * users : (k + 1) * users] = value
            lhs[k * users : (k + 1) * users, rows] = value.T


def gram(mat, lhs, out, count, users):
    product = jnp.dot(lhs[...], mat[...], preferred_element_type=F32)
    row = lax.broadcasted_iota(jnp.int32, (users, users), 0)
    col = lax.broadcasted_iota(jnp.int32, (users, users), 1)
    real = product[:users, :users] + product[users : 2 * users, users:]
    imag = product[:users, users:] - product[users : 2 * users, :users]
    packed = jnp.where(row <= col, real, imag)
    out[:users, :] = jnp.where(jnp.maximum(row, col) < count, packed * 0.0625, 0.0).astype(out.dtype)
    lane = lax.broadcasted_iota(jnp.int32, (1, users), 1)
    scale = jnp.where(lane < count, 0.25, 0.0)
    out[users:, :] = (cross(product[2 * users :], users) * scale).astype(out.dtype)


def work_buffers(antennas, users):
    return [
        pltpu.VMEM((antennas, 2 * users), BF16),
        pltpu.VMEM((2 * users + 2 * SPAD, antennas), BF16),
    ]


def inner_gram(counts, channel, received, peer, firsts, number, dtype, limit=VMEM_LIMIT, ends=False):
    cells, band, _, antennas, users = channel.shape
    symbols = received.shape[2]
    items = cells * number

    def kernel(counts_hbm, chan, samp, out, *refs):
        end_outs, refs = (refs[:2], refs[2:]) if ends else ((), refs)
        end_refs, refs = (refs[:2], refs[2:]) if ends else ((), refs)
        count_ref, win, ybuf, mat_a, lhs_a, mat_b, lhs_b, wsem, ysem, csem, esem, osem = refs
        count_copy = pltpu.make_async_copy(counts_hbm, count_ref, csem)
        count_copy.start()
        panel, sc = lax.axis_index("panel"), lax.axis_index("sc")
        side = 1 - panel if peer else panel
        start = jnp.where(side == 0, firsts[0], firsts[1])
        end_copies = [
            pltpu.make_async_copy(chan.at[c, (band - 1) * ((sc + i + 1) % 2)], end_ref.at[c], esem.at[c, i])
            for c in range(cells)
            for i, end_ref in enumerate(end_refs)
        ]
        end_writes = [
            pltpu.make_async_copy(end_ref.at[c], end_out.at[c, 0], osem.at[c, i])
            for c in range(cells)
            for i, (end_ref, end_out) in enumerate(zip(end_refs, end_outs))
        ]

        def fetch(c, i):
            return pltpu.make_async_copy(chan.at[c, start - 1 + i], win.at[c, i], wsem.at[c, i])

        def fetch_samples(c, i):
            return pltpu.make_async_copy(samp.at[c, start + i], ybuf.at[c, i], ysem.at[c, i])

        for c in range(cells):
            for i in range(number + 2):
                fetch(c, i).start()
                if i >= 2:
                    fetch_samples(c, i - 2).start()
        for copy in end_copies:
            copy.start()
        lhs_a[...] = jnp.zeros_like(lhs_a)
        lhs_b[...] = jnp.zeros_like(lhs_b)

        def wait(item):
            c, i = item // number, item % number

            @pl.when(item < items)
            def _():
                @pl.when(i == 0)
                def _():
                    fetch(c, 0).wait()
                    fetch(c, 1).wait()

                fetch(c, i + 2).wait()
                fetch_samples(c, i).wait()

        def ready(item, mat, lhs):
            item = jnp.minimum(item, items - 1)
            c, i = item // number, item % number
            prepare(win.at[c, i], win.at[c, i + 1], win.at[c, i + 2], ybuf.at[c, i], None, mat, lhs)

        def multiply(item, mat, lhs):
            item = jnp.minimum(item, items - 1)
            c, i = item // number, item % number
            gram(mat, lhs, out.at[c, i], count_ref[c, (start + i) // GRP], users)

        count_copy.wait()
        wait(0)
        ready(0, mat_a, lhs_a)

        def step(t, carry):
            wait(2 * t + 1)
            wait(2 * t + 2)
            ready(2 * t + 1, mat_b, lhs_b)
            multiply(2 * t, mat_a, lhs_a)
            ready(2 * t + 2, mat_a, lhs_a)
            multiply(2 * t + 1, mat_b, lhs_b)
            return carry

        steps = (items + 1) // 2
        lax.fori_loop(0, steps // 2, step, 0)
        for copy, write in zip(end_copies, end_writes):
            copy.wait()
            write.start()
        lax.fori_loop(steps // 2, steps, step, 0)
        for write in end_writes:
            write.wait()

    rows = users + 2 * SPAD
    return pl.pallas_call(
        kernel,
        in_specs=[HBM_SPEC] * 3,
        out_specs=[VMEM_SPEC] + [HBM_SPEC] * (2 * ends),
        out_shape=[jax.ShapeDtypeStruct((cells, number, rows, users), dtype)]
        + [jax.ShapeDtypeStruct((cells, 1, 2, antennas, users), BF16)] * (2 * ends),
        scratch_shapes=[pltpu.VMEM((cells, 2, antennas, users), BF16)] * (2 * ends)
        + [
            pltpu.SMEM(counts.shape, jnp.int32),
            pltpu.VMEM((cells, number + 2, 2, antennas, users), BF16),
            pltpu.VMEM((cells, number, symbols, 2, antennas), BF16),
            *work_buffers(antennas, users),
            *work_buffers(antennas, users),
            pltpu.SemaphoreType.DMA((cells, number + 2)),
            pltpu.SemaphoreType.DMA((cells, number)),
            pltpu.SemaphoreType.DMA,
            pltpu.SemaphoreType.DMA((cells, 2)),
            pltpu.SemaphoreType.DMA((cells, 2)),
        ],
        compiler_params=pltpu.CompilerParams(vmem_limit_bytes=limit),
        cost_estimate=pl.CostEstimate(
            flops=items * 4 * antennas * users * 2 * (users + SPAD) // (1 if peer else 16),
            bytes_accessed=cells * (number + 2) * 4 * antennas * users // (1 if peer else 16),
            transcendentals=0,
        ),
    )(counts, channel, received)


def hand_on(arrays):
    def kernel(*refs):
        refs[-1][0] = 0

    return pl.pallas_call(
        kernel,
        in_specs=[HBM_SPEC] * len(arrays),
        out_specs=[HBM_SPEC] * len(arrays),
        out_shape=[jax.ShapeDtypeStruct(a.shape, a.dtype) for a in arrays],
        scratch_shapes=[pltpu.SMEM((1,), jnp.int32)],
        input_output_aliases={i: i for i in range(len(arrays))},
        cost_estimate=pl.CostEstimate(flops=0, bytes_accessed=8 * arrays[0].size, transcendentals=0),
    )(*arrays)


def edge_scratch(counts, symbols, antennas, users):
    cells = counts.shape[0]
    return [
        pltpu.SMEM(counts.shape, jnp.int32),
        pltpu.VMEM((cells, 3, 2, antennas, users), BF16),
        pltpu.VMEM((cells, symbols, 2, antennas), BF16),
        *work_buffers(antennas, users),
        *work_buffers(antennas, users),
        pltpu.SemaphoreType.DMA((cells, 3)),
        pltpu.SemaphoreType.DMA((cells,)),
        pltpu.SemaphoreType.DMA,
    ]


def edge_work(side, counts_hbm, chan, samp, near_ref, far_ref, out, scratch):
    count_ref, win, ybuf, mat_a, lhs_a, mat_b, lhs_b, wsem, ysem, csem = scratch
    count_copy = pltpu.make_async_copy(counts_hbm, count_ref, csem)
    cells, band, _, _, users = chan.shape
    buffers = ((mat_a, lhs_a), (mat_b, lhs_b))

    def each_copy(act):
        def run(e, halo_ref):
            for c in range(cells):
                blocks = (
                    (halo_ref.at[c, 0], chan.at[c, 0], chan.at[c, 1]),
                    (chan.at[c, band - 2], chan.at[c, band - 1], halo_ref.at[c, 0]),
                )[e]
                for i, block in enumerate(blocks):
                    act(pltpu.make_async_copy(block, win.at[c, i], wsem.at[c, i]))
                act(pltpu.make_async_copy(samp.at[c, e * (band - 1)], ybuf.at[c], ysem.at[c]))

        odd = lax.axis_index("sc") % 2
        for e in range(2):
            @pl.when((side == e) & (odd != e))
            def _(e=e):
                run(e, near_ref)

            @pl.when((side == e) & (odd == e))
            def _(e=e):
                run(e, far_ref)

    def fetch():
        count_copy.start()
        each_copy(lambda copy: copy.start())
        lhs_a[...] = jnp.zeros_like(lhs_a)
        lhs_b[...] = jnp.zeros_like(lhs_b)

    def work():
        each_copy(lambda copy: copy.wait())
        count_copy.wait()
        last = lax.axis_index("sc") == side * (lax.axis_size("sc") - 1)
        stretch = jnp.where(jnp.full((1, users), last.astype(jnp.int32)) == 1, 1 / 0.75, 1.0)
        for c in range(cells):
            prepare(win.at[c, 0], win.at[c, 1], win.at[c, 2], ybuf.at[c], stretch, *buffers[c % 2])
        for c in range(cells):
            gram(*buffers[c % 2], out.at[c], count_ref[c, side * (band - 1) // GRP], users)

    return fetch, work


def edge_gram(counts, channel, received, near, far, peer, dtype):
    cells, _, _, antennas, users = channel.shape
    symbols = received.shape[2]

    def kernel(counts_hbm, chan, samp, near_ref, far_ref, out, *scratch):
        panel = lax.axis_index("panel")
        fetch, work = edge_work(1 - panel if peer else panel, counts_hbm, chan, samp, near_ref, far_ref, out, scratch)
        fetch()
        work()

    return pl.pallas_call(
        kernel,
        in_specs=[HBM_SPEC] * 5,
        out_specs=VMEM_SPEC,
        out_shape=jax.ShapeDtypeStruct((cells, users + 2 * SPAD, users), dtype),
        scratch_shapes=edge_scratch(counts, symbols, antennas, users),
        compiler_params=pltpu.CompilerParams(vmem_limit_bytes=VMEM_LIMIT),
        cost_estimate=pl.CostEstimate(
            flops=cells * 4 * antennas * users * 2 * (users + SPAD),
            bytes_accessed=cells * 12 * antennas * users,
            transcendentals=0,
        ),
    )(counts, channel, received, near, far)


def conjugate_gradient(sums, noises, users):
    row = lax.broadcasted_iota(jnp.int32, (users, users), 0)
    col = lax.broadcasted_iota(jnp.int32, (users, users), 1)
    upper = row <= col
    grams = []
    for value in sums:
        packed = value[:users].astype(BF16)
        turned = packed.T
        real = jnp.where(upper, packed, turned)
        imag = jnp.where(row == col, jnp.zeros_like(packed), jnp.where(upper, -turned, packed))
        grams.append(jnp.concatenate([real, imag], axis=1))

    def apply(matrix, vector, noise):
        product = jnp.dot(vector.astype(BF16), matrix, preferred_element_type=F32)
        return cross(product, users) + noise * vector

    def user_sum(left, right):
        total = left * right
        even = lax.broadcasted_iota(jnp.int32, total.shape, 0) % 2 == 0
        total = total + jnp.where(even, pltpu.roll(total, 2 * SPAD - 1, 0), pltpu.roll(total, 1, 0))
        return jnp.sum(total, axis=1, keepdims=True)

    direction = [value[users:] for value in sums]
    norm = [user_sum(d, d) for d in direction]
    image = [apply(*terms) for terms in zip(grams, direction, noises)]
    alpha = [n / user_sum(d, i) for n, d, i in zip(norm, direction, image)]
    estimate = [a * d for a, d in zip(alpha, direction)]
    residual = [d - a * i for d, a, i in zip(direction, alpha, image)]
    norm_next = [user_sum(r, r) for r in residual]
    direction = [r + (m / n) * d for r, m, n, d in zip(residual, norm_next, norm, direction)]
    image = [apply(*terms) for terms in zip(grams, direction, noises)]
    alpha = [n / user_sum(d, i) for n, d, i in zip(norm_next, direction, image)]
    return [e + a * d for e, a, d in zip(estimate, alpha, direction)]


def detect_first(noise_power, own, peer):
    cells, inner, rows, users = own.shape
    half, number = inner + 1, peer.shape[1]

    def kernel(noise_ref, own_ref, peer_ref, out):
        panel = lax.axis_index("panel")
        spots = [(c, i) for c in range(cells) for i in range(number)]
        sums = [own_ref[c, i] + peer_ref[c, i].astype(F32) for c, i in spots]
        values = conjugate_gradient(sums, [noise_ref[c] for c, _ in spots], users)
        for (c, i), value in zip(spots, values):
            out[c, pl.ds(i + 1 - panel, 2 * SPAD, stride=half), :] = value

    return pl.pallas_call(
        kernel,
        in_specs=[SMEM_SPEC] + [VMEM_SPEC] * 2,
        out_specs=VMEM_SPEC,
        out_shape=jax.ShapeDtypeStruct((cells, 2 * SPAD * half, users), F32),
        compiler_params=pltpu.CompilerParams(vmem_limit_bytes=VMEM_LIMIT),
        cost_estimate=pl.CostEstimate(
            flops=cells * number * 2 * 2 * 2 * SPAD * users * 2 * users,
            bytes_accessed=cells * inner * rows * users * 6,
            transcendentals=0,
        ),
    )(noise_power, own, peer)


def detect_last(noise_power, own, peer, edge_own, edge_peer, state, onehot, symbols, rounds):
    cells, inner, rows, users = own.shape
    half, number = inner + 1, peer.shape[1]
    width = onehot.shape[1] // (2 * rounds)
    keep = symbols * half

    def kernel(noise_ref, own_ref, peer_ref, edge_own_ref, edge_peer_ref, hot_ref, state_ref, *refs):
        *outs, full = refs
        panel = lax.axis_index("panel")
        full[...] = state_ref[...]
        first = inner - number
        spots = [(c, i) for c in range(cells) for i in range(number)]
        sums = [own_ref[c, first + i] + peer_ref[c, i].astype(F32) for c, i in spots]
        places = [(c, first + i + 1 - panel) for c, i in spots]
        sums += [edge_own_ref[c] + edge_peer_ref[c].astype(F32) for c in range(cells)]
        places += [(c, panel * (half - 1)) for c in range(cells)]
        values = conjugate_gradient(sums, [noise_ref[c] for c, _ in places], users)
        for (c, place), value in zip(places, values):
            full[c, pl.ds(place, 2 * SPAD, stride=half), :] = value
        found = full[...].astype(BF16)
        blocks = [
            jnp.concatenate([found[c, (2 * s + k) * half : (2 * s + k + 1) * half] for s in range(symbols)], axis=0)
            for k in range(2)
            for c in range(cells)
        ]
        lhs = jnp.concatenate(blocks, axis=1)
        placed = jnp.dot(lhs, hot_ref[...], preferred_element_type=F32).astype(BF16)
        for i, out in enumerate(outs):
            for side in range(2):
                start = (2 * i + side) * width
                out[side * keep : (side + 1) * keep, :] = placed[:, start : start + width]

    return pl.pallas_call(
        kernel,
        in_specs=[SMEM_SPEC] + [VMEM_SPEC] * 6,
        out_specs=[VMEM_SPEC] * rounds,
        out_shape=[jax.ShapeDtypeStruct((2 * keep, width), BF16)] * rounds,
        scratch_shapes=[pltpu.VMEM(state.shape, F32)],
        compiler_params=pltpu.CompilerParams(vmem_limit_bytes=VMEM_LIMIT),
        cost_estimate=pl.CostEstimate(
            flops=2 * keep * onehot.shape[0] * onehot.shape[1], bytes_accessed=4 * state.size, transcendentals=0
        ),
    )(noise_power, own, peer, edge_own, edge_peer, onehot, state)


def assemble(sources, mine, theirs, others, cells, per_device, symbols, half):
    rounds = sum(group.shape[0] for group in mine)
    total = 2 * rounds * 2 * half
    lanes = mine[0].shape[2]
    keep = symbols * half
    number = len(mine)

    def kernel(source_ref, *refs):
        mine_refs, theirs_refs = refs[:number], refs[number : 2 * number]
        own_other, peer_others = refs[2 * number], refs[2 * number + 1 : 3 * number + 1]
        out, gathered = refs[3 * number + 1 :]
        panel = lax.axis_index("panel")

        def place(ref, i, first, source, side):
            start = pl.multiple_of(source * (2 * half) + side * half, half)
            for s in range(symbols):
                gathered[s, pl.ds(start, half), :] = ref[i, first + s * half : first + (s + 1) * half, :]

        for side, group in ((panel, mine_refs), (1 - panel, theirs_refs)):
            n = 0
            for ref in group:
                for i in range(ref.shape[0]):
                    place(ref, i, ref.shape[1] - keep, source_ref[n], side)
                    n += 1
        for side, group in ((panel, (own_other,)), (1 - panel, peer_others)):
            n = rounds
            for ref in group:
                for i in range(ref.shape[0]):
                    place(ref, i, 0, source_ref[n], side)
                    n += 1
        for s in range(symbols):
            out[:, :, s] = gathered[s].T.reshape(cells, per_device, 2, total)

    return pl.pallas_call(
        kernel,
        in_specs=[SMEM_SPEC] + [VMEM_SPEC] * (3 * number + 1),
        out_specs=VMEM_SPEC,
        out_shape=jax.ShapeDtypeStruct((cells, per_device, symbols, 2, total), BF16),
        scratch_shapes=[pltpu.VMEM((symbols, total, lanes), BF16)],
        compiler_params=pltpu.CompilerParams(vmem_limit_bytes=VMEM_LIMIT),
    )(sources, *mine, *theirs, *others)


def body(channel, received, noise_power, user_count, serving_cell):
    cells, band, _, antennas, users = channel.shape
    symbols = received.shape[3]
    half = band // 2
    n_sc, n_cell = lax.axis_size("sc"), lax.axis_size("cell")
    panel, sc, cell = lax.axis_index("panel"), lax.axis_index("sc"), lax.axis_index("cell")

    samples = jnp.transpose(received, (0, 1, 3, 2, 4))

    inner = half - 1
    count = inner * 2 // 5
    first, near, far = inner_gram(
        user_count, channel, samples, True, (1, half), count, BF16, limit=56 << 20, ends=True
    )
    first_peer = lax.ppermute(first, "panel", SWAP)
    near, far = hand_on([near, far])
    near = lax.ppermute(near, "sc", [(i, i ^ 1) for i in range(n_sc)])
    far = lax.ppermute(far, "sc", [(i, ((i - 1) ^ 1) + 1) for i in range(1, n_sc - 1)])
    (second,) = inner_gram(
        user_count, channel, samples, True, (1 + count, half + count), inner - count, BF16, limit=56 << 20
    )
    second_peer = lax.ppermute(second, "panel", SWAP)
    counts, first_peer = lax.optimization_barrier((user_count, first_peer))
    (own,) = inner_gram(counts, channel, samples, False, (1, half), inner, F32)
    state = detect_first(noise_power, own, first_peer)
    near, far, state = lax.optimization_barrier((near, far, state))
    edge_peer = lax.ppermute(edge_gram(user_count, channel, samples, near, far, True, BF16), "panel", SWAP)
    edge_own = edge_gram(user_count, channel, samples, near, far, False, F32)

    capacity = cells * users // n_cell
    per_device = n_cell * capacity // n_sc
    reach = capacity // per_device
    keys = serving_cell[:, :, 0].reshape(-1)
    position = lax.iota(jnp.int32, cells * users)
    earlier = (keys[:, None] == keys[None, :]) & (position[None, :] < position[:, None])
    rank = jnp.sum(earlier.astype(jnp.int32), axis=1)
    turn = (rank // per_device - sc % reach) % reach * 2 + (keys // cells == sc // reach).astype(jnp.int32)
    column = ((turn * cells + keys % cells) * per_device + rank % per_device) * 2
    column = jnp.concatenate([column, column + 1])
    width = 2 * cells * per_device
    onehot = (column[:, None] == lax.iota(jnp.int32, 2 * reach * width)[None, :]).astype(BF16)

    messages = detect_last(noise_power, own, second_peer, edge_own, edge_peer, state, onehot, symbols, reach)
    arrived = []
    for b in range(reach):
        pairs = [
            (s * n_sc + j, j // reach * n_sc + s * reach + (j % reach + b) % reach)
            for s in range(n_cell)
            for j in range(n_sc)
        ]
        arrived.append(lax.ppermute(messages[b], ("cell", "sc"), pairs))
    turns = (sc % reach - lax.iota(jnp.int32, reach)) % reach
    sources = jnp.concatenate([cell * reach + turns, (1 - cell) * reach + turns])
    keep = symbols * half
    cut = reach // 2
    mine = [jnp.stack(arrived[:cut]), jnp.stack(arrived[cut:])]
    gives = jnp.stack([block[:keep] for block in arrived])
    theirs = [lax.ppermute(mine[0], "panel", SWAP)]
    theirs.append(lax.ppermute(jnp.stack([block[keep:] for block in arrived[cut:]]), "panel", SWAP))
    across = lax.ppermute(gives[cut:], ("cell", "panel"), [(i, 3 - i) for i in range(4)])
    gifts = lax.ppermute(jnp.concatenate([gives, theirs[0][:, :keep]]), "cell", SWAP)
    others = [gifts[:reach], gifts[reach:], across]
    routed = assemble(sources, mine, theirs, others, cells, per_device, symbols, half)
    return jnp.transpose(routed, (0, 1, 3, 2, 4))


def solution(mesh):
    return jax.shard_map(
        body,
        mesh=mesh,
        in_specs=(
            P("cell", "sc", None, "panel", None),
            P("cell", "sc", None, None, "panel"),
            P("cell"),
            P("cell", "sc"),
            P("cell", None, None),
        ),
        out_specs=P("cell", "sc", None, None, None),
        check_vma=False,
    )
```

```python
import jax
import jax.numpy as jnp
from jax import lax
from jax.experimental import pallas as pl
from jax.experimental.pallas import tpu as pltpu
from jax.sharding import PartitionSpec as P

F32, BF16 = jnp.float32, jnp.bfloat16
GRP = 16
SPAD = 16
VMEM_LIMIT = 40 << 20
SWAP = [(0, 1), (1, 0)]

SMEM_SPEC = pl.BlockSpec(memory_space=pltpu.SMEM)
VMEM_SPEC = pl.BlockSpec(memory_space=pltpu.VMEM)
HBM_SPEC = pl.BlockSpec(memory_space=pltpu.HBM)


def cross(product, users):
    left, right = product[:, :users], product[:, users:]
    rows = product.shape[0]
    even = lax.broadcasted_iota(jnp.int32, left.shape, 0) % 2 == 0
    return left + jnp.where(even, pltpu.roll(right, rows - 1, 0), -pltpu.roll(right, 1, 0))


def prepare(below, here, above, samples, stretch, mat, lhs):
    antennas, users = here.shape[1:]
    symbols = samples.shape[0]
    slab = 128
    lhs[2 * users : 2 * (users + symbols), :] = samples[...].reshape(2 * symbols, antennas)
    for k in range(2):
        for row in range(0, antennas, slab):
            rows = pl.ds(row, slab)
            outer = below[k, rows, :].astype(F32) + above[k, rows, :].astype(F32)
            middle = here[k, rows, :]
            value = outer + (middle + middle).astype(F32)
            value = (value if stretch is None else value * stretch).astype(BF16)
            mat[rows, k * users : (k + 1) * users] = value
            lhs[k * users : (k + 1) * users, rows] = value.T


def gram(mat, lhs, out, count, users):
    product = jnp.dot(lhs[...], mat[...], preferred_element_type=F32)
    row = lax.broadcasted_iota(jnp.int32, (users, users), 0)
    col = lax.broadcasted_iota(jnp.int32, (users, users), 1)
    real = product[:users, :users] + product[users : 2 * users, users:]
    imag = product[:users, users:] - product[users : 2 * users, :users]
    packed = jnp.where(row <= col, real, imag)
    out[:users, :] = jnp.where(jnp.maximum(row, col) < count, packed * 0.0625, 0.0).astype(out.dtype)
    lane = lax.broadcasted_iota(jnp.int32, (1, users), 1)
    scale = jnp.where(lane < count, 0.25, 0.0)
    out[users:, :] = (cross(product[2 * users :], users) * scale).astype(out.dtype)


def work_buffers(antennas, users):
    return [
        pltpu.VMEM((antennas, 2 * users), BF16),
        pltpu.VMEM((2 * users + 2 * SPAD, antennas), BF16),
    ]


def inner_gram(counts, channel, received, peer, firsts, number, dtype, limit=VMEM_LIMIT, ends=False):
    cells, band, _, antennas, users = channel.shape
    symbols = received.shape[2]
    items = cells * number

    def kernel(counts_hbm, chan, samp, out, *refs):
        end_outs, refs = (refs[:2], refs[2:]) if ends else ((), refs)
        end_refs, refs = (refs[:2], refs[2:]) if ends else ((), refs)
        count_ref, win, ybuf, mat_a, lhs_a, mat_b, lhs_b, wsem, ysem, csem, esem, osem = refs
        count_copy = pltpu.make_async_copy(counts_hbm, count_ref, csem)
        count_copy.start()
        panel, sc = lax.axis_index("panel"), lax.axis_index("sc")
        side = 1 - panel if peer else panel
        start = jnp.where(side == 0, firsts[0], firsts[1])
        end_copies = [
            pltpu.make_async_copy(chan.at[c, (band - 1) * ((sc + i + 1) % 2)], end_ref.at[c], esem.at[c, i])
            for c in range(cells)
            for i, end_ref in enumerate(end_refs)
        ]
        end_writes = [
            pltpu.make_async_copy(end_ref.at[c], end_out.at[c, 0], osem.at[c, i])
            for c in range(cells)
            for i, (end_ref, end_out) in enumerate(zip(end_refs, end_outs))
        ]

        def fetch(c, i):
            return pltpu.make_async_copy(chan.at[c, start - 1 + i], win.at[c, i], wsem.at[c, i])

        def fetch_samples(c, i):
            return pltpu.make_async_copy(samp.at[c, start + i], ybuf.at[c, i], ysem.at[c, i])

        for c in range(cells):
            for i in range(number + 2):
                fetch(c, i).start()
                if i >= 2:
                    fetch_samples(c, i - 2).start()
        for copy in end_copies:
            copy.start()
        for lhs in (lhs_a, lhs_b):
            lhs[2 * users :, :] = jnp.zeros((2 * SPAD, lhs.shape[1]), BF16)

        def wait(item):
            c, i = item // number, item % number

            @pl.when(item < items)
            def _():
                @pl.when(i == 0)
                def _():
                    fetch(c, 0).wait()
                    fetch(c, 1).wait()

                fetch(c, i + 2).wait()
                fetch_samples(c, i).wait()

        def ready(item, mat, lhs):
            item = jnp.minimum(item, items - 1)
            c, i = item // number, item % number
            prepare(win.at[c, i], win.at[c, i + 1], win.at[c, i + 2], ybuf.at[c, i], None, mat, lhs)

        def multiply(item, mat, lhs):
            item = jnp.minimum(item, items - 1)
            c, i = item // number, item % number
            gram(mat, lhs, out.at[c, i], count_ref[c, (start + i) // GRP], users)

        count_copy.wait()
        wait(0)
        ready(0, mat_a, lhs_a)

        def step(t, carry):
            wait(2 * t + 1)
            wait(2 * t + 2)
            ready(2 * t + 1, mat_b, lhs_b)
            multiply(2 * t, mat_a, lhs_a)
            ready(2 * t + 2, mat_a, lhs_a)
            multiply(2 * t + 1, mat_b, lhs_b)
            return carry

        steps = (items + 1) // 2
        lax.fori_loop(0, steps // 2, step, 0)
        for copy, write in zip(end_copies, end_writes):
            copy.wait()
            write.start()
        lax.fori_loop(steps // 2, steps, step, 0)
        for write in end_writes:
            write.wait()

    rows = users + 2 * SPAD
    return pl.pallas_call(
        kernel,
        in_specs=[HBM_SPEC] * 3,
        out_specs=[VMEM_SPEC] + [HBM_SPEC] * (2 * ends),
        out_shape=[jax.ShapeDtypeStruct((cells, number, rows, users), dtype)]
        + [jax.ShapeDtypeStruct((cells, 1, 2, antennas, users), BF16)] * (2 * ends),
        scratch_shapes=[pltpu.VMEM((cells, 2, antennas, users), BF16)] * (2 * ends)
        + [
            pltpu.SMEM(counts.shape, jnp.int32),
            pltpu.VMEM((cells, number + 2, 2, antennas, users), BF16),
            pltpu.VMEM((cells, number, symbols, 2, antennas), BF16),
            *work_buffers(antennas, users),
            *work_buffers(antennas, users),
            pltpu.SemaphoreType.DMA((cells, number + 2)),
            pltpu.SemaphoreType.DMA((cells, number)),
            pltpu.SemaphoreType.DMA,
            pltpu.SemaphoreType.DMA((cells, 2)),
            pltpu.SemaphoreType.DMA((cells, 2)),
        ],
        compiler_params=pltpu.CompilerParams(vmem_limit_bytes=limit),
        cost_estimate=pl.CostEstimate(
            flops=items * 4 * antennas * users * 2 * (users + SPAD) // (1 if peer else 16),
            bytes_accessed=cells * (number + 2) * 4 * antennas * users // (1 if peer else 16),
            transcendentals=0,
        ),
    )(counts, channel, received)


def hand_on(arrays):
    def kernel(*refs):
        refs[-1][0] = 0

    return pl.pallas_call(
        kernel,
        in_specs=[HBM_SPEC] * len(arrays),
        out_specs=[HBM_SPEC] * len(arrays),
        out_shape=[jax.ShapeDtypeStruct(a.shape, a.dtype) for a in arrays],
        scratch_shapes=[pltpu.SMEM((1,), jnp.int32)],
        input_output_aliases={i: i for i in range(len(arrays))},
        cost_estimate=pl.CostEstimate(flops=0, bytes_accessed=8 * arrays[0].size, transcendentals=0),
    )(*arrays)


def edge_scratch(counts, symbols, antennas, users):
    cells = counts.shape[0]
    return [
        pltpu.SMEM(counts.shape, jnp.int32),
        pltpu.VMEM((cells, 3, 2, antennas, users), BF16),
        pltpu.VMEM((cells, symbols, 2, antennas), BF16),
        *work_buffers(antennas, users),
        *work_buffers(antennas, users),
        pltpu.SemaphoreType.DMA((cells, 3)),
        pltpu.SemaphoreType.DMA((cells,)),
        pltpu.SemaphoreType.DMA,
    ]


def edge_work(side, counts_hbm, chan, samp, near_ref, far_ref, out, scratch):
    count_ref, win, ybuf, mat_a, lhs_a, mat_b, lhs_b, wsem, ysem, csem = scratch
    count_copy = pltpu.make_async_copy(counts_hbm, count_ref, csem)
    cells, band, _, _, users = chan.shape
    buffers = ((mat_a, lhs_a), (mat_b, lhs_b))

    def each_copy(act):
        def run(e, halo_ref):
            for c in range(cells):
                blocks = (
                    (halo_ref.at[c, 0], chan.at[c, 0], chan.at[c, 1]),
                    (chan.at[c, band - 2], chan.at[c, band - 1], halo_ref.at[c, 0]),
                )[e]
                for i, block in enumerate(blocks):
                    act(pltpu.make_async_copy(block, win.at[c, i], wsem.at[c, i]))
                act(pltpu.make_async_copy(samp.at[c, e * (band - 1)], ybuf.at[c], ysem.at[c]))

        odd = lax.axis_index("sc") % 2
        for e in range(2):
            @pl.when((side == e) & (odd != e))
            def _(e=e):
                run(e, near_ref)

            @pl.when((side == e) & (odd == e))
            def _(e=e):
                run(e, far_ref)

    def fetch():
        count_copy.start()
        each_copy(lambda copy: copy.start())
        for lhs in (lhs_a, lhs_b):
            lhs[2 * users :, :] = jnp.zeros((2 * SPAD, lhs.shape[1]), BF16)

    def work():
        each_copy(lambda copy: copy.wait())
        count_copy.wait()
        last = lax.axis_index("sc") == side * (lax.axis_size("sc") - 1)
        stretch = jnp.where(jnp.full((1, users), last.astype(jnp.int32)) == 1, 1 / 0.75, 1.0)
        for c in range(cells):
            prepare(win.at[c, 0], win.at[c, 1], win.at[c, 2], ybuf.at[c], stretch, *buffers[c % 2])
        for c in range(cells):
            gram(*buffers[c % 2], out.at[c], count_ref[c, side * (band - 1) // GRP], users)

    return fetch, work


def edge_gram(counts, channel, received, near, far, peer, dtype):
    cells, _, _, antennas, users = channel.shape
    symbols = received.shape[2]

    def kernel(counts_hbm, chan, samp, near_ref, far_ref, out, *scratch):
        panel = lax.axis_index("panel")
        fetch, work = edge_work(1 - panel if peer else panel, counts_hbm, chan, samp, near_ref, far_ref, out, scratch)
        fetch()
        work()

    return pl.pallas_call(
        kernel,
        in_specs=[HBM_SPEC] * 5,
        out_specs=VMEM_SPEC,
        out_shape=jax.ShapeDtypeStruct((cells, users + 2 * SPAD, users), dtype),
        scratch_shapes=edge_scratch(counts, symbols, antennas, users),
        compiler_params=pltpu.CompilerParams(vmem_limit_bytes=VMEM_LIMIT),
        cost_estimate=pl.CostEstimate(
            flops=cells * 4 * antennas * users * 2 * (users + SPAD),
            bytes_accessed=cells * 12 * antennas * users,
            transcendentals=0,
        ),
    )(counts, channel, received, near, far)


def conjugate_gradient(sums, noises, users):
    row = lax.broadcasted_iota(jnp.int32, (users, users), 0)
    col = lax.broadcasted_iota(jnp.int32, (users, users), 1)
    upper = row <= col
    grams = []
    for value in sums:
        packed = value[:users].astype(BF16)
        turned = packed.T
        real = jnp.where(upper, packed, turned)
        imag = jnp.where(row == col, jnp.zeros_like(packed), jnp.where(upper, -turned, packed))
        grams.append(jnp.concatenate([real, imag], axis=1))

    def apply(matrix, vector, noise):
        product = jnp.dot(vector.astype(BF16), matrix, preferred_element_type=F32)
        return cross(product, users) + noise * vector

    def user_sum(left, right):
        total = left * right
        even = lax.broadcasted_iota(jnp.int32, total.shape, 0) % 2 == 0
        total = total + jnp.where(even, pltpu.roll(total, 2 * SPAD - 1, 0), pltpu.roll(total, 1, 0))
        return jnp.sum(total, axis=1, keepdims=True)

    direction = [value[users:] for value in sums]
    norm = [user_sum(d, d) for d in direction]
    image = [apply(*terms) for terms in zip(grams, direction, noises)]
    alpha = [n / user_sum(d, i) for n, d, i in zip(norm, direction, image)]
    estimate = [a * d for a, d in zip(alpha, direction)]
    residual = [d - a * i for d, a, i in zip(direction, alpha, image)]
    norm_next = [user_sum(r, r) for r in residual]
    direction = [r + (m / n) * d for r, m, n, d in zip(residual, norm_next, norm, direction)]
    image = [apply(*terms) for terms in zip(grams, direction, noises)]
    alpha = [n / user_sum(d, i) for n, d, i in zip(norm_next, direction, image)]
    return [e + a * d for e, a, d in zip(estimate, alpha, direction)]


def detect_first(noise_power, own, peer):
    cells, inner, rows, users = own.shape
    half, number = inner + 1, peer.shape[1]

    def kernel(noise_ref, own_ref, peer_ref, out):
        panel = lax.axis_index("panel")
        spots = [(c, i) for c in range(cells) for i in range(number)]
        sums = [own_ref[c, i] + peer_ref[c, i].astype(F32) for c, i in spots]
        values = conjugate_gradient(sums, [noise_ref[c] for c, _ in spots], users)
        for (c, i), value in zip(spots, values):
            out[c, pl.ds(i + 1 - panel, 2 * SPAD, stride=half), :] = value

    return pl.pallas_call(
        kernel,
        in_specs=[SMEM_SPEC] + [VMEM_SPEC] * 2,
        out_specs=VMEM_SPEC,
        out_shape=jax.ShapeDtypeStruct((cells, 2 * SPAD * half, users), F32),
        compiler_params=pltpu.CompilerParams(vmem_limit_bytes=VMEM_LIMIT),
        cost_estimate=pl.CostEstimate(
            flops=cells * number * 2 * 2 * 2 * SPAD * users * 2 * users,
            bytes_accessed=cells * inner * rows * users * 6,
            transcendentals=0,
        ),
    )(noise_power, own, peer)


def detect_last(noise_power, own, peer, edge_own, edge_peer, state, onehot, symbols, rounds):
    cells, inner, rows, users = own.shape
    half, number = inner + 1, peer.shape[1]
    width = onehot.shape[1] // (2 * rounds)
    keep = symbols * half

    def kernel(noise_ref, own_ref, peer_ref, edge_own_ref, edge_peer_ref, hot_ref, state_ref, *refs):
        *outs, full = refs
        panel = lax.axis_index("panel")
        full[...] = state_ref[...]
        first = inner - number
        spots = [(c, i) for c in range(cells) for i in range(number)]
        sums = [own_ref[c, first + i] + peer_ref[c, i].astype(F32) for c, i in spots]
        places = [(c, first + i + 1 - panel) for c, i in spots]
        sums += [edge_own_ref[c] + edge_peer_ref[c].astype(F32) for c in range(cells)]
        places += [(c, panel * (half - 1)) for c in range(cells)]
        values = conjugate_gradient(sums, [noise_ref[c] for c, _ in places], users)
        for (c, place), value in zip(places, values):
            full[c, pl.ds(place, 2 * SPAD, stride=half), :] = value
        found = full[...].astype(BF16)
        blocks = [
            jnp.concatenate([found[c, (2 * s + k) * half : (2 * s + k + 1) * half] for s in range(symbols)], axis=0)
            for k in range(2)
            for c in range(cells)
        ]
        lhs = jnp.concatenate(blocks, axis=1)
        placed = jnp.dot(lhs, hot_ref[...], preferred_element_type=F32).astype(BF16)
        for i, out in enumerate(outs):
            for side in range(2):
                start = (2 * i + side) * width
                out[side * keep : (side + 1) * keep, :] = placed[:, start : start + width]

    return pl.pallas_call(
        kernel,
        in_specs=[SMEM_SPEC] + [VMEM_SPEC] * 6,
        out_specs=[VMEM_SPEC] * rounds,
        out_shape=[jax.ShapeDtypeStruct((2 * keep, width), BF16)] * rounds,
        scratch_shapes=[pltpu.VMEM(state.shape, F32)],
        compiler_params=pltpu.CompilerParams(vmem_limit_bytes=VMEM_LIMIT),
        cost_estimate=pl.CostEstimate(
            flops=2 * keep * onehot.shape[0] * onehot.shape[1], bytes_accessed=4 * state.size, transcendentals=0
        ),
    )(noise_power, own, peer, edge_own, edge_peer, onehot, state)


def assemble(sources, mine, theirs, others, cells, per_device, symbols, half):
    rounds = sum(group.shape[0] for group in mine)
    total = 2 * rounds * 2 * half
    lanes = mine[0].shape[2]
    keep = symbols * half
    number = len(mine)

    def kernel(source_ref, *refs):
        mine_refs, theirs_refs = refs[:number], refs[number : 2 * number]
        own_other, peer_others = refs[2 * number], refs[2 * number + 1 : 3 * number + 1]
        out, gathered, turned, sems = refs[3 * number + 1 :]
        panel = lax.axis_index("panel")

        def place(ref, i, first, source, side):
            start = pl.multiple_of(source * (2 * half) + side * half, half)
            for s in range(symbols):
                gathered[s, pl.ds(start, half), :] = ref[i, first + s * half : first + (s + 1) * half, :]

        for side, group in ((panel, mine_refs), (1 - panel, theirs_refs)):
            n = 0
            for ref in group:
                for i in range(ref.shape[0]):
                    place(ref, i, keep, source_ref[n], side)
                    n += 1
        for side, group in ((panel, (own_other,)), (1 - panel, peer_others)):
            n = rounds
            for ref in group:
                for i in range(ref.shape[0]):
                    place(ref, i, 0, source_ref[n], side)
                    n += 1
        copies = []
        for n, (first, last) in enumerate(((0, symbols // 2), (symbols // 2, symbols))):
            for s in range(first, last):
                turned[:, :, s] = gathered[s].T.reshape(cells, per_device, 2, total)
            part = (slice(None), slice(None), pl.ds(first, last - first))
            copies.append(pltpu.make_async_copy(turned.at[part], out.at[part], sems.at[n]))
            copies[-1].start()
        for copy in copies:
            copy.wait()

    return pl.pallas_call(
        kernel,
        in_specs=[SMEM_SPEC] + [VMEM_SPEC] * (3 * number + 1),
        out_specs=HBM_SPEC,
        out_shape=jax.ShapeDtypeStruct((cells, per_device, symbols, 2, total), BF16),
        scratch_shapes=[
            pltpu.VMEM((symbols, total, lanes), BF16),
            pltpu.VMEM((cells, per_device, symbols, 2, total), BF16),
            pltpu.SemaphoreType.DMA((2,)),
        ],
        compiler_params=pltpu.CompilerParams(vmem_limit_bytes=VMEM_LIMIT),
    )(sources, *mine, *theirs, *others)


def body(channel, received, noise_power, user_count, serving_cell):
    cells, band, _, antennas, users = channel.shape
    symbols = received.shape[3]
    half = band // 2
    n_sc, n_cell = lax.axis_size("sc"), lax.axis_size("cell")
    panel, sc, cell = lax.axis_index("panel"), lax.axis_index("sc"), lax.axis_index("cell")

    samples = jnp.transpose(received, (0, 1, 3, 2, 4))

    inner = half - 1
    count = inner * 2 // 5
    first, near, far = inner_gram(
        user_count, channel, samples, True, (1, half), count, BF16, limit=56 << 20, ends=True
    )
    first_peer = lax.ppermute(first, "panel", SWAP)
    near, far = hand_on([near, far])
    near = lax.ppermute(near, "sc", [(i, i ^ 1) for i in range(n_sc)])
    far = lax.ppermute(far, "sc", [(i, ((i - 1) ^ 1) + 1) for i in range(1, n_sc - 1)])
    (second,) = inner_gram(
        user_count, channel, samples, True, (1 + count, half + count), inner - count, BF16, limit=56 << 20
    )
    second_peer = lax.ppermute(second, "panel", SWAP)
    counts, first_peer = lax.optimization_barrier((user_count, first_peer))
    (own,) = inner_gram(counts, channel, samples, False, (1, half), inner, F32)
    state = detect_first(noise_power, own, first_peer)
    near, far, state = lax.optimization_barrier((near, far, state))
    edge_peer = lax.ppermute(edge_gram(user_count, channel, samples, near, far, True, BF16), "panel", SWAP)
    edge_own = edge_gram(user_count, channel, samples, near, far, False, F32)

    capacity = cells * users // n_cell
    per_device = n_cell * capacity // n_sc
    reach = capacity // per_device
    keys = serving_cell[:, :, 0].reshape(-1)
    position = lax.iota(jnp.int32, cells * users)
    earlier = (keys[:, None] == keys[None, :]) & (position[None, :] < position[:, None])
    rank = jnp.sum(earlier.astype(jnp.int32), axis=1)
    turn = (rank // per_device - sc % reach) % reach * 2 + (keys // cells == sc // reach).astype(jnp.int32)
    column = ((turn * cells + keys % cells) * per_device + rank % per_device) * 2
    column = jnp.concatenate([column, column + 1])
    width = 2 * cells * per_device
    onehot = (column[:, None] == lax.iota(jnp.int32, 2 * reach * width)[None, :]).astype(BF16)

    messages = detect_last(noise_power, own, second_peer, edge_own, edge_peer, state, onehot, symbols, reach)
    arrived = []
    for b in range(reach):
        pairs = [
            (s * n_sc + j, j // reach * n_sc + s * reach + (j % reach + b) % reach)
            for s in range(n_cell)
            for j in range(n_sc)
        ]
        arrived.append(lax.ppermute(messages[b], ("cell", "sc"), pairs))
    turns = (sc % reach - lax.iota(jnp.int32, reach)) % reach
    sources = jnp.concatenate([cell * reach + turns, (1 - cell) * reach + turns])
    keep = symbols * half
    mine = [jnp.stack(arrived[: reach // 2]), jnp.stack(arrived[reach // 2 :])]
    theirs = [lax.ppermute(group, "panel", SWAP) for group in mine]
    others = [lax.ppermute(jnp.stack([block[:keep] for block in arrived]), "cell", SWAP)]
    others += [lax.ppermute(group[:, :keep], "cell", SWAP) for group in theirs]
    routed = assemble(sources, mine, theirs, others, cells, per_device, symbols, half)
    return jnp.transpose(routed, (0, 1, 3, 2, 4))


def solution(mesh):
    return jax.shard_map(
        body,
        mesh=mesh,
        in_specs=(
            P("cell", "sc", None, "panel", None),
            P("cell", "sc", None, None, "panel"),
            P("cell"),
            P("cell", "sc"),
            P("cell", None, None),
        ),
        out_specs=P("cell", "sc", None, None, None),
        check_vma=False,
    )
```
